32 devices in a mesh: space: 16 (over z, y, x), dp: 2 (over core).
Axes of the slice: x: 2, y: 2, z: 4, core: 2. Of those that a mesh axis runs over, the one named last changes fastest.
Arguments:
- volumes: bfloat16 [2, 4, 64, 32, 32], P('dp', None, 'space'), may hold values from -6 to 6
- kernel_one: bfloat16 [32, 4, 3, 3, 3], replicated, may hold values from -0.625 to 0.625
- kernel_two: bfloat16 [64, 32, 3, 3, 3], replicated, may hold values from -0.21875 to 0.21875
- cotangent: bfloat16 [2, 64, 32, 256], P('dp', None, 'space'), may hold values from -6 to 6
Outputs:
- features: bfloat16 [2, 64, 32, 256], P('dp', None, 'space')
- pooled_grad: bfloat16 [2, 32, 32, 256], P('dp', None, 'space')
- grad_one: float32 [3456], P('space')
- grad_two: float32 [55296], P('space')
The draws below stay inside these ranges and needn't reach their ends.
All inputs are finite; a program needn't handle non-finite values.
Results may differ from the reference program's by a relative error of at most 0.006.
Values may be sent and summed in bfloat16 or wider, within the bound.
No kernel may reach another device: no remote copies, remote signals or barrier semaphores. Data moves between devices by JAX's collectives and lax.ppermute only.
A program may use at most 64 MiB of HBM per device.

```python
import jax
import jax.numpy as jnp
from jax import lax

CIN = 4
C1 = 32
C2 = 64
W = 32
VOLS = 2
NX = 64


def level_of(rng, extent, split, least, largest):
    loudness = 1.0
    for dim, blocks in split:
        draws = jax.random.uniform(jax.random.fold_in(jax.random.fold_in(rng, 6), dim), (blocks,), jnp.float32, least / len(split), largest / len(split))
        loudness = loudness * jnp.repeat(jnp.exp(draws), extent[dim] // blocks).reshape((-1,) + (1,) * (len(extent) - 1 - dim))
    return loudness


def centred(stream_key, shape, width, limit, cuts=(), dtype=jnp.bfloat16):
    loudness = level_of(stream_key, shape, cuts, -0.22, 0.18) if cuts else 1.0
    array = jax.random.normal(stream_key, shape, jnp.float32) * width * loudness
    return jnp.minimum(jnp.maximum(array, -limit), limit).astype(dtype)


def setup_inputs(seed: int = 0) -> dict:
    key_list = jax.random.split(jax.random.key(seed), 5)
    volumes = centred(key_list[0], (VOLS, CIN, NX, W, W), 1.0, 6.0, ((0, 2), (2, 16)))
    kernel_one = centred(key_list[1], (C1, CIN, 3, 3, 3), (CIN * 27) ** -0.5, 0.625)
    kernel_two = centred(key_list[2], (C2, C1, 3, 3, 3), (C1 * 27) ** -0.5, 0.21875)
    cotangent = centred(key_list[3], (VOLS, C2, NX // 2, (W // 2) * (W // 2)), 1.0, 6.0, ((0, 2), (2, 16)))
    return dict(volumes=volumes, kernel_one=kernel_one, kernel_two=kernel_two, cotangent=cotangent)


def silu(v):
    return v * jax.nn.sigmoid(v)

def dsilu(v):
    s = jax.nn.sigmoid(v)
    return s * (1.0 + v * (1.0 - s))

def conv_same(inputs, kernel):
    return lax.conv_general_dilated(inputs[None], kernel, (1, 1, 1), [(1, 1), (1, 1), (1, 1)], dimension_numbers=('NCDHW', 'OIDHW', 'NCDHW'), precision=lax.Precision.HIGHEST)[0]

def kernel_grad(inputs, delta):
    padded = jnp.pad(inputs, ((0, 0), (1, 1), (1, 1), (1, 1)))
    result = lax.conv_general_dilated(padded[:, None], delta[:, None], (1, 1, 1), 'VALID', dimension_numbers=('NCDHW', 'OIDHW', 'NCDHW'), precision=lax.Precision.HIGHEST)
    return jnp.transpose(result, (1, 0, 2, 3, 4))

def pool_cells(field):
    chans, depth, rows, cols = field.shape
    return field.reshape(chans, depth // 2, 2, rows // 2, 2, cols // 2, 2).mean(axis=(2, 4, 6))

def spread_cells(field):
    return jnp.repeat(jnp.repeat(jnp.repeat(field, 2, axis=1), 2, axis=2), 2, axis=3) * 0.125

def reference(volumes, kernel_one, kernel_two, cotangent):
    first = kernel_one.astype(jnp.float32)
    second = kernel_two.astype(jnp.float32)
    flipped = jnp.transpose(jnp.flip(second, (2, 3, 4)), (1, 0, 2, 3, 4))
    half = W // 2

    def one_volume(pair):
        volume, cot_flat = pair
        cot = cot_flat.reshape(cot_flat.shape[0], cot_flat.shape[1], half, half)
        inputs = volume.astype(jnp.float32)
        pre_one = conv_same(inputs, first)
        pooled = pool_cells(silu(pre_one)).astype(jnp.bfloat16)
        pooled_f = lax.optimization_barrier(pooled).astype(jnp.float32)
        pre_two = conv_same(pooled_f, second)
        feats = silu(pre_two).astype(jnp.bfloat16)
        delta_two = (cot.astype(jnp.float32) * dsilu(pre_two)).astype(jnp.bfloat16)
        delta_two_f = lax.optimization_barrier(delta_two).astype(jnp.float32)
        pgrad = conv_same(delta_two_f, flipped).astype(jnp.bfloat16)
        pgrad_f = lax.optimization_barrier(pgrad).astype(jnp.float32)
        delta_one = (spread_cells(pgrad_f) * dsilu(pre_one)).astype(jnp.bfloat16)
        delta_one_f = lax.optimization_barrier(delta_one).astype(jnp.float32)
        term_one = kernel_grad(inputs, delta_one_f)
        term_two = kernel_grad(pooled_f, delta_two_f)
        feats_flat = feats.reshape(feats.shape[0], feats.shape[1], half * half)
        pgrad_flat = pgrad.reshape(pgrad.shape[0], pgrad.shape[1], half * half)
        return (feats_flat, pgrad_flat, term_one, term_two)
    feats, pgrad, terms_one, terms_two = lax.map(one_volume, (volumes, cotangent))
    count = VOLS * NX * W * W
    grad_one = lax.optimization_barrier(jnp.sum(terms_one, axis=0)) / jnp.sqrt(jnp.float32(count))
    grad_two = lax.optimization_barrier(jnp.sum(terms_two, axis=0)) / jnp.sqrt(jnp.float32(count // 8))
    return (feats, pgrad, grad_one.reshape(-1), grad_two.reshape(-1))
```

```python
import functools
import math

import jax
import jax.numpy as jnp
import numpy as np
from jax import lax
from jax.experimental import pallas as pl
from jax.experimental.pallas import tpu as pltpu
from jax.sharding import PartitionSpec as P

F32 = jnp.float32
BF16 = jnp.bfloat16
SHIFTS = [(dy, dx) for dy in (-1, 0, 1) for dx in (-1, 0, 1)]
NN = (((1,), (0,)), ((), ()))
NT = (((1,), (1,)), ((), ()))
LANES = 1024
ONE_AT = 896


def dot(a, b, dims=NN):
    return lax.dot_general(a, b, dims, preferred_element_type=F32)


def shifted(field, width, dy, dx):
    cells = field.shape[1]
    move = dy * width + dx
    if move == 0:
        return field
    lane = lax.broadcasted_iota(jnp.int32, field.shape, 1)
    row, col = lane // width, lane % width
    keep = None
    for pos, step in ((row, dy), (col, dx)):
        if step:
            ok = pos < width - 1 if step > 0 else pos > 0
            keep = ok if keep is None else keep & ok
    return jnp.where(keep, pltpu.roll(field, (-move) % cells, 1), 0.0)


def silu_parts(v):
    s = 0.5 + 0.5 * jnp.tanh(0.5 * v)
    return v * s, s


def band_maps():
    to_kernel = np.zeros((4, 216, 108), np.float32)
    to_flat = np.zeros((4, 216, 128), np.float32)
    for p in range(4):
        for s in range(9):
            for dz in range(3):
                q = p + dz - 1
                for ci in range(4):
                    if 0 <= q <= 3:
                        row = 16 * s + 4 * q + ci
                    else:
                        row = 144 + 8 * s + (0 if q < 0 else 4) + ci
                    tap = 9 * dz + s
                    to_kernel[p, row, 4 * tap + ci] = 1
                    to_flat[p, row, 64 * (ci // 2) + 27 * (ci % 2) + tap] = 1
    return to_kernel, to_flat


def kernel_body(
    count,
    vl_ref, vo_ref, vr_ref, vl2_ref, vr2_ref,
    cot_ref, cl_ref, cr_ref, k1_ref, k2t_ref, k2_ref, to_kernel_ref, to_flat_ref,
    feat_ref, pgrad_ref, send_ref,
):
    slabs = lax.axis_size("space")
    me = lax.axis_index("space")
    half = 16

    left, own, right = (r[...].astype(F32) for r in (vl_ref, vo_ref, vr_ref))
    far_left, far_right = vl2_ref[...].astype(F32), vr2_ref[...].astype(F32)
    top = lax.broadcasted_iota(jnp.int32, (8, LANES), 0) < 4

    def edge(before, after):
        return jnp.where(top, pltpu.roll(before, 4, 0), pltpu.roll(after, 4, 0))

    edges = (
        edge(far_left, own[0:8]),
        edge(left[8:16], right[0:8]),
        edge(own[8:16], far_right),
    )
    stack = jnp.concatenate([left, own, right, *edges], axis=0)
    moved = [shifted(stack, 2 * half, dy, dx) for dy, dx in SHIFTS]
    patches = []
    for g in range(3):
        rows = [m[16 * g : 16 * g + 16] for m in moved] + [m[48 + 8 * g : 56 + 8 * g] for m in moved]
        patches.append(jnp.concatenate(rows, axis=0).astype(BF16))

    banded = jnp.concatenate(
        [dot(k1_ref[...], to_kernel_ref[p], NT).astype(BF16) for p in range(4)], axis=0
    )

    cell = lax.broadcasted_iota(jnp.int32, (LANES, half * half), 0)
    block = lax.broadcasted_iota(jnp.int32, (LANES, half * half), 1)
    pool = jnp.where((cell // 64) * half + (cell % 32) // 2 == block, 0.125, 0.0).astype(BF16)

    sums = []
    slope_one = None
    for g in range(3):
        pre = dot(banded, patches[g])
        act, s = silu_parts(pre)
        if g == 1:
            slope_one = s + act * (1.0 - s)
        sums += [act[0:32] + act[32:64], act[64:96] + act[96:128]]
    sums = jnp.concatenate(sums, axis=0)
    high = sums.astype(BF16)
    low = (sums - high.astype(F32)).astype(BF16)
    pooled = dot(high, pool) + dot(low, pool)
    plane = lax.broadcasted_iota(jnp.int32, pooled.shape, 0) // 32
    inside = ((plane >= 2) | (me > 0)) & ((plane < 4) | (me < slabs - 1))
    pooled = jnp.where(inside, pooled, 0.0).astype(BF16).astype(F32)

    moved = [shifted(pooled, half, dy, dx).astype(BF16) for dy, dx in SHIFTS]
    columns = [
        jnp.concatenate(
            [m[32 * (p + dz) : 32 * (p + dz) + 32] for dz in range(3) for m in moved], axis=0
        )
        for p in range(4)
    ]

    cots = (cl_ref[...], cot_ref[0], cot_ref[1], cr_ref[...])
    deltas = []
    for p in range(4):
        pre = dot(k2t_ref[...], columns[p])
        act, s = silu_parts(pre)
        if 1 <= p <= 2:
            feat_ref[p - 1] = act.astype(BF16)
        deltas.append((cots[p].astype(F32) * (s + act * (1.0 - s))).astype(BF16))

    flipped = jnp.concatenate([k2_ref[576:864], k2_ref[288:576], k2_ref[0:288]], axis=1)
    grads = []
    for p in range(2):
        taps = dot(flipped, jnp.concatenate(deltas[p : p + 3], axis=0))
        total = jnp.zeros((32, half * half), F32)
        for s, (dy, dx) in enumerate(SHIFTS):
            total = total + shifted(taps[32 * (8 - s) : 32 * (8 - s) + 32], half, dy, dx)
        grads.append(total.astype(BF16))
        pgrad_ref[p] = grads[p]

    term_two = dot(deltas[1], columns[1], NT) + dot(deltas[2], columns[2], NT)
    send_ref[:, 0:864] = (term_two * (1.0 / math.sqrt(count // 8))).astype(BF16)

    spread = dot(jnp.concatenate(grads, axis=0), pool, NT)
    spread = jnp.concatenate([spread[0:32], spread[0:32], spread[32:64], spread[32:64]], axis=0)
    delta_one = (spread * slope_one).astype(BF16)
    wide = dot(delta_one, patches[1], NT)
    high = wide.astype(BF16)
    low = (wide - high.astype(F32)).astype(BF16)
    term_one = jnp.zeros((32, 128), F32)
    for p in range(4):
        for part in (high, low):
            term_one = term_one + dot(part[32 * p : 32 * p + 32], to_flat_ref[p])
    term_one = (term_one * (1.0 / math.sqrt(count))).astype(BF16)
    to = lax.broadcasted_iota(jnp.int32, (64, 32), 0)
    at = lax.broadcasted_iota(jnp.int32, (64, 32), 1)
    even = dot(jnp.where(to == 2 * at, 1.0, 0.0).astype(BF16), term_one)
    odd = dot(jnp.where(to == 2 * at + 1, 1.0, 0.0).astype(BF16), term_one)
    rows = even + pltpu.roll(odd, 64, 1)
    send_ref[:, ONE_AT:LANES] = rows.astype(BF16)
    send_ref[:, 864:ONE_AT] = jnp.zeros((64, ONE_AT - 864), BF16)


def on_device(volumes, kernel_one, kernel_two, cotangent):
    _, cin, planes, width, _ = volumes.shape
    half = width // 2
    slabs = lax.axis_size("space")
    copies = lax.axis_size("dp")
    count = copies * planes * slabs * width * width

    rows = jnp.transpose(volumes[0], (1, 0, 2, 3)).reshape(planes * cin, width * width)
    cot = jnp.transpose(cotangent[0], (1, 0, 2))

    def from_left(block, far=1):
        return lax.ppermute(block, "space", [(i, i + far) for i in range(slabs - far)])

    def from_right(block, far=1):
        return lax.ppermute(block, "space", [(i + far, i) for i in range(slabs - far)])

    vl, vr = from_left(rows), from_right(rows)
    vl2, vr2 = from_left(rows[8:16], 2), from_right(rows[0:8], 2)
    cl, cr = from_left(cot[1]), from_right(cot[0])

    k1 = jnp.transpose(kernel_one, (0, 2, 3, 4, 1)).reshape(32, 108)
    k2 = jnp.transpose(kernel_two, (2, 3, 4, 1, 0)).reshape(864, 64)
    k2t = jnp.transpose(k2)
    to_kernel, to_flat = band_maps()

    feat, pgrad, send = pl.pallas_call(
        functools.partial(kernel_body, count),
        out_shape=(
            jax.ShapeDtypeStruct((2, 64, 256), BF16),
            jax.ShapeDtypeStruct((2, 32, 256), BF16),
            jax.ShapeDtypeStruct((64, LANES), BF16),
        ),
        compiler_params=pltpu.CompilerParams(vmem_limit_bytes=48 * 1024 * 1024),
        cost_estimate=pl.CostEstimate(flops=10**9, bytes_accessed=2 * 10**6, transcendentals=10**6),
    )(vl, rows, vr, vl2, vr2, cot, cl, cr, k1, k2t, k2, jnp.asarray(to_kernel, BF16), jnp.asarray(to_flat, BF16))

    share = 64 // slabs
    blocks = jnp.broadcast_to(
        send.reshape(slabs, 1, share, LANES), (slabs, copies, share, LANES)
    ).reshape(slabs * copies, share, LANES)
    parts = lax.all_to_all(blocks, ("space", "dp"), 0, 0, tiled=True)
    total = jnp.sum(parts.astype(F32), axis=0)
    grad_two = jnp.transpose(total[:, :864].reshape(share, 27, 32), (0, 2, 1)).reshape(-1)
    grad_one = total[:, ONE_AT : ONE_AT + 54].reshape(-1)
    features = jnp.transpose(feat, (1, 0, 2))[None]
    pooled_grad = jnp.transpose(pgrad, (1, 0, 2))[None]
    return (features, pooled_grad, grad_one, grad_two)


def solution(mesh):
    in_specs = (P("dp", None, "space", None, None), P(), P(), P("dp", None, "space", None))
    out_specs = (P("dp", None, "space", None), P("dp", None, "space", None), P("space"), P("space"))
    return jax.shard_map(
        on_device, mesh=mesh, in_specs=in_specs, out_specs=out_specs, check_vma=False
    )
```

```python
import functools
import math

import jax
import jax.numpy as jnp
import numpy as np
from jax import lax
from jax.experimental import pallas as pl
from jax.experimental.pallas import tpu as pltpu
from jax.sharding import PartitionSpec as P

F32 = jnp.float32
BF16 = jnp.bfloat16
SHIFTS = [(dy, dx) for dy in (-1, 0, 1) for dx in (-1, 0, 1)]
NN = (((1,), (0,)), ((), ()))
NT = (((1,), (1,)), ((), ()))
LANES = 1024
ONE_AT = 896


def dot(a, b, dims=NN):
    return lax.dot_general(a, b, dims, preferred_element_type=F32)


def shifted(field, width, dy, dx):
    cells = field.shape[1]
    move = dy * width + dx
    if move == 0:
        return field
    lane = lax.broadcasted_iota(jnp.int32, field.shape, 1)
    row, col = lane // width, lane % width
    keep = None
    for pos, step in ((row, dy), (col, dx)):
        if step:
            ok = pos < width - 1 if step > 0 else pos > 0
            keep = ok if keep is None else keep & ok
    return jnp.where(keep, pltpu.roll(field, (-move) % cells, 1), 0.0)


def silu_parts(v):
    s = 0.5 + 0.5 * jnp.tanh(0.5 * v)
    return v * s, s


def band_maps():
    to_kernel = np.zeros((4, 216, 108), np.float32)
    to_flat = np.zeros((4, 216, 128), np.float32)
    for p in range(4):
        for s in range(9):
            for dz in range(3):
                q = p + dz - 1
                for ci in range(4):
                    if 0 <= q <= 3:
                        row = 16 * s + 4 * q + ci
                    else:
                        row = 144 + 8 * s + (0 if q < 0 else 4) + ci
                    tap = 9 * dz + s
                    to_kernel[p, row, 4 * tap + ci] = 1
                    to_flat[p, row, 64 * (ci // 2) + 27 * (ci % 2) + tap] = 1
    return to_kernel, to_flat


def kernel_body(
    count,
    own_ref, cot_ref, near_ref, next_ref, far_near_ref, far_next_ref,
    k1_ref, k2t_ref, k2_ref, to_kernel_ref, to_flat_ref,
    feat_ref, pgrad_ref, send_ref,
):
    slabs = lax.axis_size("space")
    me = lax.axis_index("space")
    half = 16

    def unfold(block, rows):
        return jnp.concatenate([block[rows * b : rows * b + rows] for b in range(4)], axis=1)

    odd, upper = me % 2 == 1, (me // 2) % 2 == 1
    own = unfold(own_ref[...].astype(F32), 16)
    near, following = near_ref[...].astype(F32), next_ref[...].astype(F32)
    left = unfold(jnp.where(odd, near, following)[0:64], 16)
    right = unfold(jnp.where(odd, following, near)[0:64], 16)
    cot_left = jnp.where(odd, near, following)[64:128]
    cot_right = jnp.where(odd, following, near)[64:128]
    far_near, far_next = far_near_ref[...].astype(F32), far_next_ref[...].astype(F32)
    far_left = unfold(jnp.where(upper, far_near, far_next), 8)
    far_right = unfold(jnp.where(upper, far_next, far_near), 8)
    top = lax.broadcasted_iota(jnp.int32, (8, LANES), 0) < 4

    def edge(before, after):
        return jnp.where(top, pltpu.roll(before, 4, 0), pltpu.roll(after, 4, 0))

    edges = (
        edge(far_left, own[0:8]),
        edge(left[8:16], right[0:8]),
        edge(own[8:16], far_right),
    )
    stack = jnp.concatenate([left, own, right, *edges], axis=0)
    moved = [shifted(stack, 2 * half, dy, dx) for dy, dx in SHIFTS]
    patches = []
    for g in range(3):
        rows = [m[16 * g : 16 * g + 16] for m in moved] + [m[48 + 8 * g : 56 + 8 * g] for m in moved]
        patches.append(jnp.concatenate(rows, axis=0).astype(BF16))

    banded = jnp.concatenate(
        [dot(k1_ref[...], to_kernel_ref[p], NT).astype(BF16) for p in range(4)], axis=0
    )

    cell = lax.broadcasted_iota(jnp.int32, (LANES, half * half), 0)
    block = lax.broadcasted_iota(jnp.int32, (LANES, half * half), 1)
    pool = jnp.where((cell // 64) * half + (cell % 32) // 2 == block, 0.125, 0.0).astype(BF16)

    sums = []
    slope_one = None
    for g in range(3):
        pre = dot(banded, patches[g])
        act, s = silu_parts(pre)
        if g == 1:
            slope_one = s + act * (1.0 - s)
        sums += [act[0:32] + act[32:64], act[64:96] + act[96:128]]
    sums = jnp.concatenate(sums, axis=0)
    high = sums.astype(BF16)
    low = (sums - high.astype(F32)).astype(BF16)
    pooled = dot(high, pool) + dot(low, pool)
    plane = lax.broadcasted_iota(jnp.int32, pooled.shape, 0) // 32
    inside = ((plane >= 2) | (me > 0)) & ((plane < 4) | (me < slabs - 1))
    pooled = jnp.where(inside, pooled, 0.0).astype(BF16).astype(F32)

    moved = [shifted(pooled, half, dy, dx).astype(BF16) for dy, dx in SHIFTS]
    columns = [
        jnp.concatenate(
            [m[32 * (p + dz) : 32 * (p + dz) + 32] for dz in range(3) for m in moved], axis=0
        )
        for p in range(4)
    ]

    cots = (cot_left, cot_ref[0], cot_ref[1], cot_right)
    deltas = []
    for p in range(4):
        pre = dot(k2t_ref[...], columns[p])
        act, s = silu_parts(pre)
        if 1 <= p <= 2:
            feat_ref[p - 1] = act.astype(BF16)
        deltas.append((cots[p].astype(F32) * (s + act * (1.0 - s))).astype(BF16))

    flipped = jnp.concatenate([k2_ref[576:864], k2_ref[288:576], k2_ref[0:288]], axis=1)
    grads = []
    for p in range(2):
        taps = dot(flipped, jnp.concatenate(deltas[p : p + 3], axis=0))
        total = jnp.zeros((32, half * half), F32)
        for s, (dy, dx) in enumerate(SHIFTS):
            total = total + shifted(taps[32 * (8 - s) : 32 * (8 - s) + 32], half, dy, dx)
        grads.append(total.astype(BF16))
        pgrad_ref[p] = grads[p]

    term_two = dot(deltas[1], columns[1], NT) + dot(deltas[2], columns[2], NT)
    send_ref[:, 0:864] = (term_two * (1.0 / math.sqrt(count // 8))).astype(BF16)

    spread = dot(jnp.concatenate(grads, axis=0), pool, NT)
    spread = jnp.concatenate([spread[0:32], spread[0:32], spread[32:64], spread[32:64]], axis=0)
    delta_one = (spread * slope_one).astype(BF16)
    wide = dot(delta_one, patches[1], NT)
    high = wide.astype(BF16)
    low = (wide - high.astype(F32)).astype(BF16)
    term_one = jnp.zeros((32, 128), F32)
    for p in range(4):
        for part in (high, low):
            term_one = term_one + dot(part[32 * p : 32 * p + 32], to_flat_ref[p])
    term_one = (term_one * (1.0 / math.sqrt(count))).astype(BF16)
    to = lax.broadcasted_iota(jnp.int32, (64, 32), 0)
    at = lax.broadcasted_iota(jnp.int32, (64, 32), 1)
    even = dot(jnp.where(to == 2 * at, 1.0, 0.0).astype(BF16), term_one)
    odd = dot(jnp.where(to == 2 * at + 1, 1.0, 0.0).astype(BF16), term_one)
    rows = even + pltpu.roll(odd, 64, 1)
    send_ref[:, ONE_AT:LANES] = rows.astype(BF16)
    send_ref[:, 864:ONE_AT] = jnp.zeros((64, ONE_AT - 864), BF16)


def on_device(volumes, kernel_one, kernel_two, cotangent):
    _, cin, planes, width, _ = volumes.shape
    half = width // 2
    slabs = lax.axis_size("space")
    copies = lax.axis_size("dp")
    count = copies * planes * slabs * width * width

    rows = jnp.transpose(volumes[0].reshape(cin, planes, 4, width * width // 4), (2, 1, 0, 3))
    rows = rows.reshape(4 * planes * cin, width * width // 4)
    cot = jnp.transpose(cotangent[0], (1, 0, 2))
    me = lax.axis_index("space")

    def swap(block, pairs):
        pairs = [p for p in pairs if max(p) < slabs]
        return lax.ppermute(block, "space", pairs + [(t, f) for f, t in pairs])

    def outer(low, high, is_high):
        return jnp.where(is_high, high, low)

    odd, upper = me % 2 == 1, (me // 2) % 2 == 1
    by_plane = rows.reshape(4, 2, 8, width * width // 4)
    first, last = (by_plane[:, i].reshape(32, -1) for i in range(2))
    evens = range(0, slabs, 2)
    fours = [i + j for i in range(0, slabs, 4) for j in range(2)]
    far_near = swap(outer(last, first, upper), [(i, i + 2) for i in fours])
    far_next = swap(outer(first, last, upper), [(i + 2, i + 4) for i in fours])
    near = swap(
        jnp.concatenate([rows, outer(cot[1], cot[0], odd)], axis=0), [(i, i + 1) for i in evens]
    )
    following = swap(
        jnp.concatenate([rows, outer(cot[0], cot[1], odd)], axis=0),
        [(i + 1, i + 2) for i in evens],
    )

    k1 = jnp.transpose(kernel_one, (0, 2, 3, 4, 1)).reshape(32, 108)
    k2 = jnp.transpose(kernel_two, (2, 3, 4, 1, 0)).reshape(864, 64)
    k2t = jnp.transpose(k2)
    to_kernel, to_flat = band_maps()

    feat, pgrad, send = pl.pallas_call(
        functools.partial(kernel_body, count),
        out_shape=(
            jax.ShapeDtypeStruct((2, 64, 256), BF16),
            jax.ShapeDtypeStruct((2, 32, 256), BF16),
            jax.ShapeDtypeStruct((64, LANES), BF16),
        ),
        compiler_params=pltpu.CompilerParams(vmem_limit_bytes=48 * 1024 * 1024),
        cost_estimate=pl.CostEstimate(flops=10**9, bytes_accessed=2 * 10**6, transcendentals=10**6),
    )(rows, cot, near, following, far_near, far_next, k1, k2t, k2, jnp.asarray(to_kernel, BF16), jnp.asarray(to_flat, BF16))

    share = 64 // slabs
    blocks = jnp.broadcast_to(
        send.reshape(slabs, 1, share, LANES), (slabs, copies, share, LANES)
    ).reshape(slabs * copies, share, LANES)
    parts = lax.all_to_all(blocks, ("space", "dp"), 0, 0, tiled=True)
    total = jnp.sum(parts.astype(F32), axis=0)
    grad_two = jnp.transpose(total[:, :864].reshape(share, 27, 32), (0, 2, 1)).reshape(-1)
    grad_one = total[:, ONE_AT : ONE_AT + 54].reshape(-1)
    features = jnp.transpose(feat, (1, 0, 2))[None]
    pooled_grad = jnp.transpose(pgrad, (1, 0, 2))[None]
    return (features, pooled_grad, grad_one, grad_two)


def solution(mesh):
    in_specs = (P("dp", None, "space", None, None), P(), P(), P("dp", None, "space", None))
    out_specs = (P("dp", None, "space", None), P("dp", None, "space", None), P("space"), P("space"))
    return jax.shard_map(
        on_device, mesh=mesh, in_specs=in_specs, out_specs=out_specs, check_vma=False
    )
```

```python
import functools
import math

import jax
import jax.numpy as jnp
import numpy as np
from jax import lax
from jax.experimental import pallas as pl
from jax.experimental.pallas import tpu as pltpu
from jax.sharding import PartitionSpec as P

F32 = jnp.float32
BF16 = jnp.bfloat16
SHIFTS = [(dy, dx) for dy in (-1, 0, 1) for dx in (-1, 0, 1)]
NN = (((1,), (0,)), ((), ()))
NT = (((1,), (1,)), ((), ()))
LANES = 1024
ONE_AT = 896


def dot(a, b, dims=NN):
    return lax.dot_general(a, b, dims, preferred_element_type=F32)


def shifted(field, width, dy, dx):
    cells = field.shape[1]
    move = dy * width + dx
    if move == 0:
        return field
    lane = lax.broadcasted_iota(jnp.int32, field.shape, 1)
    row, col = lane // width, lane % width
    keep = None
    for pos, step in ((row, dy), (col, dx)):
        if step:
            ok = pos < width - 1 if step > 0 else pos > 0
            keep = ok if keep is None else keep & ok
    return jnp.where(keep, pltpu.roll(field, (-move) % cells, 1), 0.0)


def silu_parts(v):
    s = 0.5 + 0.5 * jnp.tanh(0.5 * v)
    return v * s, s


def band_maps():
    to_kernel = np.zeros((4, 216, 108), np.float32)
    to_flat = np.zeros((4, 216, 128), np.float32)
    for p in range(4):
        for s in range(9):
            for dz in range(3):
                q = p + dz - 1
                for ci in range(4):
                    if 0 <= q <= 3:
                        row = 16 * s + 4 * q + ci
                    else:
                        row = 144 + 8 * s + (0 if q < 0 else 4) + ci
                    tap = 9 * dz + s
                    to_kernel[p, row, 4 * tap + ci] = 1
                    to_flat[p, row, 64 * (ci // 2) + 27 * (ci % 2) + tap] = 1
    return to_kernel, to_flat


def kernel_body(
    count,
    own_ref, cot_ref, near_ref, next_ref, far_near_ref, far_next_ref,
    k1_ref, k2t_ref, k2_ref, to_kernel_ref, to_flat_ref,
    feat_ref, pgrad_ref, send_ref,
):
    slabs = lax.axis_size("space")
    me = lax.axis_index("space")
    half = 16

    def unfold(block, rows):
        return jnp.concatenate([block[rows * b : rows * b + rows] for b in range(4)], axis=1)

    odd, upper = me % 2 == 1, (me // 2) % 2 == 1
    own = unfold(own_ref[...].astype(F32), 16)
    near, following = near_ref[...].astype(F32), next_ref[...].astype(F32)
    left = unfold(jnp.where(odd, near, following)[0:64], 16)
    right = unfold(jnp.where(odd, following, near)[0:64], 16)
    cot_left = jnp.where(odd, near, following)[64:128]
    cot_right = jnp.where(odd, following, near)[64:128]
    far_near, far_next = far_near_ref[...].astype(F32), far_next_ref[...].astype(F32)
    far_left = unfold(jnp.where(upper, far_near, far_next), 8)
    far_right = unfold(jnp.where(upper, far_next, far_near), 8)
    top = lax.broadcasted_iota(jnp.int32, (8, LANES), 0) < 4

    def edge(before, after):
        return jnp.where(top, pltpu.roll(before, 4, 0), pltpu.roll(after, 4, 0))

    edges = (
        edge(far_left, own[0:8]),
        edge(left[8:16], right[0:8]),
        edge(own[8:16], far_right),
    )
    stack = jnp.concatenate([left, own, right, *edges], axis=0)
    moved = [shifted(stack, 2 * half, dy, dx) for dy, dx in SHIFTS]
    patches = []
    for g in range(3):
        rows = [m[16 * g : 16 * g + 16] for m in moved] + [m[48 + 8 * g : 56 + 8 * g] for m in moved]
        patches.append(jnp.concatenate(rows, axis=0).astype(BF16))

    banded = jnp.concatenate(
        [dot(k1_ref[...], to_kernel_ref[p], NT).astype(BF16) for p in range(4)], axis=0
    )

    cell = lax.broadcasted_iota(jnp.int32, (LANES, half * half), 0)
    block = lax.broadcasted_iota(jnp.int32, (LANES, half * half), 1)
    pool = jnp.where((cell // 64) * half + (cell % 32) // 2 == block, 0.125, 0.0).astype(BF16)

    sums = []
    slope_one = None
    for g in range(3):
        pre = dot(banded, patches[g])
        act, s = silu_parts(pre)
        if g == 1:
            slope_one = s + act * (1.0 - s)
        sums += [act[0:32] + act[32:64], act[64:96] + act[96:128]]
    sums = jnp.concatenate(sums, axis=0)
    high = sums.astype(BF16)
    low = (sums - high.astype(F32)).astype(BF16)
    pooled = dot(high, pool) + dot(low, pool)
    plane = lax.broadcasted_iota(jnp.int32, pooled.shape, 0) // 32
    inside = ((plane >= 2) | (me > 0)) & ((plane < 4) | (me < slabs - 1))
    pooled = jnp.where(inside, pooled, 0.0).astype(BF16).astype(F32)

    moved = [shifted(pooled, half, dy, dx).astype(BF16) for dy, dx in SHIFTS]
    columns = [
        jnp.concatenate(
            [m[32 * (p + dz) : 32 * (p + dz) + 32] for dz in range(3) for m in moved], axis=0
        )
        for p in range(4)
    ]

    cots = (cot_left, cot_ref[0], cot_ref[1], cot_right)
    deltas = []
    for p in range(4):
        pre = dot(k2t_ref[...], columns[p])
        act, s = silu_parts(pre)
        if 1 <= p <= 2:
            feat_ref[p - 1] = act.astype(BF16)
        deltas.append((cots[p].astype(F32) * (s + act * (1.0 - s))).astype(BF16))

    flipped = jnp.concatenate([k2_ref[576:864], k2_ref[288:576], k2_ref[0:288]], axis=1)
    grads = []
    for p in range(2):
        taps = dot(flipped, jnp.concatenate(deltas[p : p + 3], axis=0))
        total = jnp.zeros((32, half * half), F32)
        for s, (dy, dx) in enumerate(SHIFTS):
            total = total + shifted(taps[32 * (8 - s) : 32 * (8 - s) + 32], half, dy, dx)
        grads.append(total.astype(BF16))
        pgrad_ref[p] = grads[p]

    term_two = dot(deltas[1], columns[1], NT) + dot(deltas[2], columns[2], NT)
    send_ref[:, 0:864] = (term_two * (1.0 / math.sqrt(count // 8))).astype(BF16)

    spread = dot(jnp.concatenate(grads, axis=0), pool, NT)
    spread = jnp.concatenate([spread[0:32], spread[0:32], spread[32:64], spread[32:64]], axis=0)
    delta_one = (spread * slope_one).astype(BF16)
    wide = dot(delta_one, patches[1], NT)
    high = wide.astype(BF16)
    low = (wide - high.astype(F32)).astype(BF16)
    term_one = jnp.zeros((32, 128), F32)
    for p in range(4):
        for part in (high, low):
            term_one = term_one + dot(part[32 * p : 32 * p + 32], to_flat_ref[p])
    term_one = (term_one * (1.0 / math.sqrt(count))).astype(BF16)
    to = lax.broadcasted_iota(jnp.int32, (64, 32), 0)
    at = lax.broadcasted_iota(jnp.int32, (64, 32), 1)
    even = dot(jnp.where(to == 2 * at, 1.0, 0.0).astype(BF16), term_one)
    odd = dot(jnp.where(to == 2 * at + 1, 1.0, 0.0).astype(BF16), term_one)
    rows = even + pltpu.roll(odd, 64, 1)
    send_ref[:, ONE_AT:LANES] = rows.astype(BF16)
    send_ref[:, 864:ONE_AT] = jnp.zeros((64, ONE_AT - 864), BF16)


def on_device(volumes, kernel_one, kernel_two, cotangent):
    _, cin, planes, width, _ = volumes.shape
    half = width // 2
    slabs = lax.axis_size("space")
    copies = lax.axis_size("dp")
    count = copies * planes * slabs * width * width

    rows = jnp.transpose(volumes[0].reshape(cin, planes, 4, width * width // 4), (2, 1, 0, 3))
    rows = rows.reshape(4 * planes * cin, width * width // 4)
    cot = jnp.transpose(cotangent[0], (1, 0, 2))
    me = lax.axis_index("space")

    def swap(block, pairs):
        pairs = [p for p in pairs if max(p) < slabs]
        return lax.ppermute(block, "space", pairs + [(t, f) for f, t in pairs])

    def outer(low, high, is_high):
        return jnp.where(is_high, high, low)

    odd, upper = me % 2 == 1, (me // 2) % 2 == 1
    by_plane = rows.reshape(4, 2, 8, width * width // 4)
    first, last = (by_plane[:, i].reshape(32, -1) for i in range(2))
    evens = range(0, slabs, 2)
    fours = [i + j for i in range(0, slabs, 4) for j in range(2)]
    far_near = swap(outer(last, first, upper), [(i, i + 2) for i in fours])
    far_next = swap(outer(first, last, upper), [(i + 2, i + 4) for i in fours])
    near = swap(
        jnp.concatenate([rows, outer(cot[1], cot[0], odd)], axis=0), [(i, i + 1) for i in evens]
    )
    following = swap(
        jnp.concatenate([rows, outer(cot[0], cot[1], odd)], axis=0),
        [(i + 1, i + 2) for i in evens],
    )

    k1 = jnp.transpose(kernel_one, (0, 2, 3, 4, 1)).reshape(32, 108)
    k2 = jnp.transpose(kernel_two, (2, 3, 4, 1, 0)).reshape(864, 64)
    k2t = jnp.transpose(k2)
    to_kernel, to_flat = band_maps()

    feat, pgrad, send = pl.pallas_call(
        functools.partial(kernel_body, count),
        out_shape=(
            jax.ShapeDtypeStruct((2, 64, 256), BF16),
            jax.ShapeDtypeStruct((2, 32, 256), BF16),
            jax.ShapeDtypeStruct((64, LANES), BF16),
        ),
        compiler_params=pltpu.CompilerParams(vmem_limit_bytes=48 * 1024 * 1024),
        cost_estimate=pl.CostEstimate(flops=10**9, bytes_accessed=2 * 10**6, transcendentals=10**6),
    )(rows, cot, near, following, far_near, far_next, k1, k2t, k2, jnp.asarray(to_kernel, BF16), jnp.asarray(to_flat, BF16))

    share = 64 // slabs
    parts = lax.all_to_all(send.reshape(slabs, share, LANES), "space", 0, 0, tiled=True)
    total = jnp.sum(parts.astype(F32), axis=0)
    step = 1
    while step < copies:
        total = total + lax.ppermute(total, "dp", [(i, i ^ step) for i in range(copies)])
        step *= 2
    grad_two = jnp.transpose(total[:, :864].reshape(share, 27, 32), (0, 2, 1)).reshape(-1)
    grad_one = total[:, ONE_AT : ONE_AT + 54].reshape(-1)
    features = jnp.transpose(feat, (1, 0, 2))[None]
    pooled_grad = jnp.transpose(pgrad, (1, 0, 2))[None]
    return (features, pooled_grad, grad_one, grad_two)


def solution(mesh):
    in_specs = (P("dp", None, "space", None, None), P(), P(), P("dp", None, "space", None))
    out_specs = (P("dp", None, "space", None), P("dp", None, "space", None), P("space"), P("space"))
    return jax.shard_map(
        on_device, mesh=mesh, in_specs=in_specs, out_specs=out_specs, check_vma=False
    )
```

```python
import functools
import math

import jax
import jax.numpy as jnp
import numpy as np
from jax import lax
from jax.experimental import pallas as pl
from jax.experimental.pallas import tpu as pltpu
from jax.sharding import PartitionSpec as P

F32 = jnp.float32
BF16 = jnp.bfloat16
SHIFTS = [(dy, dx) for dy in (-1, 0, 1) for dx in (-1, 0, 1)]
NN = (((1,), (0,)), ((), ()))
NT = (((1,), (1,)), ((), ()))
LANES = 1024
ONE_AT = 896


def dot(a, b, dims=NN):
    return lax.dot_general(a, b, dims, preferred_element_type=F32)


def shifted(field, width, dy, dx):
    cells = field.shape[1]
    move = dy * width + dx
    if move == 0:
        return field
    lane = lax.broadcasted_iota(jnp.int32, field.shape, 1)
    row, col = lane // width, lane % width
    keep = None
    for pos, step in ((row, dy), (col, dx)):
        if step:
            ok = pos < width - 1 if step > 0 else pos > 0
            keep = ok if keep is None else keep & ok
    return jnp.where(keep, pltpu.roll(field, (-move) % cells, 1), 0.0)


def silu_parts(v):
    s = 0.5 + 0.5 * jnp.tanh(0.5 * v)
    return v * s, s


def band_maps():
    to_kernel = np.zeros((4, 216, 108), np.float32)
    to_flat = np.zeros((4, 216, 128), np.float32)
    for p in range(4):
        for s in range(9):
            for dz in range(3):
                q = p + dz - 1
                for ci in range(4):
                    if 0 <= q <= 3:
                        row = 16 * s + 4 * q + ci
                    else:
                        row = 144 + 8 * s + (0 if q < 0 else 4) + ci
                    tap = 9 * dz + s
                    to_kernel[p, row, 4 * tap + ci] = 1
                    to_flat[p, row, 64 * (ci // 2) + 27 * (ci % 2) + tap] = 1
    return to_kernel, to_flat


def tap_order():
    order = np.zeros((27, 32, 32, 27), np.float32)
    for tap in range(27):
        for ch in range(32):
            order[tap, ch, ch, tap] = 1
    return order.reshape(864, 864)


def prepare_body(
    vol_hbm, cot_hbm, next_ref, near_ref, far_next_ref, far_near_ref,
    vol_ref, cot_ref, cells_ref, sems,
):
    me = lax.axis_index("space")
    odd, upper = me % 2 == 1, (me // 2) % 2 == 1
    vol_copy = pltpu.make_async_copy(vol_hbm, vol_ref, sems.at[0])
    cot_copy = pltpu.make_async_copy(cot_hbm, cot_ref, sems.at[1])
    vol_copy.start()
    cot_copy.start()
    vol_copy.wait()
    cin, planes, width = vol_ref.shape[1:4]
    for plane in range(planes):
        for ch in range(cin):
            at = (plane * cin + ch) * width
            cells_ref[at : at + width] = vol_ref[0, ch, plane].astype(F32)
    count = planes * cin
    for b in range(4):
        lines = [cells_ref[pl.ds(8 * b + y, count, stride=width), :] for y in range(8)]
        rows = jnp.concatenate(lines, axis=1)
        near_ref[count * b : count * b + count] = rows.astype(BF16)
        next_ref[count * b : count * b + count] = rows.astype(BF16)
        first, last = rows[0:8], rows[8:16]
        far_near_ref[8 * b : 8 * b + 8] = jnp.where(upper, first, last).astype(BF16)
        far_next_ref[8 * b : 8 * b + 8] = jnp.where(upper, last, first).astype(BF16)
    cot_copy.wait()
    cot = cot_ref[0].astype(F32)
    cots = (cot[:, 0, :], cot[:, 1, :])
    near_ref[64:128] = jnp.where(odd, cots[0], cots[1]).astype(BF16)
    next_ref[64:128] = jnp.where(odd, cots[1], cots[0]).astype(BF16)


def finish_body(mine_ref, other_ref, one_ref, two_ref):
    total = mine_ref[...] + other_ref[...]
    rows = range(total.shape[0])
    two_ref[...] = jnp.concatenate([total[r, 0:864] for r in rows])
    one_ref[...] = jnp.concatenate([total[r, ONE_AT : ONE_AT + 54] for r in rows])


def kernel_body(
    count,
    own_next_ref, own_near_ref, next_ref, near_ref, far_next_ref, far_near_ref,
    k1_ref, k2t_ref, k2_ref, to_kernel_ref, to_flat_ref, order_ref,
    feat_ref, pgrad_ref, send_ref,
):
    slabs = lax.axis_size("space")
    me = lax.axis_index("space")
    half = 16

    def unfold(block, rows):
        return jnp.concatenate([block[rows * b : rows * b + rows] for b in range(4)], axis=1)

    odd, upper = me % 2 == 1, (me // 2) % 2 == 1
    own = unfold(own_near_ref[0:64].astype(F32), 16)
    own_cots = own_near_ref[64:128].astype(F32), own_next_ref[64:128].astype(F32)
    near, following = near_ref[...].astype(F32), next_ref[...].astype(F32)
    left = unfold(jnp.where(odd, near, following)[0:64], 16)
    right = unfold(jnp.where(odd, following, near)[0:64], 16)
    cot_left = jnp.where(odd, near, following)[64:128]
    cot_right = jnp.where(odd, following, near)[64:128]
    far_near, far_next = far_near_ref[...].astype(F32), far_next_ref[...].astype(F32)
    far_left = unfold(jnp.where(upper, far_near, far_next), 8)
    far_right = unfold(jnp.where(upper, far_next, far_near), 8)
    top = lax.broadcasted_iota(jnp.int32, (8, LANES), 0) < 4

    def edge(before, after):
        return jnp.where(top, pltpu.roll(before, 4, 0), pltpu.roll(after, 4, 0))

    edges = (
        edge(far_left, own[0:8]),
        edge(left[8:16], right[0:8]),
        edge(own[8:16], far_right),
    )
    stack = jnp.concatenate([left, own, right, *edges], axis=0)
    moved = [shifted(stack, 2 * half, dy, dx) for dy, dx in SHIFTS]
    patches = []
    for g in range(3):
        rows = [m[16 * g : 16 * g + 16] for m in moved] + [m[48 + 8 * g : 56 + 8 * g] for m in moved]
        patches.append(jnp.concatenate(rows, axis=0).astype(BF16))

    banded = jnp.concatenate(
        [dot(k1_ref[...], to_kernel_ref[p], NT).astype(BF16) for p in range(4)], axis=0
    )

    cell = lax.broadcasted_iota(jnp.int32, (LANES, half * half), 0)
    block = lax.broadcasted_iota(jnp.int32, (LANES, half * half), 1)
    pool = jnp.where((cell // 64) * half + (cell % 32) // 2 == block, 0.125, 0.0).astype(BF16)

    sums = []
    slope_one = None
    for g in range(3):
        pre = dot(banded, patches[g])
        act, s = silu_parts(pre)
        if g == 1:
            slope_one = s + act * (1.0 - s)
        sums += [act[0:32] + act[32:64], act[64:96] + act[96:128]]
    sums = jnp.concatenate(sums, axis=0)
    high = sums.astype(BF16)
    low = (sums - high.astype(F32)).astype(BF16)
    pooled = dot(high, pool) + dot(low, pool)
    plane = lax.broadcasted_iota(jnp.int32, pooled.shape, 0) // 32
    inside = ((plane >= 2) | (me > 0)) & ((plane < 4) | (me < slabs - 1))
    pooled = jnp.where(inside, pooled, 0.0).astype(BF16).astype(F32)

    moved = [shifted(pooled, half, dy, dx).astype(BF16) for dy, dx in SHIFTS]
    columns = [
        jnp.concatenate(
            [m[32 * (p + dz) : 32 * (p + dz) + 32] for dz in range(3) for m in moved], axis=0
        )
        for p in range(4)
    ]

    cots = (
        cot_left, jnp.where(odd, *own_cots), jnp.where(odd, *own_cots[::-1]), cot_right
    )
    deltas = []
    for p in range(4):
        pre = dot(k2t_ref[...], columns[p])
        act, s = silu_parts(pre)
        if 1 <= p <= 2:
            feat_ref[0, :, p - 1, :] = act.astype(BF16)
        deltas.append((cots[p] * (s + act * (1.0 - s))).astype(BF16))

    flipped = jnp.concatenate([k2_ref[576:864], k2_ref[288:576], k2_ref[0:288]], axis=1)
    grads = []
    for p in range(2):
        taps = dot(flipped, jnp.concatenate(deltas[p : p + 3], axis=0))
        total = jnp.zeros((32, half * half), F32)
        for s, (dy, dx) in enumerate(SHIFTS):
            total = total + shifted(taps[32 * (8 - s) : 32 * (8 - s) + 32], half, dy, dx)
        grads.append(total.astype(BF16))
        pgrad_ref[0, :, p, :] = grads[p]

    term_two = dot(deltas[1], columns[1], NT) + dot(deltas[2], columns[2], NT)
    term_two = (term_two * (1.0 / math.sqrt(count // 8))).astype(BF16)
    send_ref[:, 0:864] = dot(term_two, order_ref[...]).astype(BF16)

    spread = dot(jnp.concatenate(grads, axis=0), pool, NT)
    spread = jnp.concatenate([spread[0:32], spread[0:32], spread[32:64], spread[32:64]], axis=0)
    delta_one = (spread * slope_one).astype(BF16)
    wide = dot(delta_one, patches[1], NT)
    high = wide.astype(BF16)
    low = (wide - high.astype(F32)).astype(BF16)
    term_one = jnp.zeros((32, 128), F32)
    for p in range(4):
        for part in (high, low):
            term_one = term_one + dot(part[32 * p : 32 * p + 32], to_flat_ref[p])
    term_one = (term_one * (1.0 / math.sqrt(count))).astype(BF16)
    to = lax.broadcasted_iota(jnp.int32, (64, 32), 0)
    at = lax.broadcasted_iota(jnp.int32, (64, 32), 1)
    even = dot(jnp.where(to == 2 * at, 1.0, 0.0).astype(BF16), term_one)
    uneven = dot(jnp.where(to == 2 * at + 1, 1.0, 0.0).astype(BF16), term_one)
    rows = even + pltpu.roll(uneven, 64, 1)
    send_ref[:, ONE_AT:LANES] = rows.astype(BF16)
    send_ref[:, 864:ONE_AT] = jnp.zeros((64, ONE_AT - 864), BF16)


def on_device(volumes, kernel_one, kernel_two, cotangent):
    _, cin, planes, width, _ = volumes.shape
    half = width // 2
    slabs = lax.axis_size("space")
    copies = lax.axis_size("dp")
    count = copies * planes * slabs * width * width

    limit = pltpu.CompilerParams(vmem_limit_bytes=48 * 1024 * 1024)
    whole = jax.ShapeDtypeStruct((128, width * width // 4), BF16)
    part = jax.ShapeDtypeStruct((32, width * width // 4), BF16)
    to_next, to_near, to_far_next, to_far_near = pl.pallas_call(
        prepare_body,
        out_shape=(whole, whole, part, part),
        in_specs=[pl.BlockSpec(memory_space=pltpu.HBM)] * 2,
        scratch_shapes=[
            pltpu.VMEM(volumes.shape, BF16),
            pltpu.VMEM(cotangent.shape, BF16),
            pltpu.VMEM((planes * cin * width, width), F32),
            pltpu.SemaphoreType.DMA((2,)),
        ],
        compiler_params=limit,
    )(*(pltpu.with_memory_space_constraint(x, pltpu.HBM) for x in (volumes, cotangent)))

    def swap(block, pairs):
        pairs = [p for p in pairs if max(p) < slabs]
        return lax.ppermute(block, "space", pairs + [(t, f) for f, t in pairs])

    evens = range(0, slabs, 2)
    fours = [i + j for i in range(0, slabs, 4) for j in range(2)]
    following = swap(to_next, [(i + 1, i + 2) for i in evens])
    near = swap(to_near, [(i, i + 1) for i in evens])
    far_next = swap(to_far_next, [(i + 2, i + 4) for i in fours])
    far_near = swap(to_far_near, [(i, i + 2) for i in fours])

    k1 = jnp.transpose(kernel_one, (0, 2, 3, 4, 1)).reshape(32, 108)
    k2 = jnp.transpose(kernel_two, (2, 3, 4, 1, 0)).reshape(864, 64)
    k2t = jnp.transpose(k2)
    to_kernel, to_flat = band_maps()

    features, pooled_grad, send = pl.pallas_call(
        functools.partial(kernel_body, count),
        out_shape=(
            jax.ShapeDtypeStruct((1, 64, 2, half * half), BF16),
            jax.ShapeDtypeStruct((1, 32, 2, half * half), BF16),
            jax.ShapeDtypeStruct((64, LANES), BF16),
        ),
        compiler_params=limit,
        cost_estimate=pl.CostEstimate(flops=10**9, bytes_accessed=2 * 10**6, transcendentals=10**6),
    )(
        to_next, to_near, following, near, far_next, far_near, k1, k2t, k2,
        jnp.asarray(to_kernel, BF16), jnp.asarray(to_flat, BF16), jnp.asarray(tap_order(), BF16),
    )

    share = 64 // slabs
    parts = lax.all_to_all(send.reshape(slabs, share, LANES), "space", 0, 0, tiled=True)
    total = jnp.sum(parts.astype(F32), axis=0)
    step = 1
    while step < copies // 2:
        total = total + lax.ppermute(total, "dp", [(i, i ^ step) for i in range(copies)])
        step *= 2
    other = jnp.zeros_like(total)
    if copies > 1:
        other = lax.ppermute(total, "dp", [(i, i ^ step) for i in range(copies)])
    grad_one, grad_two = pl.pallas_call(
        finish_body,
        out_shape=(jax.ShapeDtypeStruct((share * 54,), F32), jax.ShapeDtypeStruct((share * 864,), F32)),
        compiler_params=limit,
    )(total, other)
    return (features, pooled_grad, grad_one, grad_two)


def solution(mesh):
    in_specs = (P("dp", None, "space", None, None), P(), P(), P("dp", None, "space", None))
    out_specs = (P("dp", None, "space", None), P("dp", None, "space", None), P("space"), P("space"))
    return jax.shard_map(
        on_device, mesh=mesh, in_specs=in_specs, out_specs=out_specs, check_vma=False
    )
```

```python
import functools
import math

import jax
import jax.numpy as jnp
import numpy as np
from jax import lax
from jax.experimental import pallas as pl
from jax.experimental.pallas import tpu as pltpu
from jax.sharding import PartitionSpec as P

F32 = jnp.float32
BF16 = jnp.bfloat16
SHIFTS = [(dy, dx) for dy in (-1, 0, 1) for dx in (-1, 0, 1)]
NN = (((1,), (0,)), ((), ()))
NT = (((1,), (1,)), ((), ()))
LANES = 1024
ONE_AT = 896


def dot(a, b, dims=NN):
    return lax.dot_general(a, b, dims, preferred_element_type=F32)


def shifted(field, width, dy, dx):
    cells = field.shape[1]
    move = dy * width + dx
    if move == 0:
        return field
    lane = lax.broadcasted_iota(jnp.int32, field.shape, 1)
    row, col = lane // width, lane % width
    keep = None
    for pos, step in ((row, dy), (col, dx)):
        if step:
            ok = pos < width - 1 if step > 0 else pos > 0
            keep = ok if keep is None else keep & ok
    return jnp.where(keep, pltpu.roll(field, (-move) % cells, 1), 0.0)


def silu_parts(v):
    s = 0.5 + 0.5 * jnp.tanh(0.5 * v)
    return v * s, s


def band_maps():
    to_kernel = np.zeros((4, 216, 108), np.float32)
    to_flat = np.zeros((4, 216, 128), np.float32)
    for p in range(4):
        for s in range(9):
            for dz in range(3):
                q = p + dz - 1
                for ci in range(4):
                    if 0 <= q <= 3:
                        row = 16 * s + 4 * q + ci
                    else:
                        row = 144 + 8 * s + (0 if q < 0 else 4) + ci
                    tap = 9 * dz + s
                    to_kernel[p, row, 4 * tap + ci] = 1
                    to_flat[p, row, 64 * (ci // 2) + 27 * (ci % 2) + tap] = 1
    return to_kernel, to_flat


def tap_order():
    order = np.zeros((27, 32, 32, 27), np.float32)
    for tap in range(27):
        for ch in range(32):
            order[tap, ch, ch, tap] = 1
    return order.reshape(864, 864)


def prepare_body(
    vol_hbm, cot_hbm, *refs,
):
    weights, (next_ref, near_ref, far_next_ref, far_near_ref) = refs[:5], refs[5:9]
    kept, (vol_ref, cot_ref, cells_ref, sems) = refs[9:14], refs[14:]
    me = lax.axis_index("space")
    odd, upper = me % 2 == 1, (me // 2) % 2 == 1
    vol_copy = pltpu.make_async_copy(vol_hbm, vol_ref, sems.at[0])
    cot_copy = pltpu.make_async_copy(cot_hbm, cot_ref, sems.at[1])
    vol_copy.start()
    cot_copy.start()
    copies = [
        pltpu.make_async_copy(src, dst, sems.at[2 + i])
        for i, (src, dst) in enumerate(zip(weights, kept))
    ]
    for copy in copies:
        copy.start()
    vol_copy.wait()
    cin, planes, width = vol_ref.shape[1:4]
    for plane in range(planes):
        for ch in range(cin):
            at = (plane * cin + ch) * width
            cells_ref[at : at + width] = vol_ref[0, ch, plane].astype(F32)
    count = planes * cin
    for b in range(4):
        lines = [cells_ref[pl.ds(8 * b + y, count, stride=width), :] for y in range(8)]
        rows = jnp.concatenate(lines, axis=1)
        near_ref[count * b : count * b + count] = rows.astype(BF16)
        next_ref[count * b : count * b + count] = rows.astype(BF16)
        first, last = rows[0:8], rows[8:16]
        far_near_ref[8 * b : 8 * b + 8] = jnp.where(upper, first, last).astype(BF16)
        far_next_ref[8 * b : 8 * b + 8] = jnp.where(upper, last, first).astype(BF16)
    cot_copy.wait()
    cot = cot_ref[0].astype(F32)
    cots = (cot[:, 0, :], cot[:, 1, :])
    near_ref[64:128] = jnp.where(odd, cots[0], cots[1]).astype(BF16)
    next_ref[64:128] = jnp.where(odd, cots[1], cots[0]).astype(BF16)
    for copy in copies:
        copy.wait()


def finish_body(mine_ref, other_ref, one_ref, two_ref):
    total = mine_ref[...] + other_ref[...]
    rows = range(total.shape[0])
    two_ref[...] = jnp.concatenate([total[r, 0:864] for r in rows])
    one_ref[...] = jnp.concatenate([total[r, ONE_AT : ONE_AT + 54] for r in rows])


def kernel_body(
    count,
    own_next_ref, own_near_ref, next_ref, near_ref, far_next_ref, far_near_ref,
    k1_ref, k2_ref, to_kernel_ref, to_flat_ref, order_ref,
    feat_ref, pgrad_ref, send_ref,
):
    slabs = lax.axis_size("space")
    me = lax.axis_index("space")
    half = 16

    def unfold(block, rows):
        return jnp.concatenate([block[rows * b : rows * b + rows] for b in range(4)], axis=1)

    odd, upper = me % 2 == 1, (me // 2) % 2 == 1
    own = unfold(own_near_ref[0:64].astype(F32), 16)
    own_cots = own_near_ref[64:128].astype(F32), own_next_ref[64:128].astype(F32)
    near, following = near_ref[...].astype(F32), next_ref[...].astype(F32)
    left = unfold(jnp.where(odd, near, following)[0:64], 16)
    right = unfold(jnp.where(odd, following, near)[0:64], 16)
    cot_left = jnp.where(odd, near, following)[64:128]
    cot_right = jnp.where(odd, following, near)[64:128]
    far_near, far_next = far_near_ref[...].astype(F32), far_next_ref[...].astype(F32)
    far_left = unfold(jnp.where(upper, far_near, far_next), 8)
    far_right = unfold(jnp.where(upper, far_next, far_near), 8)
    top = lax.broadcasted_iota(jnp.int32, (8, LANES), 0) < 4

    def edge(before, after):
        return jnp.where(top, pltpu.roll(before, 4, 0), pltpu.roll(after, 4, 0))

    edges = (
        edge(far_left, own[0:8]),
        edge(left[8:16], right[0:8]),
        edge(own[8:16], far_right),
    )
    stack = jnp.concatenate([left, own, right, *edges], axis=0)
    moved = [shifted(stack, 2 * half, dy, dx) for dy, dx in SHIFTS]
    patches = []
    for g in range(3):
        rows = [m[16 * g : 16 * g + 16] for m in moved] + [m[48 + 8 * g : 56 + 8 * g] for m in moved]
        patches.append(jnp.concatenate(rows, axis=0).astype(BF16))

    k1t = k1_ref[...].astype(F32).reshape(108, 32).T.astype(BF16)
    k2t = k2_ref[...].astype(F32).T.astype(BF16)
    banded = jnp.concatenate(
        [dot(k1t, to_kernel_ref[p], NT).astype(BF16) for p in range(4)], axis=0
    )

    cell = lax.broadcasted_iota(jnp.int32, (LANES, half * half), 0)
    block = lax.broadcasted_iota(jnp.int32, (LANES, half * half), 1)
    pool = jnp.where((cell // 64) * half + (cell % 32) // 2 == block, 0.125, 0.0).astype(BF16)

    sums = []
    slope_one = None
    for g in range(3):
        pre = dot(banded, patches[g])
        act, s = silu_parts(pre)
        if g == 1:
            slope_one = s + act * (1.0 - s)
        sums += [act[0:32] + act[32:64], act[64:96] + act[96:128]]
    sums = jnp.concatenate(sums, axis=0)
    high = sums.astype(BF16)
    low = (sums - high.astype(F32)).astype(BF16)
    pooled = dot(high, pool) + dot(low, pool)
    plane = lax.broadcasted_iota(jnp.int32, pooled.shape, 0) // 32
    inside = ((plane >= 2) | (me > 0)) & ((plane < 4) | (me < slabs - 1))
    pooled = jnp.where(inside, pooled, 0.0).astype(BF16).astype(F32)

    moved = [shifted(pooled, half, dy, dx).astype(BF16) for dy, dx in SHIFTS]
    columns = [
        jnp.concatenate(
            [m[32 * (p + dz) : 32 * (p + dz) + 32] for dz in range(3) for m in moved], axis=0
        )
        for p in range(4)
    ]

    cots = (
        cot_left, jnp.where(odd, *own_cots), jnp.where(odd, *own_cots[::-1]), cot_right
    )
    deltas = []
    for p in range(4):
        pre = dot(k2t, columns[p])
        act, s = silu_parts(pre)
        if 1 <= p <= 2:
            feat_ref[0, :, p - 1, :] = act.astype(BF16)
        deltas.append((cots[p] * (s + act * (1.0 - s))).astype(BF16))

    flipped = jnp.concatenate([k2_ref[576:864], k2_ref[288:576], k2_ref[0:288]], axis=1)
    grads = []
    for p in range(2):
        taps = dot(flipped, jnp.concatenate(deltas[p : p + 3], axis=0))
        total = jnp.zeros((32, half * half), F32)
        for s, (dy, dx) in enumerate(SHIFTS):
            total = total + shifted(taps[32 * (8 - s) : 32 * (8 - s) + 32], half, dy, dx)
        grads.append(total.astype(BF16))
        pgrad_ref[0, :, p, :] = grads[p]

    term_two = dot(deltas[1], columns[1], NT) + dot(deltas[2], columns[2], NT)
    term_two = (term_two * (1.0 / math.sqrt(count // 8))).astype(BF16)
    send_ref[:, 0:864] = dot(term_two, order_ref[...]).astype(BF16)

    spread = dot(jnp.concatenate(grads, axis=0), pool, NT)
    spread = jnp.concatenate([spread[0:32], spread[0:32], spread[32:64], spread[32:64]], axis=0)
    delta_one = (spread * slope_one).astype(BF16)
    wide = dot(delta_one, patches[1], NT)
    high = wide.astype(BF16)
    low = (wide - high.astype(F32)).astype(BF16)
    term_one = jnp.zeros((32, 128), F32)
    for p in range(4):
        for part in (high, low):
            term_one = term_one + dot(part[32 * p : 32 * p + 32], to_flat_ref[p])
    term_one = (term_one * (1.0 / math.sqrt(count))).astype(BF16)
    to = lax.broadcasted_iota(jnp.int32, (64, 32), 0)
    at = lax.broadcasted_iota(jnp.int32, (64, 32), 1)
    even = dot(jnp.where(to == 2 * at, 1.0, 0.0).astype(BF16), term_one)
    uneven = dot(jnp.where(to == 2 * at + 1, 1.0, 0.0).astype(BF16), term_one)
    rows = even + pltpu.roll(uneven, 64, 1)
    send_ref[:, ONE_AT:LANES] = rows.astype(BF16)
    send_ref[:, 864:ONE_AT] = jnp.zeros((64, ONE_AT - 864), BF16)


def on_device(volumes, kernel_one, kernel_two, cotangent):
    _, cin, planes, width, _ = volumes.shape
    half = width // 2
    slabs = lax.axis_size("space")
    copies = lax.axis_size("dp")
    count = copies * planes * slabs * width * width

    weights = (
        jnp.transpose(kernel_one, (2, 3, 4, 1, 0)).reshape(27, 4, 32),
        jnp.transpose(kernel_two, (2, 3, 4, 1, 0)).reshape(864, 64),
        *(jnp.asarray(m, BF16) for m in (*band_maps(), tap_order())),
    )
    inputs = [
        pltpu.with_memory_space_constraint(x, pltpu.HBM) for x in (volumes, cotangent, *weights)
    ]
    limit = pltpu.CompilerParams(vmem_limit_bytes=48 * 1024 * 1024)
    whole = jax.ShapeDtypeStruct((128, width * width // 4), BF16)
    part = jax.ShapeDtypeStruct((32, width * width // 4), BF16)
    to_next, to_near, to_far_next, to_far_near, *weights = pl.pallas_call(
        prepare_body,
        out_shape=(
            whole, whole, part, part, *(jax.ShapeDtypeStruct(w.shape, BF16) for w in weights)
        ),
        in_specs=[pl.BlockSpec(memory_space=pltpu.HBM)] * len(inputs),
        scratch_shapes=[
            pltpu.VMEM(volumes.shape, BF16),
            pltpu.VMEM(cotangent.shape, BF16),
            pltpu.VMEM((planes * cin * width, width), F32),
            pltpu.SemaphoreType.DMA((len(inputs),)),
        ],
        compiler_params=limit,
    )(*inputs)

    def swap(block, pairs):
        pairs = [p for p in pairs if max(p) < slabs]
        return lax.ppermute(block, "space", pairs + [(t, f) for f, t in pairs])

    evens = range(0, slabs, 2)
    fours = [i + j for i in range(0, slabs, 4) for j in range(2)]
    following = swap(to_next, [(i + 1, i + 2) for i in evens])
    near = swap(to_near, [(i, i + 1) for i in evens])
    far_next = swap(to_far_next, [(i + 2, i + 4) for i in fours])
    far_near = swap(to_far_near, [(i, i + 2) for i in fours])

    features, pooled_grad, send = pl.pallas_call(
        functools.partial(kernel_body, count),
        out_shape=(
            jax.ShapeDtypeStruct((1, 64, 2, half * half), BF16),
            jax.ShapeDtypeStruct((1, 32, 2, half * half), BF16),
            jax.ShapeDtypeStruct((64, LANES), BF16),
        ),
        compiler_params=limit,
        cost_estimate=pl.CostEstimate(flops=10**9, bytes_accessed=2 * 10**6, transcendentals=10**6),
    )(
        to_next, to_near, following, near, far_next, far_near, *weights
    )

    share = 64 // slabs
    parts = lax.all_to_all(send.reshape(slabs, share, LANES), "space", 0, 0, tiled=True)
    total = jnp.sum(parts.astype(F32), axis=0)
    step = 1
    while step < copies // 2:
        total = total + lax.ppermute(total, "dp", [(i, i ^ step) for i in range(copies)])
        step *= 2
    other = jnp.zeros_like(total)
    if copies > 1:
        other = lax.ppermute(total, "dp", [(i, i ^ step) for i in range(copies)])
    grad_one, grad_two = pl.pallas_call(
        finish_body,
        out_shape=(jax.ShapeDtypeStruct((share * 54,), F32), jax.ShapeDtypeStruct((share * 864,), F32)),
        compiler_params=limit,
    )(total, other)
    return (features, pooled_grad, grad_one, grad_two)


def solution(mesh):
    in_specs = (P("dp", None, "space", None, None), P(), P(), P("dp", None, "space", None))
    out_specs = (P("dp", None, "space", None), P("dp", None, "space", None), P("space"), P("space"))
    return jax.shard_map(
        on_device, mesh=mesh, in_specs=in_specs, out_specs=out_specs, check_vma=False
    )
```

```python
import functools
import math

import jax
import jax.numpy as jnp
import numpy as np
from jax import lax
from jax.experimental import pallas as pl
from jax.experimental.pallas import tpu as pltpu
from jax.sharding import PartitionSpec as P

F32 = jnp.float32
BF16 = jnp.bfloat16
SHIFTS = [(dy, dx) for dy in (-1, 0, 1) for dx in (-1, 0, 1)]
NN = (((1,), (0,)), ((), ()))
NT = (((1,), (1,)), ((), ()))
LANES = 1024
ONE_AT = 896


def dot(a, b, dims=NN):
    return lax.dot_general(a, b, dims, preferred_element_type=F32)


def shifted(field, width, dy, dx):
    cells = field.shape[1]
    move = dy * width + dx
    if move == 0:
        return field
    lane = lax.broadcasted_iota(jnp.int32, field.shape, 1)
    row, col = lane // width, lane % width
    keep = None
    for pos, step in ((row, dy), (col, dx)):
        if step:
            ok = pos < width - 1 if step > 0 else pos > 0
            keep = ok if keep is None else keep & ok
    return jnp.where(keep, pltpu.roll(field, (-move) % cells, 1), 0.0)


def silu_parts(v):
    s = 0.5 + 0.5 * jnp.tanh(0.5 * v)
    return v * s, s


def band_maps():
    to_kernel = np.zeros((4, 216, 108), np.float32)
    to_flat = np.zeros((4, 216, 128), np.float32)
    for p in range(4):
        for s in range(9):
            for dz in range(3):
                q = p + dz - 1
                for ci in range(4):
                    if 0 <= q <= 3:
                        row = 16 * s + 4 * q + ci
                    else:
                        row = 144 + 8 * s + (0 if q < 0 else 4) + ci
                    tap = 9 * dz + s
                    to_kernel[p, row, 4 * tap + ci] = 1
                    to_flat[p, row, 64 * (ci // 2) + 27 * (ci % 2) + tap] = 1
    return to_kernel, to_flat


def tap_order():
    order = np.zeros((27, 32, 32, 27), np.float32)
    for tap in range(27):
        for ch in range(32):
            order[tap, ch, ch, tap] = 1
    return order.reshape(864, 864)


def prepare_body(
    vol_hbm, cot_hbm, *refs,
):
    weights, (next_ref, near_ref, far_next_ref, far_near_ref) = refs[:3], refs[3:7]
    kept, (vol_ref, cot_ref, cells_ref, sems) = refs[7:10], refs[10:]
    me = lax.axis_index("space")
    odd, upper = me % 2 == 1, (me // 2) % 2 == 1
    vol_copy = pltpu.make_async_copy(vol_hbm, vol_ref, sems.at[0])
    cot_copy = pltpu.make_async_copy(cot_hbm, cot_ref, sems.at[1])
    vol_copy.start()
    cot_copy.start()
    copies = [
        pltpu.make_async_copy(src, dst, sems.at[2 + i])
        for i, (src, dst) in enumerate(zip(weights, kept))
    ]
    for copy in copies:
        copy.start()
    vol_copy.wait()
    cin, planes, width = vol_ref.shape[1:4]
    for plane in range(planes):
        for ch in range(cin):
            at = (plane * cin + ch) * width
            cells_ref[at : at + width] = vol_ref[0, ch, plane].astype(F32)
    count = planes * cin
    for b in range(4):
        lines = [cells_ref[pl.ds(8 * b + y, count, stride=width), :] for y in range(8)]
        rows = jnp.concatenate(lines, axis=1)
        near_ref[count * b : count * b + count] = rows.astype(BF16)
        next_ref[count * b : count * b + count] = rows.astype(BF16)
        first, last = rows[0:8], rows[8:16]
        far_near_ref[8 * b : 8 * b + 8] = jnp.where(upper, first, last).astype(BF16)
        far_next_ref[8 * b : 8 * b + 8] = jnp.where(upper, last, first).astype(BF16)
    cot_copy.wait()
    cot = cot_ref[0].astype(F32)
    cots = (cot[:, 0, :], cot[:, 1, :])
    near_ref[64:128] = jnp.where(odd, cots[0], cots[1]).astype(BF16)
    next_ref[64:128] = jnp.where(odd, cots[1], cots[0]).astype(BF16)
    for copy in copies:
        copy.wait()


def finish_body(mine_ref, other_ref, one_ref, two_ref):
    total = mine_ref[...] + other_ref[...]
    rows = range(total.shape[0])
    two_ref[...] = jnp.concatenate([total[r, 0:864] for r in rows])
    one_ref[...] = jnp.concatenate([total[r, ONE_AT : ONE_AT + 54] for r in rows])


def unfold(block, rows):
    return jnp.concatenate([block[rows * b : rows * b + rows] for b in range(4)], axis=1)


def pool_sums(sums, pool):
    high = sums.astype(BF16)
    low = (sums - high.astype(F32)).astype(BF16)
    return dot(high, pool) + dot(low, pool)


def spread_taps(taps, half):
    total = jnp.zeros((32, half * half), F32)
    for s, (dy, dx) in enumerate(SHIFTS):
        total = total + shifted(taps[32 * (8 - s) : 32 * (8 - s) + 32], half, dy, dx)
    return total


def inner_body(
    count,
    own_next_ref, own_near_ref, next_ref, near_ref, k1_ref, k2_ref, to_kernel_ref,
    to_flat_hbm, order_hbm,
    feat_ref, two_ref, pgrad_ref, slope_ref, patch_ref, pre_ref, act_ref, pre_two_ref,
    pool_ref, far_one_ref, far_two_ref, to_flat_ref,
    order_ref, sems,
):
    flat_copy = pltpu.make_async_copy(to_flat_hbm, to_flat_ref, sems.at[0])
    order_copy = pltpu.make_async_copy(order_hbm, order_ref, sems.at[1])
    flat_copy.start()
    order_copy.start()
    slabs = lax.axis_size("space")
    me = lax.axis_index("space")
    half = 16

    odd = me % 2 == 1
    own = unfold(own_near_ref[0:64].astype(F32), 16)
    near, following = near_ref[0:64].astype(F32), next_ref[0:64].astype(F32)
    left = unfold(jnp.where(odd, near, following), 16)
    right = unfold(jnp.where(odd, following, near), 16)
    top = lax.broadcasted_iota(jnp.int32, (8, LANES), 0) < 4
    edges = (
        jnp.where(top, 0.0, pltpu.roll(own[0:8], 4, 0)),
        jnp.where(top, pltpu.roll(left[8:16], 4, 0), pltpu.roll(right[0:8], 4, 0)),
        jnp.where(top, pltpu.roll(own[8:16], 4, 0), 0.0),
    )
    stack = jnp.concatenate([left, own, right, *edges], axis=0)
    moved = [shifted(stack, 2 * half, dy, dx) for dy, dx in SHIFTS]
    patches = []
    for g in range(3):
        rows = [m[16 * g : 16 * g + 16] for m in moved] + [m[48 + 8 * g : 56 + 8 * g] for m in moved]
        patches.append(jnp.concatenate(rows, axis=0).astype(BF16))
    patch_ref[...] = patches[1]

    k1t = k1_ref[...].astype(F32).reshape(108, 32).T.astype(BF16)
    k2t = k2_ref[...].astype(F32).T.astype(BF16)
    banded = jnp.concatenate(
        [dot(k1t, to_kernel_ref[p], NT).astype(BF16) for p in range(4)], axis=0
    )
    far_one_ref[...] = jnp.concatenate(
        [dot(k1t, to_kernel_ref[p, 144:216], NT).astype(BF16) for p in (0, 3)], axis=0
    )
    far_two_ref[0] = k2t[:, 0:288]
    far_two_ref[1] = k2t[:, 576:864]

    cell = lax.broadcasted_iota(jnp.int32, (LANES, half * half), 0)
    block = lax.broadcasted_iota(jnp.int32, (LANES, half * half), 1)
    pool = jnp.where((cell // 64) * half + (cell % 32) // 2 == block, 0.125, 0.0).astype(BF16)
    pool_ref[...] = pool

    pre = dot(banded, patches[0])
    pre_ref[0:32] = pre[0:32]
    act, _ = silu_parts(pre[32:128])
    act_ref[0:32] = act[0:32]
    sums = [act[32:64] + act[64:96]]
    pre = dot(banded, patches[1])
    act, s = silu_parts(pre)
    slope_ref[...] = s + act * (1.0 - s)
    sums += [act[0:32] + act[32:64], act[64:96] + act[96:128]]
    pre = dot(banded, patches[2])
    pre_ref[32:64] = pre[96:128]
    act, _ = silu_parts(pre[0:96])
    act_ref[32:64] = act[64:96]
    sums += [act[0:32] + act[32:64]]
    pooled = pool_sums(jnp.concatenate(sums, axis=0), pool)
    plane = lax.broadcasted_iota(jnp.int32, pooled.shape, 0) // 32
    inside = ((plane > 0) | (me > 0)) & ((plane < 3) | (me < slabs - 1))
    pooled = jnp.where(inside, pooled, 0.0).astype(BF16).astype(F32)

    moved = [shifted(pooled, half, dy, dx).astype(BF16) for dy, dx in SHIFTS]
    nothing = jnp.zeros((288, half * half), BF16)
    planes = [
        nothing,
        *(jnp.concatenate([m[32 * q : 32 * q + 32] for m in moved], axis=0) for q in range(4)),
        nothing,
    ]
    columns = [jnp.concatenate(planes[p : p + 3], axis=0) for p in range(4)]

    own_cots = own_near_ref[64:128].astype(F32), own_next_ref[64:128].astype(F32)
    cots = jnp.where(odd, *own_cots), jnp.where(odd, *own_cots[::-1])
    deltas = []
    for p in range(2):
        pre = dot(k2t, columns[p + 1])
        act, s = silu_parts(pre)
        feat_ref[0, :, p, :] = act.astype(BF16)
        deltas.append((cots[p] * (s + act * (1.0 - s))).astype(BF16))
    for i, p in enumerate((0, 3)):
        pre_two_ref[i] = dot(k2t, columns[p])

    both = jnp.concatenate(deltas, axis=0)
    for p in range(2):
        taps = [k2_ref[288 * (1 + p - q) : 288 * (1 + p - q) + 288] for q in range(2)]
        pgrad_ref[p] = spread_taps(dot(jnp.concatenate(taps, axis=1), both), half)

    term_two = dot(deltas[0], columns[1], NT) + dot(deltas[1], columns[2], NT)
    term_two = (term_two * (1.0 / math.sqrt(count // 8))).astype(BF16)
    order_copy.wait()
    two_ref[:, 0:864] = dot(term_two, order_ref[...]).astype(BF16)
    two_ref[:, 864:ONE_AT] = jnp.zeros((64, ONE_AT - 864), BF16)
    flat_copy.wait()


def outer_body(
    count,
    far_next_ref, far_near_ref, next_ref, near_ref, k2_ref,
    two_ref, part_ref, slope_ref, patch_ref, pre_ref, act_ref, pre_two_ref,
    pool_ref, far_one_ref, far_two_ref, to_flat_ref,
    pgrad_ref, send_ref,
):
    slabs = lax.axis_size("space")
    me = lax.axis_index("space")
    half = 16
    odd, upper = me % 2 == 1, (me // 2) % 2 == 1
    pool = pool_ref[...]
    far_near, far_next = far_near_ref[...].astype(F32), far_next_ref[...].astype(F32)
    far_left = unfold(jnp.where(upper, far_near, far_next), 8)
    far_right = unfold(jnp.where(upper, far_next, far_near), 8)
    top = lax.broadcasted_iota(jnp.int32, (8, LANES), 0) < 4
    edge = jnp.where(top, pltpu.roll(far_left, 4, 0), pltpu.roll(far_right, 4, 0))
    patches = jnp.concatenate(
        [shifted(edge, 2 * half, dy, dx) for dy, dx in SHIFTS], axis=0
    ).astype(BF16)
    act, _ = silu_parts(pre_ref[...] + dot(far_one_ref[...], patches))
    pooled = pool_sums(act_ref[...] + act, pool)
    plane = lax.broadcasted_iota(jnp.int32, pooled.shape, 0) // 32
    inside = ((plane > 0) | (me > 0)) & ((plane < 1) | (me < slabs - 1))
    pooled = jnp.where(inside, pooled, 0.0).astype(BF16).astype(F32)
    moved = [shifted(pooled, half, dy, dx).astype(BF16) for dy, dx in SHIFTS]

    near, following = near_ref[64:128].astype(F32), next_ref[64:128].astype(F32)
    cots = jnp.where(odd, near, following), jnp.where(odd, following, near)
    grads = []
    for p in range(2):
        columns = jnp.concatenate([m[32 * p : 32 * p + 32] for m in moved], axis=0)
        pre = pre_two_ref[p] + dot(far_two_ref[p], columns)
        act, s = silu_parts(pre)
        delta = (cots[p] * (s + act * (1.0 - s))).astype(BF16)
        taps = dot(k2_ref[576 * (1 - p) : 576 * (1 - p) + 288], delta)
        grads.append((part_ref[p] + spread_taps(taps, half)).astype(BF16))
        pgrad_ref[0, :, p, :] = grads[p]

    spread = dot(jnp.concatenate(grads, axis=0), pool, NT)
    spread = jnp.concatenate([spread[0:32], spread[0:32], spread[32:64], spread[32:64]], axis=0)
    delta_one = (spread * slope_ref[...]).astype(BF16)
    wide = dot(delta_one, patch_ref[...], NT)
    high = wide.astype(BF16)
    low = (wide - high.astype(F32)).astype(BF16)
    term_one = jnp.zeros((32, 128), F32)
    for p in range(4):
        for part in (high, low):
            term_one = term_one + dot(part[32 * p : 32 * p + 32], to_flat_ref[p])
    term_one = (term_one * (1.0 / math.sqrt(count))).astype(BF16)
    to = lax.broadcasted_iota(jnp.int32, (64, 32), 0)
    at = lax.broadcasted_iota(jnp.int32, (64, 32), 1)
    even = dot(jnp.where(to == 2 * at, 1.0, 0.0).astype(BF16), term_one)
    uneven = dot(jnp.where(to == 2 * at + 1, 1.0, 0.0).astype(BF16), term_one)
    rows = even + pltpu.roll(uneven, 64, 1)
    send_ref[:, 0:ONE_AT] = two_ref[...]
    send_ref[:, ONE_AT:LANES] = rows.astype(BF16)


def on_device(volumes, kernel_one, kernel_two, cotangent):
    _, cin, planes, width, _ = volumes.shape
    half = width // 2
    slabs = lax.axis_size("space")
    copies = lax.axis_size("dp")
    count = copies * planes * slabs * width * width

    to_kernel, to_flat = band_maps()
    weights = (
        jnp.transpose(kernel_one, (2, 3, 4, 1, 0)).reshape(27, 4, 32),
        jnp.transpose(kernel_two, (2, 3, 4, 1, 0)).reshape(864, 64),
        jnp.asarray(to_kernel, BF16),
    )
    to_flat, order = jnp.asarray(to_flat, BF16), jnp.asarray(tap_order(), BF16)

    def in_hbm(*arrays):
        return [pltpu.with_memory_space_constraint(x, pltpu.HBM) for x in arrays]

    inputs = in_hbm(volumes, cotangent, *weights)
    vmem, hbm = pl.BlockSpec(memory_space=pltpu.VMEM), pl.BlockSpec(memory_space=pltpu.HBM)
    limit = pltpu.CompilerParams(vmem_limit_bytes=48 * 1024 * 1024)
    whole = jax.ShapeDtypeStruct((128, width * width // 4), BF16)
    part = jax.ShapeDtypeStruct((32, width * width // 4), BF16)
    to_next, to_near, to_far_next, to_far_near, *weights = pl.pallas_call(
        prepare_body,
        out_shape=(
            whole, whole, part, part, *(jax.ShapeDtypeStruct(w.shape, BF16) for w in weights)
        ),
        in_specs=[hbm] * len(inputs),
        scratch_shapes=[
            pltpu.VMEM(volumes.shape, BF16),
            pltpu.VMEM(cotangent.shape, BF16),
            pltpu.VMEM((planes * cin * width, width), F32),
            pltpu.SemaphoreType.DMA((len(inputs),)),
        ],
        compiler_params=limit,
    )(*inputs)

    def swap(block, pairs):
        pairs = [p for p in pairs if max(p) < slabs]
        return lax.ppermute(block, "space", pairs + [(t, f) for f, t in pairs])

    evens = range(0, slabs, 2)
    fours = [i + j for i in range(0, slabs, 4) for j in range(2)]
    following = swap(to_next, [(i + 1, i + 2) for i in evens])
    near = swap(to_near, [(i, i + 1) for i in evens])
    far_next = swap(to_far_next, [(i + 2, i + 4) for i in fours])
    far_near = swap(to_far_near, [(i, i + 2) for i in fours])

    cells = half * half
    shapes = {
        "features": ((1, 64, 2, cells), BF16),
        "two": ((64, ONE_AT), BF16),
        "part": ((2, 32, cells), F32),
        "slope": ((128, LANES), F32),
        "patches": ((216, LANES), BF16),
        "pre": ((64, LANES), F32),
        "act": ((64, LANES), F32),
        "pre_two": ((2, 64, cells), F32),
        "pool": ((LANES, cells), BF16),
        "far_one": ((64, 72), BF16),
        "far_two": ((2, 64, 288), BF16),
        "to_flat": (to_flat.shape, BF16),
    }
    features, *inner = pl.pallas_call(
        functools.partial(inner_body, count),
        out_shape=tuple(jax.ShapeDtypeStruct(*x) for x in shapes.values()),
        in_specs=[vmem] * 7 + [hbm] * 2,
        scratch_shapes=[pltpu.VMEM(order.shape, BF16), pltpu.SemaphoreType.DMA((2,))],
        compiler_params=limit,
        cost_estimate=pl.CostEstimate(flops=10**9, bytes_accessed=2 * 10**6, transcendentals=10**6),
    )(to_next, to_near, following, near, *weights, *in_hbm(to_flat, order))
    pooled_grad, send = pl.pallas_call(
        functools.partial(outer_body, count),
        out_shape=(
            jax.ShapeDtypeStruct((1, 32, 2, cells), BF16),
            jax.ShapeDtypeStruct((64, LANES), BF16),
        ),
        compiler_params=limit,
        cost_estimate=pl.CostEstimate(flops=10**8, bytes_accessed=2 * 10**6, transcendentals=10**6),
    )(far_next, far_near, following, near, weights[1], *inner)

    share = 64 // slabs
    parts = lax.all_to_all(send.reshape(slabs, share, LANES), "space", 0, 0, tiled=True)
    total = jnp.sum(parts.astype(F32), axis=0)
    step = 1
    while step < copies // 2:
        total = total + lax.ppermute(total, "dp", [(i, i ^ step) for i in range(copies)])
        step *= 2
    other = jnp.zeros_like(total)
    if copies > 1:
        other = lax.ppermute(total, "dp", [(i, i ^ step) for i in range(copies)])
    grad_one, grad_two = pl.pallas_call(
        finish_body,
        out_shape=(jax.ShapeDtypeStruct((share * 54,), F32), jax.ShapeDtypeStruct((share * 864,), F32)),
        compiler_params=limit,
    )(total, other)
    return (features, pooled_grad, grad_one, grad_two)


def solution(mesh):
    in_specs = (P("dp", None, "space", None, None), P(), P(), P("dp", None, "space", None))
    out_specs = (P("dp", None, "space", None), P("dp", None, "space", None), P("space"), P("space"))
    return jax.shard_map(
        on_device, mesh=mesh, in_specs=in_specs, out_specs=out_specs, check_vma=False
    )
```

```python
import functools
import math

import jax
import jax.numpy as jnp
import numpy as np
from jax import lax
from jax.experimental import pallas as pl
from jax.experimental.pallas import tpu as pltpu
from jax.sharding import PartitionSpec as P

F32 = jnp.float32
BF16 = jnp.bfloat16
SHIFTS = [(dy, dx) for dy in (-1, 0, 1) for dx in (-1, 0, 1)]
NN = (((1,), (0,)), ((), ()))
NT = (((1,), (1,)), ((), ()))
LANES = 1024
ONE_AT = 896


def dot(a, b, dims=NN):
    return lax.dot_general(a, b, dims, preferred_element_type=F32)


def inside(cells, width):
    lane = lax.broadcasted_iota(jnp.int32, (1, cells), 1)
    col, row = lane & (width - 1), lax.shift_right_logical(lane, width.bit_length() - 1)

    def factor(pos, step):
        if step == 0:
            return None
        return jnp.where(pos < width - 1 if step > 0 else pos > 0, 1.0, 0.0)

    return [(factor(col, d), factor(row, d)) for d in (-1, 0, 1)]


def moved_by(field, move, factor):
    return field if move == 0 else pltpu.roll(field, (-move) % field.shape[1], 1) * factor


def all_shifts(field, width):
    factors = inside(field.shape[1], width)
    across = [moved_by(field, dx, factors[dx + 1][0]) for dx in (-1, 0, 1)]
    return [moved_by(across[dx + 1], dy * width, factors[dy + 1][1]) for dy, dx in SHIFTS]


def pool_pattern():
    cell = lax.broadcasted_iota(jnp.int32, (512, 128), 0)
    block = lax.broadcasted_iota(jnp.int32, (512, 128), 1)
    at = 16 * lax.shift_right_logical(cell, 6) + lax.shift_right_logical(cell & 31, 1)
    return jnp.where(at == block, 0.125, 0.0).astype(BF16)


def silu_parts(v):
    s = 0.5 + 0.5 * jnp.tanh(0.5 * v)
    return v * s, s


def band_maps():
    to_kernel = np.zeros((4, 216, 108), np.float32)
    to_flat = np.zeros((4, 256, 128), np.float32)
    for p in range(4):
        for s in range(9):
            for dz in range(3):
                q = p + dz - 1
                for ci in range(4):
                    if 0 <= q <= 3:
                        row = 16 * s + 4 * q + ci
                    else:
                        row = 144 + 8 * s + (0 if q < 0 else 4) + ci
                    tap = 9 * dz + s
                    to_kernel[p, row, 4 * tap + ci] = 1
                    to_flat[p, row, 64 * (ci // 2) + 27 * (ci % 2) + tap] = 1
    return to_kernel, to_flat.reshape(1024, 128)


def tap_order():
    order = np.zeros((27, 32, 32, 27), np.float32)
    for tap in range(27):
        for ch in range(32):
            order[tap, ch, ch, tap] = 1
    return order.reshape(864, 864)


def prepare_body(
    vol_hbm, cot_hbm, *refs,
):
    weights, (next_ref, near_ref, far_next_ref, far_near_ref) = refs[:3], refs[3:7]
    kept, (vol_ref, cot_ref, cells_ref, sems) = refs[7:10], refs[10:]
    me = lax.axis_index("space")
    odd, upper = me % 2 == 1, (me // 2) % 2 == 1
    vol_copy = pltpu.make_async_copy(vol_hbm, vol_ref, sems.at[0])
    cot_copy = pltpu.make_async_copy(cot_hbm, cot_ref, sems.at[1])
    vol_copy.start()
    cot_copy.start()
    copies = [
        pltpu.make_async_copy(src, dst, sems.at[2 + i])
        for i, (src, dst) in enumerate(zip(weights, kept))
    ]
    for copy in copies:
        copy.start()
    vol_copy.wait()
    cin, planes, width = vol_ref.shape[1:4]
    for plane in range(planes):
        for ch in range(cin):
            at = (plane * cin + ch) * width
            cells_ref[at : at + width] = vol_ref[0, ch, plane].astype(F32)
    count = planes * cin
    for b in range(4):
        lines = [cells_ref[pl.ds(8 * b + y, count, stride=width), :] for y in range(8)]
        rows = jnp.concatenate(lines, axis=1)
        near_ref[count * b : count * b + count] = rows.astype(BF16)
        next_ref[count * b : count * b + count] = rows.astype(BF16)
        first, last = rows[0:8], rows[8:16]
        far_near_ref[8 * b : 8 * b + 8] = jnp.where(upper, first, last).astype(BF16)
        far_next_ref[8 * b : 8 * b + 8] = jnp.where(upper, last, first).astype(BF16)
    cot_copy.wait()
    cot = cot_ref[0].astype(F32)
    cots = (cot[:, 0, :], cot[:, 1, :])
    near_ref[64:128] = jnp.where(odd, cots[0], cots[1]).astype(BF16)
    next_ref[64:128] = jnp.where(odd, cots[1], cots[0]).astype(BF16)
    for copy in copies:
        copy.wait()


def finish_body(mine_ref, other_ref, one_ref, two_ref):
    total = mine_ref[...] + other_ref[...]
    share = total.shape[0]
    first = lax.axis_index("space") * share
    two_ref[...] = jnp.concatenate([total[r, 0:864] for r in range(share)])
    low, high = (total[:, ONE_AT + 64 * h : ONE_AT + 64 * h + 54] for h in range(2))
    row = first + lax.broadcasted_iota(jnp.int32, low.shape, 0)
    one = jnp.where(row & 1 == 1, high, low)
    one_ref[...] = jnp.concatenate([one[r] for r in range(share)])


def unfold(block, rows):
    return jnp.concatenate([block[rows * b : rows * b + rows] for b in range(4)], axis=1)


def pool_sums(sums, pattern):
    rows = sums.shape[0]
    high = sums.astype(BF16)
    low = (sums - high.astype(F32)).astype(BF16)
    halves = [part[:, 512 * m : 512 * m + 512] for part in (high, low) for m in range(2)]
    out = dot(jnp.concatenate(halves, axis=0), pattern)
    out = out[0 : 2 * rows] + out[2 * rows : 4 * rows]
    return jnp.concatenate([out[0:rows], out[rows : 2 * rows]], axis=1)


def spread_cells(field, pattern):
    rows = field.shape[0]
    out = dot(jnp.concatenate([field[:, 0:128], field[:, 128:256]], axis=0), pattern, NT)
    return jnp.concatenate([out[0:rows], out[rows : 2 * rows]], axis=1)


def spread_taps(taps, half):
    factors = inside(half * half, half)
    total = None
    for dx in (-1, 0, 1):
        column = None
        for dy in (-1, 0, 1):
            s = 3 * (1 - dy) + (1 - dx)
            part = moved_by(taps[32 * s : 32 * s + 32], dy * half, factors[dy + 1][1])
            column = part if column is None else column + part
        column = moved_by(column, dx, factors[dx + 1][0])
        total = column if total is None else total + column
    return total


def inner_body(
    count,
    own_next_ref, own_near_ref, next_ref, near_ref, k1_ref, k2_ref, to_kernel_ref,
    to_flat_hbm, order_hbm,
    feat_ref, two_ref, pgrad_ref, slope_ref, patch_ref, pre_ref, act_ref, pre_two_ref,
    far_one_ref, far_two_ref, to_flat_ref,
    order_ref, sems,
):
    flat_copy = pltpu.make_async_copy(to_flat_hbm, to_flat_ref, sems.at[0])
    order_copy = pltpu.make_async_copy(order_hbm, order_ref, sems.at[1])
    flat_copy.start()
    order_copy.start()
    slabs = lax.axis_size("space")
    me = lax.axis_index("space")
    half = 16

    odd = me % 2 == 1
    own = unfold(own_near_ref[0:64].astype(F32), 16)
    near, following = near_ref[0:64].astype(F32), next_ref[0:64].astype(F32)
    left = unfold(jnp.where(odd, near, following), 16)
    right = unfold(jnp.where(odd, following, near), 16)
    top = lax.broadcasted_iota(jnp.int32, (8, LANES), 0) < 4
    edges = (
        jnp.where(top, 0.0, pltpu.roll(own[0:8], 4, 0)),
        jnp.where(top, pltpu.roll(left[8:16], 4, 0), pltpu.roll(right[0:8], 4, 0)),
        jnp.where(top, pltpu.roll(own[8:16], 4, 0), 0.0),
    )
    stack = jnp.concatenate([left, own, right, *edges], axis=0)
    moved = all_shifts(stack, 2 * half)
    patches = []
    for g in range(3):
        rows = [m[16 * g : 16 * g + 16] for m in moved] + [m[48 + 8 * g : 56 + 8 * g] for m in moved]
        patches.append(jnp.concatenate(rows, axis=0).astype(BF16))
    patch_ref[0:216] = patches[1]
    patch_ref[216:256] = jnp.zeros((40, LANES), BF16)

    k1t = k1_ref[...].astype(F32).reshape(108, 32).T.astype(BF16)
    k2t = k2_ref[...].astype(F32).T.astype(BF16)
    banded = jnp.concatenate(
        [dot(k1t, to_kernel_ref[p], NT).astype(BF16) for p in range(4)], axis=0
    )
    far_one_ref[...] = jnp.concatenate(
        [dot(k1t, to_kernel_ref[p, 144:216], NT).astype(BF16) for p in (0, 3)], axis=0
    )
    far_two_ref[0] = k2t[:, 0:288]
    far_two_ref[1] = k2t[:, 576:864]

    pattern = pool_pattern()
    pre = dot(banded, patches[0])
    pre_ref[0:32] = pre[0:32]
    act, _ = silu_parts(pre[32:128])
    act_ref[0:32] = act[0:32]
    sums = [act[32:64] + act[64:96]]
    pre = dot(banded, patches[1])
    act, s = silu_parts(pre)
    slope_ref[...] = s + act * (1.0 - s)
    sums += [act[0:32] + act[32:64], act[64:96] + act[96:128]]
    pre = dot(banded, patches[2])
    pre_ref[32:64] = pre[96:128]
    act, _ = silu_parts(pre[0:96])
    act_ref[32:64] = act[64:96]
    sums += [act[0:32] + act[32:64]]
    pooled = pool_sums(jnp.concatenate(sums, axis=0), pattern)
    plane = lax.shift_right_logical(lax.broadcasted_iota(jnp.int32, pooled.shape, 0), 5)
    real = ((plane > 0) | (me > 0)) & ((plane < 3) | (me < slabs - 1))
    pooled = jnp.where(real, pooled, 0.0).astype(BF16).astype(F32)

    moved = [m.astype(BF16) for m in all_shifts(pooled, half)]
    nothing = jnp.zeros((288, half * half), BF16)
    planes = [
        nothing,
        *(jnp.concatenate([m[32 * q : 32 * q + 32] for m in moved], axis=0) for q in range(4)),
        nothing,
    ]
    columns = [jnp.concatenate(planes[p : p + 3], axis=0) for p in range(4)]

    own_cots = own_near_ref[64:128].astype(F32), own_next_ref[64:128].astype(F32)
    cots = jnp.where(odd, *own_cots), jnp.where(odd, *own_cots[::-1])
    deltas = []
    for p in range(2):
        pre = dot(k2t, columns[p + 1])
        act, s = silu_parts(pre)
        feat_ref[0, :, p, :] = act.astype(BF16)
        deltas.append((cots[p] * (s + act * (1.0 - s))).astype(BF16))
    for i, p in enumerate((0, 3)):
        pre_two_ref[i] = dot(k2t, columns[p])

    both = jnp.concatenate(deltas, axis=0)
    for p in range(2):
        taps = [k2_ref[288 * (1 + p - q) : 288 * (1 + p - q) + 288] for q in range(2)]
        pgrad_ref[p] = spread_taps(dot(jnp.concatenate(taps, axis=1), both), half)

    term_two = dot(deltas[0], columns[1], NT) + dot(deltas[1], columns[2], NT)
    term_two = (term_two * (1.0 / math.sqrt(count // 8))).astype(BF16)
    order_copy.wait()
    two_ref[:, 0:864] = dot(term_two, order_ref[...]).astype(BF16)
    two_ref[:, 864:ONE_AT] = jnp.zeros((64, ONE_AT - 864), BF16)
    flat_copy.wait()


def outer_body(
    count,
    far_next_ref, far_near_ref, next_ref, near_ref, k2_ref,
    two_ref, part_ref, slope_ref, patch_ref, pre_ref, act_ref, pre_two_ref,
    far_one_ref, far_two_ref, to_flat_ref,
    pgrad_ref, send_ref,
):
    slabs = lax.axis_size("space")
    me = lax.axis_index("space")
    half = 16
    odd, upper = me % 2 == 1, (me // 2) % 2 == 1
    pattern = pool_pattern()
    far_near, far_next = far_near_ref[...].astype(F32), far_next_ref[...].astype(F32)
    far_left = unfold(jnp.where(upper, far_near, far_next), 8)
    far_right = unfold(jnp.where(upper, far_next, far_near), 8)
    top = lax.broadcasted_iota(jnp.int32, (8, LANES), 0) < 4
    edge = jnp.where(top, pltpu.roll(far_left, 4, 0), pltpu.roll(far_right, 4, 0))
    patches = jnp.concatenate(all_shifts(edge, 2 * half), axis=0).astype(BF16)
    act, _ = silu_parts(pre_ref[...] + dot(far_one_ref[...], patches))
    pooled = pool_sums(act_ref[...] + act, pattern)
    plane = lax.shift_right_logical(lax.broadcasted_iota(jnp.int32, pooled.shape, 0), 5)
    real = ((plane > 0) | (me > 0)) & ((plane < 1) | (me < slabs - 1))
    pooled = jnp.where(real, pooled, 0.0).astype(BF16).astype(F32)
    moved = [m.astype(BF16) for m in all_shifts(pooled, half)]

    near, following = near_ref[64:128].astype(F32), next_ref[64:128].astype(F32)
    cots = jnp.where(odd, near, following), jnp.where(odd, following, near)
    grads = []
    for p in range(2):
        columns = jnp.concatenate([m[32 * p : 32 * p + 32] for m in moved], axis=0)
        pre = pre_two_ref[p] + dot(far_two_ref[p], columns)
        act, s = silu_parts(pre)
        delta = (cots[p] * (s + act * (1.0 - s))).astype(BF16)
        taps = dot(k2_ref[576 * (1 - p) : 576 * (1 - p) + 288], delta)
        grads.append((part_ref[p] + spread_taps(taps, half)).astype(BF16))
        pgrad_ref[0, :, p, :] = grads[p]

    spread = spread_cells(jnp.concatenate(grads, axis=0), pattern)
    spread = jnp.concatenate([spread[0:32], spread[0:32], spread[32:64], spread[32:64]], axis=0)
    delta_one = (spread * slope_ref[...]).astype(BF16)
    wide = dot(delta_one, patch_ref[...], NT)
    wide = jnp.concatenate([wide[32 * p : 32 * p + 32] for p in range(4)], axis=1)
    high = wide.astype(BF16)
    low = (wide - high.astype(F32)).astype(BF16)
    term_one = dot(jnp.concatenate([high, low], axis=0), to_flat_ref[...])
    term_one = ((term_one[0:32] + term_one[32:64]) * (1.0 / math.sqrt(count))).astype(BF16)
    to = lax.shift_right_logical(lax.broadcasted_iota(jnp.int32, (64, 32), 0), 1)
    at = lax.broadcasted_iota(jnp.int32, (64, 32), 1)
    send_ref[:, 0:ONE_AT] = two_ref[...]
    send_ref[:, ONE_AT:LANES] = dot(jnp.where(to == at, 1.0, 0.0).astype(BF16), term_one).astype(BF16)


def on_device(volumes, kernel_one, kernel_two, cotangent):
    _, cin, planes, width, _ = volumes.shape
    half = width // 2
    slabs = lax.axis_size("space")
    copies = lax.axis_size("dp")
    count = copies * planes * slabs * width * width

    to_kernel, to_flat = band_maps()
    weights = (
        jnp.transpose(kernel_one, (2, 3, 4, 1, 0)).reshape(27, 4, 32),
        jnp.transpose(kernel_two, (2, 3, 4, 1, 0)).reshape(864, 64),
        jnp.asarray(to_kernel, BF16),
    )
    to_flat, order = jnp.asarray(to_flat, BF16), jnp.asarray(tap_order(), BF16)

    def in_hbm(*arrays):
        return [pltpu.with_memory_space_constraint(x, pltpu.HBM) for x in arrays]

    inputs = in_hbm(volumes, cotangent, *weights)
    vmem, hbm = pl.BlockSpec(memory_space=pltpu.VMEM), pl.BlockSpec(memory_space=pltpu.HBM)
    limit = pltpu.CompilerParams(vmem_limit_bytes=48 * 1024 * 1024)
    whole = jax.ShapeDtypeStruct((128, width * width // 4), BF16)
    part = jax.ShapeDtypeStruct((32, width * width // 4), BF16)
    to_next, to_near, to_far_next, to_far_near, *weights = pl.pallas_call(
        prepare_body,
        out_shape=(
            whole, whole, part, part, *(jax.ShapeDtypeStruct(w.shape, BF16) for w in weights)
        ),
        in_specs=[hbm] * len(inputs),
        scratch_shapes=[
            pltpu.VMEM(volumes.shape, BF16),
            pltpu.VMEM(cotangent.shape, BF16),
            pltpu.VMEM((planes * cin * width, width), F32),
            pltpu.SemaphoreType.DMA((len(inputs),)),
        ],
        compiler_params=limit,
    )(*inputs)

    def swap(block, pairs):
        pairs = [p for p in pairs if max(p) < slabs]
        return lax.ppermute(block, "space", pairs + [(t, f) for f, t in pairs])

    evens = range(0, slabs, 2)
    fours = [i + j for i in range(0, slabs, 4) for j in range(2)]
    following = swap(to_next, [(i + 1, i + 2) for i in evens])
    near = swap(to_near, [(i, i + 1) for i in evens])
    far_next = swap(to_far_next, [(i + 2, i + 4) for i in fours])
    far_near = swap(to_far_near, [(i, i + 2) for i in fours])

    cells = half * half
    shapes = {
        "features": ((1, 64, 2, cells), BF16),
        "two": ((64, ONE_AT), BF16),
        "part": ((2, 32, cells), F32),
        "slope": ((128, LANES), F32),
        "patches": ((256, LANES), BF16),
        "pre": ((64, LANES), F32),
        "act": ((64, LANES), F32),
        "pre_two": ((2, 64, cells), F32),
        "far_one": ((64, 72), BF16),
        "far_two": ((2, 64, 288), BF16),
        "to_flat": (to_flat.shape, BF16),
    }
    features, *inner = pl.pallas_call(
        functools.partial(inner_body, count),
        out_shape=tuple(jax.ShapeDtypeStruct(*x) for x in shapes.values()),
        in_specs=[vmem] * 7 + [hbm] * 2,
        scratch_shapes=[pltpu.VMEM(order.shape, BF16), pltpu.SemaphoreType.DMA((2,))],
        compiler_params=limit,
        cost_estimate=pl.CostEstimate(flops=10**9, bytes_accessed=2 * 10**6, transcendentals=10**6),
    )(to_next, to_near, following, near, *weights, *in_hbm(to_flat, order))
    pooled_grad, send = pl.pallas_call(
        functools.partial(outer_body, count),
        out_shape=(
            jax.ShapeDtypeStruct((1, 32, 2, cells), BF16),
            jax.ShapeDtypeStruct((64, LANES), BF16),
        ),
        compiler_params=limit,
        cost_estimate=pl.CostEstimate(flops=10**8, bytes_accessed=2 * 10**6, transcendentals=10**6),
    )(far_next, far_near, following, near, weights[1], *inner)

    share = 64 // slabs
    parts = lax.all_to_all(send.reshape(slabs, share, LANES), "space", 0, 0, tiled=True)
    total = jnp.sum(parts.astype(F32), axis=0)
    step = 1
    while step < copies // 2:
        total = total + lax.ppermute(total, "dp", [(i, i ^ step) for i in range(copies)])
        step *= 2
    other = jnp.zeros_like(total)
    if copies > 1:
        other = lax.ppermute(total, "dp", [(i, i ^ step) for i in range(copies)])
    grad_one, grad_two = pl.pallas_call(
        finish_body,
        out_shape=(jax.ShapeDtypeStruct((share * 54,), F32), jax.ShapeDtypeStruct((share * 864,), F32)),
        compiler_params=limit,
    )(total, other)
    return (features, pooled_grad, grad_one, grad_two)


def solution(mesh):
    in_specs = (P("dp", None, "space", None, None), P(), P(), P("dp", None, "space", None))
    out_specs = (P("dp", None, "space", None), P("dp", None, "space", None), P("space"), P("space"))
    return jax.shard_map(
        on_device, mesh=mesh, in_specs=in_specs, out_specs=out_specs, check_vma=False
    )
```

```python
import functools
import math

import jax
import jax.numpy as jnp
import numpy as np
from jax import lax
from jax.experimental import pallas as pl
from jax.experimental.pallas import tpu as pltpu
from jax.sharding import PartitionSpec as P

F32 = jnp.float32
BF16 = jnp.bfloat16
SHIFTS = [(dy, dx) for dy in (-1, 0, 1) for dx in (-1, 0, 1)]
NN = (((1,), (0,)), ((), ()))
NT = (((1,), (1,)), ((), ()))
LANES = 1024
ONE_AT = 896


def dot(a, b, dims=NN):
    return lax.dot_general(a, b, dims, preferred_element_type=F32)


def inside(cells, width):
    lane = lax.broadcasted_iota(jnp.int32, (1, cells), 1)
    col, row = lane & (width - 1), lax.shift_right_logical(lane, width.bit_length() - 1)

    def factor(pos, step):
        if step == 0:
            return None
        return jnp.where(pos < width - 1 if step > 0 else pos > 0, 1.0, 0.0)

    return [(factor(col, d), factor(row, d)) for d in (-1, 0, 1)]


def moved_by(field, move, factor):
    return field if move == 0 else pltpu.roll(field, (-move) % field.shape[1], 1) * factor


def all_shifts(field, width):
    factors = inside(field.shape[1], width)
    across = [moved_by(field, dx, factors[dx + 1][0]) for dx in (-1, 0, 1)]
    return [moved_by(across[dx + 1], dy * width, factors[dy + 1][1]) for dy, dx in SHIFTS]


def pool_pattern():
    cell = lax.broadcasted_iota(jnp.int32, (512, 128), 0)
    block = lax.broadcasted_iota(jnp.int32, (512, 128), 1)
    at = 16 * lax.shift_right_logical(cell, 6) + lax.shift_right_logical(cell & 31, 1)
    return jnp.where(at == block, 0.125, 0.0).astype(BF16)


def silu_parts(v):
    s = 0.5 + 0.5 * jnp.tanh(0.5 * v)
    return v * s, s


def band_maps():
    to_kernel = np.zeros((4, 216, 108), np.float32)
    to_flat = np.zeros((4, 256, 128), np.float32)
    for p in range(4):
        for s in range(9):
            for dz in range(3):
                q = p + dz - 1
                for ci in range(4):
                    if 0 <= q <= 3:
                        row = 16 * s + 4 * q + ci
                    else:
                        row = 144 + 8 * s + (0 if q < 0 else 4) + ci
                    tap = 9 * dz + s
                    to_kernel[p, row, 4 * tap + ci] = 1
                    to_flat[p, row, 64 * (ci // 2) + 27 * (ci % 2) + tap] = 1
    return to_kernel, to_flat.reshape(1024, 128)


def prepare_body(
    vol_hbm, cot_hbm, *refs,
):
    weights, (next_ref, near_ref, far_next_ref, far_near_ref) = refs[:4], refs[4:8]
    kept, (vol_ref, cot_ref, cells_ref, sems) = refs[8:12], refs[12:]
    me = lax.axis_index("space")
    odd, upper = me % 2 == 1, (me // 2) % 2 == 1
    vol_copy = pltpu.make_async_copy(vol_hbm, vol_ref, sems.at[0])
    cot_copy = pltpu.make_async_copy(cot_hbm, cot_ref, sems.at[1])
    vol_copy.start()
    cot_copy.start()
    copies = [
        pltpu.make_async_copy(src, dst, sems.at[2 + i])
        for i, (src, dst) in enumerate(zip(weights, kept))
    ]
    for copy in copies:
        copy.start()
    vol_copy.wait()
    cin, planes, width = vol_ref.shape[1:4]
    for plane in range(planes):
        for ch in range(cin):
            at = (plane * cin + ch) * width
            cells_ref[at : at + width] = vol_ref[0, ch, plane].astype(F32)
    count = planes * cin
    for b in range(4):
        lines = [cells_ref[pl.ds(8 * b + y, count, stride=width), :] for y in range(8)]
        rows = jnp.concatenate(lines, axis=1)
        near_ref[count * b : count * b + count] = rows.astype(BF16)
        next_ref[count * b : count * b + count] = rows.astype(BF16)
        first, last = rows[0:8], rows[8:16]
        far_near_ref[8 * b : 8 * b + 8] = jnp.where(upper, first, last).astype(BF16)
        far_next_ref[8 * b : 8 * b + 8] = jnp.where(upper, last, first).astype(BF16)
    cot_copy.wait()
    cot = cot_ref[0].astype(F32)
    cots = (cot[:, 0, :], cot[:, 1, :])
    near_ref[64:128] = jnp.where(odd, cots[0], cots[1]).astype(BF16)
    next_ref[64:128] = jnp.where(odd, cots[1], cots[0]).astype(BF16)
    for copy in copies:
        copy.wait()


def finish_body(mine_ref, other_ref, one_ref, two_ref):
    total = mine_ref[...] + other_ref[...]
    share = total.shape[0]
    first = lax.axis_index("space") * share
    two_ref[...] = jnp.concatenate([total[r, 0:864] for r in range(share)])
    low, high = (total[:, ONE_AT + 64 * h : ONE_AT + 64 * h + 54] for h in range(2))
    row = first + lax.broadcasted_iota(jnp.int32, low.shape, 0)
    one = jnp.where(row & 1 == 1, high, low)
    one_ref[...] = jnp.concatenate([one[r] for r in range(share)])


def unfold(block, rows):
    return jnp.concatenate([block[rows * b : rows * b + rows] for b in range(4)], axis=1)


def pool_sums(sums, pattern):
    rows = sums.shape[0]
    high = sums.astype(BF16)
    low = (sums - high.astype(F32)).astype(BF16)
    halves = [part[:, 512 * m : 512 * m + 512] for part in (high, low) for m in range(2)]
    out = dot(jnp.concatenate(halves, axis=0), pattern)
    out = out[0 : 2 * rows] + out[2 * rows : 4 * rows]
    return jnp.concatenate([out[0:rows], out[rows : 2 * rows]], axis=1)


def spread_cells(field, pattern):
    rows = field.shape[0]
    out = dot(jnp.concatenate([field[:, 0:128], field[:, 128:256]], axis=0), pattern, NT)
    return jnp.concatenate([out[0:rows], out[rows : 2 * rows]], axis=1)


def spread_taps(taps, half):
    factors = inside(half * half, half)
    total = None
    for dx in (-1, 0, 1):
        column = None
        for dy in (-1, 0, 1):
            s = 3 * (1 - dy) + (1 - dx)
            part = moved_by(taps[32 * s : 32 * s + 32], dy * half, factors[dy + 1][1])
            column = part if column is None else column + part
        column = moved_by(column, dx, factors[dx + 1][0])
        total = column if total is None else total + column
    return total


def inner_body(
    count,
    own_next_ref, own_near_ref, next_ref, near_ref, k1_ref, k2_ref, to_kernel_ref,
    feat_ref, two_ref, pgrad_ref, slope_ref, patch_ref, pre_ref, act_ref, pre_two_ref,
    far_one_ref, far_two_ref,
    term_ref,
):
    slabs = lax.axis_size("space")
    me = lax.axis_index("space")
    half = 16

    odd = me % 2 == 1
    own = unfold(own_near_ref[0:64].astype(F32), 16)
    near, following = near_ref[0:64].astype(F32), next_ref[0:64].astype(F32)
    left = unfold(jnp.where(odd, near, following), 16)
    right = unfold(jnp.where(odd, following, near), 16)
    top = lax.broadcasted_iota(jnp.int32, (8, LANES), 0) < 4
    edges = (
        jnp.where(top, 0.0, pltpu.roll(own[0:8], 4, 0)),
        jnp.where(top, pltpu.roll(left[8:16], 4, 0), pltpu.roll(right[0:8], 4, 0)),
        jnp.where(top, pltpu.roll(own[8:16], 4, 0), 0.0),
    )
    stack = jnp.concatenate([left, own, right, *edges], axis=0)
    moved = all_shifts(stack, 2 * half)
    patches = []
    for g in range(3):
        rows = [m[16 * g : 16 * g + 16] for m in moved] + [m[48 + 8 * g : 56 + 8 * g] for m in moved]
        patches.append(jnp.concatenate(rows, axis=0).astype(BF16))
    patch_ref[0:216] = patches[1]
    patch_ref[216:256] = jnp.zeros((40, LANES), BF16)

    k1t = k1_ref[...].astype(F32).reshape(108, 32).T.astype(BF16)
    k2t = k2_ref[...].astype(F32).T.astype(BF16)
    banded = jnp.concatenate(
        [dot(k1t, to_kernel_ref[p], NT).astype(BF16) for p in range(4)], axis=0
    )
    far_one_ref[...] = jnp.concatenate(
        [dot(k1t, to_kernel_ref[p, 144:216], NT).astype(BF16) for p in (0, 3)], axis=0
    )
    far_two_ref[0] = k2t[:, 0:288]
    far_two_ref[1] = k2t[:, 576:864]

    pattern = pool_pattern()
    pre = dot(banded, patches[0])
    pre_ref[0:32] = pre[0:32]
    act, _ = silu_parts(pre[32:128])
    act_ref[0:32] = act[0:32]
    sums = [act[32:64] + act[64:96]]
    pre = dot(banded, patches[1])
    act, s = silu_parts(pre)
    slope_ref[...] = s + act * (1.0 - s)
    sums += [act[0:32] + act[32:64], act[64:96] + act[96:128]]
    pre = dot(banded, patches[2])
    pre_ref[32:64] = pre[96:128]
    act, _ = silu_parts(pre[0:96])
    act_ref[32:64] = act[64:96]
    sums += [act[0:32] + act[32:64]]
    pooled = pool_sums(jnp.concatenate(sums, axis=0), pattern)
    plane = lax.shift_right_logical(lax.broadcasted_iota(jnp.int32, pooled.shape, 0), 5)
    real = ((plane > 0) | (me > 0)) & ((plane < 3) | (me < slabs - 1))
    pooled = jnp.where(real, pooled, 0.0).astype(BF16).astype(F32)

    moved = [m.astype(BF16) for m in all_shifts(pooled, half)]
    nothing = jnp.zeros((288, half * half), BF16)
    planes = [
        nothing,
        *(jnp.concatenate([m[32 * q : 32 * q + 32] for m in moved], axis=0) for q in range(4)),
        nothing,
    ]
    columns = [jnp.concatenate(planes[p : p + 3], axis=0) for p in range(4)]

    own_cots = own_near_ref[64:128].astype(F32), own_next_ref[64:128].astype(F32)
    cots = jnp.where(odd, *own_cots), jnp.where(odd, *own_cots[::-1])
    deltas = []
    for p in range(2):
        pre = dot(k2t, columns[p + 1])
        act, s = silu_parts(pre)
        feat_ref[0, :, p, :] = act.astype(BF16)
        deltas.append((cots[p] * (s + act * (1.0 - s))).astype(BF16))
    for i, p in enumerate((0, 3)):
        pre_two_ref[i] = dot(k2t, columns[p])

    both = jnp.concatenate(deltas, axis=0)
    for p in range(2):
        taps = [k2_ref[288 * (1 + p - q) : 288 * (1 + p - q) + 288] for q in range(2)]
        pgrad_ref[p] = spread_taps(dot(jnp.concatenate(taps, axis=1), both), half)

    term = dot(columns[1], deltas[0], NT) + dot(columns[2], deltas[1], NT)
    term_ref[...] = term * (1.0 / math.sqrt(count // 8))
    rows = [term_ref[pl.ds(ch, 27, stride=32), :] for ch in range(32)]
    two_ref[:, 0:864] = jnp.concatenate(rows, axis=0).T.astype(BF16)
    two_ref[:, 864:ONE_AT] = jnp.zeros((64, ONE_AT - 864), BF16)


def outer_body(
    count,
    far_next_ref, far_near_ref, next_ref, near_ref, k2_ref, to_flat_ref,
    two_ref, part_ref, slope_ref, patch_ref, pre_ref, act_ref, pre_two_ref,
    far_one_ref, far_two_ref,
    pgrad_hbm, send_ref,
    pgrad_ref, sem,
):
    slabs = lax.axis_size("space")
    me = lax.axis_index("space")
    half = 16
    odd, upper = me % 2 == 1, (me // 2) % 2 == 1
    pattern = pool_pattern()
    far_near, far_next = far_near_ref[...].astype(F32), far_next_ref[...].astype(F32)
    far_left = unfold(jnp.where(upper, far_near, far_next), 8)
    far_right = unfold(jnp.where(upper, far_next, far_near), 8)
    top = lax.broadcasted_iota(jnp.int32, (8, LANES), 0) < 4
    edge = jnp.where(top, pltpu.roll(far_left, 4, 0), pltpu.roll(far_right, 4, 0))
    patches = jnp.concatenate(all_shifts(edge, 2 * half), axis=0).astype(BF16)
    act, _ = silu_parts(pre_ref[...] + dot(far_one_ref[...], patches))
    pooled = pool_sums(act_ref[...] + act, pattern)
    plane = lax.shift_right_logical(lax.broadcasted_iota(jnp.int32, pooled.shape, 0), 5)
    real = ((plane > 0) | (me > 0)) & ((plane < 1) | (me < slabs - 1))
    pooled = jnp.where(real, pooled, 0.0).astype(BF16).astype(F32)
    moved = [m.astype(BF16) for m in all_shifts(pooled, half)]

    near, following = near_ref[64:128].astype(F32), next_ref[64:128].astype(F32)
    cots = jnp.where(odd, near, following), jnp.where(odd, following, near)
    grads = []
    for p in range(2):
        columns = jnp.concatenate([m[32 * p : 32 * p + 32] for m in moved], axis=0)
        pre = pre_two_ref[p] + dot(far_two_ref[p], columns)
        act, s = silu_parts(pre)
        delta = (cots[p] * (s + act * (1.0 - s))).astype(BF16)
        taps = dot(k2_ref[576 * (1 - p) : 576 * (1 - p) + 288], delta)
        grads.append((part_ref[p] + spread_taps(taps, half)).astype(BF16))
        pgrad_ref[0, :, p, :] = grads[p]
    pgrad_copy = pltpu.make_async_copy(pgrad_ref, pgrad_hbm, sem)
    pgrad_copy.start()

    spread = spread_cells(jnp.concatenate(grads, axis=0), pattern)
    spread = jnp.concatenate([spread[0:32], spread[0:32], spread[32:64], spread[32:64]], axis=0)
    delta_one = (spread * slope_ref[...]).astype(BF16)
    wide = dot(delta_one, patch_ref[...], NT)
    wide = jnp.concatenate([wide[32 * p : 32 * p + 32] for p in range(4)], axis=1)
    high = wide.astype(BF16)
    low = (wide - high.astype(F32)).astype(BF16)
    term_one = dot(jnp.concatenate([high, low], axis=0), to_flat_ref[...])
    term_one = ((term_one[0:32] + term_one[32:64]) * (1.0 / math.sqrt(count))).astype(BF16)
    to = lax.shift_right_logical(lax.broadcasted_iota(jnp.int32, (64, 32), 0), 1)
    at = lax.broadcasted_iota(jnp.int32, (64, 32), 1)
    send_ref[:, 0:ONE_AT] = two_ref[...]
    send_ref[:, ONE_AT:LANES] = dot(jnp.where(to == at, 1.0, 0.0).astype(BF16), term_one).astype(BF16)
    pgrad_copy.wait()


def on_device(volumes, kernel_one, kernel_two, cotangent):
    _, cin, planes, width, _ = volumes.shape
    half = width // 2
    slabs = lax.axis_size("space")
    copies = lax.axis_size("dp")
    count = copies * planes * slabs * width * width

    to_kernel, to_flat = band_maps()
    weights = (
        jnp.transpose(kernel_one, (2, 3, 4, 1, 0)).reshape(27, 4, 32),
        jnp.transpose(kernel_two, (2, 3, 4, 1, 0)).reshape(864, 64),
        jnp.asarray(to_kernel, BF16),
        jnp.asarray(to_flat, BF16),
    )

    def in_hbm(*arrays):
        return [pltpu.with_memory_space_constraint(x, pltpu.HBM) for x in arrays]

    inputs = in_hbm(volumes, cotangent, *weights)
    vmem, hbm = pl.BlockSpec(memory_space=pltpu.VMEM), pl.BlockSpec(memory_space=pltpu.HBM)
    limit = pltpu.CompilerParams(vmem_limit_bytes=48 * 1024 * 1024)
    whole = jax.ShapeDtypeStruct((128, width * width // 4), BF16)
    part = jax.ShapeDtypeStruct((32, width * width // 4), BF16)
    to_next, to_near, to_far_next, to_far_near, *weights = pl.pallas_call(
        prepare_body,
        out_shape=(
            whole, whole, part, part, *(jax.ShapeDtypeStruct(w.shape, BF16) for w in weights)
        ),
        in_specs=[hbm] * len(inputs),
        scratch_shapes=[
            pltpu.VMEM(volumes.shape, BF16),
            pltpu.VMEM(cotangent.shape, BF16),
            pltpu.VMEM((planes * cin * width, width), F32),
            pltpu.SemaphoreType.DMA((len(inputs),)),
        ],
        compiler_params=limit,
    )(*inputs)

    def swap(block, pairs):
        pairs = [p for p in pairs if max(p) < slabs]
        return lax.ppermute(block, "space", pairs + [(t, f) for f, t in pairs])

    evens = range(0, slabs, 2)
    fours = [i + j for i in range(0, slabs, 4) for j in range(2)]
    following = swap(to_next, [(i + 1, i + 2) for i in evens])
    near = swap(to_near, [(i, i + 1) for i in evens])
    far_next = swap(to_far_next, [(i + 2, i + 4) for i in fours])
    far_near = swap(to_far_near, [(i, i + 2) for i in fours])

    cells = half * half
    shapes = {
        "features": ((1, 64, 2, cells), BF16),
        "two": ((64, ONE_AT), BF16),
        "part": ((2, 32, cells), F32),
        "slope": ((128, LANES), F32),
        "patches": ((256, LANES), BF16),
        "pre": ((64, LANES), F32),
        "act": ((64, LANES), F32),
        "pre_two": ((2, 64, cells), F32),
        "far_one": ((64, 72), BF16),
        "far_two": ((2, 64, 288), BF16),
    }
    features, *inner = pl.pallas_call(
        functools.partial(inner_body, count),
        out_shape=tuple(jax.ShapeDtypeStruct(*x) for x in shapes.values()),
        scratch_shapes=[pltpu.VMEM((864, 64), F32)],
        compiler_params=limit,
        cost_estimate=pl.CostEstimate(flops=10**9, bytes_accessed=2 * 10**6, transcendentals=10**6),
    )(to_next, to_near, following, near, *weights[:3])
    pooled_grad, send = pl.pallas_call(
        functools.partial(outer_body, count),
        out_shape=(
            jax.ShapeDtypeStruct((1, 32, 2, cells), BF16),
            jax.ShapeDtypeStruct((64, LANES), BF16),
        ),
        out_specs=(hbm, vmem),
        scratch_shapes=[pltpu.VMEM((1, 32, 2, cells), BF16), pltpu.SemaphoreType.DMA],
        compiler_params=limit,
        cost_estimate=pl.CostEstimate(flops=10**8, bytes_accessed=2 * 10**6, transcendentals=10**6),
    )(far_next, far_near, following, near, weights[1], weights[3], *inner)

    share = 64 // slabs
    parts = lax.all_to_all(send.reshape(slabs, share, LANES), "space", 0, 0, tiled=True)
    total = jnp.sum(parts.astype(F32), axis=0)
    step = 1
    while step < copies // 2:
        total = total + lax.ppermute(total, "dp", [(i, i ^ step) for i in range(copies)])
        step *= 2
    other = jnp.zeros_like(total)
    if copies > 1:
        other = lax.ppermute(total, "dp", [(i, i ^ step) for i in range(copies)])
    grad_one, grad_two = pl.pallas_call(
        finish_body,
        out_shape=(jax.ShapeDtypeStruct((share * 54,), F32), jax.ShapeDtypeStruct((share * 864,), F32)),
        compiler_params=limit,
    )(total, other)
    return (features, pooled_grad, grad_one, grad_two)


def solution(mesh):
    in_specs = (P("dp", None, "space", None, None), P(), P(), P("dp", None, "space", None))
    out_specs = (P("dp", None, "space", None), P("dp", None, "space", None), P("space"), P("space"))
    return jax.shard_map(
        on_device, mesh=mesh, in_specs=in_specs, out_specs=out_specs, check_vma=False
    )
```

```python
import functools
import math

import jax
import jax.numpy as jnp
import numpy as np
from jax import lax
from jax.experimental import pallas as pl
from jax.experimental.pallas import tpu as pltpu
from jax.sharding import PartitionSpec as P

F32 = jnp.float32
BF16 = jnp.bfloat16
SHIFTS = [(dy, dx) for dy in (-1, 0, 1) for dx in (-1, 0, 1)]
NN = (((1,), (0,)), ((), ()))
NT = (((1,), (1,)), ((), ()))
LANES = 1024
ONE_AT = 896


def dot(a, b, dims=NN):
    return lax.dot_general(a, b, dims, preferred_element_type=F32)


def inside(cells, width):
    lane = lax.broadcasted_iota(jnp.int32, (1, cells), 1)
    col, row = lane & (width - 1), lax.shift_right_logical(lane, width.bit_length() - 1)

    def factor(pos, step):
        if step == 0:
            return None
        return jnp.where(pos < width - 1 if step > 0 else pos > 0, 1.0, 0.0)

    return [(factor(col, d), factor(row, d)) for d in (-1, 0, 1)]


def moved_by(field, move, factor):
    return field if move == 0 else pltpu.roll(field, (-move) % field.shape[1], 1) * factor


def all_shifts(field, width):
    factors = inside(field.shape[1], width)
    across = [moved_by(field, dx, factors[dx + 1][0]) for dx in (-1, 0, 1)]
    return [moved_by(across[dx + 1], dy * width, factors[dy + 1][1]) for dy, dx in SHIFTS]


def pool_pattern():
    cell = lax.broadcasted_iota(jnp.int32, (512, 128), 0)
    block = lax.broadcasted_iota(jnp.int32, (512, 128), 1)
    at = 16 * lax.shift_right_logical(cell, 6) + lax.shift_right_logical(cell & 31, 1)
    return jnp.where(at == block, 0.125, 0.0).astype(BF16)


def silu_parts(v):
    s = 0.5 + 0.5 * jnp.tanh(0.5 * v)
    return v * s, s


def band_maps():
    to_kernel = np.zeros((4, 216, 108), np.float32)
    to_flat = np.zeros((4, 256, 128), np.float32)
    for p in range(4):
        for s in range(9):
            for dz in range(3):
                q = p + dz - 1
                for ci in range(4):
                    if 0 <= q <= 3:
                        row = 16 * s + 4 * q + ci
                    else:
                        row = 144 + 8 * s + (0 if q < 0 else 4) + ci
                    tap = 9 * dz + s
                    to_kernel[p, row, 4 * tap + ci] = 1
                    to_flat[p, row, 64 * (ci // 2) + 27 * (ci % 2) + tap] = 1
    return to_kernel, to_flat.reshape(1024, 128)


def prepare_body(
    vol_hbm, cot_hbm, *refs,
):
    weights, (next_ref, near_ref, far_next_ref, far_near_ref) = refs[:4], refs[4:8]
    kept, (vol_ref, cot_ref, cells_ref, sems) = refs[8:12], refs[12:]
    me = lax.axis_index("space")
    odd, upper = me % 2 == 1, (me // 2) % 2 == 1
    vol_copy = pltpu.make_async_copy(vol_hbm, vol_ref, sems.at[0])
    cot_copy = pltpu.make_async_copy(cot_hbm, cot_ref, sems.at[1])
    vol_copy.start()
    cot_copy.start()
    copies = [
        pltpu.make_async_copy(src, dst, sems.at[2 + i])
        for i, (src, dst) in enumerate(zip(weights, kept))
    ]
    for copy in copies:
        copy.start()
    vol_copy.wait()
    cin, planes, width = vol_ref.shape[1:4]
    for plane in range(planes):
        for ch in range(cin):
            at = (plane * cin + ch) * width
            cells_ref[at : at + width] = vol_ref[0, ch, plane].astype(F32)
    count = planes * cin
    for b in range(4):
        lines = [cells_ref[pl.ds(8 * b + y, count, stride=width), :] for y in range(8)]
        rows = jnp.concatenate(lines, axis=1)
        near_ref[count * b : count * b + count] = rows.astype(BF16)
        next_ref[count * b : count * b + count] = rows.astype(BF16)
        first, last = rows[0:8], rows[8:16]
        far_near_ref[8 * b : 8 * b + 8] = jnp.where(upper, first, last).astype(BF16)
        far_next_ref[8 * b : 8 * b + 8] = jnp.where(upper, last, first).astype(BF16)
    cot_copy.wait()
    cot = cot_ref[0].astype(F32)
    cots = (cot[:, 0, :], cot[:, 1, :])
    near_ref[64:128] = jnp.where(odd, cots[0], cots[1]).astype(BF16)
    next_ref[64:128] = jnp.where(odd, cots[1], cots[0]).astype(BF16)
    for copy in copies:
        copy.wait()


def finish_body(mine_ref, other_ref, one_ref, two_ref):
    total = mine_ref[...] + other_ref[...]
    share = total.shape[0]
    first = lax.axis_index("space") * share
    two_ref[...] = jnp.concatenate([total[r, 0:864] for r in range(share)])
    low, high = (total[:, ONE_AT + 64 * h : ONE_AT + 64 * h + 54] for h in range(2))
    row = first + lax.broadcasted_iota(jnp.int32, low.shape, 0)
    one = jnp.where(row & 1 == 1, high, low)
    one_ref[...] = jnp.concatenate([one[r] for r in range(share)])


def unfold(block, rows):
    return jnp.concatenate([block[rows * b : rows * b + rows] for b in range(4)], axis=1)


def pool_sums(sums, pattern):
    rows = sums.shape[0]
    high = sums.astype(BF16)
    low = (sums - high.astype(F32)).astype(BF16)
    halves = [part[:, 512 * m : 512 * m + 512] for part in (high, low) for m in range(2)]
    out = dot(jnp.concatenate(halves, axis=0), pattern)
    out = out[0 : 2 * rows] + out[2 * rows : 4 * rows]
    return jnp.concatenate([out[0:rows], out[rows : 2 * rows]], axis=1)


def spread_cells(field, pattern):
    rows = field.shape[0]
    out = dot(jnp.concatenate([field[:, 0:128], field[:, 128:256]], axis=0), pattern, NT)
    return jnp.concatenate([out[0:rows], out[rows : 2 * rows]], axis=1)


def spread_taps(taps, half):
    factors = inside(half * half, half)
    total = None
    for dx in (-1, 0, 1):
        column = None
        for dy in (-1, 0, 1):
            s = 3 * (1 - dy) + (1 - dx)
            part = moved_by(taps[32 * s : 32 * s + 32], dy * half, factors[dy + 1][1])
            column = part if column is None else column + part
        column = moved_by(column, dx, factors[dx + 1][0])
        total = column if total is None else total + column
    return total


def inner_body(
    count,
    own_next_ref, own_near_ref, next_ref, near_ref, k1_ref, k2_ref, to_kernel_ref,
    feat_ref, two_ref, pgrad_ref, slope_ref, patch_ref, pre_ref, act_ref, pre_two_ref,
    far_one_ref, far_two_ref,
    term_ref,
):
    slabs = lax.axis_size("space")
    me = lax.axis_index("space")
    half = 16

    odd = me % 2 == 1
    own = unfold(own_near_ref[0:64].astype(F32), 16)
    near, following = near_ref[0:64].astype(F32), next_ref[0:64].astype(F32)
    left = unfold(jnp.where(odd, near, following), 16)
    right = unfold(jnp.where(odd, following, near), 16)
    top = lax.broadcasted_iota(jnp.int32, (8, LANES), 0) < 4
    edges = (
        jnp.where(top, 0.0, pltpu.roll(own[0:8], 4, 0)),
        jnp.where(top, pltpu.roll(left[8:16], 4, 0), pltpu.roll(right[0:8], 4, 0)),
        jnp.where(top, pltpu.roll(own[8:16], 4, 0), 0.0),
    )
    stack = jnp.concatenate([left, own, right, *edges], axis=0)
    moved = all_shifts(stack, 2 * half)
    patches = []
    for g in range(3):
        rows = [m[16 * g : 16 * g + 16] for m in moved] + [m[48 + 8 * g : 56 + 8 * g] for m in moved]
        patches.append(jnp.concatenate(rows, axis=0).astype(BF16))
    patch_ref[0:216] = patches[1]
    patch_ref[216:256] = jnp.zeros((40, LANES), BF16)

    k1t = k1_ref[...].astype(F32).reshape(108, 32).T.astype(BF16)
    k2t = k2_ref[...].astype(F32).T.astype(BF16)
    banded = jnp.concatenate(
        [dot(k1t, to_kernel_ref[p], NT).astype(BF16) for p in range(4)], axis=0
    )
    far_one_ref[...] = jnp.concatenate(
        [dot(k1t, to_kernel_ref[p, 144:216], NT).astype(BF16) for p in (0, 3)], axis=0
    )
    far_two_ref[0] = k2t[:, 0:288]
    far_two_ref[1] = k2t[:, 576:864]

    pattern = pool_pattern()
    pre = dot(banded, patches[0])
    pre_ref[0:32] = pre[0:32]
    act, _ = silu_parts(pre[32:128])
    act_ref[0:32] = act[0:32]
    sums = [act[32:64] + act[64:96]]
    pre = dot(banded, patches[1])
    act, s = silu_parts(pre)
    slope_ref[...] = s + act * (1.0 - s)
    sums += [act[0:32] + act[32:64], act[64:96] + act[96:128]]
    pre = dot(banded, patches[2])
    pre_ref[32:64] = pre[96:128]
    act, _ = silu_parts(pre[0:96])
    act_ref[32:64] = act[64:96]
    sums += [act[0:32] + act[32:64]]
    pooled = pool_sums(jnp.concatenate(sums, axis=0), pattern)
    plane = lax.shift_right_logical(lax.broadcasted_iota(jnp.int32, pooled.shape, 0), 5)
    real = ((plane > 0) | (me > 0)) & ((plane < 3) | (me < slabs - 1))
    pooled = jnp.where(real, pooled, 0.0).astype(BF16).astype(F32)

    moved = [m.astype(BF16) for m in all_shifts(pooled, half)]
    nothing = jnp.zeros((288, half * half), BF16)
    planes = [
        nothing,
        *(jnp.concatenate([m[32 * q : 32 * q + 32] for m in moved], axis=0) for q in range(4)),
        nothing,
    ]
    columns = [jnp.concatenate(planes[p : p + 3], axis=0) for p in range(4)]

    own_cots = own_near_ref[64:128].astype(F32), own_next_ref[64:128].astype(F32)
    cots = jnp.where(odd, *own_cots), jnp.where(odd, *own_cots[::-1])
    deltas = []
    for p in range(2):
        pre = dot(k2t, columns[p + 1])
        act, s = silu_parts(pre)
        feat_ref[p] = act.astype(BF16)
        deltas.append((cots[p] * (s + act * (1.0 - s))).astype(BF16))
    for i, p in enumerate((0, 3)):
        pre_two_ref[i] = dot(k2t, columns[p])

    both = jnp.concatenate(deltas, axis=0)
    for p in range(2):
        taps = [k2_ref[288 * (1 + p - q) : 288 * (1 + p - q) + 288] for q in range(2)]
        pgrad_ref[p] = spread_taps(dot(jnp.concatenate(taps, axis=1), both), half)

    term = dot(columns[1], deltas[0], NT) + dot(columns[2], deltas[1], NT)
    term_ref[...] = term * (1.0 / math.sqrt(count // 8))
    rows = [term_ref[pl.ds(ch, 27, stride=32), :] for ch in range(32)]
    two_ref[:, 0:864] = jnp.concatenate(rows, axis=0).T.astype(BF16)
    two_ref[:, 864:ONE_AT] = jnp.zeros((64, ONE_AT - 864), BF16)


def outer_body(
    count,
    far_next_ref, far_near_ref, next_ref, near_ref, k2_ref, to_flat_ref,
    two_ref, part_ref, slope_ref, patch_ref, pre_ref, act_ref, pre_two_ref,
    far_one_ref, far_two_ref,
    pgrad_ref, send_ref,
    rows_ref,
):
    slabs = lax.axis_size("space")
    me = lax.axis_index("space")
    half = 16
    odd, upper = me % 2 == 1, (me // 2) % 2 == 1
    pattern = pool_pattern()
    far_near, far_next = far_near_ref[...].astype(F32), far_next_ref[...].astype(F32)
    far_left = unfold(jnp.where(upper, far_near, far_next), 8)
    far_right = unfold(jnp.where(upper, far_next, far_near), 8)
    top = lax.broadcasted_iota(jnp.int32, (8, LANES), 0) < 4
    edge = jnp.where(top, pltpu.roll(far_left, 4, 0), pltpu.roll(far_right, 4, 0))
    patches = jnp.concatenate(all_shifts(edge, 2 * half), axis=0).astype(BF16)
    act, _ = silu_parts(pre_ref[...] + dot(far_one_ref[...], patches))
    pooled = pool_sums(act_ref[...] + act, pattern)
    plane = lax.shift_right_logical(lax.broadcasted_iota(jnp.int32, pooled.shape, 0), 5)
    real = ((plane > 0) | (me > 0)) & ((plane < 1) | (me < slabs - 1))
    pooled = jnp.where(real, pooled, 0.0).astype(BF16).astype(F32)
    moved = [m.astype(BF16) for m in all_shifts(pooled, half)]

    near, following = near_ref[64:128].astype(F32), next_ref[64:128].astype(F32)
    cots = jnp.where(odd, near, following), jnp.where(odd, following, near)
    grads = []
    for p in range(2):
        columns = jnp.concatenate([m[32 * p : 32 * p + 32] for m in moved], axis=0)
        pre = pre_two_ref[p] + dot(far_two_ref[p], columns)
        act, s = silu_parts(pre)
        delta = (cots[p] * (s + act * (1.0 - s))).astype(BF16)
        taps = dot(k2_ref[576 * (1 - p) : 576 * (1 - p) + 288], delta)
        grads.append((part_ref[p] + spread_taps(taps, half)).astype(BF16))
        pgrad_ref[p] = grads[p]

    spread = spread_cells(jnp.concatenate(grads, axis=0), pattern)
    spread = jnp.concatenate([spread[0:32], spread[0:32], spread[32:64], spread[32:64]], axis=0)
    delta_one = (spread * slope_ref[...]).astype(BF16)
    wide = dot(delta_one, patch_ref[...], NT)
    wide = jnp.concatenate([wide[32 * p : 32 * p + 32] for p in range(4)], axis=1)
    high = wide.astype(BF16)
    low = (wide - high.astype(F32)).astype(BF16)
    term_one = dot(jnp.concatenate([high, low], axis=0), to_flat_ref[...])
    term_one = (term_one[0:32] + term_one[32:64]) * (1.0 / math.sqrt(count))
    for i in range(2):
        rows_ref[pl.ds(i, 32, stride=2), :] = term_one
    send_ref[:, 0:ONE_AT] = two_ref[...]
    send_ref[:, ONE_AT:LANES] = rows_ref[...].astype(BF16)


def lay_out_body(feat_ref, pgrad_ref, feat_out, pgrad_out):
    for source, target in ((feat_ref, feat_out), (pgrad_ref, pgrad_out)):
        for p in range(2):
            target[0, :, p, :] = source[p]


def on_device(volumes, kernel_one, kernel_two, cotangent):
    _, cin, planes, width, _ = volumes.shape
    half = width // 2
    slabs = lax.axis_size("space")
    copies = lax.axis_size("dp")
    count = copies * planes * slabs * width * width

    to_kernel, to_flat = band_maps()
    weights = (
        jnp.transpose(kernel_one, (2, 3, 4, 1, 0)).reshape(27, 4, 32),
        jnp.transpose(kernel_two, (2, 3, 4, 1, 0)).reshape(864, 64),
        jnp.asarray(to_kernel, BF16),
        jnp.asarray(to_flat, BF16),
    )

    def in_hbm(*arrays):
        return [pltpu.with_memory_space_constraint(x, pltpu.HBM) for x in arrays]

    inputs = in_hbm(volumes, cotangent, *weights)
    hbm = pl.BlockSpec(memory_space=pltpu.HBM)
    limit = pltpu.CompilerParams(vmem_limit_bytes=48 * 1024 * 1024)
    whole = jax.ShapeDtypeStruct((128, width * width // 4), BF16)
    part = jax.ShapeDtypeStruct((32, width * width // 4), BF16)
    to_next, to_near, to_far_next, to_far_near, *weights = pl.pallas_call(
        prepare_body,
        out_shape=(
            whole, whole, part, part, *(jax.ShapeDtypeStruct(w.shape, BF16) for w in weights)
        ),
        in_specs=[hbm] * len(inputs),
        scratch_shapes=[
            pltpu.VMEM(volumes.shape, BF16),
            pltpu.VMEM(cotangent.shape, BF16),
            pltpu.VMEM((planes * cin * width, width), F32),
            pltpu.SemaphoreType.DMA((len(inputs),)),
        ],
        compiler_params=limit,
    )(*inputs)

    def swap(block, pairs):
        pairs = [p for p in pairs if max(p) < slabs]
        return lax.ppermute(block, "space", pairs + [(t, f) for f, t in pairs])

    evens = range(0, slabs, 2)
    fours = [i + j for i in range(0, slabs, 4) for j in range(2)]
    following = swap(to_next, [(i + 1, i + 2) for i in evens])
    near = swap(to_near, [(i, i + 1) for i in evens])
    far_next = swap(to_far_next, [(i + 2, i + 4) for i in fours])
    far_near = swap(to_far_near, [(i, i + 2) for i in fours])

    cells = half * half
    shapes = {
        "features": ((2, 64, cells), BF16),
        "two": ((64, ONE_AT), BF16),
        "part": ((2, 32, cells), F32),
        "slope": ((128, LANES), F32),
        "patches": ((256, LANES), BF16),
        "pre": ((64, LANES), F32),
        "act": ((64, LANES), F32),
        "pre_two": ((2, 64, cells), F32),
        "far_one": ((64, 72), BF16),
        "far_two": ((2, 64, 288), BF16),
    }
    feat, *inner = pl.pallas_call(
        functools.partial(inner_body, count),
        out_shape=tuple(jax.ShapeDtypeStruct(*x) for x in shapes.values()),
        scratch_shapes=[pltpu.VMEM((864, 64), F32)],
        compiler_params=limit,
        cost_estimate=pl.CostEstimate(flops=10**9, bytes_accessed=2 * 10**6, transcendentals=10**6),
    )(to_next, to_near, following, near, *weights[:3])
    pgrad, send = pl.pallas_call(
        functools.partial(outer_body, count),
        out_shape=(
            jax.ShapeDtypeStruct((2, 32, cells), BF16),
            jax.ShapeDtypeStruct((64, LANES), BF16),
        ),
        scratch_shapes=[pltpu.VMEM((64, 128), F32)],
        compiler_params=limit,
        cost_estimate=pl.CostEstimate(flops=10**8, bytes_accessed=2 * 10**6, transcendentals=10**6),
    )(far_next, far_near, following, near, weights[1], weights[3], *inner)

    share = 64 // slabs
    parts = lax.all_to_all(send.reshape(slabs, share, LANES), "space", 0, 0, tiled=True)
    total = jnp.sum(parts.astype(F32), axis=0)
    step = 1
    while step < copies // 2:
        total = total + lax.ppermute(total, "dp", [(i, i ^ step) for i in range(copies)])
        step *= 2
    other = jnp.zeros_like(total)
    if copies > 1:
        other = lax.ppermute(total, "dp", [(i, i ^ step) for i in range(copies)])
    grad_one, grad_two = pl.pallas_call(
        finish_body,
        out_shape=(jax.ShapeDtypeStruct((share * 54,), F32), jax.ShapeDtypeStruct((share * 864,), F32)),
        compiler_params=limit,
    )(total, other)
    features, pooled_grad = pl.pallas_call(
        lay_out_body,
        out_shape=(
            jax.ShapeDtypeStruct((1, 64, 2, cells), BF16),
            jax.ShapeDtypeStruct((1, 32, 2, cells), BF16),
        ),
        compiler_params=limit,
        cost_estimate=pl.CostEstimate(flops=10**6, bytes_accessed=2 * 10**5, transcendentals=0),
    )(feat, pgrad)
    return (features, pooled_grad, grad_one, grad_two)


def solution(mesh):
    in_specs = (P("dp", None, "space", None, None), P(), P(), P("dp", None, "space", None))
    out_specs = (P("dp", None, "space", None), P("dp", None, "space", None), P("space"), P("space"))
    return jax.shard_map(
        on_device, mesh=mesh, in_specs=in_specs, out_specs=out_specs, check_vma=False
    )
```

```python
import functools
import math

import jax
import jax.numpy as jnp
import numpy as np
from jax import lax
from jax.experimental import pallas as pl
from jax.experimental.pallas import tpu as pltpu
from jax.sharding import PartitionSpec as P

F32 = jnp.float32
BF16 = jnp.bfloat16
SHIFTS = [(dy, dx) for dy in (-1, 0, 1) for dx in (-1, 0, 1)]
NN = (((1,), (0,)), ((), ()))
NT = (((1,), (1,)), ((), ()))
LANES = 1024
HALF = 512


def dot(a, b, dims=NN):
    return lax.dot_general(a, b, dims, preferred_element_type=F32)


def inside(cells, width):
    lane = lax.broadcasted_iota(jnp.int32, (1, cells), 1)
    col, row = lane & (width - 1), lax.shift_right_logical(lane, width.bit_length() - 1)

    def factor(pos, step):
        if step == 0:
            return None
        return jnp.where(pos < width - 1 if step > 0 else pos > 0, 1.0, 0.0)

    return [(factor(col, d), factor(row, d)) for d in (-1, 0, 1)]


def moved_by(field, move, factor):
    return field if move == 0 else pltpu.roll(field, (-move) % field.shape[1], 1) * factor


def all_shifts(field, width):
    factors = inside(field.shape[1], width)
    across = [moved_by(field, dx, factors[dx + 1][0]) for dx in (-1, 0, 1)]
    return [moved_by(across[dx + 1], dy * width, factors[dy + 1][1]) for dy, dx in SHIFTS]


def pool_pattern():
    cell = lax.broadcasted_iota(jnp.int32, (512, 128), 0)
    block = lax.broadcasted_iota(jnp.int32, (512, 128), 1)
    at = 16 * lax.shift_right_logical(cell, 6) + lax.shift_right_logical(cell & 31, 1)
    return jnp.where(at == block, 0.125, 0.0).astype(BF16)


def silu_parts(v):
    s = 0.5 + 0.5 * jnp.tanh(0.5 * v)
    return v * s, s


def band_maps():
    to_kernel = np.zeros((4, 216, 108), np.float32)
    to_flat = np.zeros((4, 256, 128), np.float32)
    for p in range(4):
        for s in range(9):
            for dz in range(3):
                q = p + dz - 1
                for ci in range(4):
                    if 0 <= q <= 3:
                        row = 16 * s + 4 * q + ci
                    else:
                        row = 144 + 8 * s + (0 if q < 0 else 4) + ci
                    tap = 9 * dz + s
                    to_kernel[p, row, 4 * tap + ci] = 1
                    to_flat[p, row, 64 * (ci // 2) + 27 * (ci % 2) + tap] = 1
    return to_kernel, to_flat.reshape(1024, 128)


def prepare_body(
    vol_hbm, cot_hbm, *refs,
):
    weights, (next_ref, near_ref, far_next_ref, far_near_ref) = refs[:4], refs[4:8]
    kept, (vol_ref, cot_ref, cells_ref, sems) = refs[8:12], refs[12:]
    me = lax.axis_index("space")
    odd, upper = me % 2 == 1, (me // 2) % 2 == 1
    vol_copy = pltpu.make_async_copy(vol_hbm, vol_ref, sems.at[0])
    cot_copy = pltpu.make_async_copy(cot_hbm, cot_ref, sems.at[1])
    vol_copy.start()
    cot_copy.start()
    copies = [
        pltpu.make_async_copy(src, dst, sems.at[2 + i])
        for i, (src, dst) in enumerate(zip(weights, kept))
    ]
    for copy in copies:
        copy.start()
    vol_copy.wait()
    cin, planes, width = vol_ref.shape[1:4]
    for plane in range(planes):
        for ch in range(cin):
            at = (plane * cin + ch) * width
            cells_ref[at : at + width] = vol_ref[0, ch, plane].astype(F32)
    count = planes * cin
    for b in range(4):
        lines = [cells_ref[pl.ds(8 * b + y, count, stride=width), :] for y in range(8)]
        rows = jnp.concatenate(lines, axis=1)
        near_ref[count * b : count * b + count] = rows.astype(BF16)
        next_ref[count * b : count * b + count] = rows.astype(BF16)
        first, last = rows[0:8], rows[8:16]
        far_near_ref[8 * b : 8 * b + 8] = jnp.where(upper, first, last).astype(BF16)
        far_next_ref[8 * b : 8 * b + 8] = jnp.where(upper, last, first).astype(BF16)
    cot_copy.wait()
    cot = cot_ref[0].astype(F32)
    cots = (cot[:, 0, :], cot[:, 1, :])
    near_ref[64:128] = jnp.where(odd, cots[0], cots[1]).astype(BF16)
    next_ref[64:128] = jnp.where(odd, cots[1], cots[0]).astype(BF16)
    for copy in copies:
        copy.wait()


def finish_body(mine_ref, other_ref, one_ref, two_ref):
    mine, other = mine_ref[...], other_ref[...]
    share = mine.shape[0]
    first = lax.axis_index("space") * share
    second = lax.axis_index("dp") & 1 == 1
    halves = jnp.where(second, other, mine)[:, 0:HALF], jnp.where(second, mine, other)[:, 0:HALF]
    two = jnp.concatenate(halves, axis=1)[:, 0:864]
    two_ref[...] = jnp.concatenate([two[r] for r in range(share)])
    total = mine[:, HALF:] + other[:, HALF:]
    low, high = (total[:, 64 * h : 64 * h + 54] for h in range(2))
    row = first + lax.broadcasted_iota(jnp.int32, low.shape, 0)
    one = jnp.where(row & 1 == 1, high, low)
    one_ref[...] = jnp.concatenate([one[r] for r in range(share)])


def unfold(block, rows):
    return jnp.concatenate([block[rows * b : rows * b + rows] for b in range(4)], axis=1)


def pool_sums(sums, pattern):
    rows = sums.shape[0]
    high = sums.astype(BF16)
    low = (sums - high.astype(F32)).astype(BF16)
    halves = [part[:, 512 * m : 512 * m + 512] for part in (high, low) for m in range(2)]
    out = dot(jnp.concatenate(halves, axis=0), pattern)
    out = out[0 : 2 * rows] + out[2 * rows : 4 * rows]
    return jnp.concatenate([out[0:rows], out[rows : 2 * rows]], axis=1)


def spread_cells(field, pattern):
    rows = field.shape[0]
    out = dot(jnp.concatenate([field[:, 0:128], field[:, 128:256]], axis=0), pattern, NT)
    return jnp.concatenate([out[0:rows], out[rows : 2 * rows]], axis=1)


def spread_taps(taps, half):
    factors = inside(half * half, half)
    total = None
    for dx in (-1, 0, 1):
        column = None
        for dy in (-1, 0, 1):
            s = 3 * (1 - dy) + (1 - dx)
            part = moved_by(taps[32 * s : 32 * s + 32], dy * half, factors[dy + 1][1])
            column = part if column is None else column + part
        column = moved_by(column, dx, factors[dx + 1][0])
        total = column if total is None else total + column
    return total


def inner_body(
    count,
    own_next_ref, own_near_ref, next_ref, near_ref, k1_ref, k2_ref, to_kernel_ref,
    feat_ref, mine_ref, theirs_ref, pgrad_ref, slope_ref, patch_ref, pre_ref, act_ref, pre_two_ref,
    far_one_ref, far_two_ref,
    term_ref,
):
    slabs = lax.axis_size("space")
    me = lax.axis_index("space")
    half = 16

    odd = me % 2 == 1
    own = unfold(own_near_ref[0:64].astype(F32), 16)
    near, following = near_ref[0:64].astype(F32), next_ref[0:64].astype(F32)
    left = unfold(jnp.where(odd, near, following), 16)
    right = unfold(jnp.where(odd, following, near), 16)
    top = lax.broadcasted_iota(jnp.int32, (8, LANES), 0) < 4
    edges = (
        jnp.where(top, 0.0, pltpu.roll(own[0:8], 4, 0)),
        jnp.where(top, pltpu.roll(left[8:16], 4, 0), pltpu.roll(right[0:8], 4, 0)),
        jnp.where(top, pltpu.roll(own[8:16], 4, 0), 0.0),
    )
    stack = jnp.concatenate([left, own, right, *edges], axis=0)
    moved = all_shifts(stack, 2 * half)
    patches = []
    for g in range(3):
        rows = [m[16 * g : 16 * g + 16] for m in moved] + [m[48 + 8 * g : 56 + 8 * g] for m in moved]
        patches.append(jnp.concatenate(rows, axis=0).astype(BF16))
    patch_ref[0:216] = patches[1]
    patch_ref[216:256] = jnp.zeros((40, LANES), BF16)

    k1t = k1_ref[...].astype(F32).reshape(108, 32).T.astype(BF16)
    k2t = k2_ref[...].astype(F32).T.astype(BF16)
    banded = jnp.concatenate(
        [dot(k1t, to_kernel_ref[p], NT).astype(BF16) for p in range(4)], axis=0
    )
    far_one_ref[...] = jnp.concatenate(
        [dot(k1t, to_kernel_ref[p, 144:216], NT).astype(BF16) for p in (0, 3)], axis=0
    )
    far_two_ref[0] = k2t[:, 0:288]
    far_two_ref[1] = k2t[:, 576:864]

    pattern = pool_pattern()
    pre = dot(banded, patches[0])
    pre_ref[0:32] = pre[0:32]
    act, _ = silu_parts(pre[32:128])
    act_ref[0:32] = act[0:32]
    sums = [act[32:64] + act[64:96]]
    pre = dot(banded, patches[1])
    act, s = silu_parts(pre)
    slope_ref[...] = s + act * (1.0 - s)
    sums += [act[0:32] + act[32:64], act[64:96] + act[96:128]]
    pre = dot(banded, patches[2])
    pre_ref[32:64] = pre[96:128]
    act, _ = silu_parts(pre[0:96])
    act_ref[32:64] = act[64:96]
    sums += [act[0:32] + act[32:64]]
    pooled = pool_sums(jnp.concatenate(sums, axis=0), pattern)
    plane = lax.shift_right_logical(lax.broadcasted_iota(jnp.int32, pooled.shape, 0), 5)
    real = ((plane > 0) | (me > 0)) & ((plane < 3) | (me < slabs - 1))
    pooled = jnp.where(real, pooled, 0.0).astype(BF16).astype(F32)

    moved = [m.astype(BF16) for m in all_shifts(pooled, half)]
    nothing = jnp.zeros((288, half * half), BF16)
    planes = [
        nothing,
        *(jnp.concatenate([m[32 * q : 32 * q + 32] for m in moved], axis=0) for q in range(4)),
        nothing,
    ]
    columns = [jnp.concatenate(planes[p : p + 3], axis=0) for p in range(4)]

    own_cots = own_near_ref[64:128].astype(F32), own_next_ref[64:128].astype(F32)
    cots = jnp.where(odd, *own_cots), jnp.where(odd, *own_cots[::-1])
    deltas = []
    for p in range(2):
        pre = dot(k2t, columns[p + 1])
        act, s = silu_parts(pre)
        feat_ref[p] = act.astype(BF16)
        deltas.append((cots[p] * (s + act * (1.0 - s))).astype(BF16))
    for i, p in enumerate((0, 3)):
        pre_two_ref[i] = dot(k2t, columns[p])

    both = jnp.concatenate(deltas, axis=0)
    for p in range(2):
        taps = [k2_ref[288 * (1 + p - q) : 288 * (1 + p - q) + 288] for q in range(2)]
        pgrad_ref[p] = spread_taps(dot(jnp.concatenate(taps, axis=1), both), half)

    term = dot(columns[1], deltas[0], NT) + dot(columns[2], deltas[1], NT)
    term_ref[...] = term * (1.0 / math.sqrt(count // 8))
    rows = [term_ref[pl.ds(ch, 27, stride=32), :] for ch in range(32)]
    two = jnp.concatenate(rows, axis=0).T
    halves = two[:, 0:HALF], jnp.concatenate([two[:, HALF:], jnp.zeros((64, 2 * HALF - 864), F32)], axis=1)
    second = lax.axis_index("dp") & 1 == 1
    mine_ref[...] = jnp.where(second, halves[1], halves[0])
    theirs_ref[...] = jnp.where(second, halves[0], halves[1])


def outer_body(
    count,
    far_next_ref, far_near_ref, next_ref, near_ref, k2_ref, to_flat_ref,
    part_ref, slope_ref, patch_ref, pre_ref, act_ref, pre_two_ref,
    far_one_ref, far_two_ref,
    pgrad_ref, one_ref,
    rows_ref,
):
    slabs = lax.axis_size("space")
    me = lax.axis_index("space")
    half = 16
    odd, upper = me % 2 == 1, (me // 2) % 2 == 1
    pattern = pool_pattern()
    far_near, far_next = far_near_ref[...].astype(F32), far_next_ref[...].astype(F32)
    far_left = unfold(jnp.where(upper, far_near, far_next), 8)
    far_right = unfold(jnp.where(upper, far_next, far_near), 8)
    top = lax.broadcasted_iota(jnp.int32, (8, LANES), 0) < 4
    edge = jnp.where(top, pltpu.roll(far_left, 4, 0), pltpu.roll(far_right, 4, 0))
    patches = jnp.concatenate(all_shifts(edge, 2 * half), axis=0).astype(BF16)
    act, _ = silu_parts(pre_ref[...] + dot(far_one_ref[...], patches))
    pooled = pool_sums(act_ref[...] + act, pattern)
    plane = lax.shift_right_logical(lax.broadcasted_iota(jnp.int32, pooled.shape, 0), 5)
    real = ((plane > 0) | (me > 0)) & ((plane < 1) | (me < slabs - 1))
    pooled = jnp.where(real, pooled, 0.0).astype(BF16).astype(F32)
    moved = [m.astype(BF16) for m in all_shifts(pooled, half)]

    near, following = near_ref[64:128].astype(F32), next_ref[64:128].astype(F32)
    cots = jnp.where(odd, near, following), jnp.where(odd, following, near)
    grads = []
    for p in range(2):
        columns = jnp.concatenate([m[32 * p : 32 * p + 32] for m in moved], axis=0)
        pre = pre_two_ref[p] + dot(far_two_ref[p], columns)
        act, s = silu_parts(pre)
        delta = (cots[p] * (s + act * (1.0 - s))).astype(BF16)
        taps = dot(k2_ref[576 * (1 - p) : 576 * (1 - p) + 288], delta)
        grads.append((part_ref[p] + spread_taps(taps, half)).astype(BF16))
        pgrad_ref[p] = grads[p]

    spread = spread_cells(jnp.concatenate(grads, axis=0), pattern)
    spread = jnp.concatenate([spread[0:32], spread[0:32], spread[32:64], spread[32:64]], axis=0)
    delta_one = (spread * slope_ref[...]).astype(BF16)
    wide = dot(delta_one, patch_ref[...], NT)
    wide = jnp.concatenate([wide[32 * p : 32 * p + 32] for p in range(4)], axis=1)
    high = wide.astype(BF16)
    low = (wide - high.astype(F32)).astype(BF16)
    term_one = dot(jnp.concatenate([high, low], axis=0), to_flat_ref[...])
    term_one = (term_one[0:32] + term_one[32:64]) * (1.0 / math.sqrt(count))
    for i in range(2):
        rows_ref[pl.ds(i, 32, stride=2), :] = term_one
    one_ref[...] = rows_ref[...].astype(BF16)


def lay_out_body(feat_ref, pgrad_ref, feat_out, pgrad_out):
    for source, target in ((feat_ref, feat_out), (pgrad_ref, pgrad_out)):
        for p in range(2):
            target[0, :, p, :] = source[p]


def on_device(volumes, kernel_one, kernel_two, cotangent):
    _, cin, planes, width, _ = volumes.shape
    half = width // 2
    slabs = lax.axis_size("space")
    copies = lax.axis_size("dp")
    count = copies * planes * slabs * width * width

    to_kernel, to_flat = band_maps()
    weights = (
        jnp.transpose(kernel_one, (2, 3, 4, 1, 0)).reshape(27, 4, 32),
        jnp.transpose(kernel_two, (2, 3, 4, 1, 0)).reshape(864, 64),
        jnp.asarray(to_kernel, BF16),
        jnp.asarray(to_flat, BF16),
    )

    def in_hbm(*arrays):
        return [pltpu.with_memory_space_constraint(x, pltpu.HBM) for x in arrays]

    inputs = in_hbm(volumes, cotangent, *weights)
    hbm = pl.BlockSpec(memory_space=pltpu.HBM)
    limit = pltpu.CompilerParams(vmem_limit_bytes=48 * 1024 * 1024)
    whole = jax.ShapeDtypeStruct((128, width * width // 4), BF16)
    part = jax.ShapeDtypeStruct((32, width * width // 4), BF16)
    to_next, to_near, to_far_next, to_far_near, *weights = pl.pallas_call(
        prepare_body,
        out_shape=(
            whole, whole, part, part, *(jax.ShapeDtypeStruct(w.shape, BF16) for w in weights)
        ),
        in_specs=[hbm] * len(inputs),
        scratch_shapes=[
            pltpu.VMEM(volumes.shape, BF16),
            pltpu.VMEM(cotangent.shape, BF16),
            pltpu.VMEM((planes * cin * width, width), F32),
            pltpu.SemaphoreType.DMA((len(inputs),)),
        ],
        compiler_params=limit,
    )(*inputs)

    def swap(block, pairs):
        pairs = [p for p in pairs if max(p) < slabs]
        return lax.ppermute(block, "space", pairs + [(t, f) for f, t in pairs])

    evens = range(0, slabs, 2)
    fours = [i + j for i in range(0, slabs, 4) for j in range(2)]
    following = swap(to_next, [(i + 1, i + 2) for i in evens])
    near = swap(to_near, [(i, i + 1) for i in evens])
    far_next = swap(to_far_next, [(i + 2, i + 4) for i in fours])
    far_near = swap(to_far_near, [(i, i + 2) for i in fours])

    cells = half * half
    shapes = {
        "features": ((2, 64, cells), BF16),
        "mine": ((64, HALF), F32),
        "theirs": ((64, HALF), F32),
        "part": ((2, 32, cells), F32),
        "slope": ((128, LANES), F32),
        "patches": ((256, LANES), BF16),
        "pre": ((64, LANES), F32),
        "act": ((64, LANES), F32),
        "pre_two": ((2, 64, cells), F32),
        "far_one": ((64, 72), BF16),
        "far_two": ((2, 64, 288), BF16),
    }
    feat, mine, theirs, *inner = pl.pallas_call(
        functools.partial(inner_body, count),
        out_shape=tuple(jax.ShapeDtypeStruct(*x) for x in shapes.values()),
        scratch_shapes=[pltpu.VMEM((864, 64), F32)],
        compiler_params=limit,
        cost_estimate=pl.CostEstimate(flops=3 * 10**9, bytes_accessed=2 * 10**6, transcendentals=10**6),
    )(to_next, to_near, following, near, *weights[:3])

    def other_core(block, step):
        return lax.ppermute(block, "dp", [(i, i ^ step) for i in range(copies)])

    my_copy = lax.axis_index("dp")
    theirs = other_core(theirs, 1)
    pgrad, one = pl.pallas_call(
        functools.partial(outer_body, count),
        out_shape=(
            jax.ShapeDtypeStruct((2, 32, cells), BF16),
            jax.ShapeDtypeStruct((64, 128), BF16),
        ),
        scratch_shapes=[pltpu.VMEM((64, 128), F32)],
        compiler_params=limit,
        cost_estimate=pl.CostEstimate(flops=3 * 10**9, bytes_accessed=2 * 10**6, transcendentals=10**6),
    )(far_next, far_near, following, near, weights[1], weights[3], *inner)

    two = mine + theirs
    steps = [1 << i for i in range(1, copies.bit_length() - 1)]
    for step in steps:
        low, high = jnp.split(two, 2, axis=1)
        second = my_copy & step != 0
        two = jnp.where(second, high, low) + other_core(jnp.where(second, low, high), step)
    send = jnp.concatenate([two.astype(BF16), one], axis=1)
    share = 64 // slabs
    parts = lax.all_to_all(send.reshape(slabs, share, -1), "space", 0, 0, tiled=True)
    total = jnp.sum(parts.astype(F32), axis=0)
    for step in steps[::-1]:
        other = other_core(total, step)
        second = my_copy & step != 0
        low, high = jnp.where(second, other, total), jnp.where(second, total, other)
        total = jnp.concatenate(
            [low[:, :-128], high[:, :-128], total[:, -128:] + other[:, -128:]], axis=1
        )
    other = other_core(total, 1)
    grad_one, grad_two = pl.pallas_call(
        finish_body,
        out_shape=(jax.ShapeDtypeStruct((share * 54,), F32), jax.ShapeDtypeStruct((share * 864,), F32)),
        compiler_params=limit,
    )(total, other)
    features, pooled_grad = pl.pallas_call(
        lay_out_body,
        out_shape=(
            jax.ShapeDtypeStruct((1, 64, 2, cells), BF16),
            jax.ShapeDtypeStruct((1, 32, 2, cells), BF16),
        ),
        compiler_params=limit,
        cost_estimate=pl.CostEstimate(flops=10**6, bytes_accessed=2 * 10**5, transcendentals=0),
    )(feat, pgrad)
    return (features, pooled_grad, grad_one, grad_two)


def solution(mesh):
    in_specs = (P("dp", None, "space", None, None), P(), P(), P("dp", None, "space", None))
    out_specs = (P("dp", None, "space", None), P("dp", None, "space", None), P("space"), P("space"))
    return jax.shard_map(
        on_device, mesh=mesh, in_specs=in_specs, out_specs=out_specs, check_vma=False
    )
```

```python
import functools
import math

import jax
import jax.numpy as jnp
import numpy as np
from jax import lax
from jax.experimental import pallas as pl
from jax.experimental.pallas import tpu as pltpu
from jax.sharding import PartitionSpec as P

F32 = jnp.float32
BF16 = jnp.bfloat16
SHIFTS = [(dy, dx) for dy in (-1, 0, 1) for dx in (-1, 0, 1)]
NN = (((1,), (0,)), ((), ()))
NT = (((1,), (1,)), ((), ()))
LANES = 1024
HALF = 512
ONE_AT = 432


def dot(a, b, dims=NN):
    return lax.dot_general(a, b, dims, preferred_element_type=F32)


def inside(cells, width):
    lane = lax.broadcasted_iota(jnp.int32, (1, cells), 1)
    col, row = lane & (width - 1), lax.shift_right_logical(lane, width.bit_length() - 1)

    def factor(pos, step):
        if step == 0:
            return None
        return jnp.where(pos < width - 1 if step > 0 else pos > 0, 1.0, 0.0)

    return [(factor(col, d), factor(row, d)) for d in (-1, 0, 1)]


def moved_by(field, move, factor):
    return field if move == 0 else pltpu.roll(field, (-move) % field.shape[1], 1) * factor


def all_shifts(field, width):
    factors = inside(field.shape[1], width)
    across = [moved_by(field, dx, factors[dx + 1][0]) for dx in (-1, 0, 1)]
    return [moved_by(across[dx + 1], dy * width, factors[dy + 1][1]) for dy, dx in SHIFTS]


def pool_pattern():
    cell = lax.broadcasted_iota(jnp.int32, (512, 128), 0)
    block = lax.broadcasted_iota(jnp.int32, (512, 128), 1)
    at = 16 * lax.shift_right_logical(cell, 6) + lax.shift_right_logical(cell & 31, 1)
    return jnp.where(at == block, 0.125, 0.0).astype(BF16)


def silu_parts(v):
    s = 0.5 + 0.5 * jnp.tanh(0.5 * v)
    return v * s, s


def band_maps():
    to_kernel = np.zeros((4, 216, 108), np.float32)
    to_flat = np.zeros((4, 256, 128), np.float32)
    for p in range(4):
        for s in range(9):
            for dz in range(3):
                q = p + dz - 1
                for ci in range(4):
                    if 0 <= q <= 3:
                        row = 16 * s + 4 * q + ci
                    else:
                        row = 144 + 8 * s + (0 if q < 0 else 4) + ci
                    tap = 9 * dz + s
                    to_kernel[p, row, 4 * tap + ci] = 1
                    to_flat[p, row, (48 + 64 * (ci // 2) + 27 * (ci % 2) + tap) % 128] = 1
    return to_kernel, to_flat.reshape(1024, 128)


def prepare_body(
    vol_hbm, cot_hbm, *refs,
):
    weights, (next_ref, near_ref, far_next_ref, far_near_ref) = refs[:4], refs[4:8]
    kept, (vol_ref, cot_ref, cells_ref, sems) = refs[8:12], refs[12:]
    me = lax.axis_index("space")
    odd, upper = me % 2 == 1, (me // 2) % 2 == 1
    vol_copy = pltpu.make_async_copy(vol_hbm, vol_ref, sems.at[0])
    cot_copy = pltpu.make_async_copy(cot_hbm, cot_ref, sems.at[1])
    vol_copy.start()
    cot_copy.start()
    copies = [
        pltpu.make_async_copy(src, dst, sems.at[2 + i])
        for i, (src, dst) in enumerate(zip(weights, kept))
    ]
    for copy in copies:
        copy.start()
    vol_copy.wait()
    cin, planes, width = vol_ref.shape[1:4]
    for plane in range(planes):
        for ch in range(cin):
            at = (plane * cin + ch) * width
            cells_ref[at : at + width] = vol_ref[0, ch, plane].astype(F32)
    count = planes * cin
    blocks = []
    for b in range(4):
        lines = [cells_ref[pl.ds(8 * b + y, count, stride=width), :] for y in range(8)]
        rows = jnp.concatenate(lines, axis=1)
        near_ref[count * b : count * b + count] = rows.astype(BF16)
        next_ref[count * b : count * b + count] = rows.astype(BF16)
        blocks.append(rows)
    halves = [jnp.concatenate(blocks[2 * m : 2 * m + 2], axis=1) for m in range(2)]
    top = lax.broadcasted_iota(jnp.int32, (8, HALF), 0) < 4
    first = jnp.where(top, halves[0][0:8], pltpu.roll(halves[1][0:8], 4, 0))
    last = jnp.where(top, pltpu.roll(halves[0][8:16], 4, 0), halves[1][8:16])
    far_near_ref[...] = jnp.where(upper, first, last).astype(BF16)
    far_next_ref[...] = jnp.where(upper, last, first).astype(BF16)
    cot_copy.wait()
    cot = cot_ref[0].astype(F32)
    cots = (cot[:, 0, :], cot[:, 1, :])
    near_ref[64:128] = jnp.where(odd, cots[0], cots[1]).astype(BF16)
    next_ref[64:128] = jnp.where(odd, cots[1], cots[0]).astype(BF16)
    for copy in copies:
        copy.wait()


def finish_body(mine_ref, other_ref, one_ref, two_ref):
    mine, other = mine_ref[...], other_ref[...]
    share = mine.shape[0]
    second = lax.axis_index("dp") & 1 == 1
    halves = jnp.where(second, other, mine), jnp.where(second, mine, other)
    two = jnp.concatenate([half[:, 0:ONE_AT] for half in halves], axis=1)
    two_ref[...] = jnp.concatenate([two[r] for r in range(share)])
    one = (mine + other)[:, ONE_AT : ONE_AT + 54]
    one_ref[...] = jnp.concatenate([one[r] for r in range(share)])


def unfold(block, rows):
    return jnp.concatenate([block[rows * b : rows * b + rows] for b in range(4)], axis=1)


def pool_sums(sums, pattern):
    rows = sums.shape[0]
    high = sums.astype(BF16)
    low = (sums - high.astype(F32)).astype(BF16)
    halves = [part[:, 512 * m : 512 * m + 512] for part in (high, low) for m in range(2)]
    out = dot(jnp.concatenate(halves, axis=0), pattern)
    out = out[0 : 2 * rows] + out[2 * rows : 4 * rows]
    return jnp.concatenate([out[0:rows], out[rows : 2 * rows]], axis=1)


def spread_cells(field, pattern):
    rows = field.shape[0]
    out = dot(jnp.concatenate([field[:, 0:128], field[:, 128:256]], axis=0), pattern, NT)
    return jnp.concatenate([out[0:rows], out[rows : 2 * rows]], axis=1)


def spread_taps(taps, half):
    factors = inside(half * half, half)
    total = None
    for dx in (-1, 0, 1):
        column = None
        for dy in (-1, 0, 1):
            s = 3 * (1 - dy) + (1 - dx)
            part = moved_by(taps[32 * s : 32 * s + 32], dy * half, factors[dy + 1][1])
            column = part if column is None else column + part
        column = moved_by(column, dx, factors[dx + 1][0])
        total = column if total is None else total + column
    return total


def inner_body(
    count,
    own_next_ref, own_near_ref, next_ref, near_ref, k1_ref, k2_ref, to_kernel_ref,
    feat_ref, mine_ref, theirs_ref, pgrad_ref, slope_ref, patch_ref, pre_ref, act_ref, pre_two_ref,
    far_one_ref, far_two_ref,
    term_ref,
):
    slabs = lax.axis_size("space")
    me = lax.axis_index("space")
    half = 16

    odd = me % 2 == 1
    own = unfold(own_near_ref[0:64].astype(F32), 16)
    near, following = near_ref[0:64].astype(F32), next_ref[0:64].astype(F32)
    left = unfold(jnp.where(odd, near, following), 16)
    right = unfold(jnp.where(odd, following, near), 16)
    top = lax.broadcasted_iota(jnp.int32, (8, LANES), 0) < 4
    edges = (
        jnp.where(top, 0.0, pltpu.roll(own[0:8], 4, 0)),
        jnp.where(top, pltpu.roll(left[8:16], 4, 0), pltpu.roll(right[0:8], 4, 0)),
        jnp.where(top, pltpu.roll(own[8:16], 4, 0), 0.0),
    )
    stack = jnp.concatenate([left, own, right, *edges], axis=0)
    moved = all_shifts(stack, 2 * half)
    patches = []
    for g in range(3):
        rows = [m[16 * g : 16 * g + 16] for m in moved] + [m[48 + 8 * g : 56 + 8 * g] for m in moved]
        patches.append(jnp.concatenate(rows, axis=0).astype(BF16))
    patch_ref[0:216] = patches[1]
    patch_ref[216:256] = jnp.zeros((40, LANES), BF16)

    k1t = k1_ref[...].astype(F32).reshape(108, 32).T.astype(BF16)
    two_by_dz = jnp.concatenate(
        [k2_ref[288 * dz : 288 * dz + 288].astype(F32).T for dz in range(3)], axis=0
    ).astype(BF16)
    banded = jnp.concatenate(
        [dot(k1t, to_kernel_ref[p], NT).astype(BF16) for p in range(4)], axis=0
    )
    far_one_ref[...] = jnp.concatenate(
        [dot(k1t, to_kernel_ref[p, 144:216], NT).astype(BF16) for p in (0, 3)], axis=0
    )
    far_two_ref[0] = two_by_dz[0:64]
    far_two_ref[1] = two_by_dz[128:192]

    pattern = pool_pattern()
    pre = dot(banded, patches[0])
    pre_ref[0:32] = pre[0:32]
    act, _ = silu_parts(pre[32:128])
    act_ref[0:32] = act[0:32]
    sums = [act[32:64] + act[64:96]]
    pre = dot(banded, patches[1])
    act, s = silu_parts(pre)
    slope_ref[...] = s + act * (1.0 - s)
    sums += [act[0:32] + act[32:64], act[64:96] + act[96:128]]
    pre = dot(banded, patches[2])
    pre_ref[32:64] = pre[96:128]
    act, _ = silu_parts(pre[0:96])
    act_ref[32:64] = act[64:96]
    sums += [act[0:32] + act[32:64]]
    pooled = pool_sums(jnp.concatenate(sums, axis=0), pattern)
    plane = lax.shift_right_logical(lax.broadcasted_iota(jnp.int32, pooled.shape, 0), 5)
    real = ((plane > 0) | (me > 0)) & ((plane < 3) | (me < slabs - 1))
    pooled = jnp.where(real, pooled, 0.0).astype(BF16).astype(F32)

    moved = [m.astype(BF16) for m in all_shifts(pooled, half)]
    planes = [jnp.concatenate([m[32 * q : 32 * q + 32] for m in moved], axis=0) for q in range(4)]
    pre_two = [None] * 4
    for q, columns in enumerate(planes):
        by_dz = dot(two_by_dz, columns)
        for dz in range(3):
            p = q + 1 - dz
            if 0 <= p < 4:
                part = by_dz[64 * dz : 64 * dz + 64]
                pre_two[p] = part if pre_two[p] is None else pre_two[p] + part
    pre_two_ref[0], pre_two_ref[1] = pre_two[0], pre_two[3]

    own_cots = own_near_ref[64:128].astype(F32), own_next_ref[64:128].astype(F32)
    cots = jnp.where(odd, *own_cots), jnp.where(odd, *own_cots[::-1])
    deltas = []
    for p in range(2):
        act, s = silu_parts(pre_two[p + 1])
        feat_ref[p] = act.astype(BF16)
        deltas.append((cots[p] * (s + act * (1.0 - s))).astype(BF16))

    both = jnp.concatenate(deltas, axis=0)
    for p in range(2):
        taps = [k2_ref[288 * (1 + p - q) : 288 * (1 + p - q) + 288] for q in range(2)]
        pgrad_ref[p] = spread_taps(dot(jnp.concatenate(taps, axis=1), both), half)

    columns = [jnp.concatenate(planes[p : p + 3], axis=0) for p in range(2)]
    term = dot(columns[0], deltas[0], NT) + dot(columns[1], deltas[1], NT)
    term_ref[...] = term * (1.0 / math.sqrt(count // 8))
    rows = [term_ref[pl.ds(ch, 27, stride=32), :] for ch in range(32)]
    rows = jnp.concatenate(rows, axis=0)
    free = jnp.zeros((64, HALF - ONE_AT), F32)
    halves = [
        jnp.concatenate([rows[ONE_AT * h : ONE_AT * h + ONE_AT].T, free], axis=1) for h in range(2)
    ]
    second = lax.axis_index("dp") & 1 == 1
    mine_ref[...] = jnp.where(second, halves[1], halves[0])
    theirs_ref[...] = jnp.where(second, halves[0], halves[1])


def outer_body(
    count,
    far_next_ref, far_near_ref, next_ref, near_ref, k2_ref, to_flat_ref,
    part_ref, slope_ref, patch_ref, pre_ref, act_ref, pre_two_ref,
    far_one_ref, far_two_ref,
    pgrad_ref, one_ref,
):
    slabs = lax.axis_size("space")
    me = lax.axis_index("space")
    half = 16
    odd, upper = me % 2 == 1, (me // 2) % 2 == 1
    pattern = pool_pattern()
    far_near, far_next = far_near_ref[...].astype(F32), far_next_ref[...].astype(F32)
    far_left, far_right = jnp.where(upper, far_near, far_next), jnp.where(upper, far_next, far_near)
    top = lax.broadcasted_iota(jnp.int32, (8, LANES), 0) < 4
    edge = jnp.where(
        top,
        jnp.concatenate([far_left, pltpu.roll(far_left, 4, 0)], axis=1),
        jnp.concatenate([pltpu.roll(far_right, 4, 0), far_right], axis=1),
    )
    patches = jnp.concatenate(all_shifts(edge, 2 * half), axis=0).astype(BF16)
    act, _ = silu_parts(pre_ref[...] + dot(far_one_ref[...], patches))
    pooled = pool_sums(act_ref[...] + act, pattern)
    plane = lax.shift_right_logical(lax.broadcasted_iota(jnp.int32, pooled.shape, 0), 5)
    real = ((plane > 0) | (me > 0)) & ((plane < 1) | (me < slabs - 1))
    pooled = jnp.where(real, pooled, 0.0).astype(BF16).astype(F32)
    moved = [m.astype(BF16) for m in all_shifts(pooled, half)]

    near, following = near_ref[64:128].astype(F32), next_ref[64:128].astype(F32)
    cots = jnp.where(odd, near, following), jnp.where(odd, following, near)
    grads = []
    for p in range(2):
        columns = jnp.concatenate([m[32 * p : 32 * p + 32] for m in moved], axis=0)
        pre = pre_two_ref[p] + dot(far_two_ref[p], columns)
        act, s = silu_parts(pre)
        delta = (cots[p] * (s + act * (1.0 - s))).astype(BF16)
        taps = dot(k2_ref[576 * (1 - p) : 576 * (1 - p) + 288], delta)
        grads.append((part_ref[p] + spread_taps(taps, half)).astype(BF16))
        pgrad_ref[p] = grads[p]

    spread = spread_cells(jnp.concatenate(grads, axis=0), pattern)
    spread = jnp.concatenate([spread[0:32], spread[0:32], spread[32:64], spread[32:64]], axis=0)
    delta_one = (spread * slope_ref[...]).astype(BF16)
    wide = dot(delta_one, patch_ref[...], NT)
    wide = jnp.concatenate([wide[32 * p : 32 * p + 32] for p in range(4)], axis=1)
    high = wide.astype(BF16)
    low = (wide - high.astype(F32)).astype(BF16)
    term_one = dot(jnp.concatenate([high, low], axis=0), to_flat_ref[...])
    term_one = (term_one[0:32] + term_one[32:64]) * (1.0 / math.sqrt(count))
    lane = lax.broadcasted_iota(jnp.int32, term_one.shape, 1)
    free = (lane >= 48) & (lane < 48 + 54)
    for h, half_row in enumerate((term_one, pltpu.roll(term_one, 64, 1))):
        one_ref[pl.ds(h, 32, stride=2), :] = jnp.where(free, half_row, 0.0)


def lay_out_body(feat_ref, pgrad_ref, feat_out, pgrad_out):
    for source, target in ((feat_ref, feat_out), (pgrad_ref, pgrad_out)):
        for p in range(2):
            target[0, :, p, :] = source[p]


def on_device(volumes, kernel_one, kernel_two, cotangent):
    _, cin, planes, width, _ = volumes.shape
    half = width // 2
    slabs = lax.axis_size("space")
    copies = lax.axis_size("dp")
    count = copies * planes * slabs * width * width

    to_kernel, to_flat = band_maps()
    weights = (
        jnp.transpose(kernel_one, (2, 3, 4, 1, 0)).reshape(27, 4, 32),
        jnp.transpose(kernel_two, (2, 3, 4, 1, 0)).reshape(864, 64),
        jnp.asarray(to_kernel, BF16),
        jnp.asarray(to_flat, BF16),
    )

    def in_hbm(*arrays):
        return [pltpu.with_memory_space_constraint(x, pltpu.HBM) for x in arrays]

    inputs = in_hbm(volumes, cotangent, *weights)
    hbm = pl.BlockSpec(memory_space=pltpu.HBM)
    limit = pltpu.CompilerParams(vmem_limit_bytes=48 * 1024 * 1024)
    whole = jax.ShapeDtypeStruct((128, width * width // 4), BF16)
    part = jax.ShapeDtypeStruct((2 * cin, width * width // 2), BF16)
    to_next, to_near, to_far_next, to_far_near, *weights = pl.pallas_call(
        prepare_body,
        out_shape=(
            whole, whole, part, part, *(jax.ShapeDtypeStruct(w.shape, BF16) for w in weights)
        ),
        in_specs=[hbm] * len(inputs),
        scratch_shapes=[
            pltpu.VMEM(volumes.shape, BF16),
            pltpu.VMEM(cotangent.shape, BF16),
            pltpu.VMEM((planes * cin * width, width), F32),
            pltpu.SemaphoreType.DMA((len(inputs),)),
        ],
        compiler_params=limit,
    )(*inputs)

    def swap(block, pairs):
        pairs = [p for p in pairs if max(p) < slabs]
        return lax.ppermute(block, "space", pairs + [(t, f) for f, t in pairs])

    evens = range(0, slabs, 2)
    fours = [i + j for i in range(0, slabs, 4) for j in range(2)]
    following = swap(to_next, [(i + 1, i + 2) for i in evens])
    near = swap(to_near, [(i, i + 1) for i in evens])
    far_next = swap(to_far_next, [(i + 2, i + 4) for i in fours])
    far_near = swap(to_far_near, [(i, i + 2) for i in fours])

    cells = half * half
    shapes = {
        "features": ((2, 64, cells), BF16),
        "mine": ((64, HALF), F32),
        "theirs": ((64, HALF), F32),
        "part": ((2, 32, cells), F32),
        "slope": ((128, LANES), F32),
        "patches": ((256, LANES), BF16),
        "pre": ((64, LANES), F32),
        "act": ((64, LANES), F32),
        "pre_two": ((2, 64, cells), F32),
        "far_one": ((64, 72), BF16),
        "far_two": ((2, 64, 288), BF16),
    }
    feat, mine, theirs, *inner = pl.pallas_call(
        functools.partial(inner_body, count),
        out_shape=tuple(jax.ShapeDtypeStruct(*x) for x in shapes.values()),
        scratch_shapes=[pltpu.VMEM((864, 64), F32)],
        compiler_params=limit,
        cost_estimate=pl.CostEstimate(flops=3 * 10**9, bytes_accessed=2 * 10**6, transcendentals=10**6),
    )(to_next, to_near, following, near, *weights[:3])

    def other_core(block, step):
        return lax.ppermute(block, "dp", [(i, i ^ step) for i in range(copies)])

    my_copy = lax.axis_index("dp")
    theirs = other_core(theirs, 1)
    pgrad, one = pl.pallas_call(
        functools.partial(outer_body, count),
        out_shape=(
            jax.ShapeDtypeStruct((2, 32, cells), BF16),
            jax.ShapeDtypeStruct((64, 128), F32),
        ),
        compiler_params=limit,
        cost_estimate=pl.CostEstimate(flops=3 * 10**9, bytes_accessed=2 * 10**6, transcendentals=10**6),
    )(far_next, far_near, following, near, weights[1], weights[3], *inner)

    two = mine + theirs
    steps = [1 << i for i in range(1, copies.bit_length() - 1)]
    for step in steps:
        low, high = jnp.split(two, 2, axis=1)
        second = my_copy & step != 0
        two = jnp.where(second, high, low) + other_core(jnp.where(second, low, high), step)
    wide = jnp.pad(one, ((0, 0), (HALF - 128, 0)))
    send = jnp.concatenate([two, one], axis=1) if steps else two + wide
    share = 64 // slabs
    send = send.astype(BF16).reshape(slabs, share, -1)
    parts = lax.all_to_all(send, "space", 0, 0, tiled=True)
    total = jnp.sum(parts.astype(F32), axis=0)
    if steps:
        two, one = total[:, :-128], total[:, -128:]
        for step in steps[::-1]:
            other = other_core(two, step)
            second = my_copy & step != 0
            two = jnp.concatenate(
                [jnp.where(second, other, two), jnp.where(second, two, other)], axis=1
            )
            one = one + other_core(one, step)
        total = two + jnp.pad(one, ((0, 0), (HALF - 128, 0)))
    other = other_core(total, 1)
    grad_one, grad_two = pl.pallas_call(
        finish_body,
        out_shape=(jax.ShapeDtypeStruct((share * 54,), F32), jax.ShapeDtypeStruct((share * 864,), F32)),
        compiler_params=limit,
    )(total, other)
    features, pooled_grad = pl.pallas_call(
        lay_out_body,
        out_shape=(
            jax.ShapeDtypeStruct((1, 64, 2, cells), BF16),
            jax.ShapeDtypeStruct((1, 32, 2, cells), BF16),
        ),
        compiler_params=limit,
        cost_estimate=pl.CostEstimate(flops=10**6, bytes_accessed=2 * 10**5, transcendentals=0),
    )(feat, pgrad)
    return (features, pooled_grad, grad_one, grad_two)


def solution(mesh):
    in_specs = (P("dp", None, "space", None, None), P(), P(), P("dp", None, "space", None))
    out_specs = (P("dp", None, "space", None), P("dp", None, "space", None), P("space"), P("space"))
    return jax.shard_map(
        on_device, mesh=mesh, in_specs=in_specs, out_specs=out_specs, check_vma=False
    )
```

```python
import functools
import math

import jax
import jax.numpy as jnp
import numpy as np
from jax import lax
from jax.experimental import pallas as pl
from jax.experimental.pallas import tpu as pltpu
from jax.sharding import PartitionSpec as P

F32 = jnp.float32
BF16 = jnp.bfloat16
SHIFTS = [(dy, dx) for dy in (-1, 0, 1) for dx in (-1, 0, 1)]
NN = (((1,), (0,)), ((), ()))
NT = (((1,), (1,)), ((), ()))
LANES = 1024
HALF = 512
ONE_AT = 896


def dot(a, b, dims=NN):
    return lax.dot_general(a, b, dims, preferred_element_type=F32)


def inside(cells, width):
    lane = lax.broadcasted_iota(jnp.int32, (1, cells), 1)
    col, row = lane & (width - 1), lax.shift_right_logical(lane, width.bit_length() - 1)

    def factor(pos, step):
        if step == 0:
            return None
        return jnp.where(pos < width - 1 if step > 0 else pos > 0, 1.0, 0.0)

    return [(factor(col, d), factor(row, d)) for d in (-1, 0, 1)]


def moved_by(field, move, factor):
    return field if move == 0 else pltpu.roll(field, (-move) % field.shape[1], 1) * factor


def all_shifts(field, width):
    factors = inside(field.shape[1], width)
    across = [moved_by(field, dx, factors[dx + 1][0]) for dx in (-1, 0, 1)]
    return [moved_by(across[dx + 1], dy * width, factors[dy + 1][1]) for dy, dx in SHIFTS]


def pool_pattern():
    cell = lax.broadcasted_iota(jnp.int32, (512, 128), 0)
    block = lax.broadcasted_iota(jnp.int32, (512, 128), 1)
    at = 16 * lax.shift_right_logical(cell, 6) + lax.shift_right_logical(cell & 31, 1)
    return jnp.where(at == block, 0.125, 0.0).astype(BF16)


def silu_parts(v):
    s = 0.5 + 0.5 * jnp.tanh(0.5 * v)
    return v * s, s


def band_maps():
    to_kernel = np.zeros((4, 256, 108), np.float32)
    to_flat = np.zeros((4, 256, 128), np.float32)
    for p in range(4):
        for s in range(9):
            for dz in range(3):
                q = p + dz - 1
                for ci in range(4):
                    if 0 <= q <= 3:
                        row = 16 * s + 4 * q + ci
                    else:
                        row = 144 + 8 * s + (0 if q < 0 else 4) + ci
                    tap = 9 * dz + s
                    to_kernel[p, row, 4 * tap + ci] = 1
                    to_flat[p, row, 64 * (ci // 2) + 27 * (ci % 2) + tap] = 1
    return to_kernel, to_flat.reshape(1024, 128)


def prepare_body(
    vol_hbm, cot_hbm, *refs,
):
    weights, (next_ref, near_ref, far_next_ref, far_near_ref) = refs[:4], refs[4:8]
    kept, (vol_ref, cot_ref, cells_ref, sems) = refs[8:12], refs[12:]
    me = lax.axis_index("space")
    odd, upper = me % 2 == 1, (me // 2) % 2 == 1
    vol_copy = pltpu.make_async_copy(vol_hbm, vol_ref, sems.at[0])
    cot_copy = pltpu.make_async_copy(cot_hbm, cot_ref, sems.at[1])
    vol_copy.start()
    cot_copy.start()
    copies = [
        pltpu.make_async_copy(src, dst, sems.at[2 + i])
        for i, (src, dst) in enumerate(zip(weights, kept))
    ]
    for copy in copies:
        copy.start()
    vol_copy.wait()
    cin, planes, width = vol_ref.shape[1:4]
    for plane in range(planes):
        for ch in range(cin):
            at = (plane * cin + ch) * width
            cells_ref[at : at + width] = vol_ref[0, ch, plane].astype(F32)
    count = planes * cin
    blocks = []
    for b in range(4):
        lines = [cells_ref[pl.ds(8 * b + y, count, stride=width), :] for y in range(8)]
        rows = jnp.concatenate(lines, axis=1)
        near_ref[count * b : count * b + count] = rows.astype(BF16)
        next_ref[count * b : count * b + count] = rows.astype(BF16)
        blocks.append(rows)
    halves = [jnp.concatenate(blocks[2 * m : 2 * m + 2], axis=1) for m in range(2)]
    top = lax.broadcasted_iota(jnp.int32, (8, HALF), 0) < 4
    first = jnp.where(top, halves[0][0:8], pltpu.roll(halves[1][0:8], 4, 0))
    last = jnp.where(top, pltpu.roll(halves[0][8:16], 4, 0), halves[1][8:16])
    far_near_ref[...] = jnp.where(upper, first, last).astype(BF16)
    far_next_ref[...] = jnp.where(upper, last, first).astype(BF16)
    cot_copy.wait()
    cot = cot_ref[0].astype(F32)
    cots = (cot[:, 0, :], cot[:, 1, :])
    near_ref[64:128] = jnp.where(odd, cots[0], cots[1]).astype(BF16)
    next_ref[64:128] = jnp.where(odd, cots[1], cots[0]).astype(BF16)
    for copy in copies:
        copy.wait()


def finish_body(mine_ref, other_ref, one_ref, two_ref):
    total = mine_ref[...] + other_ref[...]
    share = total.shape[0]
    two_ref[...] = jnp.concatenate([total[r, 0:864] for r in range(share)])
    one = total[:, ONE_AT : ONE_AT + 54] + total[:, ONE_AT + 64 : ONE_AT + 118]
    one_ref[...] = jnp.concatenate([one[r] for r in range(share)])


def unfold(block, rows):
    return jnp.concatenate([block[rows * b : rows * b + rows] for b in range(4)], axis=1)


def pool_sums(sums, pattern):
    rows = sums.shape[0]
    high = sums.astype(BF16)
    low = (sums - high.astype(F32)).astype(BF16)
    halves = [part[:, 512 * m : 512 * m + 512] for part in (high, low) for m in range(2)]
    out = dot(jnp.concatenate(halves, axis=0), pattern)
    out = out[0 : 2 * rows] + out[2 * rows : 4 * rows]
    return jnp.concatenate([out[0:rows], out[rows : 2 * rows]], axis=1)


def spread_cells(field, pattern):
    rows = field.shape[0]
    high = field.astype(BF16)
    low = (field - high.astype(F32)).astype(BF16)
    halves = [part[:, 128 * m : 128 * m + 128] for part in (high, low) for m in range(2)]
    out = dot(jnp.concatenate(halves, axis=0), pattern, NT)
    out = out[0 : 2 * rows] + out[2 * rows : 4 * rows]
    return jnp.concatenate([out[0:rows], out[rows : 2 * rows]], axis=1)


def spread_taps(taps, half):
    factors = inside(half * half, half)
    total = None
    for dx in (-1, 0, 1):
        column = None
        for dy in (-1, 0, 1):
            s = 3 * (1 - dy) + (1 - dx)
            part = moved_by(taps[32 * s : 32 * s + 32], dy * half, factors[dy + 1][1])
            column = part if column is None else column + part
        column = moved_by(column, dx, factors[dx + 1][0])
        total = column if total is None else total + column
    return total


def inner_body(
    count,
    own_next_ref, own_near_ref, next_ref, near_ref, k1_ref, k2_ref, to_kernel_ref, to_flat_ref,
    feat_ref, send_ref, part_ref, pre_ref, act_ref, pre_two_ref, far_one_ref, far_two_ref,
    term_ref, rows_ref,
):
    slabs = lax.axis_size("space")
    me = lax.axis_index("space")
    half = 16

    odd = me % 2 == 1
    own = unfold(own_near_ref[0:64].astype(F32), 16)
    near, following = near_ref[0:64].astype(F32), next_ref[0:64].astype(F32)
    left = unfold(jnp.where(odd, near, following), 16)
    right = unfold(jnp.where(odd, following, near), 16)
    top = lax.broadcasted_iota(jnp.int32, (8, LANES), 0) < 4
    edges = (
        jnp.where(top, 0.0, pltpu.roll(own[0:8], 4, 0)),
        jnp.where(top, pltpu.roll(left[8:16], 4, 0), pltpu.roll(right[0:8], 4, 0)),
        jnp.where(top, pltpu.roll(own[8:16], 4, 0), 0.0),
    )
    moved = all_shifts(jnp.concatenate([left, own, right, *edges], axis=0), 2 * half)
    patches = []
    for g in range(3):
        rows = [m[16 * g : 16 * g + 16] for m in moved] + [m[48 + 8 * g : 56 + 8 * g] for m in moved]
        rows.append(jnp.zeros((40, LANES), F32))
        patches.append(jnp.concatenate(rows, axis=0).astype(BF16))

    k1t = k1_ref[...].astype(F32).reshape(108, 32).T.astype(BF16)
    two_by_dz = jnp.concatenate(
        [k2_ref[288 * dz : 288 * dz + 288].astype(F32).T for dz in range(3)], axis=0
    ).astype(BF16)
    banded = jnp.concatenate(
        [dot(k1t, to_kernel_ref[p], NT).astype(BF16) for p in range(4)], axis=0
    )
    far_one_ref[...] = jnp.concatenate(
        [dot(k1t, to_kernel_ref[p, 144:216], NT).astype(BF16) for p in (0, 3)], axis=0
    )
    far_two_ref[0] = two_by_dz[0:64]
    far_two_ref[1] = two_by_dz[128:192]
    pattern = pool_pattern()

    pre = dot(banded, patches[0])
    pre_ref[0:32] = pre[0:32]
    act, s = silu_parts(pre[32:128])
    act_ref[0:32] = act[0:32]
    slopes = [(s + act * (1.0 - s))[32:96]]
    sums = [act[32:64] + act[64:96]]
    act, s = silu_parts(dot(banded, patches[1]))
    slopes.append(s + act * (1.0 - s))
    sums += [act[0:32] + act[32:64], act[64:96] + act[96:128]]
    pre = dot(banded, patches[2])
    pre_ref[32:64] = pre[96:128]
    act, s = silu_parts(pre[0:96])
    act_ref[32:64] = act[64:96]
    slopes.append((s + act * (1.0 - s))[0:64])
    sums += [act[0:32] + act[32:64]]
    pooled = pool_sums(jnp.concatenate(sums, axis=0), pattern)
    plane = lax.shift_right_logical(lax.broadcasted_iota(jnp.int32, pooled.shape, 0), 5)
    real = ((plane > 0) | (me > 0)) & ((plane < 3) | (me < slabs - 1))
    pooled = jnp.where(real, pooled, 0.0).astype(BF16).astype(F32)

    moved = [m.astype(BF16) for m in all_shifts(pooled, half)]
    planes = [jnp.concatenate([m[32 * q : 32 * q + 32] for m in moved], axis=0) for q in range(4)]
    pre_two = [None] * 4
    for q, columns in enumerate(planes):
        by_dz = dot(two_by_dz, columns)
        for dz in range(3):
            p = q + 1 - dz
            if 0 <= p < 4:
                part = by_dz[64 * dz : 64 * dz + 64]
                pre_two[p] = part if pre_two[p] is None else pre_two[p] + part
    pre_two_ref[0], pre_two_ref[1] = pre_two[0], pre_two[3]

    own_cots = own_near_ref[64:128].astype(F32), own_next_ref[64:128].astype(F32)
    cots = jnp.where(odd, *own_cots), jnp.where(odd, *own_cots[::-1])
    deltas = []
    for p in range(2):
        act, s = silu_parts(pre_two[p + 1])
        feat_ref[p] = act.astype(BF16)
        deltas.append((cots[p] * (s + act * (1.0 - s))).astype(BF16))

    grads = []
    for p in range(-1, 3):
        sources = [q for q in range(2) if abs(q - p) < 2]
        taps = [k2_ref[288 * (1 + p - q) : 288 * (1 + p - q) + 288] for q in sources]
        given = jnp.concatenate([deltas[q] for q in sources], axis=0)
        grads.append(spread_taps(dot(jnp.concatenate(taps, axis=1), given), half))
    part_ref[0], part_ref[1] = grads[1], grads[2]

    grads = jnp.where(real, jnp.concatenate(grads, axis=0), 0.0)
    spread = spread_cells(grads, pattern)
    spread = [spread[32 * q : 32 * q + 32] for q in range(4)]
    wide = []
    for g, under in enumerate(((0,), (1, 2), (3,))):
        field = jnp.concatenate([spread[q] for q in under for _ in range(2)], axis=0)
        wide.append(dot((field * slopes[g]).astype(BF16), patches[g], NT))
    wide = wide[1] + jnp.concatenate([wide[2], wide[0]], axis=0)
    wide = jnp.concatenate([wide[32 * p : 32 * p + 32] for p in range(4)], axis=1)
    high = wide.astype(BF16)
    low = (wide - high.astype(F32)).astype(BF16)
    term_one = dot(jnp.concatenate([high, low], axis=0), to_flat_ref[...])
    term_one = (term_one[0:32] + term_one[32:64]) * (1.0 / math.sqrt(count))
    for h, half_row in enumerate((term_one, pltpu.roll(term_one, 64, 1))):
        rows_ref[pl.ds(h, 32, stride=2), :] = half_row
    rows = rows_ref[...]
    rounded = rows.astype(BF16).astype(F32)
    lane = lax.broadcasted_iota(jnp.int32, rows.shape, 1)
    pair = jnp.where(lane < 64, rounded, pltpu.roll(rows - rounded, 64, 1))
    send_ref[:, ONE_AT:LANES] = pair.astype(BF16)

    columns = [jnp.concatenate(planes[p : p + 3], axis=0) for p in range(2)]
    term = dot(columns[0], deltas[0], NT) + dot(columns[1], deltas[1], NT)
    term_ref[...] = term * (1.0 / math.sqrt(count // 8))
    rows = [term_ref[pl.ds(ch, 27, stride=32), :] for ch in range(32)]
    send_ref[:, 0:864] = jnp.concatenate(rows, axis=0).T.astype(BF16)
    send_ref[:, 864:ONE_AT] = jnp.zeros((64, ONE_AT - 864), BF16)


def outer_body(
    far_next_ref, far_near_ref, next_ref, near_ref, k2_ref,
    feat_ref, part_ref, pre_ref, act_ref, pre_two_ref, far_one_ref, far_two_ref,
    feat_out, pgrad_out,
):
    slabs = lax.axis_size("space")
    me = lax.axis_index("space")
    half = 16
    odd, upper = me % 2 == 1, (me // 2) % 2 == 1
    pattern = pool_pattern()
    far_near, far_next = far_near_ref[...].astype(F32), far_next_ref[...].astype(F32)
    far_left, far_right = jnp.where(upper, far_near, far_next), jnp.where(upper, far_next, far_near)
    top = lax.broadcasted_iota(jnp.int32, (8, LANES), 0) < 4
    edge = jnp.where(
        top,
        jnp.concatenate([far_left, pltpu.roll(far_left, 4, 0)], axis=1),
        jnp.concatenate([pltpu.roll(far_right, 4, 0), far_right], axis=1),
    )
    patches = jnp.concatenate(all_shifts(edge, 2 * half), axis=0).astype(BF16)
    act, _ = silu_parts(pre_ref[...] + dot(far_one_ref[...], patches))
    pooled = pool_sums(act_ref[...] + act, pattern)
    plane = lax.shift_right_logical(lax.broadcasted_iota(jnp.int32, pooled.shape, 0), 5)
    real = ((plane > 0) | (me > 0)) & ((plane < 1) | (me < slabs - 1))
    pooled = jnp.where(real, pooled, 0.0).astype(BF16).astype(F32)
    moved = [m.astype(BF16) for m in all_shifts(pooled, half)]

    near, following = near_ref[64:128].astype(F32), next_ref[64:128].astype(F32)
    cots = jnp.where(odd, near, following), jnp.where(odd, following, near)
    for p in range(2):
        columns = jnp.concatenate([m[32 * p : 32 * p + 32] for m in moved], axis=0)
        pre = pre_two_ref[p] + dot(far_two_ref[p], columns)
        act, s = silu_parts(pre)
        delta = (cots[p] * (s + act * (1.0 - s))).astype(BF16)
        taps = dot(k2_ref[576 * (1 - p) : 576 * (1 - p) + 288], delta)
        pgrad_out[0, :, p, :] = (part_ref[p] + spread_taps(taps, half)).astype(BF16)
        feat_out[0, :, p, :] = feat_ref[p]


def on_device(volumes, kernel_one, kernel_two, cotangent):
    _, cin, planes, width, _ = volumes.shape
    half = width // 2
    slabs = lax.axis_size("space")
    copies = lax.axis_size("dp")
    count = copies * planes * slabs * width * width

    to_kernel, to_flat = band_maps()
    weights = (
        jnp.transpose(kernel_one, (2, 3, 4, 1, 0)).reshape(27, 4, 32),
        jnp.transpose(kernel_two, (2, 3, 4, 1, 0)).reshape(864, 64),
        jnp.asarray(to_kernel, BF16),
        jnp.asarray(to_flat, BF16),
    )

    def in_hbm(*arrays):
        return [pltpu.with_memory_space_constraint(x, pltpu.HBM) for x in arrays]

    inputs = in_hbm(volumes, cotangent, *weights)
    hbm = pl.BlockSpec(memory_space=pltpu.HBM)
    limit = pltpu.CompilerParams(vmem_limit_bytes=48 * 1024 * 1024)
    whole = jax.ShapeDtypeStruct((128, width * width // 4), BF16)
    part = jax.ShapeDtypeStruct((2 * cin, width * width // 2), BF16)
    to_next, to_near, to_far_next, to_far_near, *weights = pl.pallas_call(
        prepare_body,
        out_shape=(
            whole, whole, part, part, *(jax.ShapeDtypeStruct(w.shape, BF16) for w in weights)
        ),
        in_specs=[hbm] * len(inputs),
        scratch_shapes=[
            pltpu.VMEM(volumes.shape, BF16),
            pltpu.VMEM(cotangent.shape, BF16),
            pltpu.VMEM((planes * cin * width, width), F32),
            pltpu.SemaphoreType.DMA((len(inputs),)),
        ],
        compiler_params=limit,
    )(*inputs)

    def swap(block, pairs):
        pairs = [p for p in pairs if max(p) < slabs]
        return lax.ppermute(block, "space", pairs + [(t, f) for f, t in pairs])

    evens = range(0, slabs, 2)
    fours = [i + j for i in range(0, slabs, 4) for j in range(2)]
    following = swap(to_next, [(i + 1, i + 2) for i in evens])
    near = swap(to_near, [(i, i + 1) for i in evens])
    far_next = swap(to_far_next, [(i + 2, i + 4) for i in fours])
    far_near = swap(to_far_near, [(i, i + 2) for i in fours])

    cells = half * half
    shapes = {
        "features": ((2, 64, cells), BF16),
        "send": ((64, LANES), BF16),
        "part": ((2, 32, cells), F32),
        "pre": ((64, LANES), F32),
        "act": ((64, LANES), F32),
        "pre_two": ((2, 64, cells), F32),
        "far_one": ((64, 72), BF16),
        "far_two": ((2, 64, 288), BF16),
    }
    feat, send, *inner = pl.pallas_call(
        functools.partial(inner_body, count),
        out_shape=tuple(jax.ShapeDtypeStruct(*x) for x in shapes.values()),
        scratch_shapes=[pltpu.VMEM((864, 64), F32), pltpu.VMEM((64, 128), F32)],
        compiler_params=limit,
        cost_estimate=pl.CostEstimate(flops=4 * 10**9, bytes_accessed=2 * 10**6, transcendentals=10**6),
    )(to_next, to_near, following, near, *weights)
    share = 64 // slabs
    parts = lax.all_to_all(send.reshape(slabs, share, LANES), "space", 0, 0, tiled=True)
    features, pooled_grad = pl.pallas_call(
        outer_body,
        out_shape=(
            jax.ShapeDtypeStruct((1, 64, 2, cells), BF16),
            jax.ShapeDtypeStruct((1, 32, 2, cells), BF16),
        ),
        compiler_params=limit,
        cost_estimate=pl.CostEstimate(flops=2 * 10**9, bytes_accessed=10**6, transcendentals=10**5),
    )(far_next, far_near, following, near, weights[1], feat, *inner)
    parts, features, pooled_grad = lax.optimization_barrier((parts, features, pooled_grad))
    total = jnp.sum(parts.astype(F32), axis=0)

    def other_core(block, step):
        return lax.ppermute(block, "dp", [(i, i ^ step) for i in range(copies)])

    step = 1
    while 2 * step < copies:
        total = total + other_core(total, step)
        step *= 2
    other = other_core(total, step)
    grad_one, grad_two = pl.pallas_call(
        finish_body,
        out_shape=(jax.ShapeDtypeStruct((share * 54,), F32), jax.ShapeDtypeStruct((share * 864,), F32)),
        compiler_params=limit,
    )(total, other)
    return (features, pooled_grad, grad_one, grad_two)


def solution(mesh):
    in_specs = (P("dp", None, "space", None, None), P(), P(), P("dp", None, "space", None))
    out_specs = (P("dp", None, "space", None), P("dp", None, "space", None), P("space"), P("space"))
    return jax.shard_map(
        on_device, mesh=mesh, in_specs=in_specs, out_specs=out_specs, check_vma=False
    )
```

```python
import functools
import math

import jax
import jax.numpy as jnp
import numpy as np
from jax import lax
from jax.experimental import pallas as pl
from jax.experimental.pallas import tpu as pltpu
from jax.sharding import PartitionSpec as P

F32 = jnp.float32
BF16 = jnp.bfloat16
SHIFTS = [(dy, dx) for dy in (-1, 0, 1) for dx in (-1, 0, 1)]
NN = (((1,), (0,)), ((), ()))
NT = (((1,), (1,)), ((), ()))
LANES = 1024
HALF = 512
ONE_AT = 896


def dot(a, b, dims=NN):
    return lax.dot_general(a, b, dims, preferred_element_type=F32)


def inside(cells, width):
    lane = lax.broadcasted_iota(jnp.int32, (1, cells), 1)
    col, row = lane & (width - 1), lax.shift_right_logical(lane, width.bit_length() - 1)

    def factor(pos, step):
        if step == 0:
            return None
        return jnp.where(pos < width - 1 if step > 0 else pos > 0, 1.0, 0.0)

    return [(factor(col, d), factor(row, d)) for d in (-1, 0, 1)]


def moved_by(field, move, factor):
    return field if move == 0 else pltpu.roll(field, (-move) % field.shape[1], 1) * factor


def all_shifts(field, width):
    factors = inside(field.shape[1], width)
    across = [moved_by(field, dx, factors[dx + 1][0]) for dx in (-1, 0, 1)]
    return [moved_by(across[dx + 1], dy * width, factors[dy + 1][1]) for dy, dx in SHIFTS]


def pool_pattern():
    cell = lax.broadcasted_iota(jnp.int32, (512, 128), 0)
    block = lax.broadcasted_iota(jnp.int32, (512, 128), 1)
    at = 16 * lax.shift_right_logical(cell, 6) + lax.shift_right_logical(cell & 31, 1)
    return jnp.where(at == block, 0.125, 0.0).astype(BF16)


def silu_parts(v):
    s = 0.5 + 0.5 * jnp.tanh(0.5 * v)
    return v * s, s


def band_maps():
    to_kernel = np.zeros((4, 256, 108), np.float32)
    to_flat = np.zeros((4, 256, 128), np.float32)
    for p in range(4):
        for s in range(9):
            for dz in range(3):
                q = p + dz - 1
                for ci in range(4):
                    if 0 <= q <= 3:
                        row = 16 * s + 4 * q + ci
                    else:
                        row = 144 + 8 * s + (0 if q < 0 else 4) + ci
                    tap = 9 * dz + s
                    to_kernel[p, row, 4 * tap + ci] = 1
                    to_flat[p, row, 64 * (ci // 2) + 27 * (ci % 2) + tap] = 1
    return to_kernel, to_flat.reshape(1024, 128)


def prepare_body(
    vol_hbm, cot_hbm, *refs,
):
    weights, (next_ref, near_ref, far_next_ref, far_near_ref) = refs[:4], refs[4:8]
    kept, (vol_ref, cot_ref, cells_ref, sems) = refs[8:12], refs[12:]
    me = lax.axis_index("space")
    odd, upper = me % 2 == 1, (me // 2) % 2 == 1
    vol_copy = pltpu.make_async_copy(vol_hbm, vol_ref, sems.at[0])
    cot_copy = pltpu.make_async_copy(cot_hbm, cot_ref, sems.at[1])
    vol_copy.start()
    cot_copy.start()
    copies = [
        pltpu.make_async_copy(src, dst, sems.at[2 + i])
        for i, (src, dst) in enumerate(zip(weights, kept))
    ]
    for copy in copies:
        copy.start()
    vol_copy.wait()
    cin, planes, width = vol_ref.shape[1:4]
    for plane in range(planes):
        for ch in range(cin):
            at = (plane * cin + ch) * width
            cells_ref[at : at + width] = vol_ref[0, ch, plane].astype(F32)
    count = planes * cin
    blocks = []
    for b in range(4):
        lines = [cells_ref[pl.ds(8 * b + y, count, stride=width), :] for y in range(8)]
        rows = jnp.concatenate(lines, axis=1)
        near_ref[count * b : count * b + count] = rows.astype(BF16)
        next_ref[count * b : count * b + count] = rows.astype(BF16)
        blocks.append(rows)
    halves = [jnp.concatenate(blocks[2 * m : 2 * m + 2], axis=1) for m in range(2)]
    top = lax.broadcasted_iota(jnp.int32, (8, HALF), 0) < 4
    first = jnp.where(top, halves[0][0:8], pltpu.roll(halves[1][0:8], 4, 0))
    last = jnp.where(top, pltpu.roll(halves[0][8:16], 4, 0), halves[1][8:16])
    far_near_ref[...] = jnp.where(upper, first, last).astype(BF16)
    far_next_ref[...] = jnp.where(upper, last, first).astype(BF16)
    cot_copy.wait()
    cot = cot_ref[0].astype(F32)
    cots = (cot[:, 0, :], cot[:, 1, :])
    near_ref[64:128] = jnp.where(odd, cots[0], cots[1]).astype(BF16)
    next_ref[64:128] = jnp.where(odd, cots[1], cots[0]).astype(BF16)
    for copy in copies:
        copy.wait()


def finish_body(mine_ref, other_ref, one_ref, two_ref):
    total = mine_ref[...] + other_ref[...]
    share = total.shape[0]
    two_ref[...] = jnp.concatenate([total[r, 0:864] for r in range(share)])
    one = total[:, ONE_AT : ONE_AT + 54] + total[:, ONE_AT + 64 : ONE_AT + 118]
    one_ref[...] = jnp.concatenate([one[r] for r in range(share)])


def unfold(block, rows):
    return jnp.concatenate([block[rows * b : rows * b + rows] for b in range(4)], axis=1)


def pool_sums(sums, pattern):
    rows = sums.shape[0]
    high = sums.astype(BF16)
    low = (sums - high.astype(F32)).astype(BF16)
    halves = [part[:, 512 * m : 512 * m + 512] for part in (high, low) for m in range(2)]
    out = dot(jnp.concatenate(halves, axis=0), pattern)
    out = out[0 : 2 * rows] + out[2 * rows : 4 * rows]
    return jnp.concatenate([out[0:rows], out[rows : 2 * rows]], axis=1)


def spread_cells(field, pattern):
    rows = field.shape[0]
    high = field.astype(BF16)
    low = (field - high.astype(F32)).astype(BF16)
    halves = [part[:, 128 * m : 128 * m + 128] for part in (high, low) for m in range(2)]
    out = dot(jnp.concatenate(halves, axis=0), pattern, NT)
    out = out[0 : 2 * rows] + out[2 * rows : 4 * rows]
    return jnp.concatenate([out[0:rows], out[rows : 2 * rows]], axis=1)


def spread_taps(taps, half):
    factors = inside(half * half, half)
    total = None
    for dx in (-1, 0, 1):
        column = None
        for dy in (-1, 0, 1):
            s = 3 * (1 - dy) + (1 - dx)
            part = moved_by(taps[32 * s : 32 * s + 32], dy * half, factors[dy + 1][1])
            column = part if column is None else column + part
        column = moved_by(column, dx, factors[dx + 1][0])
        total = column if total is None else total + column
    return total


def inner_body(
    count,
    own_next_ref, own_near_ref, next_ref, near_ref, k1_ref, k2_ref, to_kernel_ref, to_flat_ref,
    feat_ref, send_ref, part_ref, pre_ref, act_ref, pre_two_ref, far_one_ref, far_two_ref,
    term_ref, rows_ref,
):
    slabs = lax.axis_size("space")
    me = lax.axis_index("space")
    half = 16

    odd = me % 2 == 1
    own = unfold(own_near_ref[0:64].astype(F32), 16)
    near, following = near_ref[0:64].astype(F32), next_ref[0:64].astype(F32)
    left = unfold(jnp.where(odd, near, following), 16)
    right = unfold(jnp.where(odd, following, near), 16)
    top = lax.broadcasted_iota(jnp.int32, (8, LANES), 0) < 4
    edges = (
        jnp.where(top, 0.0, pltpu.roll(own[0:8], 4, 0)),
        jnp.where(top, pltpu.roll(left[8:16], 4, 0), pltpu.roll(right[0:8], 4, 0)),
        jnp.where(top, pltpu.roll(own[8:16], 4, 0), 0.0),
    )
    moved = all_shifts(jnp.concatenate([left, own, right, *edges], axis=0), 2 * half)
    patches = []
    for g in range(3):
        rows = [m[16 * g : 16 * g + 16] for m in moved] + [m[48 + 8 * g : 56 + 8 * g] for m in moved]
        rows.append(jnp.zeros((40, LANES), F32))
        patches.append(jnp.concatenate(rows, axis=0).astype(BF16))

    k1t = k1_ref[...].astype(F32).reshape(108, 32).T.astype(BF16)
    two_by_dz = jnp.concatenate(
        [k2_ref[288 * dz : 288 * dz + 288].astype(F32).T for dz in range(3)], axis=0
    ).astype(BF16)
    banded = jnp.concatenate(
        [dot(k1t, to_kernel_ref[p], NT).astype(BF16) for p in range(4)], axis=0
    )
    far_one_ref[...] = jnp.concatenate(
        [dot(k1t, to_kernel_ref[p, 144:216], NT).astype(BF16) for p in (0, 3)], axis=0
    )
    far_two_ref[0] = two_by_dz[0:64]
    far_two_ref[1] = two_by_dz[128:192]
    pattern = pool_pattern()

    pre = dot(banded, patches[0])
    pre_ref[0:32] = pre[0:32]
    act, s = silu_parts(pre[32:128])
    act_ref[0:32] = act[0:32]
    slopes = [(s + act * (1.0 - s))[32:96]]
    sums = [act[32:64] + act[64:96]]
    act, s = silu_parts(dot(banded, patches[1]))
    slopes.append(s + act * (1.0 - s))
    sums += [act[0:32] + act[32:64], act[64:96] + act[96:128]]
    pre = dot(banded, patches[2])
    pre_ref[32:64] = pre[96:128]
    act, s = silu_parts(pre[0:96])
    act_ref[32:64] = act[64:96]
    slopes.append((s + act * (1.0 - s))[0:64])
    sums += [act[0:32] + act[32:64]]
    pooled = pool_sums(jnp.concatenate(sums, axis=0), pattern)
    plane = lax.shift_right_logical(lax.broadcasted_iota(jnp.int32, pooled.shape, 0), 5)
    real = ((plane > 0) | (me > 0)) & ((plane < 3) | (me < slabs - 1))
    pooled = jnp.where(real, pooled, 0.0).astype(BF16).astype(F32)

    moved = [m.astype(BF16) for m in all_shifts(pooled, half)]
    planes = [jnp.concatenate([m[32 * q : 32 * q + 32] for m in moved], axis=0) for q in range(4)]
    pre_two = [None] * 4
    for q, columns in enumerate(planes):
        by_dz = dot(two_by_dz, columns)
        for dz in range(3):
            p = q + 1 - dz
            if 0 <= p < 4:
                part = by_dz[64 * dz : 64 * dz + 64]
                pre_two[p] = part if pre_two[p] is None else pre_two[p] + part
    pre_two_ref[0], pre_two_ref[1] = pre_two[0], pre_two[3]

    own_cots = own_near_ref[64:128].astype(F32), own_next_ref[64:128].astype(F32)
    cots = jnp.where(odd, *own_cots), jnp.where(odd, *own_cots[::-1])
    deltas = []
    for p in range(2):
        act, s = silu_parts(pre_two[p + 1])
        feat_ref[p] = act.astype(BF16)
        deltas.append((cots[p] * (s + act * (1.0 - s))).astype(BF16))

    grads = []
    for p in range(-1, 3):
        sources = [q for q in range(2) if abs(q - p) < 2]
        taps = [k2_ref[288 * (1 + p - q) : 288 * (1 + p - q) + 288] for q in sources]
        given = jnp.concatenate([deltas[q] for q in sources], axis=0)
        grads.append(spread_taps(dot(jnp.concatenate(taps, axis=1), given), half))
    part_ref[0], part_ref[1] = grads[1], grads[2]

    grads = jnp.where(real, jnp.concatenate(grads, axis=0), 0.0)
    spread = spread_cells(grads, pattern)
    spread = [spread[32 * q : 32 * q + 32] for q in range(4)]
    wide = []
    for g, under in enumerate(((0,), (1, 2), (3,))):
        field = jnp.concatenate([spread[q] for q in under for _ in range(2)], axis=0)
        wide.append(dot((field * slopes[g]).astype(BF16), patches[g], NT))
    wide = wide[1] + jnp.concatenate([wide[2], wide[0]], axis=0)
    wide = jnp.concatenate([wide[32 * p : 32 * p + 32] for p in range(4)], axis=1)
    high = wide.astype(BF16)
    low = (wide - high.astype(F32)).astype(BF16)
    term_one = dot(jnp.concatenate([high, low], axis=0), to_flat_ref[...])
    term_one = (term_one[0:32] + term_one[32:64]) * (1.0 / math.sqrt(count))
    for h, half_row in enumerate((term_one, pltpu.roll(term_one, 64, 1))):
        rows_ref[pl.ds(h, 32, stride=2), :] = half_row
    rows = rows_ref[...]
    rounded = rows.astype(BF16).astype(F32)
    lane = lax.broadcasted_iota(jnp.int32, rows.shape, 1)
    pair = jnp.where(lane < 64, rounded, pltpu.roll(rows - rounded, 64, 1))
    send_ref[:, ONE_AT:LANES] = pair.astype(BF16)

    columns = [jnp.concatenate(planes[p : p + 3], axis=0) for p in range(2)]
    term = dot(columns[0], deltas[0], NT) + dot(columns[1], deltas[1], NT)
    term_ref[...] = term * (1.0 / math.sqrt(count // 8))
    rows = [term_ref[pl.ds(ch, 27, stride=32), :] for ch in range(32)]
    send_ref[:, 0:864] = jnp.concatenate(rows, axis=0).T.astype(BF16)
    send_ref[:, 864:ONE_AT] = jnp.zeros((64, ONE_AT - 864), BF16)


def outer_body(
    far_next_ref, far_near_ref, next_ref, near_ref, k2_ref,
    feat_ref, part_ref, pre_ref, act_ref, pre_two_ref, far_one_ref, far_two_ref,
    feat_out, pgrad_out,
):
    slabs = lax.axis_size("space")
    me = lax.axis_index("space")
    half = 16
    odd, upper = me % 2 == 1, (me // 2) % 2 == 1
    pattern = pool_pattern()
    far_near, far_next = far_near_ref[...].astype(F32), far_next_ref[...].astype(F32)
    far_left, far_right = jnp.where(upper, far_near, far_next), jnp.where(upper, far_next, far_near)
    top = lax.broadcasted_iota(jnp.int32, (8, LANES), 0) < 4
    edge = jnp.where(
        top,
        jnp.concatenate([far_left, pltpu.roll(far_left, 4, 0)], axis=1),
        jnp.concatenate([pltpu.roll(far_right, 4, 0), far_right], axis=1),
    )
    patches = jnp.concatenate(all_shifts(edge, 2 * half), axis=0).astype(BF16)
    act, _ = silu_parts(pre_ref[...] + dot(far_one_ref[...], patches))
    pooled = pool_sums(act_ref[...] + act, pattern)
    plane = lax.shift_right_logical(lax.broadcasted_iota(jnp.int32, pooled.shape, 0), 5)
    real = ((plane > 0) | (me > 0)) & ((plane < 1) | (me < slabs - 1))
    pooled = jnp.where(real, pooled, 0.0).astype(BF16).astype(F32)
    moved = [m.astype(BF16) for m in all_shifts(pooled, half)]

    near, following = near_ref[64:128].astype(F32), next_ref[64:128].astype(F32)
    cots = jnp.where(odd, near, following), jnp.where(odd, following, near)
    for p in range(2):
        columns = jnp.concatenate([m[32 * p : 32 * p + 32] for m in moved], axis=0)
        pre = pre_two_ref[p] + dot(far_two_ref[p], columns)
        act, s = silu_parts(pre)
        delta = (cots[p] * (s + act * (1.0 - s))).astype(BF16)
        taps = dot(k2_ref[576 * (1 - p) : 576 * (1 - p) + 288], delta)
        pgrad_out[0, :, p, :] = (part_ref[p] + spread_taps(taps, half)).astype(BF16)
        feat_out[0, :, p, :] = feat_ref[p]


def on_device(volumes, kernel_one, kernel_two, cotangent):
    _, cin, planes, width, _ = volumes.shape
    half = width // 2
    slabs = lax.axis_size("space")
    copies = lax.axis_size("dp")
    count = copies * planes * slabs * width * width

    to_kernel, to_flat = band_maps()
    weights = (
        jnp.transpose(kernel_one, (2, 3, 4, 1, 0)).reshape(27, 4, 32),
        jnp.transpose(kernel_two, (2, 3, 4, 1, 0)).reshape(864, 64),
        jnp.asarray(to_kernel, BF16),
        jnp.asarray(to_flat, BF16),
    )

    def in_hbm(*arrays):
        return [pltpu.with_memory_space_constraint(x, pltpu.HBM) for x in arrays]

    inputs = in_hbm(volumes, cotangent, *weights)
    hbm = pl.BlockSpec(memory_space=pltpu.HBM)
    limit = pltpu.CompilerParams(vmem_limit_bytes=48 * 1024 * 1024)
    whole = jax.ShapeDtypeStruct((128, width * width // 4), BF16)
    part = jax.ShapeDtypeStruct((2 * cin, width * width // 2), BF16)
    to_next, to_near, to_far_next, to_far_near, *weights = pl.pallas_call(
        prepare_body,
        out_shape=(
            whole, whole, part, part, *(jax.ShapeDtypeStruct(w.shape, BF16) for w in weights)
        ),
        in_specs=[hbm] * len(inputs),
        scratch_shapes=[
            pltpu.VMEM(volumes.shape, BF16),
            pltpu.VMEM(cotangent.shape, BF16),
            pltpu.VMEM((planes * cin * width, width), F32),
            pltpu.SemaphoreType.DMA((len(inputs),)),
        ],
        compiler_params=limit,
    )(*inputs)

    def swap(block, pairs):
        pairs = [p for p in pairs if max(p) < slabs]
        return lax.ppermute(block, "space", pairs + [(t, f) for f, t in pairs])

    evens = range(0, slabs, 2)
    fours = [i + j for i in range(0, slabs, 4) for j in range(2)]
    following = swap(to_next, [(i + 1, i + 2) for i in evens])
    near = swap(to_near, [(i, i + 1) for i in evens])
    far_next = swap(to_far_next, [(i + 2, i + 4) for i in fours])
    far_near = swap(to_far_near, [(i, i + 2) for i in fours])

    cells = half * half
    shapes = {
        "features": ((2, 64, cells), BF16),
        "send": ((64, LANES), BF16),
        "part": ((2, 32, cells), F32),
        "pre": ((64, LANES), F32),
        "act": ((64, LANES), F32),
        "pre_two": ((2, 64, cells), F32),
        "far_one": ((64, 72), BF16),
        "far_two": ((2, 64, 288), BF16),
    }
    feat, send, *inner = pl.pallas_call(
        functools.partial(inner_body, count),
        out_shape=tuple(jax.ShapeDtypeStruct(*x) for x in shapes.values()),
        scratch_shapes=[pltpu.VMEM((864, 64), F32), pltpu.VMEM((64, 128), F32)],
        compiler_params=limit,
        cost_estimate=pl.CostEstimate(flops=2 * 10**10, bytes_accessed=2 * 10**6, transcendentals=10**6),
    )(to_next, to_near, following, near, *weights)
    share = 64 // slabs
    parts = lax.all_to_all(send.reshape(slabs, share, LANES), "space", 0, 0, tiled=True)
    features, pooled_grad = pl.pallas_call(
        outer_body,
        out_shape=(
            jax.ShapeDtypeStruct((1, 64, 2, cells), BF16),
            jax.ShapeDtypeStruct((1, 32, 2, cells), BF16),
        ),
        compiler_params=limit,
        cost_estimate=pl.CostEstimate(flops=4 * 10**10, bytes_accessed=10**6, transcendentals=10**5),
    )(far_next, far_near, following, near, weights[1], feat, *inner)
    parts, features, pooled_grad = lax.optimization_barrier((parts, features, pooled_grad))
    total = jnp.sum(parts.astype(F32), axis=0)

    def other_core(block, step):
        return lax.ppermute(block, "dp", [(i, i ^ step) for i in range(copies)])

    step = 1
    while 2 * step < copies:
        total = total + other_core(total, step)
        step *= 2
    other = other_core(total, step)
    grad_one, grad_two = pl.pallas_call(
        finish_body,
        out_shape=(jax.ShapeDtypeStruct((share * 54,), F32), jax.ShapeDtypeStruct((share * 864,), F32)),
        compiler_params=limit,
    )(total, other)
    return (features, pooled_grad, grad_one, grad_two)


def solution(mesh):
    in_specs = (P("dp", None, "space", None, None), P(), P(), P("dp", None, "space", None))
    out_specs = (P("dp", None, "space", None), P("dp", None, "space", None), P("space"), P("space"))
    return jax.shard_map(
        on_device, mesh=mesh, in_specs=in_specs, out_specs=out_specs, check_vma=False
    )
```

```python
import functools
import math

import jax
import jax.numpy as jnp
import numpy as np
from jax import lax
from jax.experimental import pallas as pl
from jax.experimental.pallas import tpu as pltpu
from jax.sharding import PartitionSpec as P

F32 = jnp.float32
BF16 = jnp.bfloat16
SHIFTS = [(dy, dx) for dy in (-1, 0, 1) for dx in (-1, 0, 1)]
NN = (((1,), (0,)), ((), ()))
NT = (((1,), (1,)), ((), ()))
LANES = 1024
HALF = 512
ONE_AT = 896


def dot(a, b, dims=NN):
    return lax.dot_general(a, b, dims, preferred_element_type=F32)


def inside(cells, width):
    lane = lax.broadcasted_iota(jnp.int32, (1, cells), 1)
    col, row = lane & (width - 1), lax.shift_right_logical(lane, width.bit_length() - 1)

    def factor(pos, step):
        if step == 0:
            return None
        return jnp.where(pos < width - 1 if step > 0 else pos > 0, 1.0, 0.0)

    return [(factor(col, d), factor(row, d)) for d in (-1, 0, 1)]


def moved_by(field, move, factor):
    return field if move == 0 else pltpu.roll(field, (-move) % field.shape[1], 1) * factor


def all_shifts(field, width):
    factors = inside(field.shape[1], width)
    across = [moved_by(field, dx, factors[dx + 1][0]) for dx in (-1, 0, 1)]
    return [moved_by(across[dx + 1], dy * width, factors[dy + 1][1]) for dy, dx in SHIFTS]


def pool_pattern():
    cell = lax.broadcasted_iota(jnp.int32, (512, 128), 0)
    block = lax.broadcasted_iota(jnp.int32, (512, 128), 1)
    at = 16 * lax.shift_right_logical(cell, 6) + lax.shift_right_logical(cell & 31, 1)
    return jnp.where(at == block, 0.125, 0.0).astype(BF16)


def silu_parts(v):
    s = 0.5 + 0.5 * jnp.tanh(0.5 * v)
    return v * s, s


def band_maps():
    to_kernel = np.zeros((4, 256, 108), np.float32)
    to_flat = np.zeros((4, 256, 128), np.float32)
    for p in range(4):
        for s in range(9):
            for dz in range(3):
                q = p + dz - 1
                for ci in range(4):
                    if 0 <= q <= 3:
                        row = 16 * s + 4 * q + ci
                    else:
                        row = 144 + 8 * s + (0 if q < 0 else 4) + ci
                    tap = 9 * dz + s
                    to_kernel[p, row, 4 * tap + ci] = 1
                    to_flat[p, row, 64 * (ci // 2) + 27 * (ci % 2) + tap] = 1
    return to_kernel, to_flat.reshape(1024, 128)


def prepare_body(
    vol_hbm, cot_hbm, *refs,
):
    weights, (next_ref, near_ref, far_next_ref, far_near_ref) = refs[:4], refs[4:8]
    kept, (vol_ref, cot_ref, cells_ref, sems) = refs[8:12], refs[12:]
    me = lax.axis_index("space")
    odd, upper = me % 2 == 1, (me // 2) % 2 == 1
    vol_copy = pltpu.make_async_copy(vol_hbm, vol_ref, sems.at[0])
    cot_copy = pltpu.make_async_copy(cot_hbm, cot_ref, sems.at[1])
    vol_copy.start()
    cot_copy.start()
    copies = [
        pltpu.make_async_copy(src, dst, sems.at[2 + i])
        for i, (src, dst) in enumerate(zip(weights, kept))
    ]
    for copy in copies:
        copy.start()
    vol_copy.wait()
    cin, planes, width = vol_ref.shape[1:4]
    for plane in range(planes):
        for ch in range(cin):
            at = (plane * cin + ch) * width
            cells_ref[at : at + width] = vol_ref[0, ch, plane].astype(F32)
    count = planes * cin
    blocks = []
    for b in range(4):
        lines = [cells_ref[pl.ds(8 * b + y, count, stride=width), :] for y in range(8)]
        rows = jnp.concatenate(lines, axis=1)
        near_ref[count * b : count * b + count] = rows.astype(BF16)
        next_ref[count * b : count * b + count] = rows.astype(BF16)
        blocks.append(rows)
    halves = [jnp.concatenate(blocks[2 * m : 2 * m + 2], axis=1) for m in range(2)]
    top = lax.broadcasted_iota(jnp.int32, (8, HALF), 0) < 4
    first = jnp.where(top, halves[0][0:8], pltpu.roll(halves[1][0:8], 4, 0))
    last = jnp.where(top, pltpu.roll(halves[0][8:16], 4, 0), halves[1][8:16])
    far_near_ref[...] = jnp.where(upper, first, last).astype(BF16)
    far_next_ref[...] = jnp.where(upper, last, first).astype(BF16)
    cot_copy.wait()
    cot = cot_ref[0].astype(F32)
    cots = (cot[:, 0, :], cot[:, 1, :])
    near_ref[64:128] = jnp.where(odd, cots[0], cots[1]).astype(BF16)
    next_ref[64:128] = jnp.where(odd, cots[1], cots[0]).astype(BF16)
    for copy in copies:
        copy.wait()


def finish_body(mine_ref, other_ref, one_ref, two_ref):
    total = mine_ref[...] + other_ref[...]
    share = total.shape[0]
    two_ref[...] = jnp.concatenate([total[r, 0:864] for r in range(share)])
    one = total[:, ONE_AT : ONE_AT + 54] + total[:, ONE_AT + 64 : ONE_AT + 118]
    one_ref[...] = jnp.concatenate([one[r] for r in range(share)])


def unfold(block, rows):
    return jnp.concatenate([block[rows * b : rows * b + rows] for b in range(4)], axis=1)


def pool_sums(sums, pattern):
    rows = sums.shape[0]
    high = sums.astype(BF16)
    low = (sums - high.astype(F32)).astype(BF16)
    halves = [part[:, 512 * m : 512 * m + 512] for part in (high, low) for m in range(2)]
    out = dot(jnp.concatenate(halves, axis=0), pattern)
    out = out[0 : 2 * rows] + out[2 * rows : 4 * rows]
    return jnp.concatenate([out[0:rows], out[rows : 2 * rows]], axis=1)


def spread_cells(field, pattern):
    rows = field.shape[0]
    high = field.astype(BF16)
    low = (field - high.astype(F32)).astype(BF16)
    halves = [part[:, 128 * m : 128 * m + 128] for part in (high, low) for m in range(2)]
    out = dot(jnp.concatenate(halves, axis=0), pattern, NT)
    out = out[0 : 2 * rows] + out[2 * rows : 4 * rows]
    return jnp.concatenate([out[0:rows], out[rows : 2 * rows]], axis=1)


def spread_taps(taps, half):
    factors = inside(half * half, half)
    total = None
    for dx in (-1, 0, 1):
        column = None
        for dy in (-1, 0, 1):
            s = 3 * (1 - dy) + (1 - dx)
            part = moved_by(taps[32 * s : 32 * s + 32], dy * half, factors[dy + 1][1])
            column = part if column is None else column + part
        column = moved_by(column, dx, factors[dx + 1][0])
        total = column if total is None else total + column
    return total


def inner_body(
    count,
    own_next_ref, own_near_ref, next_ref, near_ref, k1_ref, k2_ref, to_kernel_ref, to_flat_ref,
    feat_ref, send_ref, part_ref, pre_ref, act_ref, pre_two_ref, far_one_ref, far_two_ref,
    term_ref, rows_ref,
):
    slabs = lax.axis_size("space")
    me = lax.axis_index("space")
    half = 16

    odd = me % 2 == 1
    own = unfold(own_near_ref[0:64].astype(F32), 16)
    near, following = near_ref[0:64].astype(F32), next_ref[0:64].astype(F32)
    left = unfold(jnp.where(odd, near, following), 16)
    right = unfold(jnp.where(odd, following, near), 16)
    top = lax.broadcasted_iota(jnp.int32, (8, LANES), 0) < 4
    edges = (
        jnp.where(top, 0.0, pltpu.roll(own[0:8], 4, 0)),
        jnp.where(top, pltpu.roll(left[8:16], 4, 0), pltpu.roll(right[0:8], 4, 0)),
        jnp.where(top, pltpu.roll(own[8:16], 4, 0), 0.0),
    )
    moved = all_shifts(jnp.concatenate([left, own, right, *edges], axis=0), 2 * half)
    patches = []
    for g in range(3):
        rows = [m[16 * g : 16 * g + 16] for m in moved] + [m[48 + 8 * g : 56 + 8 * g] for m in moved]
        rows.append(jnp.zeros((40, LANES), F32))
        patches.append(jnp.concatenate(rows, axis=0).astype(BF16))

    k1t = k1_ref[...].astype(F32).reshape(108, 32).T.astype(BF16)
    two_by_dz = jnp.concatenate(
        [k2_ref[288 * dz : 288 * dz + 288].astype(F32).T for dz in range(3)], axis=0
    ).astype(BF16)
    banded = jnp.concatenate(
        [dot(k1t, to_kernel_ref[p], NT).astype(BF16) for p in range(4)], axis=0
    )
    far_one_ref[...] = jnp.concatenate(
        [dot(k1t, to_kernel_ref[p, 144:216], NT).astype(BF16) for p in (0, 3)], axis=0
    )
    far_two_ref[0] = two_by_dz[0:64]
    far_two_ref[1] = two_by_dz[128:192]
    pattern = pool_pattern()

    pre = dot(banded, patches[0])
    pre_ref[0:32] = pre[0:32]
    act, s = silu_parts(pre[32:128])
    act_ref[0:32] = act[0:32]
    slopes = [(s + act * (1.0 - s))[32:96]]
    sums = [act[32:64] + act[64:96]]
    act, s = silu_parts(dot(banded, patches[1]))
    slopes.append(s + act * (1.0 - s))
    sums += [act[0:32] + act[32:64], act[64:96] + act[96:128]]
    pre = dot(banded, patches[2])
    pre_ref[32:64] = pre[96:128]
    act, s = silu_parts(pre[0:96])
    act_ref[32:64] = act[64:96]
    slopes.append((s + act * (1.0 - s))[0:64])
    sums += [act[0:32] + act[32:64]]
    pooled = pool_sums(jnp.concatenate(sums, axis=0), pattern)
    plane = lax.shift_right_logical(lax.broadcasted_iota(jnp.int32, pooled.shape, 0), 5)
    real = ((plane > 0) | (me > 0)) & ((plane < 3) | (me < slabs - 1))
    pooled = jnp.where(real, pooled, 0.0).astype(BF16).astype(F32)

    moved = [m.astype(BF16) for m in all_shifts(pooled, half)]
    planes = [jnp.concatenate([m[32 * q : 32 * q + 32] for m in moved], axis=0) for q in range(4)]
    pre_two = [None] * 4
    for q, columns in enumerate(planes):
        by_dz = dot(two_by_dz, columns)
        for dz in range(3):
            p = q + 1 - dz
            if 0 <= p < 4:
                part = by_dz[64 * dz : 64 * dz + 64]
                pre_two[p] = part if pre_two[p] is None else pre_two[p] + part
    pre_two_ref[0], pre_two_ref[1] = pre_two[0], pre_two[3]

    own_cots = own_near_ref[64:128].astype(F32), own_next_ref[64:128].astype(F32)
    cots = jnp.where(odd, *own_cots), jnp.where(odd, *own_cots[::-1])
    deltas = []
    for p in range(2):
        act, s = silu_parts(pre_two[p + 1])
        feat_ref[p] = act.astype(BF16)
        deltas.append((cots[p] * (s + act * (1.0 - s))).astype(BF16))

    grads = []
    for p in range(-1, 3):
        sources = [q for q in range(2) if abs(q - p) < 2]
        taps = [k2_ref[288 * (1 + p - q) : 288 * (1 + p - q) + 288] for q in sources]
        given = jnp.concatenate([deltas[q] for q in sources], axis=0)
        grads.append(spread_taps(dot(jnp.concatenate(taps, axis=1), given), half))
    part_ref[0], part_ref[1] = grads[1], grads[2]

    grads = jnp.where(real, jnp.concatenate(grads, axis=0), 0.0)
    spread = spread_cells(grads, pattern)
    spread = [spread[32 * q : 32 * q + 32] for q in range(4)]
    wide = []
    for g, under in enumerate(((0,), (1, 2), (3,))):
        field = jnp.concatenate([spread[q] for q in under for _ in range(2)], axis=0)
        wide.append(dot((field * slopes[g]).astype(BF16), patches[g], NT))
    wide = wide[1] + jnp.concatenate([wide[2], wide[0]], axis=0)
    wide = jnp.concatenate([wide[32 * p : 32 * p + 32] for p in range(4)], axis=1)
    high = wide.astype(BF16)
    low = (wide - high.astype(F32)).astype(BF16)
    term_one = dot(jnp.concatenate([high, low], axis=0), to_flat_ref[...])
    term_one = (term_one[0:32] + term_one[32:64]) * (1.0 / math.sqrt(count))
    for h, half_row in enumerate((term_one, pltpu.roll(term_one, 64, 1))):
        rows_ref[pl.ds(h, 32, stride=2), :] = half_row
    rows = rows_ref[...]
    rounded = rows.astype(BF16).astype(F32)
    lane = lax.broadcasted_iota(jnp.int32, rows.shape, 1)
    pair = jnp.where(lane < 64, rounded, pltpu.roll(rows - rounded, 64, 1))
    send_ref[:, ONE_AT:LANES] = pair.astype(BF16)

    columns = [jnp.concatenate(planes[p : p + 3], axis=0) for p in range(2)]
    term = dot(columns[0], deltas[0], NT) + dot(columns[1], deltas[1], NT)
    term_ref[...] = term * (1.0 / math.sqrt(count // 8))
    rows = [term_ref[pl.ds(ch, 27, stride=32), :] for ch in range(32)]
    send_ref[:, 0:864] = jnp.concatenate(rows, axis=0).T.astype(BF16)
    send_ref[:, 864:ONE_AT] = jnp.zeros((64, ONE_AT - 864), BF16)


def outer_body(
    far_next_ref, far_near_ref, next_ref, near_ref, k2_ref,
    feat_ref, part_ref, pre_ref, act_ref, pre_two_ref, far_one_ref, far_two_ref,
    feat_out, pgrad_out,
):
    slabs = lax.axis_size("space")
    me = lax.axis_index("space")
    half = 16
    odd, upper = me % 2 == 1, (me // 2) % 2 == 1
    pattern = pool_pattern()
    far_near, far_next = far_near_ref[...].astype(F32), far_next_ref[...].astype(F32)
    far_left, far_right = jnp.where(upper, far_near, far_next), jnp.where(upper, far_next, far_near)
    top = lax.broadcasted_iota(jnp.int32, (8, LANES), 0) < 4
    edge = jnp.where(
        top,
        jnp.concatenate([far_left, pltpu.roll(far_left, 4, 0)], axis=1),
        jnp.concatenate([pltpu.roll(far_right, 4, 0), far_right], axis=1),
    )
    patches = jnp.concatenate(all_shifts(edge, 2 * half), axis=0).astype(BF16)
    act, _ = silu_parts(pre_ref[...] + dot(far_one_ref[...], patches))
    pooled = pool_sums(act_ref[...] + act, pattern)
    plane = lax.shift_right_logical(lax.broadcasted_iota(jnp.int32, pooled.shape, 0), 5)
    real = ((plane > 0) | (me > 0)) & ((plane < 1) | (me < slabs - 1))
    pooled = jnp.where(real, pooled, 0.0).astype(BF16).astype(F32)
    moved = [m.astype(BF16) for m in all_shifts(pooled, half)]

    near, following = near_ref[64:128].astype(F32), next_ref[64:128].astype(F32)
    cots = jnp.where(odd, near, following), jnp.where(odd, following, near)
    for p in range(2):
        columns = jnp.concatenate([m[32 * p : 32 * p + 32] for m in moved], axis=0)
        pre = pre_two_ref[p] + dot(far_two_ref[p], columns)
        act, s = silu_parts(pre)
        delta = (cots[p] * (s + act * (1.0 - s))).astype(BF16)
        taps = dot(k2_ref[576 * (1 - p) : 576 * (1 - p) + 288], delta)
        pgrad_out[0, :, p, :] = (part_ref[p] + spread_taps(taps, half)).astype(BF16)
        feat_out[0, :, p, :] = feat_ref[p]


def on_device(volumes, kernel_one, kernel_two, cotangent):
    _, cin, planes, width, _ = volumes.shape
    half = width // 2
    slabs = lax.axis_size("space")
    copies = lax.axis_size("dp")
    count = copies * planes * slabs * width * width

    to_kernel, to_flat = band_maps()
    weights = (
        jnp.transpose(kernel_one, (2, 3, 4, 1, 0)).reshape(27, 4, 32),
        jnp.transpose(kernel_two, (2, 3, 4, 1, 0)).reshape(864, 64),
        jnp.asarray(to_kernel, BF16),
        jnp.asarray(to_flat, BF16),
    )

    def in_hbm(*arrays):
        return [pltpu.with_memory_space_constraint(x, pltpu.HBM) for x in arrays]

    inputs = in_hbm(volumes, cotangent, *weights)
    hbm = pl.BlockSpec(memory_space=pltpu.HBM)
    limit = pltpu.CompilerParams(vmem_limit_bytes=48 * 1024 * 1024)
    whole = jax.ShapeDtypeStruct((128, width * width // 4), BF16)
    part = jax.ShapeDtypeStruct((2 * cin, width * width // 2), BF16)
    to_next, to_near, to_far_next, to_far_near, *weights = pl.pallas_call(
        prepare_body,
        out_shape=(
            whole, whole, part, part, *(jax.ShapeDtypeStruct(w.shape, BF16) for w in weights)
        ),
        in_specs=[hbm] * len(inputs),
        scratch_shapes=[
            pltpu.VMEM(volumes.shape, BF16),
            pltpu.VMEM(cotangent.shape, BF16),
            pltpu.VMEM((planes * cin * width, width), F32),
            pltpu.SemaphoreType.DMA((len(inputs),)),
        ],
        compiler_params=limit,
    )(*inputs)

    def swap(block, pairs):
        pairs = [p for p in pairs if max(p) < slabs]
        return lax.ppermute(block, "space", pairs + [(t, f) for f, t in pairs])

    evens = range(0, slabs, 2)
    fours = [i + j for i in range(0, slabs, 4) for j in range(2)]
    following = swap(to_next, [(i + 1, i + 2) for i in evens])
    near = swap(to_near, [(i, i + 1) for i in evens])
    far_next = swap(to_far_next, [(i + 2, i + 4) for i in fours])

    cells = half * half
    shapes = {
        "features": ((2, 64, cells), BF16),
        "send": ((64, LANES), BF16),
        "part": ((2, 32, cells), F32),
        "pre": ((64, LANES), F32),
        "act": ((64, LANES), F32),
        "pre_two": ((2, 64, cells), F32),
        "far_one": ((64, 72), BF16),
        "far_two": ((2, 64, 288), BF16),
    }
    feat, send, *inner = pl.pallas_call(
        functools.partial(inner_body, count),
        out_shape=tuple(jax.ShapeDtypeStruct(*x) for x in shapes.values()),
        scratch_shapes=[pltpu.VMEM((864, 64), F32), pltpu.VMEM((64, 128), F32)],
        compiler_params=limit,
        cost_estimate=pl.CostEstimate(flops=2 * 10**10, bytes_accessed=2 * 10**6, transcendentals=10**6),
    )(to_next, to_near, following, near, *weights)
    share = 64 // slabs
    send, to_far_near = lax.optimization_barrier((send.reshape(slabs, share, LANES), to_far_near))
    parts = lax.all_to_all(send, "space", 0, 0, tiled=True)
    far_near = swap(to_far_near, [(i, i + 2) for i in fours])
    features, pooled_grad = pl.pallas_call(
        outer_body,
        out_shape=(
            jax.ShapeDtypeStruct((1, 64, 2, cells), BF16),
            jax.ShapeDtypeStruct((1, 32, 2, cells), BF16),
        ),
        compiler_params=limit,
        cost_estimate=pl.CostEstimate(flops=4 * 10**10, bytes_accessed=10**6, transcendentals=10**5),
    )(far_next, far_near, following, near, weights[1], feat, *inner)
    parts, features, pooled_grad = lax.optimization_barrier((parts, features, pooled_grad))
    total = jnp.sum(parts.astype(F32), axis=0)

    def other_core(block, step):
        return lax.ppermute(block, "dp", [(i, i ^ step) for i in range(copies)])

    step = 1
    while 2 * step < copies:
        total = total + other_core(total, step)
        step *= 2
    other = other_core(total, step)
    grad_one, grad_two = pl.pallas_call(
        finish_body,
        out_shape=(jax.ShapeDtypeStruct((share * 54,), F32), jax.ShapeDtypeStruct((share * 864,), F32)),
        compiler_params=limit,
    )(total, other)
    return (features, pooled_grad, grad_one, grad_two)


def solution(mesh):
    in_specs = (P("dp", None, "space", None, None), P(), P(), P("dp", None, "space", None))
    out_specs = (P("dp", None, "space", None), P("dp", None, "space", None), P("space"), P("space"))
    return jax.shard_map(
        on_device, mesh=mesh, in_specs=in_specs, out_specs=out_specs, check_vma=False
    )
```

```python
import functools
import math

import jax
import jax.numpy as jnp
import numpy as np
from jax import lax
from jax.experimental import pallas as pl
from jax.experimental.pallas import tpu as pltpu
from jax.sharding import PartitionSpec as P

F32 = jnp.float32
BF16 = jnp.bfloat16
SHIFTS = [(dy, dx) for dy in (-1, 0, 1) for dx in (-1, 0, 1)]
NN = (((1,), (0,)), ((), ()))
NT = (((1,), (1,)), ((), ()))
LANES = 1024
HALF = 512
ONE_AT = 896


def dot(a, b, dims=NN):
    return lax.dot_general(a, b, dims, preferred_element_type=F32)


def inside(cells, width):
    lane = lax.broadcasted_iota(jnp.int32, (1, cells), 1)
    col, row = lane & (width - 1), lax.shift_right_logical(lane, width.bit_length() - 1)

    def factor(pos, step):
        if step == 0:
            return None
        return jnp.where(pos < width - 1 if step > 0 else pos > 0, 1.0, 0.0)

    return [(factor(col, d), factor(row, d)) for d in (-1, 0, 1)]


def moved_by(field, move, factor):
    return field if move == 0 else pltpu.roll(field, (-move) % field.shape[1], 1) * factor


def all_shifts(field, width):
    factors = inside(field.shape[1], width)
    across = [moved_by(field, dx, factors[dx + 1][0]) for dx in (-1, 0, 1)]
    return [moved_by(across[dx + 1], dy * width, factors[dy + 1][1]) for dy, dx in SHIFTS]


def pool_pattern():
    cell = lax.broadcasted_iota(jnp.int32, (512, 128), 0)
    block = lax.broadcasted_iota(jnp.int32, (512, 128), 1)
    at = 16 * lax.shift_right_logical(cell, 6) + lax.shift_right_logical(cell & 31, 1)
    return jnp.where(at == block, 0.125, 0.0).astype(BF16)


def silu_parts(v):
    s = 0.5 + 0.5 * jnp.tanh(0.5 * v)
    return v * s, s


def band_maps():
    to_kernel = np.zeros((4, 256, 108), np.float32)
    to_flat = np.zeros((4, 256, 128), np.float32)
    for p in range(4):
        for s in range(9):
            for dz in range(3):
                q = p + dz - 1
                for ci in range(4):
                    if 0 <= q <= 3:
                        row = 16 * s + 4 * q + ci
                    else:
                        row = 144 + 8 * s + (0 if q < 0 else 4) + ci
                    tap = 9 * dz + s
                    to_kernel[p, row, 4 * tap + ci] = 1
                    to_flat[p, row, 64 * (ci // 2) + 27 * (ci % 2) + tap] = 1
    return to_kernel, to_flat.reshape(1024, 128)


def prepare_body(
    vol_hbm, cot_hbm, *refs,
):
    weights, (next_ref, near_ref, far_next_ref, far_near_ref) = refs[:4], refs[4:8]
    kept, (vol_ref, cot_ref, cells_ref, sems) = refs[8:12], refs[12:]
    me = lax.axis_index("space")
    odd, upper = me % 2 == 1, (me // 2) % 2 == 1
    vol_copy = pltpu.make_async_copy(vol_hbm, vol_ref, sems.at[0])
    cot_copy = pltpu.make_async_copy(cot_hbm, cot_ref, sems.at[1])
    vol_copy.start()
    cot_copy.start()
    copies = [
        pltpu.make_async_copy(src, dst, sems.at[2 + i])
        for i, (src, dst) in enumerate(zip(weights, kept))
    ]
    for copy in copies:
        copy.start()
    vol_copy.wait()
    cin, planes, width = vol_ref.shape[1:4]
    for plane in range(planes):
        for ch in range(cin):
            at = (plane * cin + ch) * width
            cells_ref[at : at + width] = vol_ref[0, ch, plane].astype(F32)
    count = planes * cin
    blocks = []
    for b in range(4):
        lines = [cells_ref[pl.ds(8 * b + y, count, stride=width), :] for y in range(8)]
        rows = jnp.concatenate(lines, axis=1)
        near_ref[count * b : count * b + count] = rows.astype(BF16)
        next_ref[count * b : count * b + count] = rows.astype(BF16)
        blocks.append(rows)
    halves = [jnp.concatenate(blocks[2 * m : 2 * m + 2], axis=1) for m in range(2)]
    top = lax.broadcasted_iota(jnp.int32, (8, HALF), 0) < 4
    first = jnp.where(top, halves[0][0:8], pltpu.roll(halves[1][0:8], 4, 0))
    last = jnp.where(top, pltpu.roll(halves[0][8:16], 4, 0), halves[1][8:16])
    far_near_ref[...] = jnp.where(upper, first, last).astype(BF16)
    far_next_ref[...] = jnp.where(upper, last, first).astype(BF16)
    cot_copy.wait()
    cot = cot_ref[0].astype(F32)
    cots = (cot[:, 0, :], cot[:, 1, :])
    near_ref[64:128] = jnp.where(odd, cots[0], cots[1]).astype(BF16)
    next_ref[64:128] = jnp.where(odd, cots[1], cots[0]).astype(BF16)
    for copy in copies:
        copy.wait()


def finish_body(mine_ref, other_ref, one_ref, two_ref):
    total = mine_ref[...] + other_ref[...]
    share = total.shape[0]
    two_ref[...] = jnp.concatenate([total[r, 0:864] for r in range(share)])
    one = total[:, ONE_AT : ONE_AT + 54] + total[:, ONE_AT + 64 : ONE_AT + 118]
    one_ref[...] = jnp.concatenate([one[r] for r in range(share)])


def unfold(block, rows):
    return jnp.concatenate([block[rows * b : rows * b + rows] for b in range(4)], axis=1)


def pool_sums(sums, pattern):
    rows = sums.shape[0]
    high = sums.astype(BF16)
    low = (sums - high.astype(F32)).astype(BF16)
    halves = [part[:, 512 * m : 512 * m + 512] for part in (high, low) for m in range(2)]
    out = dot(jnp.concatenate(halves, axis=0), pattern)
    out = out[0 : 2 * rows] + out[2 * rows : 4 * rows]
    return jnp.concatenate([out[0:rows], out[rows : 2 * rows]], axis=1)


def spread_cells(field, pattern):
    rows = field.shape[0]
    high = field.astype(BF16)
    low = (field - high.astype(F32)).astype(BF16)
    halves = [part[:, 128 * m : 128 * m + 128] for part in (high, low) for m in range(2)]
    out = dot(jnp.concatenate(halves, axis=0), pattern, NT)
    out = out[0 : 2 * rows] + out[2 * rows : 4 * rows]
    return jnp.concatenate([out[0:rows], out[rows : 2 * rows]], axis=1)


def spread_taps(taps, half):
    factors = inside(half * half, half)
    total = None
    for dx in (-1, 0, 1):
        column = None
        for dy in (-1, 0, 1):
            s = 3 * (1 - dy) + (1 - dx)
            part = moved_by(taps[32 * s : 32 * s + 32], dy * half, factors[dy + 1][1])
            column = part if column is None else column + part
        column = moved_by(column, dx, factors[dx + 1][0])
        total = column if total is None else total + column
    return total


def inner_body(
    count,
    own_next_ref, own_near_ref, next_ref, near_ref, k1_ref, k2_ref, to_kernel_ref, to_flat_ref,
    feat_ref, send_ref, part_ref, pre_ref, act_ref, pre_two_ref, far_one_ref, far_two_ref,
    term_ref, rows_ref,
):
    slabs = lax.axis_size("space")
    me = lax.axis_index("space")
    half = 16

    odd = me % 2 == 1
    own = unfold(own_near_ref[0:64].astype(F32), 16)
    near, following = near_ref[0:64].astype(F32), next_ref[0:64].astype(F32)
    left = unfold(jnp.where(odd, near, following), 16)
    right = unfold(jnp.where(odd, following, near), 16)
    top = lax.broadcasted_iota(jnp.int32, (8, LANES), 0) < 4
    edges = (
        jnp.where(top, 0.0, pltpu.roll(own[0:8], 4, 0)),
        jnp.where(top, pltpu.roll(left[8:16], 4, 0), pltpu.roll(right[0:8], 4, 0)),
        jnp.where(top, pltpu.roll(own[8:16], 4, 0), 0.0),
    )
    moved = all_shifts(jnp.concatenate([left, own, right, *edges], axis=0), 2 * half)
    patches = []
    for g in range(3):
        rows = [m[16 * g : 16 * g + 16] for m in moved] + [m[48 + 8 * g : 56 + 8 * g] for m in moved]
        rows.append(jnp.zeros((40, LANES), F32))
        patches.append(jnp.concatenate(rows, axis=0).astype(BF16))

    k1t = k1_ref[...].astype(F32).reshape(108, 32).T.astype(BF16)
    two_by_dz = jnp.concatenate(
        [k2_ref[288 * dz : 288 * dz + 288].astype(F32).T for dz in range(3)], axis=0
    ).astype(BF16)
    banded = jnp.concatenate(
        [dot(k1t, to_kernel_ref[p], NT).astype(BF16) for p in range(4)], axis=0
    )
    far_one_ref[...] = jnp.concatenate(
        [dot(k1t, to_kernel_ref[p, 144:216], NT).astype(BF16) for p in (0, 3)], axis=0
    )
    far_two_ref[0] = two_by_dz[0:64]
    far_two_ref[1] = two_by_dz[128:192]
    pattern = pool_pattern()

    pre = dot(banded, patches[0])
    pre_ref[0:32] = pre[0:32]
    act, s = silu_parts(pre[32:128])
    act_ref[0:32] = act[0:32]
    slopes = [(s + act * (1.0 - s))[32:96]]
    sums = [act[32:64] + act[64:96]]
    act, s = silu_parts(dot(banded, patches[1]))
    slopes.append(s + act * (1.0 - s))
    sums += [act[0:32] + act[32:64], act[64:96] + act[96:128]]
    pre = dot(banded, patches[2])
    pre_ref[32:64] = pre[96:128]
    act, s = silu_parts(pre[0:96])
    act_ref[32:64] = act[64:96]
    slopes.append((s + act * (1.0 - s))[0:64])
    sums += [act[0:32] + act[32:64]]
    pooled = pool_sums(jnp.concatenate(sums, axis=0), pattern)
    plane = lax.shift_right_logical(lax.broadcasted_iota(jnp.int32, pooled.shape, 0), 5)
    real = ((plane > 0) | (me > 0)) & ((plane < 3) | (me < slabs - 1))
    pooled = jnp.where(real, pooled, 0.0).astype(BF16).astype(F32)

    moved = [m.astype(BF16) for m in all_shifts(pooled, half)]
    planes = [jnp.concatenate([m[32 * q : 32 * q + 32] for m in moved], axis=0) for q in range(4)]
    pre_two = [None] * 4
    for q, columns in enumerate(planes):
        by_dz = dot(two_by_dz, columns)
        for dz in range(3):
            p = q + 1 - dz
            if 0 <= p < 4:
                part = by_dz[64 * dz : 64 * dz + 64]
                pre_two[p] = part if pre_two[p] is None else pre_two[p] + part
    pre_two_ref[0], pre_two_ref[1] = pre_two[0], pre_two[3]

    own_cots = own_near_ref[64:128].astype(F32), own_next_ref[64:128].astype(F32)
    cots = jnp.where(odd, *own_cots), jnp.where(odd, *own_cots[::-1])
    deltas = []
    for p in range(2):
        act, s = silu_parts(pre_two[p + 1])
        feat_ref[p] = act.astype(BF16)
        deltas.append((cots[p] * (s + act * (1.0 - s))).astype(BF16))

    grads = []
    for p in range(-1, 3):
        sources = [q for q in range(2) if abs(q - p) < 2]
        taps = [k2_ref[288 * (1 + p - q) : 288 * (1 + p - q) + 288] for q in sources]
        given = jnp.concatenate([deltas[q] for q in sources], axis=0)
        grads.append(spread_taps(dot(jnp.concatenate(taps, axis=1), given), half))
    part_ref[0], part_ref[1] = grads[1], grads[2]

    grads = jnp.where(real, jnp.concatenate(grads, axis=0), 0.0)
    spread = spread_cells(grads, pattern)
    spread = [spread[32 * q : 32 * q + 32] for q in range(4)]
    wide = []
    for g, under in enumerate(((0,), (1, 2), (3,))):
        field = jnp.concatenate([spread[q] for q in under for _ in range(2)], axis=0)
        wide.append(dot((field * slopes[g]).astype(BF16), patches[g], NT))
    wide = wide[1] + jnp.concatenate([wide[2], wide[0]], axis=0)
    wide = jnp.concatenate([wide[32 * p : 32 * p + 32] for p in range(4)], axis=1)
    high = wide.astype(BF16)
    low = (wide - high.astype(F32)).astype(BF16)
    term_one = dot(jnp.concatenate([high, low], axis=0), to_flat_ref[...])
    term_one = (term_one[0:32] + term_one[32:64]) * (1.0 / math.sqrt(count))
    for h, half_row in enumerate((term_one, pltpu.roll(term_one, 64, 1))):
        rows_ref[pl.ds(h, 32, stride=2), :] = half_row
    rows = rows_ref[...]
    rounded = rows.astype(BF16).astype(F32)
    lane = lax.broadcasted_iota(jnp.int32, rows.shape, 1)
    pair = jnp.where(lane < 64, rounded, pltpu.roll(rows - rounded, 64, 1))
    send_ref[:, ONE_AT:LANES] = pair.astype(BF16)

    columns = [jnp.concatenate(planes[p : p + 3], axis=0) for p in range(2)]
    term = dot(columns[0], deltas[0], NT) + dot(columns[1], deltas[1], NT)
    term_ref[...] = term * (1.0 / math.sqrt(count // 8))
    rows = [term_ref[pl.ds(ch, 27, stride=32), :] for ch in range(32)]
    send_ref[:, 0:864] = jnp.concatenate(rows, axis=0).T.astype(BF16)
    send_ref[:, 864:ONE_AT] = jnp.zeros((64, ONE_AT - 864), BF16)


def outer_body(
    far_next_ref, far_near_ref, next_ref, near_ref, k2_ref,
    feat_ref, part_ref, pre_ref, act_ref, pre_two_ref, far_one_ref, far_two_ref,
    feat_out, pgrad_out,
):
    slabs = lax.axis_size("space")
    me = lax.axis_index("space")
    half = 16
    odd, upper = me % 2 == 1, (me // 2) % 2 == 1
    pattern = pool_pattern()
    far_near, far_next = far_near_ref[...].astype(F32), far_next_ref[...].astype(F32)
    far_left, far_right = jnp.where(upper, far_near, far_next), jnp.where(upper, far_next, far_near)
    top = lax.broadcasted_iota(jnp.int32, (8, LANES), 0) < 4
    edge = jnp.where(
        top,
        jnp.concatenate([far_left, pltpu.roll(far_left, 4, 0)], axis=1),
        jnp.concatenate([pltpu.roll(far_right, 4, 0), far_right], axis=1),
    )
    patches = jnp.concatenate(all_shifts(edge, 2 * half), axis=0).astype(BF16)
    act, _ = silu_parts(pre_ref[...] + dot(far_one_ref[...], patches))
    pooled = pool_sums(act_ref[...] + act, pattern)
    plane = lax.shift_right_logical(lax.broadcasted_iota(jnp.int32, pooled.shape, 0), 5)
    real = ((plane > 0) | (me > 0)) & ((plane < 1) | (me < slabs - 1))
    pooled = jnp.where(real, pooled, 0.0).astype(BF16).astype(F32)
    moved = [m.astype(BF16) for m in all_shifts(pooled, half)]

    near, following = near_ref[64:128].astype(F32), next_ref[64:128].astype(F32)
    cots = jnp.where(odd, near, following), jnp.where(odd, following, near)
    for p in range(2):
        columns = jnp.concatenate([m[32 * p : 32 * p + 32] for m in moved], axis=0)
        pre = pre_two_ref[p] + dot(far_two_ref[p], columns)
        act, s = silu_parts(pre)
        delta = (cots[p] * (s + act * (1.0 - s))).astype(BF16)
        taps = dot(k2_ref[576 * (1 - p) : 576 * (1 - p) + 288], delta)
        pgrad_out[0, :, p, :] = (part_ref[p] + spread_taps(taps, half)).astype(BF16)
        feat_out[0, :, p, :] = feat_ref[p]


def on_device(volumes, kernel_one, kernel_two, cotangent):
    _, cin, planes, width, _ = volumes.shape
    half = width // 2
    slabs = lax.axis_size("space")
    copies = lax.axis_size("dp")
    count = copies * planes * slabs * width * width

    to_kernel, to_flat = band_maps()
    weights = (
        jnp.transpose(kernel_one, (2, 3, 4, 1, 0)).reshape(27, 4, 32),
        jnp.transpose(kernel_two, (2, 3, 4, 1, 0)).reshape(864, 64),
        jnp.asarray(to_kernel, BF16),
        jnp.asarray(to_flat, BF16),
    )

    def in_hbm(*arrays):
        return [pltpu.with_memory_space_constraint(x, pltpu.HBM) for x in arrays]

    inputs = in_hbm(volumes, cotangent, *weights)
    hbm = pl.BlockSpec(memory_space=pltpu.HBM)
    limit = pltpu.CompilerParams(vmem_limit_bytes=48 * 1024 * 1024)
    whole = jax.ShapeDtypeStruct((128, width * width // 4), BF16)
    part = jax.ShapeDtypeStruct((2 * cin, width * width // 2), BF16)
    to_next, to_near, to_far_next, to_far_near, *weights = pl.pallas_call(
        prepare_body,
        out_shape=(
            whole, whole, part, part, *(jax.ShapeDtypeStruct(w.shape, BF16) for w in weights)
        ),
        in_specs=[hbm] * len(inputs),
        scratch_shapes=[
            pltpu.VMEM(volumes.shape, BF16),
            pltpu.VMEM(cotangent.shape, BF16),
            pltpu.VMEM((planes * cin * width, width), F32),
            pltpu.SemaphoreType.DMA((len(inputs),)),
        ],
        compiler_params=limit,
    )(*inputs)

    def swap(block, pairs):
        pairs = [p for p in pairs if max(p) < slabs]
        return lax.ppermute(block, "space", pairs + [(t, f) for f, t in pairs])

    evens = range(0, slabs, 2)
    fours = [i + j for i in range(0, slabs, 4) for j in range(2)]
    following = swap(to_next, [(i + 1, i + 2) for i in evens])
    near = swap(to_near, [(i, i + 1) for i in evens])
    far_next = swap(to_far_next, [(i + 2, i + 4) for i in fours])

    cells = half * half
    shapes = {
        "features": ((2, 64, cells), BF16),
        "send": ((64, LANES), BF16),
        "part": ((2, 32, cells), F32),
        "pre": ((64, LANES), F32),
        "act": ((64, LANES), F32),
        "pre_two": ((2, 64, cells), F32),
        "far_one": ((64, 72), BF16),
        "far_two": ((2, 64, 288), BF16),
    }
    feat, send, *inner = pl.pallas_call(
        functools.partial(inner_body, count),
        out_shape=tuple(jax.ShapeDtypeStruct(*x) for x in shapes.values()),
        scratch_shapes=[pltpu.VMEM((864, 64), F32), pltpu.VMEM((64, 128), F32)],
        compiler_params=limit,
        cost_estimate=pl.CostEstimate(flops=2 * 10**10, bytes_accessed=2 * 10**6, transcendentals=10**6),
    )(to_next, to_near, following, near, *weights)
    share = 64 // slabs
    send = send.reshape(slabs, share, LANES)
    parts = lax.all_to_all(send, "space", 0, 0, tiled=True)
    _, _, to_far_near = lax.optimization_barrier((send, far_next, to_far_near))
    far_near = swap(to_far_near, [(i, i + 2) for i in fours])
    features, pooled_grad = pl.pallas_call(
        outer_body,
        out_shape=(
            jax.ShapeDtypeStruct((1, 64, 2, cells), BF16),
            jax.ShapeDtypeStruct((1, 32, 2, cells), BF16),
        ),
        compiler_params=limit,
        cost_estimate=pl.CostEstimate(flops=2 * 10**9, bytes_accessed=10**6, transcendentals=10**5),
    )(far_next, far_near, following, near, weights[1], feat, *inner)
    parts, features, pooled_grad = lax.optimization_barrier((parts, features, pooled_grad))
    total = jnp.sum(parts.astype(F32), axis=0)

    def other_core(block, step):
        return lax.ppermute(block, "dp", [(i, i ^ step) for i in range(copies)])

    step = 1
    while 2 * step < copies:
        total = total + other_core(total, step)
        step *= 2
    other = other_core(total, step)
    grad_one, grad_two = pl.pallas_call(
        finish_body,
        out_shape=(jax.ShapeDtypeStruct((share * 54,), F32), jax.ShapeDtypeStruct((share * 864,), F32)),
        compiler_params=limit,
    )(total, other)
    return (features, pooled_grad, grad_one, grad_two)


def solution(mesh):
    in_specs = (P("dp", None, "space", None, None), P(), P(), P("dp", None, "space", None))
    out_specs = (P("dp", None, "space", None), P("dp", None, "space", None), P("space"), P("space"))
    return jax.shard_map(
        on_device, mesh=mesh, in_specs=in_specs, out_specs=out_specs, check_vma=False
    )
```

```python
import functools
import math

import jax
import jax.numpy as jnp
import numpy as np
from jax import lax
from jax.experimental import pallas as pl
from jax.experimental.pallas import tpu as pltpu
from jax.sharding import PartitionSpec as P

F32 = jnp.float32
BF16 = jnp.bfloat16
SHIFTS = [(dy, dx) for dy in (-1, 0, 1) for dx in (-1, 0, 1)]
NN = (((1,), (0,)), ((), ()))
NT = (((1,), (1,)), ((), ()))
LANES = 1024
HALF = 512
ONE_AT = 896


def dot(a, b, dims=NN):
    return lax.dot_general(a, b, dims, preferred_element_type=F32)


def inside(cells, width):
    lane = lax.broadcasted_iota(jnp.int32, (1, cells), 1)
    col, row = lane & (width - 1), lax.shift_right_logical(lane, width.bit_length() - 1)

    def factor(pos, step):
        if step == 0:
            return None
        return jnp.where(pos < width - 1 if step > 0 else pos > 0, 1.0, 0.0)

    return [(factor(col, d), factor(row, d)) for d in (-1, 0, 1)]


def moved_by(field, move, factor):
    return field if move == 0 else pltpu.roll(field, (-move) % field.shape[1], 1) * factor


def all_shifts(field, width):
    factors = inside(field.shape[1], width)
    across = [moved_by(field, dx, factors[dx + 1][0]) for dx in (-1, 0, 1)]
    return [moved_by(across[dx + 1], dy * width, factors[dy + 1][1]) for dy, dx in SHIFTS]


def pool_pattern():
    cell = lax.broadcasted_iota(jnp.int32, (512, 128), 0)
    block = lax.broadcasted_iota(jnp.int32, (512, 128), 1)
    at = 16 * lax.shift_right_logical(cell, 6) + lax.shift_right_logical(cell & 31, 1)
    return jnp.where(at == block, 0.125, 0.0).astype(BF16)


def silu_parts(v):
    s = 0.5 + 0.5 * jnp.tanh(0.5 * v)
    return v * s, s


def band_maps():
    to_kernel = np.zeros((4, 256, 108), np.float32)
    to_flat = np.zeros((4, 256, 128), np.float32)
    for p in range(4):
        for s in range(9):
            for dz in range(3):
                q = p + dz - 1
                for ci in range(4):
                    if 0 <= q <= 3:
                        row = 16 * s + 4 * q + ci
                    else:
                        row = 144 + 8 * s + (0 if q < 0 else 4) + ci
                    tap = 9 * dz + s
                    to_kernel[p, row, 4 * tap + ci] = 1
                    to_flat[p, row, 64 * (ci // 2) + 27 * (ci % 2) + tap] = 1
    return to_kernel, to_flat.reshape(1024, 128)


def prepare_body(
    vol_hbm, cot_hbm, *refs,
):
    weights, (next_ref, near_ref, far_next_ref, far_near_ref) = refs[:4], refs[4:8]
    kept, (vol_ref, cot_ref, cells_ref, sems) = refs[8:12], refs[12:]
    me = lax.axis_index("space")
    odd, upper = me % 2 == 1, (me // 2) % 2 == 1
    vol_copy = pltpu.make_async_copy(vol_hbm, vol_ref, sems.at[0])
    cot_copy = pltpu.make_async_copy(cot_hbm, cot_ref, sems.at[1])
    vol_copy.start()
    cot_copy.start()
    copies = [
        pltpu.make_async_copy(src, dst, sems.at[2 + i])
        for i, (src, dst) in enumerate(zip(weights, kept))
    ]
    for copy in copies:
        copy.start()
    vol_copy.wait()
    cin, planes, width = vol_ref.shape[1:4]
    for plane in range(planes):
        for ch in range(cin):
            at = (plane * cin + ch) * width
            cells_ref[at : at + width] = vol_ref[0, ch, plane].astype(F32)
    count = planes * cin
    blocks = []
    for b in range(4):
        lines = [cells_ref[pl.ds(8 * b + y, count, stride=width), :] for y in range(8)]
        rows = jnp.concatenate(lines, axis=1)
        near_ref[count * b : count * b + count] = rows.astype(BF16)
        next_ref[count * b : count * b + count] = rows.astype(BF16)
        blocks.append(rows)
    halves = [jnp.concatenate(blocks[2 * m : 2 * m + 2], axis=1) for m in range(2)]
    top = lax.broadcasted_iota(jnp.int32, (8, HALF), 0) < 4
    first = jnp.where(top, halves[0][0:8], pltpu.roll(halves[1][0:8], 4, 0))
    last = jnp.where(top, pltpu.roll(halves[0][8:16], 4, 0), halves[1][8:16])
    far_near_ref[...] = jnp.where(upper, first, last).astype(BF16)
    far_next_ref[...] = jnp.where(upper, last, first).astype(BF16)
    cot_copy.wait()
    cot = cot_ref[0].astype(F32)
    cots = (cot[:, 0, :], cot[:, 1, :])
    near_ref[64:128] = jnp.where(odd, cots[0], cots[1]).astype(BF16)
    next_ref[64:128] = jnp.where(odd, cots[1], cots[0]).astype(BF16)
    for copy in copies:
        copy.wait()


def finish_body(mine_ref, other_ref, one_ref, two_ref):
    total = mine_ref[...] + other_ref[...]
    share = total.shape[0]
    two_ref[...] = jnp.concatenate([total[r, 0:864] for r in range(share)])
    one = total[:, ONE_AT : ONE_AT + 54] + total[:, ONE_AT + 64 : ONE_AT + 118]
    one_ref[...] = jnp.concatenate([one[r] for r in range(share)])


def unfold(block, rows):
    return jnp.concatenate([block[rows * b : rows * b + rows] for b in range(4)], axis=1)


def pool_sums(sums, pattern):
    rows = sums.shape[0]
    high = sums.astype(BF16)
    low = (sums - high.astype(F32)).astype(BF16)
    halves = [part[:, 512 * m : 512 * m + 512] for part in (high, low) for m in range(2)]
    out = dot(jnp.concatenate(halves, axis=0), pattern)
    out = out[0 : 2 * rows] + out[2 * rows : 4 * rows]
    return jnp.concatenate([out[0:rows], out[rows : 2 * rows]], axis=1)


def spread_cells(field, pattern):
    rows = field.shape[0]
    high = field.astype(BF16)
    low = (field - high.astype(F32)).astype(BF16)
    halves = [part[:, 128 * m : 128 * m + 128] for part in (high, low) for m in range(2)]
    out = dot(jnp.concatenate(halves, axis=0), pattern, NT)
    out = out[0 : 2 * rows] + out[2 * rows : 4 * rows]
    return jnp.concatenate([out[0:rows], out[rows : 2 * rows]], axis=1)


def spread_taps(taps, half):
    factors = inside(half * half, half)
    total = None
    for dx in (-1, 0, 1):
        column = None
        for dy in (-1, 0, 1):
            s = 3 * (1 - dy) + (1 - dx)
            part = moved_by(taps[32 * s : 32 * s + 32], dy * half, factors[dy + 1][1])
            column = part if column is None else column + part
        column = moved_by(column, dx, factors[dx + 1][0])
        total = column if total is None else total + column
    return total


def inner_body(
    count,
    own_next_ref, own_near_ref, next_ref, near_ref, k1_ref, k2_ref, to_kernel_ref, to_flat_ref,
    feat_ref, send_ref, part_ref, pre_ref, act_ref, pre_two_ref, far_one_ref, far_two_ref,
    term_ref, rows_ref,
):
    slabs = lax.axis_size("space")
    me = lax.axis_index("space")
    half = 16

    odd = me % 2 == 1
    own = unfold(own_near_ref[0:64].astype(F32), 16)
    near, following = near_ref[0:64].astype(F32), next_ref[0:64].astype(F32)
    left = unfold(jnp.where(odd, near, following), 16)
    right = unfold(jnp.where(odd, following, near), 16)
    top = lax.broadcasted_iota(jnp.int32, (8, LANES), 0) < 4
    edges = (
        jnp.where(top, 0.0, pltpu.roll(own[0:8], 4, 0)),
        jnp.where(top, pltpu.roll(left[8:16], 4, 0), pltpu.roll(right[0:8], 4, 0)),
        jnp.where(top, pltpu.roll(own[8:16], 4, 0), 0.0),
    )
    moved = all_shifts(jnp.concatenate([left, own, right, *edges], axis=0), 2 * half)
    patches = []
    for g in range(3):
        rows = [m[16 * g : 16 * g + 16] for m in moved] + [m[48 + 8 * g : 56 + 8 * g] for m in moved]
        rows.append(jnp.zeros((40, LANES), F32))
        patches.append(jnp.concatenate(rows, axis=0).astype(BF16))

    k1t = k1_ref[...].astype(F32).reshape(108, 32).T.astype(BF16)
    two_by_dz = jnp.concatenate(
        [k2_ref[288 * dz : 288 * dz + 288].astype(F32).T for dz in range(3)], axis=0
    ).astype(BF16)
    banded = jnp.concatenate(
        [dot(k1t, to_kernel_ref[p], NT).astype(BF16) for p in range(4)], axis=0
    )
    far_one_ref[...] = jnp.concatenate(
        [dot(k1t, to_kernel_ref[p, 144:216], NT).astype(BF16) for p in (0, 3)], axis=0
    )
    far_two_ref[0] = two_by_dz[0:64]
    far_two_ref[1] = two_by_dz[128:192]
    pattern = pool_pattern()

    pre = dot(banded, patches[0])
    pre_ref[0:32] = pre[0:32]
    act, s = silu_parts(pre[32:128])
    act_ref[0:32] = act[0:32]
    slopes = [(s + act * (1.0 - s))[32:96]]
    sums = [act[32:64] + act[64:96]]
    act, s = silu_parts(dot(banded, patches[1]))
    slopes.append(s + act * (1.0 - s))
    sums += [act[0:32] + act[32:64], act[64:96] + act[96:128]]
    pre = dot(banded, patches[2])
    pre_ref[32:64] = pre[96:128]
    act, s = silu_parts(pre[0:96])
    act_ref[32:64] = act[64:96]
    slopes.append((s + act * (1.0 - s))[0:64])
    sums += [act[0:32] + act[32:64]]
    pooled = pool_sums(jnp.concatenate(sums, axis=0), pattern)
    plane = lax.shift_right_logical(lax.broadcasted_iota(jnp.int32, pooled.shape, 0), 5)
    real = ((plane > 0) | (me > 0)) & ((plane < 3) | (me < slabs - 1))
    pooled = jnp.where(real, pooled, 0.0).astype(BF16).astype(F32)

    moved = [m.astype(BF16) for m in all_shifts(pooled, half)]
    planes = [jnp.concatenate([m[32 * q : 32 * q + 32] for m in moved], axis=0) for q in range(4)]
    pre_two = [None] * 4
    for q, columns in enumerate(planes):
        by_dz = dot(two_by_dz, columns)
        for dz in range(3):
            p = q + 1 - dz
            if 0 <= p < 4:
                part = by_dz[64 * dz : 64 * dz + 64]
                pre_two[p] = part if pre_two[p] is None else pre_two[p] + part
    pre_two_ref[0], pre_two_ref[1] = pre_two[0], pre_two[3]

    own_cots = own_near_ref[64:128].astype(F32), own_next_ref[64:128].astype(F32)
    cots = jnp.where(odd, *own_cots), jnp.where(odd, *own_cots[::-1])
    deltas = []
    for p in range(2):
        act, s = silu_parts(pre_two[p + 1])
        feat_ref[p] = act.astype(BF16)
        deltas.append((cots[p] * (s + act * (1.0 - s))).astype(BF16))

    grads = []
    for p in range(-1, 3):
        sources = [q for q in range(2) if abs(q - p) < 2]
        taps = [k2_ref[288 * (1 + p - q) : 288 * (1 + p - q) + 288] for q in sources]
        given = jnp.concatenate([deltas[q] for q in sources], axis=0)
        grads.append(spread_taps(dot(jnp.concatenate(taps, axis=1), given), half))
    part_ref[0], part_ref[1] = grads[1], grads[2]

    grads = jnp.where(real, jnp.concatenate(grads, axis=0), 0.0)
    spread = spread_cells(grads, pattern)
    spread = [spread[32 * q : 32 * q + 32] for q in range(4)]
    wide = []
    for g, under in enumerate(((0,), (1, 2), (3,))):
        field = jnp.concatenate([spread[q] for q in under for _ in range(2)], axis=0)
        wide.append(dot((field * slopes[g]).astype(BF16), patches[g], NT))
    wide = wide[1] + jnp.concatenate([wide[2], wide[0]], axis=0)
    wide = jnp.concatenate([wide[32 * p : 32 * p + 32] for p in range(4)], axis=1)
    high = wide.astype(BF16)
    low = (wide - high.astype(F32)).astype(BF16)
    term_one = dot(jnp.concatenate([high, low], axis=0), to_flat_ref[...])
    term_one = (term_one[0:32] + term_one[32:64]) * (1.0 / math.sqrt(count))
    for h, half_row in enumerate((term_one, pltpu.roll(term_one, 64, 1))):
        rows_ref[pl.ds(h, 32, stride=2), :] = half_row
    rows = rows_ref[...]
    rounded = rows.astype(BF16).astype(F32)
    lane = lax.broadcasted_iota(jnp.int32, rows.shape, 1)
    pair = jnp.where(lane < 64, rounded, pltpu.roll(rows - rounded, 64, 1))
    send_ref[:, ONE_AT:LANES] = pair.astype(BF16)

    columns = [jnp.concatenate(planes[p : p + 3], axis=0) for p in range(2)]
    term = dot(columns[0], deltas[0], NT) + dot(columns[1], deltas[1], NT)
    term_ref[...] = term * (1.0 / math.sqrt(count // 8))
    rows = [term_ref[pl.ds(ch, 27, stride=32), :] for ch in range(32)]
    send_ref[:, 0:864] = jnp.concatenate(rows, axis=0).T.astype(BF16)
    send_ref[:, 864:ONE_AT] = jnp.zeros((64, ONE_AT - 864), BF16)


def outer_body(
    far_next_ref, far_near_ref, next_ref, near_ref, k2_ref,
    feat_ref, part_ref, pre_ref, act_ref, pre_two_ref, far_one_ref, far_two_ref,
    feat_out, pgrad_out,
):
    slabs = lax.axis_size("space")
    me = lax.axis_index("space")
    half = 16
    odd, upper = me % 2 == 1, (me // 2) % 2 == 1
    pattern = pool_pattern()
    far_near, far_next = far_near_ref[...].astype(F32), far_next_ref[...].astype(F32)
    far_left, far_right = jnp.where(upper, far_near, far_next), jnp.where(upper, far_next, far_near)
    top = lax.broadcasted_iota(jnp.int32, (8, LANES), 0) < 4
    edge = jnp.where(
        top,
        jnp.concatenate([far_left, pltpu.roll(far_left, 4, 0)], axis=1),
        jnp.concatenate([pltpu.roll(far_right, 4, 0), far_right], axis=1),
    )
    patches = jnp.concatenate(all_shifts(edge, 2 * half), axis=0).astype(BF16)
    act, _ = silu_parts(pre_ref[...] + dot(far_one_ref[...], patches))
    pooled = pool_sums(act_ref[...] + act, pattern)
    plane = lax.shift_right_logical(lax.broadcasted_iota(jnp.int32, pooled.shape, 0), 5)
    real = ((plane > 0) | (me > 0)) & ((plane < 1) | (me < slabs - 1))
    pooled = jnp.where(real, pooled, 0.0).astype(BF16).astype(F32)
    moved = [m.astype(BF16) for m in all_shifts(pooled, half)]

    near, following = near_ref[64:128].astype(F32), next_ref[64:128].astype(F32)
    cots = jnp.where(odd, near, following), jnp.where(odd, following, near)
    for p in range(2):
        columns = jnp.concatenate([m[32 * p : 32 * p + 32] for m in moved], axis=0)
        pre = pre_two_ref[p] + dot(far_two_ref[p], columns)
        act, s = silu_parts(pre)
        delta = (cots[p] * (s + act * (1.0 - s))).astype(BF16)
        taps = dot(k2_ref[576 * (1 - p) : 576 * (1 - p) + 288], delta)
        pgrad_out[0, :, p, :] = (part_ref[p] + spread_taps(taps, half)).astype(BF16)
        feat_out[0, :, p, :] = feat_ref[p]


def on_device(volumes, kernel_one, kernel_two, cotangent):
    _, cin, planes, width, _ = volumes.shape
    half = width // 2
    slabs = lax.axis_size("space")
    copies = lax.axis_size("dp")
    count = copies * planes * slabs * width * width

    to_kernel, to_flat = band_maps()
    weights = (
        jnp.transpose(kernel_one, (2, 3, 4, 1, 0)).reshape(27, 4, 32),
        jnp.transpose(kernel_two, (2, 3, 4, 1, 0)).reshape(864, 64),
        jnp.asarray(to_kernel, BF16),
        jnp.asarray(to_flat, BF16),
    )

    def in_hbm(*arrays):
        return [pltpu.with_memory_space_constraint(x, pltpu.HBM) for x in arrays]

    inputs = in_hbm(volumes, cotangent, *weights)
    hbm = pl.BlockSpec(memory_space=pltpu.HBM)
    limit = pltpu.CompilerParams(vmem_limit_bytes=48 * 1024 * 1024)
    whole = jax.ShapeDtypeStruct((128, width * width // 4), BF16)
    part = jax.ShapeDtypeStruct((2 * cin, width * width // 2), BF16)
    to_next, to_near, to_far_next, to_far_near, *weights = pl.pallas_call(
        prepare_body,
        out_shape=(
            whole, whole, part, part, *(jax.ShapeDtypeStruct(w.shape, BF16) for w in weights)
        ),
        in_specs=[hbm] * len(inputs),
        scratch_shapes=[
            pltpu.VMEM(volumes.shape, BF16),
            pltpu.VMEM(cotangent.shape, BF16),
            pltpu.VMEM((planes * cin * width, width), F32),
            pltpu.SemaphoreType.DMA((len(inputs),)),
        ],
        compiler_params=limit,
    )(*inputs)

    def swap(block, pairs):
        pairs = [p for p in pairs if max(p) < slabs]
        return lax.ppermute(block, "space", pairs + [(t, f) for f, t in pairs])

    evens = range(0, slabs, 2)
    fours = [i + j for i in range(0, slabs, 4) for j in range(2)]
    following = swap(to_next, [(i + 1, i + 2) for i in evens])
    near = swap(to_near, [(i, i + 1) for i in evens])
    far_next = swap(to_far_next, [(i + 2, i + 4) for i in fours])

    cells = half * half
    shapes = {
        "features": ((2, 64, cells), BF16),
        "send": ((64, LANES), BF16),
        "part": ((2, 32, cells), F32),
        "pre": ((64, LANES), F32),
        "act": ((64, LANES), F32),
        "pre_two": ((2, 64, cells), F32),
        "far_one": ((64, 72), BF16),
        "far_two": ((2, 64, 288), BF16),
    }
    feat, send, *inner = pl.pallas_call(
        functools.partial(inner_body, count),
        out_shape=tuple(jax.ShapeDtypeStruct(*x) for x in shapes.values()),
        scratch_shapes=[pltpu.VMEM((864, 64), F32), pltpu.VMEM((64, 128), F32)],
        compiler_params=limit,
        cost_estimate=pl.CostEstimate(flops=2 * 10**10, bytes_accessed=2 * 10**6, transcendentals=10**6),
    )(to_next, to_near, following, near, *weights)
    share = 64 // slabs
    send, far_next = lax.optimization_barrier((send.reshape(slabs, share, LANES), far_next))
    parts = lax.all_to_all(send, "space", 0, 0, tiled=True)
    _, to_far_near = lax.optimization_barrier((send, to_far_near))
    far_near = swap(to_far_near, [(i, i + 2) for i in fours])
    features, pooled_grad = pl.pallas_call(
        outer_body,
        out_shape=(
            jax.ShapeDtypeStruct((1, 64, 2, cells), BF16),
            jax.ShapeDtypeStruct((1, 32, 2, cells), BF16),
        ),
        compiler_params=limit,
        cost_estimate=pl.CostEstimate(flops=2 * 10**9, bytes_accessed=10**6, transcendentals=10**5),
    )(far_next, far_near, following, near, weights[1], feat, *inner)
    parts, features, pooled_grad = lax.optimization_barrier((parts, features, pooled_grad))
    total = jnp.sum(parts.astype(F32), axis=0)

    def other_core(block, step):
        return lax.ppermute(block, "dp", [(i, i ^ step) for i in range(copies)])

    step = 1
    while 2 * step < copies:
        total = total + other_core(total, step)
        step *= 2
    other = other_core(total, step)
    grad_one, grad_two = pl.pallas_call(
        finish_body,
        out_shape=(jax.ShapeDtypeStruct((share * 54,), F32), jax.ShapeDtypeStruct((share * 864,), F32)),
        compiler_params=limit,
    )(total, other)
    return (features, pooled_grad, grad_one, grad_two)


def solution(mesh):
    in_specs = (P("dp", None, "space", None, None), P(), P(), P("dp", None, "space", None))
    out_specs = (P("dp", None, "space", None), P("dp", None, "space", None), P("space"), P("space"))
    return jax.shard_map(
        on_device, mesh=mesh, in_specs=in_specs, out_specs=out_specs, check_vma=False
    )
```

```python
import functools
import math

import jax
import jax.numpy as jnp
import numpy as np
from jax import lax
from jax.experimental import pallas as pl
from jax.experimental.pallas import tpu as pltpu
from jax.sharding import PartitionSpec as P

F32 = jnp.float32
BF16 = jnp.bfloat16
SHIFTS = [(dy, dx) for dy in (-1, 0, 1) for dx in (-1, 0, 1)]
NN = (((1,), (0,)), ((), ()))
NT = (((1,), (1,)), ((), ()))
LANES = 1024
HALF = 512
ONE_AT = 896


def dot(a, b, dims=NN):
    return lax.dot_general(a, b, dims, preferred_element_type=F32)


def inside(cells, width):
    lane = lax.broadcasted_iota(jnp.int32, (1, cells), 1)
    col, row = lane & (width - 1), lax.shift_right_logical(lane, width.bit_length() - 1)

    def factor(pos, step):
        if step == 0:
            return None
        return jnp.where(pos < width - 1 if step > 0 else pos > 0, 1.0, 0.0)

    return [(factor(col, d), factor(row, d)) for d in (-1, 0, 1)]


def moved_by(field, move, factor):
    return field if move == 0 else pltpu.roll(field, (-move) % field.shape[1], 1) * factor


def all_shifts(field, width):
    factors = inside(field.shape[1], width)
    across = [moved_by(field, dx, factors[dx + 1][0]) for dx in (-1, 0, 1)]
    return [moved_by(across[dx + 1], dy * width, factors[dy + 1][1]) for dy, dx in SHIFTS]


def pool_pattern():
    cell = lax.broadcasted_iota(jnp.int32, (512, 128), 0)
    block = lax.broadcasted_iota(jnp.int32, (512, 128), 1)
    at = 16 * lax.shift_right_logical(cell, 6) + lax.shift_right_logical(cell & 31, 1)
    return jnp.where(at == block, 0.125, 0.0).astype(BF16)


def silu_parts(v):
    s = 0.5 + 0.5 * jnp.tanh(0.5 * v)
    return v * s, s


def band_maps():
    to_kernel = np.zeros((4, 256, 108), np.float32)
    to_flat = np.zeros((4, 256, 128), np.float32)
    for p in range(4):
        for s in range(9):
            for dz in range(3):
                q = p + dz - 1
                for ci in range(4):
                    if 0 <= q <= 3:
                        row = 16 * s + 4 * q + ci
                    else:
                        row = 144 + 8 * s + (0 if q < 0 else 4) + ci
                    tap = 9 * dz + s
                    to_kernel[p, row, 4 * tap + ci] = 1
                    to_flat[p, row, 64 * (ci // 2) + 27 * (ci % 2) + tap] = 1
    return to_kernel, to_flat.reshape(1024, 128)


def prepare_body(
    vol_hbm, cot_hbm, *refs,
):
    weights, (next_ref, near_ref, far_next_ref, far_near_ref) = refs[:4], refs[4:8]
    kept, (vol_ref, cot_ref, cells_ref, sems) = refs[8:12], refs[12:]
    me = lax.axis_index("space")
    odd, upper = me % 2 == 1, (me // 2) % 2 == 1
    vol_copy = pltpu.make_async_copy(vol_hbm, vol_ref, sems.at[0])
    cot_copy = pltpu.make_async_copy(cot_hbm, cot_ref, sems.at[1])
    vol_copy.start()
    cot_copy.start()
    copies = [
        pltpu.make_async_copy(src, dst, sems.at[2 + i])
        for i, (src, dst) in enumerate(zip(weights, kept))
    ]
    for copy in copies:
        copy.start()
    vol_copy.wait()
    cin, planes, width = vol_ref.shape[1:4]
    for plane in range(planes):
        for ch in range(cin):
            at = (plane * cin + ch) * width
            cells_ref[at : at + width] = vol_ref[0, ch, plane].astype(F32)
    count = planes * cin
    blocks = []
    for b in range(4):
        lines = [cells_ref[pl.ds(8 * b + y, count, stride=width), :] for y in range(8)]
        rows = jnp.concatenate(lines, axis=1)
        near_ref[count * b : count * b + count] = rows.astype(BF16)
        next_ref[count * b : count * b + count] = rows.astype(BF16)
        blocks.append(rows)
    halves = [jnp.concatenate(blocks[2 * m : 2 * m + 2], axis=1) for m in range(2)]
    top = lax.broadcasted_iota(jnp.int32, (8, HALF), 0) < 4
    first = jnp.where(top, halves[0][0:8], pltpu.roll(halves[1][0:8], 4, 0))
    last = jnp.where(top, pltpu.roll(halves[0][8:16], 4, 0), halves[1][8:16])
    far_near_ref[...] = jnp.where(upper, first, last).astype(BF16)
    far_next_ref[...] = jnp.where(upper, last, first).astype(BF16)
    cot_copy.wait()
    cot = cot_ref[0].astype(F32)
    cots = (cot[:, 0, :], cot[:, 1, :])
    near_ref[64:128] = jnp.where(odd, cots[0], cots[1]).astype(BF16)
    next_ref[64:128] = jnp.where(odd, cots[1], cots[0]).astype(BF16)
    for copy in copies:
        copy.wait()


def finish_body(mine_ref, other_ref, one_ref, two_ref):
    total = mine_ref[...] + other_ref[...]
    share = total.shape[0] // 2
    total = jnp.concatenate([total[0:share], total[share:]], axis=1)
    two_ref[...] = jnp.concatenate([total[r, 0:864] for r in range(share)])
    one = total[:, ONE_AT : ONE_AT + 54] + total[:, ONE_AT + 64 : ONE_AT + 118]
    one_ref[...] = jnp.concatenate([one[r] for r in range(share)])


def unfold(block, rows):
    return jnp.concatenate([block[rows * b : rows * b + rows] for b in range(4)], axis=1)


def pool_sums(sums, pattern):
    rows = sums.shape[0]
    high = sums.astype(BF16)
    low = (sums - high.astype(F32)).astype(BF16)
    halves = [part[:, 512 * m : 512 * m + 512] for part in (high, low) for m in range(2)]
    out = dot(jnp.concatenate(halves, axis=0), pattern)
    out = out[0 : 2 * rows] + out[2 * rows : 4 * rows]
    return jnp.concatenate([out[0:rows], out[rows : 2 * rows]], axis=1)


def spread_cells(field, pattern):
    rows = field.shape[0]
    high = field.astype(BF16)
    low = (field - high.astype(F32)).astype(BF16)
    halves = [part[:, 128 * m : 128 * m + 128] for part in (high, low) for m in range(2)]
    out = dot(jnp.concatenate(halves, axis=0), pattern, NT)
    out = out[0 : 2 * rows] + out[2 * rows : 4 * rows]
    return jnp.concatenate([out[0:rows], out[rows : 2 * rows]], axis=1)


def spread_taps(taps, half):
    factors = inside(half * half, half)
    total = None
    for dx in (-1, 0, 1):
        column = None
        for dy in (-1, 0, 1):
            s = 3 * (1 - dy) + (1 - dx)
            part = moved_by(taps[32 * s : 32 * s + 32], dy * half, factors[dy + 1][1])
            column = part if column is None else column + part
        column = moved_by(column, dx, factors[dx + 1][0])
        total = column if total is None else total + column
    return total


def inner_body(
    count,
    own_next_ref, own_near_ref, next_ref, near_ref, k1_ref, k2_ref, to_kernel_ref, to_flat_ref,
    feat_ref, send_ref, part_ref, pre_ref, act_ref, pre_two_ref, far_one_ref, far_two_ref,
    term_ref, pair_ref, rows_ref, out_ref,
):
    slabs = lax.axis_size("space")
    me = lax.axis_index("space")
    half = 16

    odd = me % 2 == 1
    own = unfold(own_near_ref[0:64].astype(F32), 16)
    near, following = near_ref[0:64].astype(F32), next_ref[0:64].astype(F32)
    left = unfold(jnp.where(odd, near, following), 16)
    right = unfold(jnp.where(odd, following, near), 16)
    top = lax.broadcasted_iota(jnp.int32, (8, LANES), 0) < 4
    edges = (
        jnp.where(top, 0.0, pltpu.roll(own[0:8], 4, 0)),
        jnp.where(top, pltpu.roll(left[8:16], 4, 0), pltpu.roll(right[0:8], 4, 0)),
        jnp.where(top, pltpu.roll(own[8:16], 4, 0), 0.0),
    )
    moved = all_shifts(jnp.concatenate([left, own, right, *edges], axis=0), 2 * half)
    patches = []
    for g in range(3):
        rows = [m[16 * g : 16 * g + 16] for m in moved] + [m[48 + 8 * g : 56 + 8 * g] for m in moved]
        rows.append(jnp.zeros((40, LANES), F32))
        patches.append(jnp.concatenate(rows, axis=0).astype(BF16))

    k1t = k1_ref[...].astype(F32).reshape(108, 32).T.astype(BF16)
    two_by_dz = jnp.concatenate(
        [k2_ref[288 * dz : 288 * dz + 288].astype(F32).T for dz in range(3)], axis=0
    ).astype(BF16)
    banded = jnp.concatenate(
        [dot(k1t, to_kernel_ref[p], NT).astype(BF16) for p in range(4)], axis=0
    )
    far_one_ref[...] = jnp.concatenate(
        [dot(k1t, to_kernel_ref[p, 144:216], NT).astype(BF16) for p in (0, 3)], axis=0
    )
    far_two_ref[0] = two_by_dz[0:64]
    far_two_ref[1] = two_by_dz[128:192]
    pattern = pool_pattern()

    pre = dot(banded, patches[0])
    pre_ref[0:32] = pre[0:32]
    act, s = silu_parts(pre[32:128])
    act_ref[0:32] = act[0:32]
    slopes = [(s + act * (1.0 - s))[32:96]]
    sums = [act[32:64] + act[64:96]]
    act, s = silu_parts(dot(banded, patches[1]))
    slopes.append(s + act * (1.0 - s))
    sums += [act[0:32] + act[32:64], act[64:96] + act[96:128]]
    pre = dot(banded, patches[2])
    pre_ref[32:64] = pre[96:128]
    act, s = silu_parts(pre[0:96])
    act_ref[32:64] = act[64:96]
    slopes.append((s + act * (1.0 - s))[0:64])
    sums += [act[0:32] + act[32:64]]
    pooled = pool_sums(jnp.concatenate(sums, axis=0), pattern)
    plane = lax.shift_right_logical(lax.broadcasted_iota(jnp.int32, pooled.shape, 0), 5)
    real = ((plane > 0) | (me > 0)) & ((plane < 3) | (me < slabs - 1))
    pooled = jnp.where(real, pooled, 0.0).astype(BF16).astype(F32)

    moved = [m.astype(BF16) for m in all_shifts(pooled, half)]
    planes = [jnp.concatenate([m[32 * q : 32 * q + 32] for m in moved], axis=0) for q in range(4)]
    pre_two = [None] * 4
    for q, columns in enumerate(planes):
        by_dz = dot(two_by_dz, columns)
        for dz in range(3):
            p = q + 1 - dz
            if 0 <= p < 4:
                part = by_dz[64 * dz : 64 * dz + 64]
                pre_two[p] = part if pre_two[p] is None else pre_two[p] + part
    pre_two_ref[0], pre_two_ref[1] = pre_two[0], pre_two[3]

    own_cots = own_near_ref[64:128].astype(F32), own_next_ref[64:128].astype(F32)
    cots = jnp.where(odd, *own_cots), jnp.where(odd, *own_cots[::-1])
    deltas = []
    for p in range(2):
        act, s = silu_parts(pre_two[p + 1])
        feat_ref[p] = act.astype(BF16)
        deltas.append((cots[p] * (s + act * (1.0 - s))).astype(BF16))

    share = 64 // slabs

    def place(columns, at):
        for first in range(0, columns.shape[1], 128):
            tile = (at + first) % HALF // 128
            rows_ref[tile] = columns[:, first : first + 128]
            for r in range(share):
                target = pl.ds((at + first) // HALF * share + r, slabs, stride=2 * share)
                out_ref[tile, target, :] = rows_ref[tile, pl.ds(r, slabs, stride=share), :]

    columns = [jnp.concatenate(planes[p : p + 3], axis=0) for p in range(2)]
    term = dot(columns[0], deltas[0], NT) + dot(columns[1], deltas[1], NT)
    term_ref[...] = term * (1.0 / math.sqrt(count // 8))
    rows = jnp.concatenate([term_ref[pl.ds(ch, 27, stride=32), :] for ch in range(32)], axis=0)
    place(rows[0:HALF].T, 0)
    rows = jnp.concatenate([rows[HALF:864], jnp.zeros((ONE_AT - 864, 64), F32)], axis=0)
    place(rows.T, HALF)

    grads = []
    for p in range(-1, 3):
        sources = [q for q in range(2) if abs(q - p) < 2]
        taps = [k2_ref[288 * (1 + p - q) : 288 * (1 + p - q) + 288] for q in sources]
        given = jnp.concatenate([deltas[q] for q in sources], axis=0)
        grads.append(spread_taps(dot(jnp.concatenate(taps, axis=1), given), half))
    part_ref[0], part_ref[1] = grads[1], grads[2]

    grads = jnp.where(real, jnp.concatenate(grads, axis=0), 0.0)
    spread = spread_cells(grads, pattern)
    spread = [spread[32 * q : 32 * q + 32] for q in range(4)]
    wide = []
    for g, under in enumerate(((0,), (1, 2), (3,))):
        field = jnp.concatenate([spread[q] for q in under for _ in range(2)], axis=0)
        wide.append(dot((field * slopes[g]).astype(BF16), patches[g], NT))
    wide = wide[1] + jnp.concatenate([wide[2], wide[0]], axis=0)
    wide = jnp.concatenate([wide[32 * p : 32 * p + 32] for p in range(4)], axis=1)
    high = wide.astype(BF16)
    low = (wide - high.astype(F32)).astype(BF16)
    term_one = dot(jnp.concatenate([high, low], axis=0), to_flat_ref[...])
    term_one = (term_one[0:32] + term_one[32:64]) * (1.0 / math.sqrt(count))
    for h, half_row in enumerate((term_one, pltpu.roll(term_one, 64, 1))):
        pair_ref[pl.ds(h, 32, stride=2), :] = half_row
    rows = pair_ref[...]
    rounded = rows.astype(BF16).astype(F32)
    lane = lax.broadcasted_iota(jnp.int32, rows.shape, 1)
    pair = jnp.where(lane < 64, rounded, pltpu.roll(rows - rounded, 64, 1))
    place(pair, ONE_AT)
    for tile in range(4):
        send_ref[:, 128 * tile : 128 * tile + 128] = out_ref[tile].astype(BF16)


def outer_body(
    far_next_ref, far_near_ref, next_ref, near_ref, k2_ref,
    feat_ref, part_ref, pre_ref, act_ref, pre_two_ref, far_one_ref, far_two_ref,
    feat_out, pgrad_out,
):
    slabs = lax.axis_size("space")
    me = lax.axis_index("space")
    half = 16
    odd, upper = me % 2 == 1, (me // 2) % 2 == 1
    pattern = pool_pattern()
    far_near, far_next = far_near_ref[...].astype(F32), far_next_ref[...].astype(F32)
    far_left, far_right = jnp.where(upper, far_near, far_next), jnp.where(upper, far_next, far_near)
    top = lax.broadcasted_iota(jnp.int32, (8, LANES), 0) < 4
    edge = jnp.where(
        top,
        jnp.concatenate([far_left, pltpu.roll(far_left, 4, 0)], axis=1),
        jnp.concatenate([pltpu.roll(far_right, 4, 0), far_right], axis=1),
    )
    patches = jnp.concatenate(all_shifts(edge, 2 * half), axis=0).astype(BF16)
    act, _ = silu_parts(pre_ref[...] + dot(far_one_ref[...], patches))
    pooled = pool_sums(act_ref[...] + act, pattern)
    plane = lax.shift_right_logical(lax.broadcasted_iota(jnp.int32, pooled.shape, 0), 5)
    real = ((plane > 0) | (me > 0)) & ((plane < 1) | (me < slabs - 1))
    pooled = jnp.where(real, pooled, 0.0).astype(BF16).astype(F32)
    moved = [m.astype(BF16) for m in all_shifts(pooled, half)]

    near, following = near_ref[64:128].astype(F32), next_ref[64:128].astype(F32)
    cots = jnp.where(odd, near, following), jnp.where(odd, following, near)
    for p in range(2):
        columns = jnp.concatenate([m[32 * p : 32 * p + 32] for m in moved], axis=0)
        pre = pre_two_ref[p] + dot(far_two_ref[p], columns)
        act, s = silu_parts(pre)
        delta = (cots[p] * (s + act * (1.0 - s))).astype(BF16)
        taps = dot(k2_ref[576 * (1 - p) : 576 * (1 - p) + 288], delta)
        pgrad_out[0, :, p, :] = (part_ref[p] + spread_taps(taps, half)).astype(BF16)
        feat_out[0, :, p, :] = feat_ref[p]


def on_device(volumes, kernel_one, kernel_two, cotangent):
    _, cin, planes, width, _ = volumes.shape
    half = width // 2
    slabs = lax.axis_size("space")
    copies = lax.axis_size("dp")
    count = copies * planes * slabs * width * width

    to_kernel, to_flat = band_maps()
    weights = (
        jnp.transpose(kernel_one, (2, 3, 4, 1, 0)).reshape(27, 4, 32),
        jnp.transpose(kernel_two, (2, 3, 4, 1, 0)).reshape(864, 64),
        jnp.asarray(to_kernel, BF16),
        jnp.asarray(to_flat, BF16),
    )

    def in_hbm(*arrays):
        return [pltpu.with_memory_space_constraint(x, pltpu.HBM) for x in arrays]

    inputs = in_hbm(volumes, cotangent, *weights)
    hbm = pl.BlockSpec(memory_space=pltpu.HBM)
    limit = pltpu.CompilerParams(vmem_limit_bytes=48 * 1024 * 1024)
    whole = jax.ShapeDtypeStruct((128, width * width // 4), BF16)
    part = jax.ShapeDtypeStruct((2 * cin, width * width // 2), BF16)
    to_next, to_near, to_far_next, to_far_near, *weights = pl.pallas_call(
        prepare_body,
        out_shape=(
            whole, whole, part, part, *(jax.ShapeDtypeStruct(w.shape, BF16) for w in weights)
        ),
        in_specs=[hbm] * len(inputs),
        scratch_shapes=[
            pltpu.VMEM(volumes.shape, BF16),
            pltpu.VMEM(cotangent.shape, BF16),
            pltpu.VMEM((planes * cin * width, width), F32),
            pltpu.SemaphoreType.DMA((len(inputs),)),
        ],
        compiler_params=limit,
    )(*inputs)

    def swap(block, pairs):
        pairs = [p for p in pairs if max(p) < slabs]
        return lax.ppermute(block, "space", pairs + [(t, f) for f, t in pairs])

    evens = range(0, slabs, 2)
    fours = [i + j for i in range(0, slabs, 4) for j in range(2)]
    following = swap(to_next, [(i + 1, i + 2) for i in evens])
    near = swap(to_near, [(i, i + 1) for i in evens])
    far_next = swap(to_far_next, [(i + 2, i + 4) for i in fours])

    cells = half * half
    shapes = {
        "features": ((2, 64, cells), BF16),
        "send": ((128, HALF), BF16),
        "part": ((2, 32, cells), F32),
        "pre": ((64, LANES), F32),
        "act": ((64, LANES), F32),
        "pre_two": ((2, 64, cells), F32),
        "far_one": ((64, 72), BF16),
        "far_two": ((2, 64, 288), BF16),
    }
    feat, send, *inner = pl.pallas_call(
        functools.partial(inner_body, count),
        out_shape=tuple(jax.ShapeDtypeStruct(*x) for x in shapes.values()),
        scratch_shapes=[
            pltpu.VMEM(shape, F32) for shape in ((864, 64), (64, 128), (4, 64, 128), (4, 128, 128))
        ],
        compiler_params=limit,
        cost_estimate=pl.CostEstimate(flops=2 * 10**10, bytes_accessed=2 * 10**6, transcendentals=10**6),
    )(to_next, to_near, following, near, *weights)
    share = 64 // slabs
    send, far_next = lax.optimization_barrier((send.reshape(slabs, 2 * share, HALF), far_next))
    parts = lax.all_to_all(send, "space", 0, 0, tiled=True)
    _, to_far_near = lax.optimization_barrier((send, to_far_near))
    far_near = swap(to_far_near, [(i, i + 2) for i in fours])
    features, pooled_grad = pl.pallas_call(
        outer_body,
        out_shape=(
            jax.ShapeDtypeStruct((1, 64, 2, cells), BF16),
            jax.ShapeDtypeStruct((1, 32, 2, cells), BF16),
        ),
        compiler_params=limit,
        cost_estimate=pl.CostEstimate(flops=2 * 10**9, bytes_accessed=10**6, transcendentals=10**5),
    )(far_next, far_near, following, near, weights[1], feat, *inner)
    parts, features, pooled_grad = lax.optimization_barrier((parts, features, pooled_grad))
    total = jnp.sum(parts.astype(F32), axis=0)

    def other_core(block, step):
        return lax.ppermute(block, "dp", [(i, i ^ step) for i in range(copies)])

    step = 1
    while 2 * step < copies:
        total = total + other_core(total, step)
        step *= 2
    other = other_core(total, step)
    grad_one, grad_two = pl.pallas_call(
        finish_body,
        out_shape=(jax.ShapeDtypeStruct((share * 54,), F32), jax.ShapeDtypeStruct((share * 864,), F32)),
        compiler_params=limit,
    )(total, other)
    return (features, pooled_grad, grad_one, grad_two)


def solution(mesh):
    in_specs = (P("dp", None, "space", None, None), P(), P(), P("dp", None, "space", None))
    out_specs = (P("dp", None, "space", None), P("dp", None, "space", None), P("space"), P("space"))
    return jax.shard_map(
        on_device, mesh=mesh, in_specs=in_specs, out_specs=out_specs, check_vma=False
    )
```

```python
import functools
import math

import jax
import jax.numpy as jnp
import numpy as np
from jax import lax
from jax.experimental import pallas as pl
from jax.experimental.pallas import tpu as pltpu
from jax.sharding import PartitionSpec as P

F32 = jnp.float32
BF16 = jnp.bfloat16
SHIFTS = [(dy, dx) for dy in (-1, 0, 1) for dx in (-1, 0, 1)]
NN = (((1,), (0,)), ((), ()))
NT = (((1,), (1,)), ((), ()))
LANES = 1024
HALF = 512
ONE_AT = 896


def dot(a, b, dims=NN):
    return lax.dot_general(a, b, dims, preferred_element_type=F32)


def inside(cells, width):
    lane = lax.broadcasted_iota(jnp.int32, (1, cells), 1)
    col, row = lane & (width - 1), lax.shift_right_logical(lane, width.bit_length() - 1)

    def factor(pos, step):
        if step == 0:
            return None
        return jnp.where(pos < width - 1 if step > 0 else pos > 0, 1.0, 0.0)

    return [(factor(col, d), factor(row, d)) for d in (-1, 0, 1)]


def moved_by(field, move, factor):
    return field if move == 0 else pltpu.roll(field, (-move) % field.shape[1], 1) * factor


def all_shifts(field, width):
    factors = inside(field.shape[1], width)
    across = [moved_by(field, dx, factors[dx + 1][0]) for dx in (-1, 0, 1)]
    return [moved_by(across[dx + 1], dy * width, factors[dy + 1][1]) for dy, dx in SHIFTS]


def pool_pattern():
    cell = lax.broadcasted_iota(jnp.int32, (512, 128), 0)
    block = lax.broadcasted_iota(jnp.int32, (512, 128), 1)
    at = 16 * lax.shift_right_logical(cell, 6) + lax.shift_right_logical(cell & 31, 1)
    return jnp.where(at == block, 0.125, 0.0).astype(BF16)


def silu_parts(v):
    s = 0.5 + 0.5 * jnp.tanh(0.5 * v)
    return v * s, s


def band_maps():
    to_kernel = np.zeros((4, 256, 108), np.float32)
    to_flat = np.zeros((4, 256, 128), np.float32)
    for p in range(4):
        for s in range(9):
            for dz in range(3):
                q = p + dz - 1
                for ci in range(4):
                    if 0 <= q <= 3:
                        row = 16 * s + 4 * q + ci
                    else:
                        row = 144 + 8 * s + (0 if q < 0 else 4) + ci
                    tap = 9 * dz + s
                    to_kernel[p, row, 4 * tap + ci] = 1
                    to_flat[p, row, 64 * (ci // 2) + 27 * (ci % 2) + tap] = 1
    return to_kernel, to_flat.reshape(1024, 128)


def prepare_body(
    vol_hbm, cot_hbm, *refs,
):
    weights, (next_ref, near_ref, far_next_ref, far_near_ref) = refs[:4], refs[4:8]
    kept, (vol_ref, cot_ref, cells_ref, sems) = refs[8:12], refs[12:]
    me = lax.axis_index("space")
    odd, upper = me % 2 == 1, (me // 2) % 2 == 1
    vol_copy = pltpu.make_async_copy(vol_hbm, vol_ref, sems.at[0])
    cot_copy = pltpu.make_async_copy(cot_hbm, cot_ref, sems.at[1])
    vol_copy.start()
    cot_copy.start()
    copies = [
        pltpu.make_async_copy(src, dst, sems.at[2 + i])
        for i, (src, dst) in enumerate(zip(weights, kept))
    ]
    for copy in copies:
        copy.start()
    vol_copy.wait()
    cin, planes, width = vol_ref.shape[1:4]
    for plane in range(planes):
        for ch in range(cin):
            at = (plane * cin + ch) * width
            cells_ref[at : at + width] = vol_ref[0, ch, plane].astype(F32)
    count = planes * cin
    blocks = []
    for b in range(4):
        lines = [cells_ref[pl.ds(8 * b + y, count, stride=width), :] for y in range(8)]
        rows = jnp.concatenate(lines, axis=1)
        near_ref[count * b : count * b + count] = rows.astype(BF16)
        next_ref[count * b : count * b + count] = rows.astype(BF16)
        blocks.append(rows)
    halves = [jnp.concatenate(blocks[2 * m : 2 * m + 2], axis=1) for m in range(2)]
    top = lax.broadcasted_iota(jnp.int32, (8, HALF), 0) < 4
    first = jnp.where(top, halves[0][0:8], pltpu.roll(halves[1][0:8], 4, 0))
    last = jnp.where(top, pltpu.roll(halves[0][8:16], 4, 0), halves[1][8:16])
    far_near_ref[...] = jnp.where(upper, first, last).astype(BF16)
    far_next_ref[...] = jnp.where(upper, last, first).astype(BF16)
    cot_copy.wait()
    cot = cot_ref[0].astype(F32)
    cots = (cot[:, 0, :], cot[:, 1, :])
    near_ref[64:128] = jnp.where(odd, cots[0], cots[1]).astype(BF16)
    next_ref[64:128] = jnp.where(odd, cots[1], cots[0]).astype(BF16)
    for copy in copies:
        copy.wait()


def sum_body(parts_ref, total_ref):
    total = parts_ref[0].astype(F32)
    for i in range(1, parts_ref.shape[0]):
        total = total + parts_ref[i].astype(F32)
    total_ref[...] = total


def finish_body(mine_ref, other_ref, one_ref, two_ref):
    total = mine_ref[...] + other_ref[...]
    share = total.shape[0] // 2
    total = jnp.concatenate([total[0:share], total[share:]], axis=1)
    two_ref[...] = jnp.concatenate([total[r, 0:864] for r in range(share)])
    one = total[:, ONE_AT : ONE_AT + 54] + total[:, ONE_AT + 64 : ONE_AT + 118]
    one_ref[...] = jnp.concatenate([one[r] for r in range(share)])


def unfold(block, rows):
    return jnp.concatenate([block[rows * b : rows * b + rows] for b in range(4)], axis=1)


def pool_sums(sums, pattern):
    rows = sums.shape[0]
    high = sums.astype(BF16)
    low = (sums - high.astype(F32)).astype(BF16)
    halves = [part[:, 512 * m : 512 * m + 512] for part in (high, low) for m in range(2)]
    out = dot(jnp.concatenate(halves, axis=0), pattern)
    out = out[0 : 2 * rows] + out[2 * rows : 4 * rows]
    return jnp.concatenate([out[0:rows], out[rows : 2 * rows]], axis=1)


def spread_cells(field, pattern):
    rows = field.shape[0]
    high = field.astype(BF16)
    low = (field - high.astype(F32)).astype(BF16)
    halves = [part[:, 128 * m : 128 * m + 128] for part in (high, low) for m in range(2)]
    out = dot(jnp.concatenate(halves, axis=0), pattern, NT)
    out = out[0 : 2 * rows] + out[2 * rows : 4 * rows]
    return jnp.concatenate([out[0:rows], out[rows : 2 * rows]], axis=1)


def spread_taps(taps, half):
    factors = inside(half * half, half)
    total = None
    for dx in (-1, 0, 1):
        column = None
        for dy in (-1, 0, 1):
            s = 3 * (1 - dy) + (1 - dx)
            part = moved_by(taps[32 * s : 32 * s + 32], dy * half, factors[dy + 1][1])
            column = part if column is None else column + part
        column = moved_by(column, dx, factors[dx + 1][0])
        total = column if total is None else total + column
    return total


def inner_body(
    count,
    own_next_ref, own_near_ref, next_ref, near_ref, k1_ref, k2_ref, to_kernel_ref, to_flat_ref,
    feat_ref, send_ref, part_ref, pre_ref, act_ref, pre_two_ref, far_one_ref, far_two_ref,
    term_ref, pair_ref, rows_ref, out_ref,
):
    slabs = lax.axis_size("space")
    me = lax.axis_index("space")
    half = 16

    odd = me % 2 == 1
    own = unfold(own_near_ref[0:64].astype(F32), 16)
    near, following = near_ref[0:64].astype(F32), next_ref[0:64].astype(F32)
    left = unfold(jnp.where(odd, near, following), 16)
    right = unfold(jnp.where(odd, following, near), 16)
    top = lax.broadcasted_iota(jnp.int32, (8, LANES), 0) < 4
    edges = (
        jnp.where(top, 0.0, pltpu.roll(own[0:8], 4, 0)),
        jnp.where(top, pltpu.roll(left[8:16], 4, 0), pltpu.roll(right[0:8], 4, 0)),
        jnp.where(top, pltpu.roll(own[8:16], 4, 0), 0.0),
    )
    moved = all_shifts(jnp.concatenate([left, own, right, *edges], axis=0), 2 * half)
    patches = []
    for g in range(3):
        rows = [m[16 * g : 16 * g + 16] for m in moved] + [m[48 + 8 * g : 56 + 8 * g] for m in moved]
        rows.append(jnp.zeros((40, LANES), F32))
        patches.append(jnp.concatenate(rows, axis=0).astype(BF16))

    k1t = k1_ref[...].astype(F32).reshape(108, 32).T.astype(BF16)
    two_by_dz = jnp.concatenate(
        [k2_ref[288 * dz : 288 * dz + 288].astype(F32).T for dz in range(3)], axis=0
    ).astype(BF16)
    banded = jnp.concatenate(
        [dot(k1t, to_kernel_ref[p], NT).astype(BF16) for p in range(4)], axis=0
    )
    far_one_ref[...] = jnp.concatenate(
        [dot(k1t, to_kernel_ref[p, 144:216], NT).astype(BF16) for p in (0, 3)], axis=0
    )
    far_two_ref[0] = two_by_dz[0:64]
    far_two_ref[1] = two_by_dz[128:192]
    pattern = pool_pattern()

    pre = dot(banded, patches[0])
    pre_ref[0:32] = pre[0:32]
    act, s = silu_parts(pre[32:128])
    act_ref[0:32] = act[0:32]
    slopes = [(s + act * (1.0 - s))[32:96]]
    sums = [act[32:64] + act[64:96]]
    act, s = silu_parts(dot(banded, patches[1]))
    slopes.append(s + act * (1.0 - s))
    sums += [act[0:32] + act[32:64], act[64:96] + act[96:128]]
    pre = dot(banded, patches[2])
    pre_ref[32:64] = pre[96:128]
    act, s = silu_parts(pre[0:96])
    act_ref[32:64] = act[64:96]
    slopes.append((s + act * (1.0 - s))[0:64])
    sums += [act[0:32] + act[32:64]]
    pooled = pool_sums(jnp.concatenate(sums, axis=0), pattern)
    plane = lax.shift_right_logical(lax.broadcasted_iota(jnp.int32, pooled.shape, 0), 5)
    real = ((plane > 0) | (me > 0)) & ((plane < 3) | (me < slabs - 1))
    pooled = jnp.where(real, pooled, 0.0).astype(BF16).astype(F32)

    moved = [m.astype(BF16) for m in all_shifts(pooled, half)]
    planes = [jnp.concatenate([m[32 * q : 32 * q + 32] for m in moved], axis=0) for q in range(4)]
    pre_two = [None] * 4
    for q, columns in enumerate(planes):
        by_dz = dot(two_by_dz, columns)
        for dz in range(3):
            p = q + 1 - dz
            if 0 <= p < 4:
                part = by_dz[64 * dz : 64 * dz + 64]
                pre_two[p] = part if pre_two[p] is None else pre_two[p] + part
    pre_two_ref[0], pre_two_ref[1] = pre_two[0], pre_two[3]

    own_cots = own_near_ref[64:128].astype(F32), own_next_ref[64:128].astype(F32)
    cots = jnp.where(odd, *own_cots), jnp.where(odd, *own_cots[::-1])
    deltas = []
    for p in range(2):
        act, s = silu_parts(pre_two[p + 1])
        feat_ref[p] = act.astype(BF16)
        deltas.append((cots[p] * (s + act * (1.0 - s))).astype(BF16))

    share = 64 // slabs

    def place(columns, at):
        for first in range(0, columns.shape[1], 128):
            tile = (at + first) % HALF // 128
            rows_ref[tile] = columns[:, first : first + 128]
            for r in range(share):
                target = pl.ds((at + first) // HALF * share + r, slabs, stride=2 * share)
                out_ref[tile, target, :] = rows_ref[tile, pl.ds(r, slabs, stride=share), :]

    columns = [jnp.concatenate(planes[p : p + 3], axis=0) for p in range(2)]
    term = dot(columns[0], deltas[0], NT) + dot(columns[1], deltas[1], NT)
    term_ref[...] = term * (1.0 / math.sqrt(count // 8))
    rows = jnp.concatenate([term_ref[pl.ds(ch, 27, stride=32), :] for ch in range(32)], axis=0)
    place(rows[0:HALF].T, 0)
    rows = jnp.concatenate([rows[HALF:864], jnp.zeros((ONE_AT - 864, 64), F32)], axis=0)
    place(rows.T, HALF)

    grads = []
    for p in range(-1, 3):
        sources = [q for q in range(2) if abs(q - p) < 2]
        taps = [k2_ref[288 * (1 + p - q) : 288 * (1 + p - q) + 288] for q in sources]
        given = jnp.concatenate([deltas[q] for q in sources], axis=0)
        grads.append(spread_taps(dot(jnp.concatenate(taps, axis=1), given), half))
    part_ref[0], part_ref[1] = grads[1], grads[2]

    grads = jnp.where(real, jnp.concatenate(grads, axis=0), 0.0)
    spread = spread_cells(grads, pattern)
    spread = [spread[32 * q : 32 * q + 32] for q in range(4)]
    wide = []
    for g, under in enumerate(((0,), (1, 2), (3,))):
        field = jnp.concatenate([spread[q] for q in under for _ in range(2)], axis=0)
        wide.append(dot((field * slopes[g]).astype(BF16), patches[g], NT))
    wide = wide[1] + jnp.concatenate([wide[2], wide[0]], axis=0)
    wide = jnp.concatenate([wide[32 * p : 32 * p + 32] for p in range(4)], axis=1)
    high = wide.astype(BF16)
    low = (wide - high.astype(F32)).astype(BF16)
    term_one = dot(jnp.concatenate([high, low], axis=0), to_flat_ref[...])
    term_one = (term_one[0:32] + term_one[32:64]) * (1.0 / math.sqrt(count))
    for h, half_row in enumerate((term_one, pltpu.roll(term_one, 64, 1))):
        pair_ref[pl.ds(h, 32, stride=2), :] = half_row
    rows = pair_ref[...]
    rounded = rows.astype(BF16).astype(F32)
    lane = lax.broadcasted_iota(jnp.int32, rows.shape, 1)
    pair = jnp.where(lane < 64, rounded, pltpu.roll(rows - rounded, 64, 1))
    place(pair, ONE_AT)
    for tile in range(4):
        send_ref[:, 128 * tile : 128 * tile + 128] = out_ref[tile].astype(BF16)


def outer_body(
    far_next_ref, far_near_ref, next_ref, near_ref, k2_ref,
    feat_ref, part_ref, pre_ref, act_ref, pre_two_ref, far_one_ref, far_two_ref,
    feat_out, pgrad_out,
):
    slabs = lax.axis_size("space")
    me = lax.axis_index("space")
    half = 16
    odd, upper = me % 2 == 1, (me // 2) % 2 == 1
    pattern = pool_pattern()
    far_near, far_next = far_near_ref[...].astype(F32), far_next_ref[...].astype(F32)
    far_left, far_right = jnp.where(upper, far_near, far_next), jnp.where(upper, far_next, far_near)
    top = lax.broadcasted_iota(jnp.int32, (8, LANES), 0) < 4
    edge = jnp.where(
        top,
        jnp.concatenate([far_left, pltpu.roll(far_left, 4, 0)], axis=1),
        jnp.concatenate([pltpu.roll(far_right, 4, 0), far_right], axis=1),
    )
    patches = jnp.concatenate(all_shifts(edge, 2 * half), axis=0).astype(BF16)
    act, _ = silu_parts(pre_ref[...] + dot(far_one_ref[...], patches))
    pooled = pool_sums(act_ref[...] + act, pattern)
    plane = lax.shift_right_logical(lax.broadcasted_iota(jnp.int32, pooled.shape, 0), 5)
    real = ((plane > 0) | (me > 0)) & ((plane < 1) | (me < slabs - 1))
    pooled = jnp.where(real, pooled, 0.0).astype(BF16).astype(F32)
    moved = [m.astype(BF16) for m in all_shifts(pooled, half)]

    near, following = near_ref[64:128].astype(F32), next_ref[64:128].astype(F32)
    cots = jnp.where(odd, near, following), jnp.where(odd, following, near)
    for p in range(2):
        columns = jnp.concatenate([m[32 * p : 32 * p + 32] for m in moved], axis=0)
        pre = pre_two_ref[p] + dot(far_two_ref[p], columns)
        act, s = silu_parts(pre)
        delta = (cots[p] * (s + act * (1.0 - s))).astype(BF16)
        taps = dot(k2_ref[576 * (1 - p) : 576 * (1 - p) + 288], delta)
        pgrad_out[0, :, p, :] = (part_ref[p] + spread_taps(taps, half)).astype(BF16)
        feat_out[0, :, p, :] = feat_ref[p]


def on_device(volumes, kernel_one, kernel_two, cotangent):
    _, cin, planes, width, _ = volumes.shape
    half = width // 2
    slabs = lax.axis_size("space")
    copies = lax.axis_size("dp")
    count = copies * planes * slabs * width * width

    to_kernel, to_flat = band_maps()
    weights = (
        jnp.transpose(kernel_one, (2, 3, 4, 1, 0)).reshape(27, 4, 32),
        jnp.transpose(kernel_two, (2, 3, 4, 1, 0)).reshape(864, 64),
        jnp.asarray(to_kernel, BF16),
        jnp.asarray(to_flat, BF16),
    )

    def in_hbm(*arrays):
        return [pltpu.with_memory_space_constraint(x, pltpu.HBM) for x in arrays]

    inputs = in_hbm(volumes, cotangent, *weights)
    hbm = pl.BlockSpec(memory_space=pltpu.HBM)
    limit = pltpu.CompilerParams(vmem_limit_bytes=48 * 1024 * 1024)
    whole = jax.ShapeDtypeStruct((128, width * width // 4), BF16)
    part = jax.ShapeDtypeStruct((2 * cin, width * width // 2), BF16)
    to_next, to_near, to_far_next, to_far_near, *weights = pl.pallas_call(
        prepare_body,
        out_shape=(
            whole, whole, part, part, *(jax.ShapeDtypeStruct(w.shape, BF16) for w in weights)
        ),
        in_specs=[hbm] * len(inputs),
        scratch_shapes=[
            pltpu.VMEM(volumes.shape, BF16),
            pltpu.VMEM(cotangent.shape, BF16),
            pltpu.VMEM((planes * cin * width, width), F32),
            pltpu.SemaphoreType.DMA((len(inputs),)),
        ],
        compiler_params=limit,
    )(*inputs)

    def swap(block, pairs):
        pairs = [p for p in pairs if max(p) < slabs]
        return lax.ppermute(block, "space", pairs + [(t, f) for f, t in pairs])

    evens = range(0, slabs, 2)
    fours = [i + j for i in range(0, slabs, 4) for j in range(2)]
    following = swap(to_next, [(i + 1, i + 2) for i in evens])
    near = swap(to_near, [(i, i + 1) for i in evens])
    far_next = swap(to_far_next, [(i + 2, i + 4) for i in fours])

    cells = half * half
    shapes = {
        "features": ((2, 64, cells), BF16),
        "send": ((128, HALF), BF16),
        "part": ((2, 32, cells), F32),
        "pre": ((64, LANES), F32),
        "act": ((64, LANES), F32),
        "pre_two": ((2, 64, cells), F32),
        "far_one": ((64, 72), BF16),
        "far_two": ((2, 64, 288), BF16),
    }
    feat, send, *inner = pl.pallas_call(
        functools.partial(inner_body, count),
        out_shape=tuple(jax.ShapeDtypeStruct(*x) for x in shapes.values()),
        scratch_shapes=[
            pltpu.VMEM(shape, F32) for shape in ((864, 64), (64, 128), (4, 64, 128), (4, 128, 128))
        ],
        compiler_params=limit,
        cost_estimate=pl.CostEstimate(flops=2 * 10**10, bytes_accessed=2 * 10**6, transcendentals=10**6),
    )(to_next, to_near, following, near, *weights)
    share = 64 // slabs
    send, far_next = lax.optimization_barrier((send.reshape(slabs, 2 * share, HALF), far_next))
    send = pltpu.with_memory_space_constraint(send, pltpu.VMEM)
    parts = lax.all_to_all(send, "space", 0, 0, tiled=True)
    _, to_far_near = lax.optimization_barrier((send, to_far_near))
    far_near = swap(to_far_near, [(i, i + 2) for i in fours])
    features, pooled_grad = pl.pallas_call(
        outer_body,
        out_shape=(
            jax.ShapeDtypeStruct((1, 64, 2, cells), BF16),
            jax.ShapeDtypeStruct((1, 32, 2, cells), BF16),
        ),
        compiler_params=limit,
        cost_estimate=pl.CostEstimate(flops=2 * 10**9, bytes_accessed=10**6, transcendentals=10**5),
    )(far_next, far_near, following, near, weights[1], feat, *inner)
    parts, features, pooled_grad = lax.optimization_barrier((parts, features, pooled_grad))
    total = pl.pallas_call(
        sum_body,
        out_shape=jax.ShapeDtypeStruct(parts.shape[1:], F32),
        compiler_params=limit,
    )(parts)

    def other_core(block, step):
        return lax.ppermute(block, "dp", [(i, i ^ step) for i in range(copies)])

    step = 1
    while 2 * step < copies:
        total = total + other_core(total, step)
        step *= 2
    other = other_core(total, step)
    grad_one, grad_two = pl.pallas_call(
        finish_body,
        out_shape=(jax.ShapeDtypeStruct((share * 54,), F32), jax.ShapeDtypeStruct((share * 864,), F32)),
        compiler_params=limit,
    )(total, other)
    return (features, pooled_grad, grad_one, grad_two)


def solution(mesh):
    in_specs = (P("dp", None, "space", None, None), P(), P(), P("dp", None, "space", None))
    out_specs = (P("dp", None, "space", None), P("dp", None, "space", None), P("space"), P("space"))
    return jax.shard_map(
        on_device, mesh=mesh, in_specs=in_specs, out_specs=out_specs, check_vma=False
    )
```

```python
import functools
import math

import jax
import jax.numpy as jnp
import numpy as np
from jax import lax
from jax.experimental import pallas as pl
from jax.experimental.pallas import tpu as pltpu
from jax.sharding import PartitionSpec as P

F32 = jnp.float32
BF16 = jnp.bfloat16
SHIFTS = [(dy, dx) for dy in (-1, 0, 1) for dx in (-1, 0, 1)]
NN = (((1,), (0,)), ((), ()))
NT = (((1,), (1,)), ((), ()))
LANES = 1024
HALF = 512
ONE_AT = 896


def dot(a, b, dims=NN):
    return lax.dot_general(a, b, dims, preferred_element_type=F32)


def inside(cells, width):
    lane = lax.broadcasted_iota(jnp.int32, (1, cells), 1)
    col, row = lane & (width - 1), lax.shift_right_logical(lane, width.bit_length() - 1)

    def factor(pos, step):
        if step == 0:
            return None
        return jnp.where(pos < width - 1 if step > 0 else pos > 0, 1.0, 0.0)

    return [(factor(col, d), factor(row, d)) for d in (-1, 0, 1)]


def moved_by(field, move, factor):
    return field if move == 0 else pltpu.roll(field, (-move) % field.shape[1], 1) * factor


def all_shifts(field, width):
    factors = inside(field.shape[1], width)
    across = [moved_by(field, dx, factors[dx + 1][0]) for dx in (-1, 0, 1)]
    return [moved_by(across[dx + 1], dy * width, factors[dy + 1][1]) for dy, dx in SHIFTS]


def pool_pattern():
    cell = lax.broadcasted_iota(jnp.int32, (512, 128), 0)
    block = lax.broadcasted_iota(jnp.int32, (512, 128), 1)
    at = 16 * lax.shift_right_logical(cell, 6) + lax.shift_right_logical(cell & 31, 1)
    return jnp.where(at == block, 0.125, 0.0).astype(BF16)


def silu_parts(v):
    s = 0.5 + 0.5 * jnp.tanh(0.5 * v)
    return v * s, s


def band_maps():
    to_kernel = np.zeros((4, 256, 108), np.float32)
    to_flat = np.zeros((4, 256, 128), np.float32)
    for p in range(4):
        for s in range(9):
            for dz in range(3):
                q = p + dz - 1
                for ci in range(4):
                    if 0 <= q <= 3:
                        row = 16 * s + 4 * q + ci
                    else:
                        row = 144 + 8 * s + (0 if q < 0 else 4) + ci
                    tap = 9 * dz + s
                    to_kernel[p, row, 4 * tap + ci] = 1
                    to_flat[p, row, 64 * (ci // 2) + 27 * (ci % 2) + tap] = 1
    return to_kernel, to_flat.reshape(1024, 128)


def prepare_body(
    vol_hbm, cot_hbm, *refs,
):
    weights, (next_ref, near_ref, far_next_ref, far_near_ref) = refs[:4], refs[4:8]
    kept, (vol_ref, cot_ref, cells_ref, sems) = refs[8:12], refs[12:]
    me = lax.axis_index("space")
    odd, upper = me % 2 == 1, (me // 2) % 2 == 1
    vol_copy = pltpu.make_async_copy(vol_hbm, vol_ref, sems.at[0])
    cot_copy = pltpu.make_async_copy(cot_hbm, cot_ref, sems.at[1])
    vol_copy.start()
    cot_copy.start()
    copies = [
        pltpu.make_async_copy(src, dst, sems.at[2 + i])
        for i, (src, dst) in enumerate(zip(weights, kept))
    ]
    for copy in copies:
        copy.start()
    vol_copy.wait()
    cin, planes, width = vol_ref.shape[1:4]
    for plane in range(planes):
        for ch in range(cin):
            at = (plane * cin + ch) * width
            cells_ref[at : at + width] = vol_ref[0, ch, plane].astype(F32)
    count = planes * cin
    blocks = []
    for b in range(4):
        lines = [cells_ref[pl.ds(8 * b + y, count, stride=width), :] for y in range(8)]
        rows = jnp.concatenate(lines, axis=1)
        near_ref[count * b : count * b + count] = rows.astype(BF16)
        next_ref[count * b : count * b + count] = rows.astype(BF16)
        blocks.append(rows)
    halves = [jnp.concatenate(blocks[2 * m : 2 * m + 2], axis=1) for m in range(2)]
    top = lax.broadcasted_iota(jnp.int32, (8, HALF), 0) < 4
    first = jnp.where(top, halves[0][0:8], pltpu.roll(halves[1][0:8], 4, 0))
    last = jnp.where(top, pltpu.roll(halves[0][8:16], 4, 0), halves[1][8:16])
    far_near_ref[...] = jnp.where(upper, first, last).astype(BF16)
    far_next_ref[...] = jnp.where(upper, last, first).astype(BF16)
    cot_copy.wait()
    cot = cot_ref[0].astype(F32)
    cots = (cot[:, 0, :], cot[:, 1, :])
    near_ref[64:128] = jnp.where(odd, cots[0], cots[1]).astype(BF16)
    next_ref[64:128] = jnp.where(odd, cots[1], cots[0]).astype(BF16)
    for copy in copies:
        copy.wait()


def sum_body(parts_ref, total_ref):
    total = parts_ref[0].astype(F32)
    for i in range(1, parts_ref.shape[0]):
        total = total + parts_ref[i].astype(F32)
    total_ref[...] = total


def finish_body(mine_ref, other_ref, one_ref, two_ref):
    total = mine_ref[...] + other_ref[...]
    share = total.shape[0] // 2
    total = jnp.concatenate([total[0:share], total[share:]], axis=1)
    two_ref[...] = jnp.concatenate([total[r, 0:864] for r in range(share)])
    one = total[:, ONE_AT : ONE_AT + 54] + total[:, ONE_AT + 64 : ONE_AT + 118]
    one_ref[...] = jnp.concatenate([one[r] for r in range(share)])


def unfold(block, rows):
    return jnp.concatenate([block[rows * b : rows * b + rows] for b in range(4)], axis=1)


def pool_sums(sums, pattern):
    rows = sums.shape[0]
    high = sums.astype(BF16)
    low = (sums - high.astype(F32)).astype(BF16)
    halves = [part[:, 512 * m : 512 * m + 512] for part in (high, low) for m in range(2)]
    out = dot(jnp.concatenate(halves, axis=0), pattern)
    out = out[0 : 2 * rows] + out[2 * rows : 4 * rows]
    return jnp.concatenate([out[0:rows], out[rows : 2 * rows]], axis=1)


def spread_cells(field, pattern):
    rows = field.shape[0]
    high = field.astype(BF16)
    low = (field - high.astype(F32)).astype(BF16)
    halves = [part[:, 128 * m : 128 * m + 128] for part in (high, low) for m in range(2)]
    out = dot(jnp.concatenate(halves, axis=0), pattern, NT)
    out = out[0 : 2 * rows] + out[2 * rows : 4 * rows]
    return jnp.concatenate([out[0:rows], out[rows : 2 * rows]], axis=1)


def spread_taps(taps, half):
    factors = inside(half * half, half)
    total = None
    for dx in (-1, 0, 1):
        column = None
        for dy in (-1, 0, 1):
            s = 3 * (1 - dy) + (1 - dx)
            part = moved_by(taps[32 * s : 32 * s + 32], dy * half, factors[dy + 1][1])
            column = part if column is None else column + part
        column = moved_by(column, dx, factors[dx + 1][0])
        total = column if total is None else total + column
    return total


def inner_body(
    count,
    own_next_ref, own_near_ref, next_ref, near_ref, k1_ref, k2_ref, to_kernel_ref, to_flat_ref,
    feat_ref, send_ref, part_ref, pre_ref, act_ref, pre_two_ref, far_one_ref, far_two_ref,
    term_ref, pair_ref, rows_ref, out_ref,
):
    slabs = lax.axis_size("space")
    me = lax.axis_index("space")
    half = 16

    odd = me % 2 == 1
    own = unfold(own_near_ref[0:64].astype(F32), 16)
    near, following = near_ref[0:64].astype(F32), next_ref[0:64].astype(F32)
    left = unfold(jnp.where(odd, near, following), 16)
    right = unfold(jnp.where(odd, following, near), 16)
    top = lax.broadcasted_iota(jnp.int32, (8, LANES), 0) < 4
    edges = (
        jnp.where(top, 0.0, pltpu.roll(own[0:8], 4, 0)),
        jnp.where(top, pltpu.roll(left[8:16], 4, 0), pltpu.roll(right[0:8], 4, 0)),
        jnp.where(top, pltpu.roll(own[8:16], 4, 0), 0.0),
    )
    moved = all_shifts(jnp.concatenate([left, own, right, *edges], axis=0), 2 * half)
    patches = []
    for g in range(3):
        rows = [m[16 * g : 16 * g + 16] for m in moved] + [m[48 + 8 * g : 56 + 8 * g] for m in moved]
        rows.append(jnp.zeros((40, LANES), F32))
        patches.append(jnp.concatenate(rows, axis=0).astype(BF16))

    k1t = k1_ref[...].astype(F32).reshape(108, 32).T.astype(BF16)
    two_by_dz = jnp.concatenate(
        [k2_ref[288 * dz : 288 * dz + 288].astype(F32).T for dz in range(3)], axis=0
    ).astype(BF16)
    banded = jnp.concatenate(
        [dot(k1t, to_kernel_ref[p], NT).astype(BF16) for p in range(4)], axis=0
    )
    far_one_ref[...] = jnp.concatenate(
        [dot(k1t, to_kernel_ref[p, 144:216], NT).astype(BF16) for p in (0, 3)], axis=0
    )
    far_two_ref[0] = two_by_dz[0:64]
    far_two_ref[1] = two_by_dz[128:192]
    pattern = pool_pattern()

    pre = dot(banded, patches[0])
    pre_ref[0:32] = pre[0:32]
    act, s = silu_parts(pre[32:128])
    act_ref[0:32] = act[0:32]
    slopes = [(s + act * (1.0 - s))[32:96]]
    sums = [act[32:64] + act[64:96]]
    act, s = silu_parts(dot(banded, patches[1]))
    slopes.append(s + act * (1.0 - s))
    sums += [act[0:32] + act[32:64], act[64:96] + act[96:128]]
    pre = dot(banded, patches[2])
    pre_ref[32:64] = pre[96:128]
    act, s = silu_parts(pre[0:96])
    act_ref[32:64] = act[64:96]
    slopes.append((s + act * (1.0 - s))[0:64])
    sums += [act[0:32] + act[32:64]]
    pooled = pool_sums(jnp.concatenate(sums, axis=0), pattern)
    plane = lax.shift_right_logical(lax.broadcasted_iota(jnp.int32, pooled.shape, 0), 5)
    real = ((plane > 0) | (me > 0)) & ((plane < 3) | (me < slabs - 1))
    pooled = jnp.where(real, pooled, 0.0).astype(BF16).astype(F32)

    moved = [m.astype(BF16) for m in all_shifts(pooled, half)]
    planes = [jnp.concatenate([m[32 * q : 32 * q + 32] for m in moved], axis=0) for q in range(4)]
    pre_two = [None] * 4
    for q, columns in enumerate(planes):
        by_dz = dot(two_by_dz, columns)
        for dz in range(3):
            p = q + 1 - dz
            if 0 <= p < 4:
                part = by_dz[64 * dz : 64 * dz + 64]
                pre_two[p] = part if pre_two[p] is None else pre_two[p] + part
    pre_two_ref[0], pre_two_ref[1] = pre_two[0], pre_two[3]

    own_cots = own_near_ref[64:128].astype(F32), own_next_ref[64:128].astype(F32)
    cots = jnp.where(odd, *own_cots), jnp.where(odd, *own_cots[::-1])
    deltas = []
    for p in range(2):
        act, s = silu_parts(pre_two[p + 1])
        feat_ref[p] = act.astype(BF16)
        deltas.append((cots[p] * (s + act * (1.0 - s))).astype(BF16))

    share = 64 // slabs

    def place(columns, at):
        for first in range(0, columns.shape[1], 128):
            tile = (at + first) % HALF // 128
            rows_ref[tile] = columns[:, first : first + 128]
            for r in range(share):
                target = pl.ds((at + first) // HALF * share + r, slabs, stride=2 * share)
                out_ref[tile, target, :] = rows_ref[tile, pl.ds(r, slabs, stride=share), :]

    columns = [jnp.concatenate(planes[p : p + 3], axis=0) for p in range(2)]
    term = dot(columns[0], deltas[0], NT) + dot(columns[1], deltas[1], NT)
    term_ref[...] = term * (1.0 / math.sqrt(count // 8))
    rows = jnp.concatenate([term_ref[pl.ds(ch, 27, stride=32), :] for ch in range(32)], axis=0)
    place(rows[0:HALF].T, 0)
    rows = jnp.concatenate([rows[HALF:864], jnp.zeros((ONE_AT - 864, 64), F32)], axis=0)
    place(rows.T, HALF)

    grads = []
    for p in range(-1, 3):
        sources = [q for q in range(2) if abs(q - p) < 2]
        taps = [k2_ref[288 * (1 + p - q) : 288 * (1 + p - q) + 288] for q in sources]
        given = jnp.concatenate([deltas[q] for q in sources], axis=0)
        grads.append(spread_taps(dot(jnp.concatenate(taps, axis=1), given), half))
    part_ref[0], part_ref[1] = grads[1], grads[2]

    grads = jnp.where(real, jnp.concatenate(grads, axis=0), 0.0)
    spread = spread_cells(grads, pattern)
    spread = [spread[32 * q : 32 * q + 32] for q in range(4)]
    wide = []
    for g, under in enumerate(((0,), (1, 2), (3,))):
        field = jnp.concatenate([spread[q] for q in under for _ in range(2)], axis=0)
        wide.append(dot((field * slopes[g]).astype(BF16), patches[g], NT))
    wide = wide[1] + jnp.concatenate([wide[2], wide[0]], axis=0)
    wide = jnp.concatenate([wide[32 * p : 32 * p + 32] for p in range(4)], axis=1)
    high = wide.astype(BF16)
    low = (wide - high.astype(F32)).astype(BF16)
    term_one = dot(jnp.concatenate([high, low], axis=0), to_flat_ref[...])
    term_one = (term_one[0:32] + term_one[32:64]) * (1.0 / math.sqrt(count))
    for h, half_row in enumerate((term_one, pltpu.roll(term_one, 64, 1))):
        pair_ref[pl.ds(h, 32, stride=2), :] = half_row
    rows = pair_ref[...]
    rounded = rows.astype(BF16).astype(F32)
    lane = lax.broadcasted_iota(jnp.int32, rows.shape, 1)
    pair = jnp.where(lane < 64, rounded, pltpu.roll(rows - rounded, 64, 1))
    place(pair, ONE_AT)
    for tile in range(4):
        send_ref[:, 128 * tile : 128 * tile + 128] = out_ref[tile].astype(BF16)


def outer_body(
    far_next_ref, far_near_ref, next_ref, near_ref, k2_ref,
    feat_ref, part_ref, pre_ref, act_ref, pre_two_ref, far_one_ref, far_two_ref,
    feat_out, pgrad_out,
):
    slabs = lax.axis_size("space")
    me = lax.axis_index("space")
    half = 16
    odd, upper = me % 2 == 1, (me // 2) % 2 == 1
    pattern = pool_pattern()
    far_near, far_next = far_near_ref[...].astype(F32), far_next_ref[...].astype(F32)
    far_left, far_right = jnp.where(upper, far_near, far_next), jnp.where(upper, far_next, far_near)
    top = lax.broadcasted_iota(jnp.int32, (8, LANES), 0) < 4
    edge = jnp.where(
        top,
        jnp.concatenate([far_left, pltpu.roll(far_left, 4, 0)], axis=1),
        jnp.concatenate([pltpu.roll(far_right, 4, 0), far_right], axis=1),
    )
    patches = jnp.concatenate(all_shifts(edge, 2 * half), axis=0).astype(BF16)
    act, _ = silu_parts(pre_ref[...] + dot(far_one_ref[...], patches))
    pooled = pool_sums(act_ref[...] + act, pattern)
    plane = lax.shift_right_logical(lax.broadcasted_iota(jnp.int32, pooled.shape, 0), 5)
    real = ((plane > 0) | (me > 0)) & ((plane < 1) | (me < slabs - 1))
    pooled = jnp.where(real, pooled, 0.0).astype(BF16).astype(F32)
    moved = [m.astype(BF16) for m in all_shifts(pooled, half)]

    near, following = near_ref[64:128].astype(F32), next_ref[64:128].astype(F32)
    cots = jnp.where(odd, near, following), jnp.where(odd, following, near)
    for p in range(2):
        columns = jnp.concatenate([m[32 * p : 32 * p + 32] for m in moved], axis=0)
        pre = pre_two_ref[p] + dot(far_two_ref[p], columns)
        act, s = silu_parts(pre)
        delta = (cots[p] * (s + act * (1.0 - s))).astype(BF16)
        taps = dot(k2_ref[576 * (1 - p) : 576 * (1 - p) + 288], delta)
        pgrad_out[0, :, p, :] = (part_ref[p] + spread_taps(taps, half)).astype(BF16)
        feat_out[0, :, p, :] = feat_ref[p]


def on_device(volumes, kernel_one, kernel_two, cotangent):
    _, cin, planes, width, _ = volumes.shape
    half = width // 2
    slabs = lax.axis_size("space")
    copies = lax.axis_size("dp")
    count = copies * planes * slabs * width * width

    to_kernel, to_flat = band_maps()
    weights = (
        jnp.transpose(kernel_one, (2, 3, 4, 1, 0)).reshape(27, 4, 32),
        jnp.transpose(kernel_two, (2, 3, 4, 1, 0)).reshape(864, 64),
        jnp.asarray(to_kernel, BF16),
        jnp.asarray(to_flat, BF16),
    )

    def in_hbm(*arrays):
        return [pltpu.with_memory_space_constraint(x, pltpu.HBM) for x in arrays]

    inputs = in_hbm(volumes, cotangent, *weights)
    hbm = pl.BlockSpec(memory_space=pltpu.HBM)
    limit = pltpu.CompilerParams(vmem_limit_bytes=48 * 1024 * 1024)
    whole = jax.ShapeDtypeStruct((128, width * width // 4), BF16)
    part = jax.ShapeDtypeStruct((2 * cin, width * width // 2), BF16)
    to_next, to_near, to_far_next, to_far_near, *weights = pl.pallas_call(
        prepare_body,
        out_shape=(
            whole, whole, part, part, *(jax.ShapeDtypeStruct(w.shape, BF16) for w in weights)
        ),
        in_specs=[hbm] * len(inputs),
        scratch_shapes=[
            pltpu.VMEM(volumes.shape, BF16),
            pltpu.VMEM(cotangent.shape, BF16),
            pltpu.VMEM((planes * cin * width, width), F32),
            pltpu.SemaphoreType.DMA((len(inputs),)),
        ],
        compiler_params=limit,
    )(*inputs)

    def swap(block, pairs):
        pairs = [p for p in pairs if max(p) < slabs]
        return lax.ppermute(block, "space", pairs + [(t, f) for f, t in pairs])

    evens = range(0, slabs, 2)
    fours = [i + j for i in range(0, slabs, 4) for j in range(2)]
    following = swap(to_next, [(i + 1, i + 2) for i in evens])
    near = swap(to_near, [(i, i + 1) for i in evens])
    far_next = swap(to_far_next, [(i + 2, i + 4) for i in fours])

    cells = half * half
    shapes = {
        "features": ((2, 64, cells), BF16),
        "send": ((128, HALF), BF16),
        "part": ((2, 32, cells), F32),
        "pre": ((64, LANES), F32),
        "act": ((64, LANES), F32),
        "pre_two": ((2, 64, cells), F32),
        "far_one": ((64, 72), BF16),
        "far_two": ((2, 64, 288), BF16),
    }
    feat, send, *inner = pl.pallas_call(
        functools.partial(inner_body, count),
        out_shape=tuple(
            (pltpu.VMEM if name == "send" else jax.ShapeDtypeStruct)(*x) for name, x in shapes.items()
        ),
        scratch_shapes=[
            pltpu.VMEM(shape, F32) for shape in ((864, 64), (64, 128), (4, 64, 128), (4, 128, 128))
        ],
        compiler_params=limit,
        cost_estimate=pl.CostEstimate(flops=2 * 10**10, bytes_accessed=2 * 10**6, transcendentals=10**6),
    )(to_next, to_near, following, near, *weights)
    share = 64 // slabs
    send, far_next = lax.optimization_barrier((send.reshape(slabs, 2 * share, HALF), far_next))
    parts = lax.all_to_all(send, "space", 0, 0, tiled=True)
    _, to_far_near = lax.optimization_barrier((send, to_far_near))
    far_near = swap(to_far_near, [(i, i + 2) for i in fours])
    features, pooled_grad = pl.pallas_call(
        outer_body,
        out_shape=(
            jax.ShapeDtypeStruct((1, 64, 2, cells), BF16),
            jax.ShapeDtypeStruct((1, 32, 2, cells), BF16),
        ),
        compiler_params=limit,
        cost_estimate=pl.CostEstimate(flops=2 * 10**9, bytes_accessed=10**6, transcendentals=10**5),
    )(far_next, far_near, following, near, weights[1], feat, *inner)
    parts, features, pooled_grad = lax.optimization_barrier((parts, features, pooled_grad))
    total = pl.pallas_call(
        sum_body,
        out_shape=jax.ShapeDtypeStruct(parts.shape[1:], F32),
        compiler_params=limit,
    )(parts)

    def other_core(block, step):
        return lax.ppermute(block, "dp", [(i, i ^ step) for i in range(copies)])

    step = 1
    while 2 * step < copies:
        total = total + other_core(total, step)
        step *= 2
    other = other_core(total, step)
    grad_one, grad_two = pl.pallas_call(
        finish_body,
        out_shape=(jax.ShapeDtypeStruct((share * 54,), F32), jax.ShapeDtypeStruct((share * 864,), F32)),
        compiler_params=limit,
    )(total, other)
    return (features, pooled_grad, grad_one, grad_two)


def solution(mesh):
    in_specs = (P("dp", None, "space", None, None), P(), P(), P("dp", None, "space", None))
    out_specs = (P("dp", None, "space", None), P("dp", None, "space", None), P("space"), P("space"))
    return jax.shard_map(
        on_device, mesh=mesh, in_specs=in_specs, out_specs=out_specs, check_vma=False
    )
```

```python
import functools
import math

import jax
import jax.numpy as jnp
import numpy as np
from jax import lax
from jax.experimental import pallas as pl
from jax.experimental.pallas import tpu as pltpu
from jax.sharding import PartitionSpec as P

F32 = jnp.float32
BF16 = jnp.bfloat16
SHIFTS = [(dy, dx) for dy in (-1, 0, 1) for dx in (-1, 0, 1)]
NN = (((1,), (0,)), ((), ()))
NT = (((1,), (1,)), ((), ()))
LANES = 1024
HALF = 512
ONE_AT = 896


def dot(a, b, dims=NN):
    return lax.dot_general(a, b, dims, preferred_element_type=F32)


def inside(cells, width):
    lane = lax.broadcasted_iota(jnp.int32, (1, cells), 1)
    col, row = lane & (width - 1), lax.shift_right_logical(lane, width.bit_length() - 1)

    def factor(pos, step):
        if step == 0:
            return None
        return jnp.where(pos < width - 1 if step > 0 else pos > 0, 1.0, 0.0)

    return [(factor(col, d), factor(row, d)) for d in (-1, 0, 1)]


def moved_by(field, move, factor):
    return field if move == 0 else pltpu.roll(field, (-move) % field.shape[1], 1) * factor


def all_shifts(field, width):
    factors = [
        [f if f is None else f.astype(field.dtype) for f in pair]
        for pair in inside(field.shape[1], width)
    ]
    across = [moved_by(field, dx, factors[dx + 1][0]) for dx in (-1, 0, 1)]
    return [moved_by(across[dx + 1], dy * width, factors[dy + 1][1]) for dy, dx in SHIFTS]


def pool_pattern():
    cell = lax.broadcasted_iota(jnp.int32, (512, 128), 0)
    block = lax.broadcasted_iota(jnp.int32, (512, 128), 1)
    at = 16 * lax.shift_right_logical(cell, 6) + lax.shift_right_logical(cell & 31, 1)
    return jnp.where(at == block, 0.125, 0.0).astype(BF16)


def silu_parts(v):
    s = 0.5 + 0.5 * jnp.tanh(0.5 * v)
    return v * s, s


def band_maps():
    to_kernel = np.zeros((4, 256, 108), np.float32)
    to_flat = np.zeros((4, 256, 128), np.float32)
    for p in range(4):
        for s in range(9):
            for dz in range(3):
                q = p + dz - 1
                for ci in range(4):
                    if 0 <= q <= 3:
                        row = 16 * s + 4 * q + ci
                    else:
                        row = 144 + 8 * s + (0 if q < 0 else 4) + ci
                    tap = 9 * dz + s
                    to_kernel[p, row, 4 * tap + ci] = 1
                    to_flat[p, row, 64 * (ci // 2) + 27 * (ci % 2) + tap] = 1
    return to_kernel, to_flat.reshape(1024, 128)


def prepare_body(
    vol_hbm, cot_hbm, *refs,
):
    weights, (next_ref, near_ref, far_next_ref, far_near_ref) = refs[:4], refs[4:8]
    kept, (vol_ref, cot_ref, cells_ref, sems) = refs[8:12], refs[12:]
    me = lax.axis_index("space")
    odd, upper = me % 2 == 1, (me // 2) % 2 == 1
    vol_copy = pltpu.make_async_copy(vol_hbm, vol_ref, sems.at[0])
    cot_copy = pltpu.make_async_copy(cot_hbm, cot_ref, sems.at[1])
    vol_copy.start()
    cot_copy.start()
    copies = [
        pltpu.make_async_copy(src, dst, sems.at[2 + i])
        for i, (src, dst) in enumerate(zip(weights, kept))
    ]
    for copy in copies:
        copy.start()
    vol_copy.wait()
    cin, planes, width = vol_ref.shape[1:4]
    for plane in range(planes):
        for ch in range(cin):
            at = (plane * cin + ch) * width
            cells_ref[at : at + width] = vol_ref[0, ch, plane].astype(F32)
    count = planes * cin
    blocks = []
    for b in range(4):
        lines = [cells_ref[pl.ds(8 * b + y, count, stride=width), :] for y in range(8)]
        rows = jnp.concatenate(lines, axis=1)
        near_ref[count * b : count * b + count] = rows.astype(BF16)
        next_ref[count * b : count * b + count] = rows.astype(BF16)
        blocks.append(rows)
    halves = [jnp.concatenate(blocks[2 * m : 2 * m + 2], axis=1) for m in range(2)]
    top = lax.broadcasted_iota(jnp.int32, (8, HALF), 0) < 4
    first = jnp.where(top, halves[0][0:8], pltpu.roll(halves[1][0:8], 4, 0))
    last = jnp.where(top, pltpu.roll(halves[0][8:16], 4, 0), halves[1][8:16])
    far_near_ref[...] = jnp.where(upper, first, last).astype(BF16)
    far_next_ref[...] = jnp.where(upper, last, first).astype(BF16)
    cot_copy.wait()
    cot = cot_ref[0].astype(F32)
    cots = (cot[:, 0, :], cot[:, 1, :])
    near_ref[64:128] = jnp.where(odd, cots[0], cots[1]).astype(BF16)
    next_ref[64:128] = jnp.where(odd, cots[1], cots[0]).astype(BF16)
    for copy in copies:
        copy.wait()


def sum_body(parts_ref, total_ref):
    total = parts_ref[0].astype(F32)
    for i in range(1, parts_ref.shape[0]):
        total = total + parts_ref[i].astype(F32)
    total_ref[...] = total


def finish_body(mine_ref, other_ref, one_ref, two_ref):
    total = mine_ref[...] + other_ref[...]
    share = total.shape[0] // 2
    total = jnp.concatenate([total[0:share], total[share:]], axis=1)
    two_ref[...] = jnp.concatenate([total[r, 0:864] for r in range(share)])
    one = total[:, ONE_AT : ONE_AT + 54] + total[:, ONE_AT + 64 : ONE_AT + 118]
    one_ref[...] = jnp.concatenate([one[r] for r in range(share)])


def unfold(block, rows):
    return jnp.concatenate([block[rows * b : rows * b + rows] for b in range(4)], axis=1)


def pool_sums(sums, pattern):
    rows = sums.shape[0]
    high = sums.astype(BF16)
    low = (sums - high.astype(F32)).astype(BF16)
    halves = [part[:, 512 * m : 512 * m + 512] for part in (high, low) for m in range(2)]
    out = dot(jnp.concatenate(halves, axis=0), pattern)
    out = out[0 : 2 * rows] + out[2 * rows : 4 * rows]
    return jnp.concatenate([out[0:rows], out[rows : 2 * rows]], axis=1)


def spread_cells(field, pattern):
    rows = field.shape[0]
    high = field.astype(BF16)
    low = (field - high.astype(F32)).astype(BF16)
    halves = [part[:, 128 * m : 128 * m + 128] for part in (high, low) for m in range(2)]
    out = dot(jnp.concatenate(halves, axis=0), pattern, NT)
    out = out[0 : 2 * rows] + out[2 * rows : 4 * rows]
    return jnp.concatenate([out[0:rows], out[rows : 2 * rows]], axis=1)


def spread_taps(taps, half):
    factors = inside(half * half, half)
    total = None
    for dx in (-1, 0, 1):
        column = None
        for dy in (-1, 0, 1):
            s = 3 * (1 - dy) + (1 - dx)
            part = moved_by(taps[32 * s : 32 * s + 32], dy * half, factors[dy + 1][1])
            column = part if column is None else column + part
        column = moved_by(column, dx, factors[dx + 1][0])
        total = column if total is None else total + column
    return total


def inner_body(
    count,
    own_next_ref, own_near_ref, next_ref, near_ref, k1_ref, k2_ref, to_kernel_ref, to_flat_ref,
    feat_ref, send_ref, part_ref, pre_ref, act_ref, pre_two_ref, far_one_ref, far_two_ref,
    term_ref, pair_ref, rows_ref, out_ref,
):
    slabs = lax.axis_size("space")
    me = lax.axis_index("space")
    half = 16

    odd = me % 2 == 1
    own = unfold(own_near_ref[0:64].astype(F32), 16)
    near, following = near_ref[0:64].astype(F32), next_ref[0:64].astype(F32)
    left = unfold(jnp.where(odd, near, following), 16)
    right = unfold(jnp.where(odd, following, near), 16)
    top = lax.broadcasted_iota(jnp.int32, (8, LANES), 0) < 4
    edges = (
        jnp.where(top, 0.0, pltpu.roll(own[0:8], 4, 0)),
        jnp.where(top, pltpu.roll(left[8:16], 4, 0), pltpu.roll(right[0:8], 4, 0)),
        jnp.where(top, pltpu.roll(own[8:16], 4, 0), 0.0),
    )
    moved_edges = all_shifts(jnp.concatenate(edges, axis=0), 2 * half)
    moved = all_shifts(jnp.concatenate([left, own, right], axis=0).astype(BF16), 2 * half)
    patches = []
    for g in range(3):
        rows = [m[8 * g : 8 * g + 8] for m in moved_edges] + [jnp.zeros((40, LANES), F32)]
        rows = jnp.concatenate(rows, axis=0).astype(BF16)
        patches.append(jnp.concatenate([*(m[16 * g : 16 * g + 16] for m in moved), rows], axis=0))

    k1t = k1_ref[...].astype(F32).reshape(108, 32).T.astype(BF16)
    two_by_dz = jnp.concatenate(
        [k2_ref[288 * dz : 288 * dz + 288].astype(F32).T for dz in range(3)], axis=0
    ).astype(BF16)
    banded = jnp.concatenate(
        [dot(k1t, to_kernel_ref[p], NT).astype(BF16) for p in range(4)], axis=0
    )
    far_one_ref[...] = jnp.concatenate(
        [dot(k1t, to_kernel_ref[p, 144:216], NT).astype(BF16) for p in (0, 3)], axis=0
    )
    far_two_ref[0] = two_by_dz[0:64]
    far_two_ref[1] = two_by_dz[128:192]
    pattern = pool_pattern()

    pre = dot(banded, patches[0])
    pre_ref[0:32] = pre[0:32]
    act, s = silu_parts(pre[32:128])
    act_ref[0:32] = act[0:32]
    slopes = [(s + act * (1.0 - s))[32:96]]
    sums = [act[32:64] + act[64:96]]
    act, s = silu_parts(dot(banded, patches[1]))
    slopes.append(s + act * (1.0 - s))
    sums += [act[0:32] + act[32:64], act[64:96] + act[96:128]]
    pre = dot(banded, patches[2])
    pre_ref[32:64] = pre[96:128]
    act, s = silu_parts(pre[0:96])
    act_ref[32:64] = act[64:96]
    slopes.append((s + act * (1.0 - s))[0:64])
    sums += [act[0:32] + act[32:64]]
    pooled = pool_sums(jnp.concatenate(sums, axis=0), pattern)
    plane = lax.shift_right_logical(lax.broadcasted_iota(jnp.int32, pooled.shape, 0), 5)
    real = ((plane > 0) | (me > 0)) & ((plane < 3) | (me < slabs - 1))
    pooled = jnp.where(real, pooled, 0.0).astype(BF16)

    moved = all_shifts(pooled, half)
    planes = [jnp.concatenate([m[32 * q : 32 * q + 32] for m in moved], axis=0) for q in range(4)]
    pre_two = [None] * 4
    for q, columns in enumerate(planes):
        by_dz = dot(two_by_dz, columns)
        for dz in range(3):
            p = q + 1 - dz
            if 0 <= p < 4:
                part = by_dz[64 * dz : 64 * dz + 64]
                pre_two[p] = part if pre_two[p] is None else pre_two[p] + part
    pre_two_ref[0], pre_two_ref[1] = pre_two[0], pre_two[3]

    own_cots = own_near_ref[64:128].astype(F32), own_next_ref[64:128].astype(F32)
    cots = jnp.where(odd, *own_cots), jnp.where(odd, *own_cots[::-1])
    deltas = []
    for p in range(2):
        act, s = silu_parts(pre_two[p + 1])
        feat_ref[p] = act.astype(BF16)
        deltas.append((cots[p] * (s + act * (1.0 - s))).astype(BF16))

    share = 64 // slabs

    def place(columns, at):
        for first in range(0, columns.shape[1], 128):
            tile = (at + first) % HALF // 128
            rows_ref[tile] = columns[:, first : first + 128]
            for r in range(share):
                target = pl.ds((at + first) // HALF * share + r, slabs, stride=2 * share)
                out_ref[tile, target, :] = rows_ref[tile, pl.ds(r, slabs, stride=share), :]

    columns = [jnp.concatenate(planes[p : p + 3], axis=0) for p in range(2)]
    term = dot(columns[0], deltas[0], NT) + dot(columns[1], deltas[1], NT)
    term_ref[...] = term * (1.0 / math.sqrt(count // 8))
    rows = jnp.concatenate([term_ref[pl.ds(ch, 27, stride=32), :] for ch in range(32)], axis=0)
    place(rows[0:HALF].T, 0)
    rows = jnp.concatenate([rows[HALF:864], jnp.zeros((ONE_AT - 864, 64), F32)], axis=0)
    place(rows.T, HALF)

    grads = []
    for p in range(-1, 3):
        sources = [q for q in range(2) if abs(q - p) < 2]
        taps = [k2_ref[288 * (1 + p - q) : 288 * (1 + p - q) + 288] for q in sources]
        given = jnp.concatenate([deltas[q] for q in sources], axis=0)
        grads.append(spread_taps(dot(jnp.concatenate(taps, axis=1), given), half))
    part_ref[0], part_ref[1] = grads[1], grads[2]

    grads = jnp.where(real, jnp.concatenate(grads, axis=0), 0.0)
    spread = spread_cells(grads, pattern)
    spread = [spread[32 * q : 32 * q + 32] for q in range(4)]
    wide = []
    for g, under in enumerate(((0,), (1, 2), (3,))):
        field = jnp.concatenate([spread[q] for q in under for _ in range(2)], axis=0)
        wide.append(dot((field * slopes[g]).astype(BF16), patches[g], NT))
    wide = wide[1] + jnp.concatenate([wide[2], wide[0]], axis=0)
    wide = jnp.concatenate([wide[32 * p : 32 * p + 32] for p in range(4)], axis=1)
    high = wide.astype(BF16)
    low = (wide - high.astype(F32)).astype(BF16)
    term_one = dot(jnp.concatenate([high, low], axis=0), to_flat_ref[...])
    term_one = (term_one[0:32] + term_one[32:64]) * (1.0 / math.sqrt(count))
    for h, half_row in enumerate((term_one, pltpu.roll(term_one, 64, 1))):
        pair_ref[pl.ds(h, 32, stride=2), :] = half_row
    rows = pair_ref[...]
    rounded = rows.astype(BF16).astype(F32)
    lane = lax.broadcasted_iota(jnp.int32, rows.shape, 1)
    pair = jnp.where(lane < 64, rounded, pltpu.roll(rows - rounded, 64, 1))
    place(pair, ONE_AT)
    for tile in range(4):
        send_ref[:, 128 * tile : 128 * tile + 128] = out_ref[tile].astype(BF16)


def outer_body(
    far_next_ref, far_near_ref, next_ref, near_ref, k2_ref,
    feat_ref, part_ref, pre_ref, act_ref, pre_two_ref, far_one_ref, far_two_ref,
    feat_out, pgrad_out,
):
    slabs = lax.axis_size("space")
    me = lax.axis_index("space")
    half = 16
    odd, upper = me % 2 == 1, (me // 2) % 2 == 1
    pattern = pool_pattern()
    far_near, far_next = far_near_ref[...].astype(F32), far_next_ref[...].astype(F32)
    far_left, far_right = jnp.where(upper, far_near, far_next), jnp.where(upper, far_next, far_near)
    top = lax.broadcasted_iota(jnp.int32, (8, LANES), 0) < 4
    edge = jnp.where(
        top,
        jnp.concatenate([far_left, pltpu.roll(far_left, 4, 0)], axis=1),
        jnp.concatenate([pltpu.roll(far_right, 4, 0), far_right], axis=1),
    )
    patches = jnp.concatenate(all_shifts(edge, 2 * half), axis=0).astype(BF16)
    act, _ = silu_parts(pre_ref[...] + dot(far_one_ref[...], patches))
    pooled = pool_sums(act_ref[...] + act, pattern)
    plane = lax.shift_right_logical(lax.broadcasted_iota(jnp.int32, pooled.shape, 0), 5)
    real = ((plane > 0) | (me > 0)) & ((plane < 1) | (me < slabs - 1))
    pooled = jnp.where(real, pooled, 0.0).astype(BF16)
    moved = all_shifts(pooled, half)

    near, following = near_ref[64:128].astype(F32), next_ref[64:128].astype(F32)
    cots = jnp.where(odd, near, following), jnp.where(odd, following, near)
    for p in range(2):
        columns = jnp.concatenate([m[32 * p : 32 * p + 32] for m in moved], axis=0)
        pre = pre_two_ref[p] + dot(far_two_ref[p], columns)
        act, s = silu_parts(pre)
        delta = (cots[p] * (s + act * (1.0 - s))).astype(BF16)
        taps = dot(k2_ref[576 * (1 - p) : 576 * (1 - p) + 288], delta)
        pgrad_out[0, :, p, :] = (part_ref[p] + spread_taps(taps, half)).astype(BF16)
        feat_out[0, :, p, :] = feat_ref[p]


def on_device(volumes, kernel_one, kernel_two, cotangent):
    _, cin, planes, width, _ = volumes.shape
    half = width // 2
    slabs = lax.axis_size("space")
    copies = lax.axis_size("dp")
    count = copies * planes * slabs * width * width

    to_kernel, to_flat = band_maps()
    weights = (
        jnp.transpose(kernel_one, (2, 3, 4, 1, 0)).reshape(27, 4, 32),
        jnp.transpose(kernel_two, (2, 3, 4, 1, 0)).reshape(864, 64),
        jnp.asarray(to_kernel, BF16),
        jnp.asarray(to_flat, BF16),
    )

    def in_hbm(*arrays):
        return [pltpu.with_memory_space_constraint(x, pltpu.HBM) for x in arrays]

    inputs = in_hbm(volumes, cotangent, *weights)
    hbm = pl.BlockSpec(memory_space=pltpu.HBM)
    limit = pltpu.CompilerParams(vmem_limit_bytes=48 * 1024 * 1024)
    whole = jax.ShapeDtypeStruct((128, width * width // 4), BF16)
    part = jax.ShapeDtypeStruct((2 * cin, width * width // 2), BF16)
    to_next, to_near, to_far_next, to_far_near, *weights = pl.pallas_call(
        prepare_body,
        out_shape=(
            whole, whole, part, part, *(jax.ShapeDtypeStruct(w.shape, BF16) for w in weights)
        ),
        in_specs=[hbm] * len(inputs),
        scratch_shapes=[
            pltpu.VMEM(volumes.shape, BF16),
            pltpu.VMEM(cotangent.shape, BF16),
            pltpu.VMEM((planes * cin * width, width), F32),
            pltpu.SemaphoreType.DMA((len(inputs),)),
        ],
        compiler_params=limit,
    )(*inputs)

    def swap(block, pairs):
        pairs = [p for p in pairs if max(p) < slabs]
        return lax.ppermute(block, "space", pairs + [(t, f) for f, t in pairs])

    evens = range(0, slabs, 2)
    fours = [i + j for i in range(0, slabs, 4) for j in range(2)]
    following = swap(to_next, [(i + 1, i + 2) for i in evens])
    near = swap(to_near, [(i, i + 1) for i in evens])
    far_next = swap(to_far_next, [(i + 2, i + 4) for i in fours])

    cells = half * half
    shapes = {
        "features": ((2, 64, cells), BF16),
        "send": ((128, HALF), BF16),
        "part": ((2, 32, cells), F32),
        "pre": ((64, LANES), F32),
        "act": ((64, LANES), F32),
        "pre_two": ((2, 64, cells), F32),
        "far_one": ((64, 72), BF16),
        "far_two": ((2, 64, 288), BF16),
    }
    feat, send, *inner = pl.pallas_call(
        functools.partial(inner_body, count),
        out_shape=tuple(jax.ShapeDtypeStruct(*x) for x in shapes.values()),
        scratch_shapes=[
            pltpu.VMEM(shape, F32) for shape in ((864, 64), (64, 128), (4, 64, 128), (4, 128, 128))
        ],
        compiler_params=limit,
        cost_estimate=pl.CostEstimate(flops=2 * 10**10, bytes_accessed=2 * 10**6, transcendentals=10**6),
    )(to_next, to_near, following, near, *weights)
    share = 64 // slabs
    send, far_next = lax.optimization_barrier((send.reshape(slabs, 2 * share, HALF), far_next))
    send = pltpu.with_memory_space_constraint(send, pltpu.VMEM)
    parts = lax.all_to_all(send, "space", 0, 0, tiled=True)
    _, to_far_near = lax.optimization_barrier((send, to_far_near))
    far_near = swap(to_far_near, [(i, i + 2) for i in fours])
    features, pooled_grad = pl.pallas_call(
        outer_body,
        out_shape=(
            jax.ShapeDtypeStruct((1, 64, 2, cells), BF16),
            jax.ShapeDtypeStruct((1, 32, 2, cells), BF16),
        ),
        compiler_params=limit,
        cost_estimate=pl.CostEstimate(flops=2 * 10**9, bytes_accessed=10**6, transcendentals=10**5),
    )(far_next, far_near, following, near, weights[1], feat, *inner)
    parts, features, pooled_grad = lax.optimization_barrier((parts, features, pooled_grad))
    total = pl.pallas_call(
        sum_body,
        out_shape=jax.ShapeDtypeStruct(parts.shape[1:], F32),
        compiler_params=limit,
    )(parts)

    def other_core(block, step):
        return lax.ppermute(block, "dp", [(i, i ^ step) for i in range(copies)])

    step = 1
    while 2 * step < copies:
        total = total + other_core(total, step)
        step *= 2
    other = other_core(total, step)
    grad_one, grad_two = pl.pallas_call(
        finish_body,
        out_shape=(jax.ShapeDtypeStruct((share * 54,), F32), jax.ShapeDtypeStruct((share * 864,), F32)),
        compiler_params=limit,
    )(total, other)
    return (features, pooled_grad, grad_one, grad_two)


def solution(mesh):
    in_specs = (P("dp", None, "space", None, None), P(), P(), P("dp", None, "space", None))
    out_specs = (P("dp", None, "space", None), P("dp", None, "space", None), P("space"), P("space"))
    return jax.shard_map(
        on_device, mesh=mesh, in_specs=in_specs, out_specs=out_specs, check_vma=False
    )
```

```python
import functools
import math

import jax
import jax.numpy as jnp
import numpy as np
from jax import lax
from jax.experimental import pallas as pl
from jax.experimental.pallas import tpu as pltpu
from jax.sharding import PartitionSpec as P

F32 = jnp.float32
BF16 = jnp.bfloat16
SHIFTS = [(dy, dx) for dy in (-1, 0, 1) for dx in (-1, 0, 1)]
NN = (((1,), (0,)), ((), ()))
NT = (((1,), (1,)), ((), ()))
LANES = 1024
HALF = 512
ONE_AT = 896


def dot(a, b, dims=NN):
    return lax.dot_general(a, b, dims, preferred_element_type=F32)


def inside(cells, width):
    lane = lax.broadcasted_iota(jnp.int32, (1, cells), 1)
    col, row = lane & (width - 1), lax.shift_right_logical(lane, width.bit_length() - 1)

    def factor(pos, step):
        if step == 0:
            return None
        return jnp.where(pos < width - 1 if step > 0 else pos > 0, 1.0, 0.0)

    return [(factor(col, d), factor(row, d)) for d in (-1, 0, 1)]


def moved_by(field, move, factor):
    return field if move == 0 else pltpu.roll(field, (-move) % field.shape[1], 1) * factor


def all_shifts(field, width):
    factors = [
        [f if f is None else f.astype(field.dtype) for f in pair]
        for pair in inside(field.shape[1], width)
    ]
    across = [moved_by(field, dx, factors[dx + 1][0]) for dx in (-1, 0, 1)]
    return [moved_by(across[dx + 1], dy * width, factors[dy + 1][1]) for dy, dx in SHIFTS]


def pool_pattern():
    cell = lax.broadcasted_iota(jnp.int32, (512, 128), 0)
    block = lax.broadcasted_iota(jnp.int32, (512, 128), 1)
    at = 16 * lax.shift_right_logical(cell, 6) + lax.shift_right_logical(cell & 31, 1)
    return jnp.where(at == block, 0.125, 0.0).astype(BF16)


def silu_parts(v):
    s = 0.5 + 0.5 * jnp.tanh(0.5 * v)
    return v * s, s


def band_maps():
    to_kernel = np.zeros((4, 256, 108), np.float32)
    to_flat = np.zeros((4, 256, 128), np.float32)
    for p in range(4):
        for s in range(9):
            for dz in range(3):
                q = p + dz - 1
                for ci in range(4):
                    if 0 <= q <= 3:
                        row = 16 * s + 4 * q + ci
                    else:
                        row = 144 + 8 * s + (0 if q < 0 else 4) + ci
                    tap = 9 * dz + s
                    to_kernel[p, row, 4 * tap + ci] = 1
                    to_flat[p, row, 64 * (ci // 2) + 27 * (ci % 2) + tap] = 1
    return to_kernel, to_flat.reshape(1024, 128)


def prepare_body(
    vol_hbm, cot_hbm, *refs,
):
    weights, (next_ref, near_ref, far_next_ref, far_near_ref) = refs[:4], refs[4:8]
    kept, (vol_ref, cot_ref, cells_ref, sems) = refs[8:12], refs[12:]
    me = lax.axis_index("space")
    odd, upper = me % 2 == 1, (me // 2) % 2 == 1
    vol_copy = pltpu.make_async_copy(vol_hbm, vol_ref, sems.at[0])
    cot_copy = pltpu.make_async_copy(cot_hbm, cot_ref, sems.at[1])
    vol_copy.start()
    cot_copy.start()
    copies = [
        pltpu.make_async_copy(src, dst, sems.at[2 + i])
        for i, (src, dst) in enumerate(zip(weights, kept))
    ]
    for copy in copies:
        copy.start()
    vol_copy.wait()
    cin, planes, width = vol_ref.shape[1:4]
    for plane in range(planes):
        for ch in range(cin):
            at = (plane * cin + ch) * width
            cells_ref[at : at + width] = vol_ref[0, ch, plane].astype(F32)
    count = planes * cin
    blocks = []
    for b in range(4):
        lines = [cells_ref[pl.ds(8 * b + y, count, stride=width), :] for y in range(8)]
        rows = jnp.concatenate(lines, axis=1)
        near_ref[count * b : count * b + count] = rows.astype(BF16)
        next_ref[count * b : count * b + count] = rows.astype(BF16)
        blocks.append(rows)
    halves = [jnp.concatenate(blocks[2 * m : 2 * m + 2], axis=1) for m in range(2)]
    top = lax.broadcasted_iota(jnp.int32, (8, HALF), 0) < 4
    first = jnp.where(top, halves[0][0:8], pltpu.roll(halves[1][0:8], 4, 0))
    last = jnp.where(top, pltpu.roll(halves[0][8:16], 4, 0), halves[1][8:16])
    far_near_ref[...] = jnp.where(upper, first, last).astype(BF16)
    far_next_ref[...] = jnp.where(upper, last, first).astype(BF16)
    cot_copy.wait()
    cot = cot_ref[0].astype(F32)
    cots = (cot[:, 0, :], cot[:, 1, :])
    near_ref[64:128] = jnp.where(odd, cots[0], cots[1]).astype(BF16)
    next_ref[64:128] = jnp.where(odd, cots[1], cots[0]).astype(BF16)
    for copy in copies:
        copy.wait()


def sum_body(parts_ref, total_ref):
    total = parts_ref[0].astype(F32)
    for i in range(1, parts_ref.shape[0]):
        total = total + parts_ref[i].astype(F32)
    total_ref[...] = total


def finish_body(mine_ref, other_ref, one_ref, two_ref):
    total = mine_ref[...] + other_ref[...]
    share = total.shape[0] // 2
    total = jnp.concatenate([total[0:share], total[share:]], axis=1)
    two_ref[...] = jnp.concatenate([total[r, 0:864] for r in range(share)])
    one = total[:, ONE_AT : ONE_AT + 54] + total[:, ONE_AT + 64 : ONE_AT + 118]
    one_ref[...] = jnp.concatenate([one[r] for r in range(share)])


def unfold(block, rows):
    return jnp.concatenate([block[rows * b : rows * b + rows] for b in range(4)], axis=1)


def pool_sums(sums, pattern):
    rows = sums.shape[0]
    high = sums.astype(BF16)
    low = (sums - high.astype(F32)).astype(BF16)
    halves = [part[:, 512 * m : 512 * m + 512] for part in (high, low) for m in range(2)]
    out = dot(jnp.concatenate(halves, axis=0), pattern)
    out = out[0 : 2 * rows] + out[2 * rows : 4 * rows]
    return jnp.concatenate([out[0:rows], out[rows : 2 * rows]], axis=1)


def spread_cells(field, pattern):
    rows = field.shape[0]
    high = field.astype(BF16)
    low = (field - high.astype(F32)).astype(BF16)
    halves = [
        jnp.concatenate([part[:, 128 * m : 128 * m + 128] for part in (high, low)], axis=1)
        for m in range(2)
    ]
    out = dot(jnp.concatenate(halves, axis=0), jnp.concatenate([pattern, pattern], axis=1), NT)
    return jnp.concatenate([out[0:rows], out[rows : 2 * rows]], axis=1)


def spread_taps(taps, half):
    factors = inside(half * half, half)
    total = None
    for dx in (-1, 0, 1):
        column = None
        for dy in (-1, 0, 1):
            s = 3 * (1 - dy) + (1 - dx)
            part = moved_by(taps[32 * s : 32 * s + 32], dy * half, factors[dy + 1][1])
            column = part if column is None else column + part
        column = moved_by(column, dx, factors[dx + 1][0])
        total = column if total is None else total + column
    return total


def inner_body(
    count,
    own_next_ref, own_near_ref, next_ref, near_ref, k1_ref, k2_ref, to_kernel_ref, to_flat_ref,
    feat_ref, send_ref, part_ref, pre_ref, act_ref, pre_two_ref, far_one_ref, far_two_ref,
    term_ref, pair_ref, rows_ref, out_ref,
):
    slabs = lax.axis_size("space")
    me = lax.axis_index("space")
    half = 16

    odd = me % 2 == 1
    own = unfold(own_near_ref[0:64].astype(F32), 16)
    near, following = near_ref[0:64].astype(F32), next_ref[0:64].astype(F32)
    left = unfold(jnp.where(odd, near, following), 16)
    right = unfold(jnp.where(odd, following, near), 16)
    top = lax.broadcasted_iota(jnp.int32, (8, LANES), 0) < 4
    edges = (
        jnp.where(top, 0.0, pltpu.roll(own[0:8], 4, 0)),
        jnp.where(top, pltpu.roll(left[8:16], 4, 0), pltpu.roll(right[0:8], 4, 0)),
        jnp.where(top, pltpu.roll(own[8:16], 4, 0), 0.0),
    )
    moved_edges = all_shifts(jnp.concatenate(edges, axis=0), 2 * half)
    moved = all_shifts(jnp.concatenate([left, own, right], axis=0).astype(BF16), 2 * half)
    patches = []
    for g in range(3):
        rows = [m[8 * g : 8 * g + 8] for m in moved_edges] + [jnp.zeros((40, LANES), F32)]
        rows = jnp.concatenate(rows, axis=0).astype(BF16)
        patches.append(jnp.concatenate([*(m[16 * g : 16 * g + 16] for m in moved), rows], axis=0))

    k1t = k1_ref[...].astype(F32).reshape(108, 32).T.astype(BF16)
    two_by_dz = jnp.concatenate(
        [k2_ref[288 * dz : 288 * dz + 288].astype(F32).T for dz in range(3)], axis=0
    ).astype(BF16)
    banded = jnp.concatenate(
        [dot(k1t, to_kernel_ref[p], NT).astype(BF16) for p in range(4)], axis=0
    )
    far_one_ref[...] = jnp.concatenate(
        [dot(k1t, to_kernel_ref[p, 144:216], NT).astype(BF16) for p in (0, 3)], axis=0
    )
    far_two_ref[0] = two_by_dz[0:64]
    far_two_ref[1] = two_by_dz[128:192]
    pattern = pool_pattern()

    pre = dot(banded, patches[0])
    pre_ref[0:32] = pre[0:32]
    act, s = silu_parts(pre[32:128])
    act_ref[0:32] = act[0:32]
    slopes = [(s + act * (1.0 - s))[32:96]]
    sums = [act[32:64] + act[64:96]]
    act, s = silu_parts(dot(banded, patches[1]))
    slopes.append(s + act * (1.0 - s))
    sums += [act[0:32] + act[32:64], act[64:96] + act[96:128]]
    pre = dot(banded, patches[2])
    pre_ref[32:64] = pre[96:128]
    act, s = silu_parts(pre[0:96])
    act_ref[32:64] = act[64:96]
    slopes.append((s + act * (1.0 - s))[0:64])
    sums += [act[0:32] + act[32:64]]
    pooled = pool_sums(jnp.concatenate(sums, axis=0), pattern)
    plane = lax.shift_right_logical(lax.broadcasted_iota(jnp.int32, pooled.shape, 0), 5)
    real = ((plane > 0) | (me > 0)) & ((plane < 3) | (me < slabs - 1))
    pooled = jnp.where(real, pooled, 0.0).astype(BF16)

    moved = all_shifts(pooled, half)
    planes = [jnp.concatenate([m[32 * q : 32 * q + 32] for m in moved], axis=0) for q in range(4)]
    pre_two = [None] * 4
    for q, columns in enumerate(planes):
        by_dz = dot(two_by_dz, columns)
        for dz in range(3):
            p = q + 1 - dz
            if 0 <= p < 4:
                part = by_dz[64 * dz : 64 * dz + 64]
                pre_two[p] = part if pre_two[p] is None else pre_two[p] + part
    pre_two_ref[0], pre_two_ref[1] = pre_two[0], pre_two[3]

    own_cots = own_near_ref[64:128].astype(F32), own_next_ref[64:128].astype(F32)
    cots = jnp.where(odd, *own_cots), jnp.where(odd, *own_cots[::-1])
    deltas = []
    for p in range(2):
        act, s = silu_parts(pre_two[p + 1])
        feat_ref[p] = act.astype(BF16)
        deltas.append((cots[p] * (s + act * (1.0 - s))).astype(BF16))

    share = 64 // slabs

    def place(columns, at):
        for first in range(0, columns.shape[1], 128):
            tile = (at + first) % HALF // 128
            rows_ref[tile] = columns[:, first : first + 128]
            for r in range(share):
                target = pl.ds((at + first) // HALF * share + r, slabs, stride=2 * share)
                out_ref[tile, target, :] = rows_ref[tile, pl.ds(r, slabs, stride=share), :]

    both = jnp.concatenate(deltas, axis=0)
    products = [dot(columns, both, NT) for columns in planes]
    for dz in range(3):
        term = products[dz] + pltpu.roll(products[dz + 1], 64, 1)
        term_ref[288 * dz : 288 * dz + 288] = term * (1.0 / math.sqrt(count // 8))
    rows = jnp.concatenate([term_ref[pl.ds(ch, 27, stride=32), :] for ch in range(32)], axis=0)
    place(rows[0:HALF].T[0:64], 0)
    rows = jnp.concatenate([rows[HALF:864], jnp.zeros((ONE_AT - 864, 128), F32)], axis=0)
    place(rows.T[0:64], HALF)

    grads = []
    for p in range(-1, 3):
        sources = [q for q in range(2) if abs(q - p) < 2]
        taps = [k2_ref[288 * (1 + p - q) : 288 * (1 + p - q) + 288] for q in sources]
        given = jnp.concatenate([deltas[q] for q in sources], axis=0)
        grads.append(spread_taps(dot(jnp.concatenate(taps, axis=1), given), half))
    part_ref[0], part_ref[1] = grads[1], grads[2]

    grads = jnp.where(real, jnp.concatenate(grads, axis=0), 0.0)
    spread = spread_cells(grads, pattern)
    spread = [spread[32 * q : 32 * q + 32] for q in range(4)]
    wide = []
    for g, under in enumerate(((0,), (1, 2), (3,))):
        field = jnp.concatenate([spread[q] for q in under for _ in range(2)], axis=0)
        wide.append(dot((field * slopes[g]).astype(BF16), patches[g], NT))
    wide = wide[1] + jnp.concatenate([wide[2], wide[0]], axis=0)
    wide = jnp.concatenate([wide[32 * p : 32 * p + 32] for p in range(4)], axis=1)
    high = wide.astype(BF16)
    low = (wide - high.astype(F32)).astype(BF16)
    term_one = dot(jnp.concatenate([high, low], axis=0), to_flat_ref[...])
    term_one = (term_one[0:32] + term_one[32:64]) * (1.0 / math.sqrt(count))
    for h, half_row in enumerate((term_one, pltpu.roll(term_one, 64, 1))):
        pair_ref[pl.ds(h, 32, stride=2), :] = half_row
    rows = pair_ref[...]
    rounded = rows.astype(BF16).astype(F32)
    lane = lax.broadcasted_iota(jnp.int32, rows.shape, 1)
    pair = jnp.where(lane < 64, rounded, pltpu.roll(rows - rounded, 64, 1))
    place(pair, ONE_AT)
    for tile in range(4):
        send_ref[:, 128 * tile : 128 * tile + 128] = out_ref[tile].astype(BF16)


def outer_body(
    far_next_ref, far_near_ref, next_ref, near_ref, k2_ref,
    feat_ref, part_ref, pre_ref, act_ref, pre_two_ref, far_one_ref, far_two_ref,
    feat_out, pgrad_out,
):
    slabs = lax.axis_size("space")
    me = lax.axis_index("space")
    half = 16
    odd, upper = me % 2 == 1, (me // 2) % 2 == 1
    pattern = pool_pattern()
    far_near, far_next = far_near_ref[...].astype(F32), far_next_ref[...].astype(F32)
    far_left, far_right = jnp.where(upper, far_near, far_next), jnp.where(upper, far_next, far_near)
    top = lax.broadcasted_iota(jnp.int32, (8, LANES), 0) < 4
    edge = jnp.where(
        top,
        jnp.concatenate([far_left, pltpu.roll(far_left, 4, 0)], axis=1),
        jnp.concatenate([pltpu.roll(far_right, 4, 0), far_right], axis=1),
    )
    patches = jnp.concatenate(all_shifts(edge, 2 * half), axis=0).astype(BF16)
    act, _ = silu_parts(pre_ref[...] + dot(far_one_ref[...], patches))
    pooled = pool_sums(act_ref[...] + act, pattern)
    plane = lax.shift_right_logical(lax.broadcasted_iota(jnp.int32, pooled.shape, 0), 5)
    real = ((plane > 0) | (me > 0)) & ((plane < 1) | (me < slabs - 1))
    pooled = jnp.where(real, pooled, 0.0).astype(BF16)
    moved = all_shifts(pooled, half)

    near, following = near_ref[64:128].astype(F32), next_ref[64:128].astype(F32)
    cots = jnp.where(odd, near, following), jnp.where(odd, following, near)
    for p in range(2):
        columns = jnp.concatenate([m[32 * p : 32 * p + 32] for m in moved], axis=0)
        pre = pre_two_ref[p] + dot(far_two_ref[p], columns)
        act, s = silu_parts(pre)
        delta = (cots[p] * (s + act * (1.0 - s))).astype(BF16)
        taps = dot(k2_ref[576 * (1 - p) : 576 * (1 - p) + 288], delta)
        pgrad_out[0, :, p, :] = (part_ref[p] + spread_taps(taps, half)).astype(BF16)
        feat_out[0, :, p, :] = feat_ref[p]


def on_device(volumes, kernel_one, kernel_two, cotangent):
    _, cin, planes, width, _ = volumes.shape
    half = width // 2
    slabs = lax.axis_size("space")
    copies = lax.axis_size("dp")
    count = copies * planes * slabs * width * width

    to_kernel, to_flat = band_maps()
    weights = (
        jnp.transpose(kernel_one, (2, 3, 4, 1, 0)).reshape(27, 4, 32),
        jnp.transpose(kernel_two, (2, 3, 4, 1, 0)).reshape(864, 64),
        jnp.asarray(to_kernel, BF16),
        jnp.asarray(to_flat, BF16),
    )

    def in_hbm(*arrays):
        return [pltpu.with_memory_space_constraint(x, pltpu.HBM) for x in arrays]

    inputs = in_hbm(volumes, cotangent, *weights)
    hbm = pl.BlockSpec(memory_space=pltpu.HBM)
    limit = pltpu.CompilerParams(vmem_limit_bytes=48 * 1024 * 1024)
    whole = jax.ShapeDtypeStruct((128, width * width // 4), BF16)
    part = jax.ShapeDtypeStruct((2 * cin, width * width // 2), BF16)
    to_next, to_near, to_far_next, to_far_near, *weights = pl.pallas_call(
        prepare_body,
        out_shape=(
            whole, whole, part, part, *(jax.ShapeDtypeStruct(w.shape, BF16) for w in weights)
        ),
        in_specs=[hbm] * len(inputs),
        scratch_shapes=[
            pltpu.VMEM(volumes.shape, BF16),
            pltpu.VMEM(cotangent.shape, BF16),
            pltpu.VMEM((planes * cin * width, width), F32),
            pltpu.SemaphoreType.DMA((len(inputs),)),
        ],
        compiler_params=limit,
    )(*inputs)

    def swap(block, pairs):
        pairs = [p for p in pairs if max(p) < slabs]
        return lax.ppermute(block, "space", pairs + [(t, f) for f, t in pairs])

    evens = range(0, slabs, 2)
    fours = [i + j for i in range(0, slabs, 4) for j in range(2)]
    following = swap(to_next, [(i + 1, i + 2) for i in evens])
    near = swap(to_near, [(i, i + 1) for i in evens])
    far_next = swap(to_far_next, [(i + 2, i + 4) for i in fours])

    cells = half * half
    shapes = {
        "features": ((2, 64, cells), BF16),
        "send": ((128, HALF), BF16),
        "part": ((2, 32, cells), F32),
        "pre": ((64, LANES), F32),
        "act": ((64, LANES), F32),
        "pre_two": ((2, 64, cells), F32),
        "far_one": ((64, 72), BF16),
        "far_two": ((2, 64, 288), BF16),
    }
    feat, send, *inner = pl.pallas_call(
        functools.partial(inner_body, count),
        out_shape=tuple(jax.ShapeDtypeStruct(*x) for x in shapes.values()),
        scratch_shapes=[
            pltpu.VMEM(shape, F32) for shape in ((864, 128), (64, 128), (4, 64, 128), (4, 128, 128))
        ],
        compiler_params=limit,
        cost_estimate=pl.CostEstimate(flops=2 * 10**10, bytes_accessed=2 * 10**6, transcendentals=10**6),
    )(to_next, to_near, following, near, *weights)
    share = 64 // slabs
    send, far_next = lax.optimization_barrier((send.reshape(slabs, 2 * share, HALF), far_next))
    send = pltpu.with_memory_space_constraint(send, pltpu.VMEM)
    parts = lax.all_to_all(send, "space", 0, 0, tiled=True)
    _, to_far_near = lax.optimization_barrier((send, to_far_near))
    far_near = swap(to_far_near, [(i, i + 2) for i in fours])
    features, pooled_grad = pl.pallas_call(
        outer_body,
        out_shape=(
            jax.ShapeDtypeStruct((1, 64, 2, cells), BF16),
            jax.ShapeDtypeStruct((1, 32, 2, cells), BF16),
        ),
        compiler_params=limit,
        cost_estimate=pl.CostEstimate(flops=2 * 10**9, bytes_accessed=10**6, transcendentals=10**5),
    )(far_next, far_near, following, near, weights[1], feat, *inner)
    parts, features, pooled_grad = lax.optimization_barrier((parts, features, pooled_grad))
    total = pl.pallas_call(
        sum_body,
        out_shape=jax.ShapeDtypeStruct(parts.shape[1:], F32),
        compiler_params=limit,
    )(parts)

    def other_core(block, step):
        return lax.ppermute(block, "dp", [(i, i ^ step) for i in range(copies)])

    step = 1
    while 2 * step < copies:
        total = total + other_core(total, step)
        step *= 2
    other = other_core(total, step)
    grad_one, grad_two = pl.pallas_call(
        finish_body,
        out_shape=(jax.ShapeDtypeStruct((share * 54,), F32), jax.ShapeDtypeStruct((share * 864,), F32)),
        compiler_params=limit,
    )(total, other)
    return (features, pooled_grad, grad_one, grad_two)


def solution(mesh):
    in_specs = (P("dp", None, "space", None, None), P(), P(), P("dp", None, "space", None))
    out_specs = (P("dp", None, "space", None), P("dp", None, "space", None), P("space"), P("space"))
    return jax.shard_map(
        on_device, mesh=mesh, in_specs=in_specs, out_specs=out_specs, check_vma=False
    )
```

```python
import functools
import math

import jax
import jax.numpy as jnp
import numpy as np
from jax import lax
from jax.experimental import pallas as pl
from jax.experimental.pallas import tpu as pltpu
from jax.sharding import PartitionSpec as P

F32 = jnp.float32
BF16 = jnp.bfloat16
SHIFTS = [(dy, dx) for dy in (-1, 0, 1) for dx in (-1, 0, 1)]
NN = (((1,), (0,)), ((), ()))
NT = (((1,), (1,)), ((), ()))
LANES = 1024
HALF = 512
ONE_AT = 896


def dot(a, b, dims=NN):
    return lax.dot_general(a, b, dims, preferred_element_type=F32)


def inside(cells, width):
    lane = lax.broadcasted_iota(jnp.int32, (1, cells), 1)
    col, row = lane & (width - 1), lax.shift_right_logical(lane, width.bit_length() - 1)

    def factor(pos, step):
        if step == 0:
            return None
        return jnp.where(pos < width - 1 if step > 0 else pos > 0, 1.0, 0.0)

    return [(factor(col, d), factor(row, d)) for d in (-1, 0, 1)]


def moved_by(field, move, factor):
    return field if move == 0 else pltpu.roll(field, (-move) % field.shape[1], 1) * factor


def all_shifts(field, width):
    factors = [
        [f if f is None else f.astype(field.dtype) for f in pair]
        for pair in inside(field.shape[1], width)
    ]
    across = [moved_by(field, dx, factors[dx + 1][0]) for dx in (-1, 0, 1)]
    return [moved_by(across[dx + 1], dy * width, factors[dy + 1][1]) for dy, dx in SHIFTS]


def pool_pattern():
    cell = lax.broadcasted_iota(jnp.int32, (512, 128), 0)
    block = lax.broadcasted_iota(jnp.int32, (512, 128), 1)
    at = 16 * lax.shift_right_logical(cell, 6) + lax.shift_right_logical(cell & 31, 1)
    return jnp.where(at == block, 0.125, 0.0).astype(BF16)


def silu_parts(v):
    s = 0.5 + 0.5 * jnp.tanh(0.5 * v)
    return v * s, s


def band_maps():
    to_kernel = np.zeros((4, 256, 108), np.float32)
    to_flat = np.zeros((4, 256, 128), np.float32)
    for p in range(4):
        for s in range(9):
            for dz in range(3):
                q = p + dz - 1
                for ci in range(4):
                    if 0 <= q <= 3:
                        row = 16 * s + 4 * q + ci
                    else:
                        row = 144 + 8 * s + (0 if q < 0 else 4) + ci
                    tap = 9 * dz + s
                    to_kernel[p, row, 4 * tap + ci] = 1
                    to_flat[p, row, 64 * (ci // 2) + 27 * (ci % 2) + tap] = 1
    return to_kernel, to_flat.reshape(1024, 128)


def prepare_body(
    vol_hbm, cot_hbm, *refs,
):
    weights, (next_ref, near_ref, far_next_ref, far_near_ref) = refs[:4], refs[4:8]
    kept, (vol_ref, cot_ref, cells_ref, sems) = refs[8:12], refs[12:]
    me = lax.axis_index("space")
    odd, upper = me % 2 == 1, (me // 2) % 2 == 1
    vol_copy = pltpu.make_async_copy(vol_hbm, vol_ref, sems.at[0])
    cot_copy = pltpu.make_async_copy(cot_hbm, cot_ref, sems.at[1])
    vol_copy.start()
    cot_copy.start()
    copies = [
        pltpu.make_async_copy(src, dst, sems.at[2 + i])
        for i, (src, dst) in enumerate(zip(weights, kept))
    ]
    for copy in copies:
        copy.start()
    vol_copy.wait()
    cin, planes, width = vol_ref.shape[1:4]
    for plane in range(planes):
        for ch in range(cin):
            at = (plane * cin + ch) * width
            cells_ref[at : at + width] = vol_ref[0, ch, plane].astype(F32)
    count = planes * cin
    blocks = []
    for b in range(4):
        lines = [cells_ref[pl.ds(8 * b + y, count, stride=width), :] for y in range(8)]
        rows = jnp.concatenate(lines, axis=1)
        near_ref[count * b : count * b + count] = rows.astype(BF16)
        next_ref[count * b : count * b + count] = rows.astype(BF16)
        blocks.append(rows)
    halves = [jnp.concatenate(blocks[2 * m : 2 * m + 2], axis=1) for m in range(2)]
    top = lax.broadcasted_iota(jnp.int32, (8, HALF), 0) < 4
    first = jnp.where(top, halves[0][0:8], pltpu.roll(halves[1][0:8], 4, 0))
    last = jnp.where(top, pltpu.roll(halves[0][8:16], 4, 0), halves[1][8:16])
    far_near_ref[...] = jnp.where(upper, first, last).astype(BF16)
    far_next_ref[...] = jnp.where(upper, last, first).astype(BF16)
    cot_copy.wait()
    cot = cot_ref[0].astype(F32)
    cots = (cot[:, 0, :], cot[:, 1, :])
    near_ref[64:128] = jnp.where(odd, cots[0], cots[1]).astype(BF16)
    next_ref[64:128] = jnp.where(odd, cots[1], cots[0]).astype(BF16)
    for copy in copies:
        copy.wait()


def sum_body(parts_ref, total_ref):
    total = parts_ref[0].astype(F32)
    for i in range(1, parts_ref.shape[0]):
        total = total + parts_ref[i].astype(F32)
    total_ref[...] = total


def finish_body(mine_ref, other_ref, one_ref, two_ref):
    total = mine_ref[...] + other_ref[...]
    share = total.shape[0] // 2
    total = jnp.concatenate([total[0:share], total[share:]], axis=1)
    two_ref[...] = jnp.concatenate([total[r, 0:864] for r in range(share)])
    one = total[:, ONE_AT : ONE_AT + 54] + total[:, ONE_AT + 64 : ONE_AT + 118]
    one_ref[...] = jnp.concatenate([one[r] for r in range(share)])


def unfold(block, rows):
    return jnp.concatenate([block[rows * b : rows * b + rows] for b in range(4)], axis=1)


def pool_sums(sums, pattern):
    rows = sums.shape[0]
    high = sums.astype(BF16)
    low = (sums - high.astype(F32)).astype(BF16)
    halves = [part[:, 512 * m : 512 * m + 512] for part in (high, low) for m in range(2)]
    out = dot(jnp.concatenate(halves, axis=0), pattern)
    out = out[0 : 2 * rows] + out[2 * rows : 4 * rows]
    return jnp.concatenate([out[0:rows], out[rows : 2 * rows]], axis=1)


def spread_cells(field, pattern):
    rows = field.shape[0]
    high = field.astype(BF16)
    low = (field - high.astype(F32)).astype(BF16)
    halves = [
        jnp.concatenate([part[:, 128 * m : 128 * m + 128] for part in (high, low)], axis=1)
        for m in range(2)
    ]
    out = dot(jnp.concatenate(halves, axis=0), jnp.concatenate([pattern, pattern], axis=1), NT)
    return jnp.concatenate([out[0:rows], out[rows : 2 * rows]], axis=1)


def spread_taps(taps, half):
    factors = inside(half * half, half)
    total = None
    for dx in (-1, 0, 1):
        column = None
        for dy in (-1, 0, 1):
            s = 3 * (1 - dy) + (1 - dx)
            part = moved_by(taps[32 * s : 32 * s + 32], dy * half, factors[dy + 1][1])
            column = part if column is None else column + part
        column = moved_by(column, dx, factors[dx + 1][0])
        total = column if total is None else total + column
    return total


def inner_body(
    count,
    own_next_ref, own_near_ref, next_ref, near_ref, k1_ref, k2_ref, to_kernel_ref, to_flat_ref,
    feat_ref, send_ref, part_ref, pre_ref, act_ref, pre_two_ref, far_one_ref,
    term_ref, pair_ref, rows_ref, out_ref,
):
    slabs = lax.axis_size("space")
    me = lax.axis_index("space")
    half = 16

    odd = me % 2 == 1
    own = unfold(own_near_ref[0:64].astype(F32), 16)
    near, following = near_ref[0:64].astype(F32), next_ref[0:64].astype(F32)
    left = unfold(jnp.where(odd, near, following), 16)
    right = unfold(jnp.where(odd, following, near), 16)
    top = lax.broadcasted_iota(jnp.int32, (8, LANES), 0) < 4
    edges = (
        jnp.where(top, 0.0, pltpu.roll(own[0:8], 4, 0)),
        jnp.where(top, pltpu.roll(left[8:16], 4, 0), pltpu.roll(right[0:8], 4, 0)),
        jnp.where(top, pltpu.roll(own[8:16], 4, 0), 0.0),
    )
    moved_edges = all_shifts(jnp.concatenate(edges, axis=0), 2 * half)
    moved = all_shifts(jnp.concatenate([left, own, right], axis=0).astype(BF16), 2 * half)
    patches = []
    for g in range(3):
        rows = [m[8 * g : 8 * g + 8] for m in moved_edges] + [jnp.zeros((40, LANES), F32)]
        rows = jnp.concatenate(rows, axis=0).astype(BF16)
        patches.append(jnp.concatenate([*(m[16 * g : 16 * g + 16] for m in moved), rows], axis=0))

    k1t = k1_ref[...].astype(F32).reshape(108, 32).T.astype(BF16)
    k2 = k2_ref[...]
    two_by_dz = jnp.concatenate(
        [k2[288 * dz : 288 * dz + 256].astype(F32).T for dz in range(3)], axis=0
    ).astype(BF16)
    nothing = jnp.zeros((288, 64), BF16)
    ninth = []
    for p in range(4):
        taps = [q + 1 - p for q in range(4)]
        taps = [k2[288 * dz + 256 : 288 * dz + 288] if 0 <= dz < 3 else nothing[0:32] for dz in taps]
        ninth.append(jnp.concatenate(taps, axis=0).astype(F32).T)
    ninth = jnp.concatenate(ninth, axis=0).astype(BF16)
    back = jnp.concatenate(
        [jnp.concatenate([k2, nothing], axis=0), jnp.concatenate([nothing, k2], axis=0)], axis=1
    )
    banded = jnp.concatenate(
        [dot(k1t, to_kernel_ref[p], NT).astype(BF16) for p in range(4)], axis=0
    )
    far_one_ref[...] = jnp.concatenate(
        [dot(k1t, to_kernel_ref[p, 144:216], NT).astype(BF16) for p in (0, 3)], axis=0
    )
    pattern = pool_pattern()

    pre = dot(banded, patches[0])
    pre_ref[0:32] = pre[0:32]
    act, s = silu_parts(pre[32:128])
    act_ref[0:32] = act[0:32]
    slopes = [(s + act * (1.0 - s))[32:96]]
    sums = [act[32:64] + act[64:96]]
    act, s = silu_parts(dot(banded, patches[1]))
    slopes.append(s + act * (1.0 - s))
    sums += [act[0:32] + act[32:64], act[64:96] + act[96:128]]
    pre = dot(banded, patches[2])
    pre_ref[32:64] = pre[96:128]
    act, s = silu_parts(pre[0:96])
    act_ref[32:64] = act[64:96]
    slopes.append((s + act * (1.0 - s))[0:64])
    sums += [act[0:32] + act[32:64]]
    pooled = pool_sums(jnp.concatenate(sums, axis=0), pattern)
    plane = lax.shift_right_logical(lax.broadcasted_iota(jnp.int32, pooled.shape, 0), 5)
    real = ((plane > 0) | (me > 0)) & ((plane < 3) | (me < slabs - 1))
    pooled = jnp.where(real, pooled, 0.0).astype(BF16)

    moved = all_shifts(pooled, half)
    planes = [jnp.concatenate([m[32 * q : 32 * q + 32] for m in moved], axis=0) for q in range(4)]
    pre_two = dot(ninth, moved[8])
    pre_two = [pre_two[64 * p : 64 * p + 64] for p in range(4)]
    for q, columns in enumerate(planes):
        by_dz = dot(two_by_dz, columns[0:256])
        for dz in range(3):
            p = q + 1 - dz
            if 0 <= p < 4:
                pre_two[p] = pre_two[p] + by_dz[64 * dz : 64 * dz + 64]
    pre_two_ref[0], pre_two_ref[1] = pre_two[0], pre_two[3]

    own_cots = own_near_ref[64:128].astype(F32), own_next_ref[64:128].astype(F32)
    cots = jnp.where(odd, *own_cots), jnp.where(odd, *own_cots[::-1])
    deltas = []
    for p in range(2):
        act, s = silu_parts(pre_two[p + 1])
        feat_ref[p] = act.astype(BF16)
        deltas.append((cots[p] * (s + act * (1.0 - s))).astype(BF16))

    share = 64 // slabs

    def place(columns, at):
        for first in range(0, columns.shape[1], 128):
            tile = (at + first) % HALF // 128
            rows_ref[tile] = columns[:, first : first + 128]
            for r in range(share):
                target = pl.ds((at + first) // HALF * share + r, slabs, stride=2 * share)
                out_ref[tile, target, :] = rows_ref[tile, pl.ds(r, slabs, stride=share), :]

    both = jnp.concatenate(deltas, axis=0)
    products = [dot(columns, both, NT) for columns in planes]
    for dz in range(3):
        term = products[dz] + pltpu.roll(products[dz + 1], 64, 1)
        term_ref[288 * dz : 288 * dz + 288] = term * (1.0 / math.sqrt(count // 8))
    rows = jnp.concatenate([term_ref[pl.ds(ch, 27, stride=32), :] for ch in range(32)], axis=0)
    place(rows[0:HALF].T[0:64], 0)
    rows = jnp.concatenate([rows[HALF:864], jnp.zeros((ONE_AT - 864, 128), F32)], axis=0)
    place(rows.T[0:64], HALF)

    taps = dot(back, both)
    grads = [spread_taps(taps[288 * p : 288 * p + 288], half) for p in range(4)]
    part_ref[0], part_ref[1] = grads[1], grads[2]

    grads = jnp.where(real, jnp.concatenate(grads, axis=0), 0.0)
    spread = spread_cells(grads, pattern)
    spread = [spread[32 * q : 32 * q + 32] for q in range(4)]
    wide = []
    for g, under in enumerate(((0,), (1, 2), (3,))):
        field = jnp.concatenate([spread[q] for q in under for _ in range(2)], axis=0)
        wide.append(dot((field * slopes[g]).astype(BF16), patches[g], NT))
    wide = wide[1] + jnp.concatenate([wide[2], wide[0]], axis=0)
    wide = jnp.concatenate([wide[32 * p : 32 * p + 32] for p in range(4)], axis=1)
    high = wide.astype(BF16)
    low = (wide - high.astype(F32)).astype(BF16)
    term_one = dot(jnp.concatenate([high, low], axis=0), to_flat_ref[...])
    term_one = (term_one[0:32] + term_one[32:64]) * (1.0 / math.sqrt(count))
    for h, half_row in enumerate((term_one, pltpu.roll(term_one, 64, 1))):
        pair_ref[pl.ds(h, 32, stride=2), :] = half_row
    rows = pair_ref[...]
    rounded = rows.astype(BF16).astype(F32)
    lane = lax.broadcasted_iota(jnp.int32, rows.shape, 1)
    pair = jnp.where(lane < 64, rounded, pltpu.roll(rows - rounded, 64, 1))
    place(pair, ONE_AT)
    for tile in range(4):
        send_ref[:, 128 * tile : 128 * tile + 128] = out_ref[tile].astype(BF16)


def outer_body(
    far_next_ref, far_near_ref, next_ref, near_ref, k2_ref,
    feat_ref, part_ref, pre_ref, act_ref, pre_two_ref, far_one_ref,
    feat_out, pgrad_out,
):
    slabs = lax.axis_size("space")
    me = lax.axis_index("space")
    half = 16
    odd, upper = me % 2 == 1, (me // 2) % 2 == 1
    pattern = pool_pattern()
    far_near, far_next = far_near_ref[...].astype(F32), far_next_ref[...].astype(F32)
    far_left, far_right = jnp.where(upper, far_near, far_next), jnp.where(upper, far_next, far_near)
    top = lax.broadcasted_iota(jnp.int32, (8, LANES), 0) < 4
    edge = jnp.where(
        top,
        jnp.concatenate([far_left, pltpu.roll(far_left, 4, 0)], axis=1),
        jnp.concatenate([pltpu.roll(far_right, 4, 0), far_right], axis=1),
    )
    patches = jnp.concatenate(all_shifts(edge, 2 * half), axis=0).astype(BF16)
    act, _ = silu_parts(pre_ref[...] + dot(far_one_ref[...], patches))
    pooled = pool_sums(act_ref[...] + act, pattern)
    plane = lax.shift_right_logical(lax.broadcasted_iota(jnp.int32, pooled.shape, 0), 5)
    real = ((plane > 0) | (me > 0)) & ((plane < 1) | (me < slabs - 1))
    pooled = jnp.where(real, pooled, 0.0).astype(BF16)
    moved = all_shifts(pooled, half)

    near, following = near_ref[64:128].astype(F32), next_ref[64:128].astype(F32)
    cots = jnp.where(odd, near, following), jnp.where(odd, following, near)
    for p in range(2):
        columns = jnp.concatenate([m[32 * p : 32 * p + 32] for m in moved], axis=0)
        weights = k2_ref[576 * p : 576 * p + 288].astype(F32).T.astype(BF16)
        pre = pre_two_ref[p] + dot(weights, columns)
        act, s = silu_parts(pre)
        delta = (cots[p] * (s + act * (1.0 - s))).astype(BF16)
        taps = dot(k2_ref[576 * (1 - p) : 576 * (1 - p) + 288], delta)
        pgrad_out[0, :, p, :] = (part_ref[p] + spread_taps(taps, half)).astype(BF16)
        feat_out[0, :, p, :] = feat_ref[p]


def on_device(volumes, kernel_one, kernel_two, cotangent):
    _, cin, planes, width, _ = volumes.shape
    half = width // 2
    slabs = lax.axis_size("space")
    copies = lax.axis_size("dp")
    count = copies * planes * slabs * width * width

    to_kernel, to_flat = band_maps()
    weights = (
        jnp.transpose(kernel_one, (2, 3, 4, 1, 0)).reshape(27, 4, 32),
        jnp.transpose(kernel_two, (2, 3, 4, 1, 0)).reshape(864, 64),
        jnp.asarray(to_kernel, BF16),
        jnp.asarray(to_flat, BF16),
    )

    def in_hbm(*arrays):
        return [pltpu.with_memory_space_constraint(x, pltpu.HBM) for x in arrays]

    inputs = in_hbm(volumes, cotangent, *weights)
    hbm = pl.BlockSpec(memory_space=pltpu.HBM)
    limit = pltpu.CompilerParams(vmem_limit_bytes=48 * 1024 * 1024)
    whole = jax.ShapeDtypeStruct((128, width * width // 4), BF16)
    part = jax.ShapeDtypeStruct((2 * cin, width * width // 2), BF16)
    to_next, to_near, to_far_next, to_far_near, *weights = pl.pallas_call(
        prepare_body,
        out_shape=(
            whole, whole, part, part, *(jax.ShapeDtypeStruct(w.shape, BF16) for w in weights)
        ),
        in_specs=[hbm] * len(inputs),
        scratch_shapes=[
            pltpu.VMEM(volumes.shape, BF16),
            pltpu.VMEM(cotangent.shape, BF16),
            pltpu.VMEM((planes * cin * width, width), F32),
            pltpu.SemaphoreType.DMA((len(inputs),)),
        ],
        compiler_params=limit,
    )(*inputs)

    def swap(block, pairs):
        pairs = [p for p in pairs if max(p) < slabs]
        return lax.ppermute(block, "space", pairs + [(t, f) for f, t in pairs])

    evens = range(0, slabs, 2)
    fours = [i + j for i in range(0, slabs, 4) for j in range(2)]
    following = swap(to_next, [(i + 1, i + 2) for i in evens])
    near = swap(to_near, [(i, i + 1) for i in evens])
    far_next = swap(to_far_next, [(i + 2, i + 4) for i in fours])

    cells = half * half
    shapes = {
        "features": ((2, 64, cells), BF16),
        "send": ((128, HALF), BF16),
        "part": ((2, 32, cells), F32),
        "pre": ((64, LANES), F32),
        "act": ((64, LANES), F32),
        "pre_two": ((2, 64, cells), F32),
        "far_one": ((64, 72), BF16),
    }
    feat, send, *inner = pl.pallas_call(
        functools.partial(inner_body, count),
        out_shape=tuple(jax.ShapeDtypeStruct(*x) for x in shapes.values()),
        scratch_shapes=[
            pltpu.VMEM(shape, F32) for shape in ((864, 128), (64, 128), (4, 64, 128), (4, 128, 128))
        ],
        compiler_params=limit,
        cost_estimate=pl.CostEstimate(flops=2 * 10**10, bytes_accessed=2 * 10**6, transcendentals=10**6),
    )(to_next, to_near, following, near, *weights)
    share = 64 // slabs
    send, far_next = lax.optimization_barrier((send.reshape(slabs, 2 * share, HALF), far_next))
    send = pltpu.with_memory_space_constraint(send, pltpu.VMEM)
    parts = lax.all_to_all(send, "space", 0, 0, tiled=True)
    _, to_far_near = lax.optimization_barrier((send, to_far_near))
    far_near = swap(to_far_near, [(i, i + 2) for i in fours])
    features, pooled_grad = pl.pallas_call(
        outer_body,
        out_shape=(
            jax.ShapeDtypeStruct((1, 64, 2, cells), BF16),
            jax.ShapeDtypeStruct((1, 32, 2, cells), BF16),
        ),
        compiler_params=limit,
        cost_estimate=pl.CostEstimate(flops=2 * 10**9, bytes_accessed=10**6, transcendentals=10**5),
    )(far_next, far_near, following, near, weights[1], feat, *inner)
    parts, features, pooled_grad = lax.optimization_barrier((parts, features, pooled_grad))
    total = pl.pallas_call(
        sum_body,
        out_shape=jax.ShapeDtypeStruct(parts.shape[1:], F32),
        compiler_params=limit,
    )(parts)

    def other_core(block, step):
        return lax.ppermute(block, "dp", [(i, i ^ step) for i in range(copies)])

    step = 1
    while 2 * step < copies:
        total = total + other_core(total, step)
        step *= 2
    other = other_core(total, step)
    grad_one, grad_two = pl.pallas_call(
        finish_body,
        out_shape=(jax.ShapeDtypeStruct((share * 54,), F32), jax.ShapeDtypeStruct((share * 864,), F32)),
        compiler_params=limit,
    )(total, other)
    return (features, pooled_grad, grad_one, grad_two)


def solution(mesh):
    in_specs = (P("dp", None, "space", None, None), P(), P(), P("dp", None, "space", None))
    out_specs = (P("dp", None, "space", None), P("dp", None, "space", None), P("space"), P("space"))
    return jax.shard_map(
        on_device, mesh=mesh, in_specs=in_specs, out_specs=out_specs, check_vma=False
    )
```

```python
import functools
import math

import jax
import jax.numpy as jnp
import numpy as np
from jax import lax
from jax.experimental import pallas as pl
from jax.experimental.pallas import tpu as pltpu
from jax.sharding import PartitionSpec as P

F32 = jnp.float32
BF16 = jnp.bfloat16
SHIFTS = [(dy, dx) for dy in (-1, 0, 1) for dx in (-1, 0, 1)]
NN = (((1,), (0,)), ((), ()))
NT = (((1,), (1,)), ((), ()))
LANES = 1024
HALF = 512
ONE_AT = 896


def dot(a, b, dims=NN):
    return lax.dot_general(a, b, dims, preferred_element_type=F32)


def inside(cells, width):
    lane = lax.broadcasted_iota(jnp.int32, (1, cells), 1)
    col, row = lane & (width - 1), lax.shift_right_logical(lane, width.bit_length() - 1)

    def factor(pos, step):
        if step == 0:
            return None
        return jnp.where(pos < width - 1 if step > 0 else pos > 0, 1.0, 0.0)

    return [(factor(col, d), factor(row, d)) for d in (-1, 0, 1)]


def moved_by(field, move, factor):
    return field if move == 0 else pltpu.roll(field, (-move) % field.shape[1], 1) * factor


def all_shifts(field, width):
    factors = [
        [f if f is None else f.astype(field.dtype) for f in pair]
        for pair in inside(field.shape[1], width)
    ]
    across = [moved_by(field, dx, factors[dx + 1][0]) for dx in (-1, 0, 1)]
    return [moved_by(across[dx + 1], dy * width, factors[dy + 1][1]) for dy, dx in SHIFTS]


def pool_pattern():
    cell = lax.broadcasted_iota(jnp.int32, (512, 128), 0)
    block = lax.broadcasted_iota(jnp.int32, (512, 128), 1)
    at = 16 * lax.shift_right_logical(cell, 6) + lax.shift_right_logical(cell & 31, 1)
    return jnp.where(at == block, 0.125, 0.0).astype(BF16)


def silu_parts(v):
    s = 0.5 + 0.5 * jnp.tanh(0.5 * v)
    return v * s, s


def band_maps():
    to_kernel = np.zeros((4, 256, 108), np.float32)
    to_flat = np.zeros((4, 256, 128), np.float32)
    for p in range(4):
        for s in range(9):
            for dz in range(3):
                q = p + dz - 1
                for ci in range(4):
                    if 0 <= q <= 3:
                        row = 16 * s + 4 * q + ci
                    else:
                        row = 144 + 8 * s + (0 if q < 0 else 4) + ci
                    tap = 9 * dz + s
                    to_kernel[p, row, 4 * tap + ci] = 1
                    to_flat[p, row, 64 * (ci // 2) + 27 * (ci % 2) + tap] = 1
    return to_kernel, to_flat.reshape(1024, 128)


def prepare_body(
    vol_hbm, cot_hbm, *refs,
):
    weights, (next_ref, near_ref, far_next_ref, far_near_ref) = refs[:4], refs[4:8]
    kept, (vol_ref, cot_ref, cells_ref, sems) = refs[8:12], refs[12:]
    me = lax.axis_index("space")
    odd, upper = me % 2 == 1, (me // 2) % 2 == 1
    vol_copy = pltpu.make_async_copy(vol_hbm, vol_ref, sems.at[0])
    cot_copy = pltpu.make_async_copy(cot_hbm, cot_ref, sems.at[1])
    vol_copy.start()
    cot_copy.start()
    copies = [
        pltpu.make_async_copy(src, dst, sems.at[2 + i])
        for i, (src, dst) in enumerate(zip(weights, kept))
    ]
    for copy in copies:
        copy.start()
    vol_copy.wait()
    cin, planes, width = vol_ref.shape[1:4]
    for plane in range(planes):
        for ch in range(cin):
            at = (plane * cin + ch) * width
            cells_ref[at : at + width] = vol_ref[0, ch, plane].astype(F32)
    count = planes * cin
    blocks = []
    for b in range(4):
        lines = [cells_ref[pl.ds(8 * b + y, count, stride=width), :] for y in range(8)]
        rows = jnp.concatenate(lines, axis=1)
        near_ref[count * b : count * b + count] = rows.astype(BF16)
        next_ref[count * b : count * b + count] = rows.astype(BF16)
        blocks.append(rows)
    halves = [jnp.concatenate(blocks[2 * m : 2 * m + 2], axis=1) for m in range(2)]
    top = lax.broadcasted_iota(jnp.int32, (8, HALF), 0) < 4
    first = jnp.where(top, halves[0][0:8], pltpu.roll(halves[1][0:8], 4, 0))
    last = jnp.where(top, pltpu.roll(halves[0][8:16], 4, 0), halves[1][8:16])
    far_near_ref[...] = jnp.where(upper, first, last).astype(BF16)
    far_next_ref[...] = jnp.where(upper, last, first).astype(BF16)
    cot_copy.wait()
    cot = cot_ref[0].astype(F32)
    cots = (cot[:, 0, :], cot[:, 1, :])
    near_ref[64:128] = jnp.where(odd, cots[0], cots[1]).astype(BF16)
    next_ref[64:128] = jnp.where(odd, cots[1], cots[0]).astype(BF16)
    for copy in copies:
        copy.wait()


def sum_body(parts_ref, total_ref):
    total = parts_ref[0].astype(F32)
    for i in range(1, parts_ref.shape[0]):
        total = total + parts_ref[i].astype(F32)
    total_ref[...] = total


def finish_body(mine_ref, other_ref, one_ref, two_ref):
    total = mine_ref[...] + other_ref[...]
    share = total.shape[0] // 2
    total = jnp.concatenate([total[0:share], total[share:]], axis=1)
    two_ref[...] = jnp.concatenate([total[r, 0:864] for r in range(share)])
    one = total[:, ONE_AT : ONE_AT + 54] + total[:, ONE_AT + 64 : ONE_AT + 118]
    one_ref[...] = jnp.concatenate([one[r] for r in range(share)])


def unfold(block, rows):
    return jnp.concatenate([block[rows * b : rows * b + rows] for b in range(4)], axis=1)


def pool_sums(sums, pattern):
    rows = sums.shape[0]
    high = sums.astype(BF16)
    low = (sums - high.astype(F32)).astype(BF16)
    halves = [part[:, 512 * m : 512 * m + 512] for part in (high, low) for m in range(2)]
    out = dot(jnp.concatenate(halves, axis=0), pattern)
    out = out[0 : 2 * rows] + out[2 * rows : 4 * rows]
    return jnp.concatenate([out[0:rows], out[rows : 2 * rows]], axis=1)


def spread_cells(field, pattern):
    rows = field.shape[0]
    high = field.astype(BF16)
    low = (field - high.astype(F32)).astype(BF16)
    halves = [
        jnp.concatenate([part[:, 128 * m : 128 * m + 128] for part in (high, low)], axis=1)
        for m in range(2)
    ]
    out = dot(jnp.concatenate(halves, axis=0), jnp.concatenate([pattern, pattern], axis=1), NT)
    return jnp.concatenate([out[0:rows], out[rows : 2 * rows]], axis=1)


def spread_taps(taps, half):
    factors = inside(half * half, half)
    total = None
    for dx in (-1, 0, 1):
        column = None
        for dy in (-1, 0, 1):
            s = 3 * (1 - dy) + (1 - dx)
            part = moved_by(taps[32 * s : 32 * s + 32], dy * half, factors[dy + 1][1])
            column = part if column is None else column + part
        column = moved_by(column, dx, factors[dx + 1][0])
        total = column if total is None else total + column
    return total


def inner_body(
    count,
    own_next_ref, own_near_ref, next_ref, near_ref, k1_ref, k2_ref, to_kernel_ref, to_flat_ref,
    feat_ref, send_ref, part_ref, pre_ref, act_ref, pre_two_ref, far_one_ref, far_two_ref,
    term_ref, pair_ref, rows_ref, out_ref,
):
    slabs = lax.axis_size("space")
    me = lax.axis_index("space")
    half = 16

    odd = me % 2 == 1
    own = unfold(own_near_ref[0:64].astype(F32), 16)
    near, following = near_ref[0:64].astype(F32), next_ref[0:64].astype(F32)
    left = unfold(jnp.where(odd, near, following), 16)
    right = unfold(jnp.where(odd, following, near), 16)
    top = lax.broadcasted_iota(jnp.int32, (8, LANES), 0) < 4
    edges = (
        jnp.where(top, 0.0, pltpu.roll(own[0:8], 4, 0)),
        jnp.where(top, pltpu.roll(left[8:16], 4, 0), pltpu.roll(right[0:8], 4, 0)),
        jnp.where(top, pltpu.roll(own[8:16], 4, 0), 0.0),
    )
    moved_edges = all_shifts(jnp.concatenate(edges, axis=0), 2 * half)
    moved = all_shifts(jnp.concatenate([left, own, right], axis=0).astype(BF16), 2 * half)
    patches = []
    for g in range(3):
        rows = [m[8 * g : 8 * g + 8] for m in moved_edges] + [jnp.zeros((40, LANES), F32)]
        rows = jnp.concatenate(rows, axis=0).astype(BF16)
        patches.append(jnp.concatenate([*(m[16 * g : 16 * g + 16] for m in moved), rows], axis=0))

    k1t = k1_ref[...].astype(F32).reshape(108, 32).T.astype(BF16)
    two_by_dz = jnp.concatenate(
        [k2_ref[288 * dz : 288 * dz + 288].astype(F32).T for dz in range(3)], axis=0
    ).astype(BF16)
    banded = jnp.concatenate(
        [dot(k1t, to_kernel_ref[p], NT).astype(BF16) for p in range(4)], axis=0
    )
    far_one_ref[...] = jnp.concatenate(
        [dot(k1t, to_kernel_ref[p, 144:216], NT).astype(BF16) for p in (0, 3)], axis=0
    )
    far_two_ref[0] = two_by_dz[0:64]
    far_two_ref[1] = two_by_dz[128:192]
    pattern = pool_pattern()

    pre = dot(banded, patches[0])
    pre_ref[0:32] = pre[0:32]
    act, s = silu_parts(pre[32:128])
    act_ref[0:32] = act[0:32]
    slopes = [(s + act * (1.0 - s))[32:96]]
    sums = [act[32:64] + act[64:96]]
    act, s = silu_parts(dot(banded, patches[1]))
    slopes.append(s + act * (1.0 - s))
    sums += [act[0:32] + act[32:64], act[64:96] + act[96:128]]
    pre = dot(banded, patches[2])
    pre_ref[32:64] = pre[96:128]
    act, s = silu_parts(pre[0:96])
    act_ref[32:64] = act[64:96]
    slopes.append((s + act * (1.0 - s))[0:64])
    sums += [act[0:32] + act[32:64]]
    pooled = pool_sums(jnp.concatenate(sums, axis=0), pattern)
    plane = lax.shift_right_logical(lax.broadcasted_iota(jnp.int32, pooled.shape, 0), 5)
    real = ((plane > 0) | (me > 0)) & ((plane < 3) | (me < slabs - 1))
    pooled = jnp.where(real, pooled, 0.0).astype(BF16)

    moved = all_shifts(pooled, half)
    planes = [jnp.concatenate([m[32 * q : 32 * q + 32] for m in moved], axis=0) for q in range(4)]
    pre_two = [None] * 4
    for q, columns in enumerate(planes):
        by_dz = dot(two_by_dz, columns)
        for dz in range(3):
            p = q + 1 - dz
            if 0 <= p < 4:
                part = by_dz[64 * dz : 64 * dz + 64]
                pre_two[p] = part if pre_two[p] is None else pre_two[p] + part
    pre_two_ref[0], pre_two_ref[1] = pre_two[0], pre_two[3]

    own_cots = own_near_ref[64:128].astype(F32), own_next_ref[64:128].astype(F32)
    cots = jnp.where(odd, *own_cots), jnp.where(odd, *own_cots[::-1])
    deltas = []
    for p in range(2):
        act, s = silu_parts(pre_two[p + 1])
        feat_ref[p] = act.astype(BF16)
        deltas.append((cots[p] * (s + act * (1.0 - s))).astype(BF16))

    share = 64 // slabs

    def place(columns, at):
        for first in range(0, columns.shape[1], 128):
            tile = (at + first) % HALF // 128
            rows_ref[tile] = columns[:, first : first + 128]
            for r in range(share):
                target = pl.ds((at + first) // HALF * share + r, slabs, stride=2 * share)
                out_ref[tile, target, :] = rows_ref[tile, pl.ds(r, slabs, stride=share), :]

    both = jnp.concatenate(deltas, axis=0)
    products = [dot(columns, both, NT) for columns in planes]
    for dz in range(3):
        term = products[dz] + pltpu.roll(products[dz + 1], 64, 1)
        term_ref[288 * dz : 288 * dz + 288] = term * (1.0 / math.sqrt(count // 8))
    rows = jnp.concatenate([term_ref[pl.ds(ch, 27, stride=32), :] for ch in range(32)], axis=0)
    place(rows[0:HALF].T[0:64], 0)
    rows = jnp.concatenate([rows[HALF:864], jnp.zeros((ONE_AT - 864, 128), F32)], axis=0)
    place(rows.T[0:64], HALF)

    grads = []
    for p in range(-1, 3):
        sources = [q for q in range(2) if abs(q - p) < 2]
        taps = [k2_ref[288 * (1 + p - q) : 288 * (1 + p - q) + 288] for q in sources]
        given = jnp.concatenate([deltas[q] for q in sources], axis=0)
        grads.append(spread_taps(dot(jnp.concatenate(taps, axis=1), given), half))
    part_ref[0], part_ref[1] = grads[1], grads[2]

    grads = jnp.where(real, jnp.concatenate(grads, axis=0), 0.0)
    spread = spread_cells(grads, pattern)
    spread = [spread[32 * q : 32 * q + 32] for q in range(4)]
    wide = []
    for g, under in enumerate(((0,), (1, 2), (3,))):
        field = jnp.concatenate([spread[q] for q in under for _ in range(2)], axis=0)
        wide.append(dot((field * slopes[g]).astype(BF16), patches[g], NT))
    wide = wide[1] + jnp.concatenate([wide[2], wide[0]], axis=0)
    wide = jnp.concatenate([wide[32 * p : 32 * p + 32] for p in range(4)], axis=1)
    high = wide.astype(BF16)
    low = (wide - high.astype(F32)).astype(BF16)
    term_one = dot(jnp.concatenate([high, low], axis=0), to_flat_ref[...])
    term_one = (term_one[0:32] + term_one[32:64]) * (1.0 / math.sqrt(count))
    for h, half_row in enumerate((term_one, pltpu.roll(term_one, 64, 1))):
        pair_ref[pl.ds(h, 32, stride=2), :] = half_row
    rows = pair_ref[...]
    rounded = rows.astype(BF16).astype(F32)
    lane = lax.broadcasted_iota(jnp.int32, rows.shape, 1)
    pair = jnp.where(lane < 64, rounded, pltpu.roll(rows - rounded, 64, 1))
    place(pair, ONE_AT)
    for tile in range(4):
        send_ref[:, 128 * tile : 128 * tile + 128] = out_ref[tile].astype(BF16)


def outer_body(
    far_next_ref, far_near_ref, next_ref, near_ref, k2_ref,
    feat_ref, part_ref, pre_ref, act_ref, pre_two_ref, far_one_ref, far_two_ref,
    feat_out, pgrad_out,
):
    slabs = lax.axis_size("space")
    me = lax.axis_index("space")
    half = 16
    odd, upper = me % 2 == 1, (me // 2) % 2 == 1
    pattern = pool_pattern()
    far_near, far_next = far_near_ref[...].astype(F32), far_next_ref[...].astype(F32)
    far_left, far_right = jnp.where(upper, far_near, far_next), jnp.where(upper, far_next, far_near)
    top = lax.broadcasted_iota(jnp.int32, (8, LANES), 0) < 4
    edge = jnp.where(
        top,
        jnp.concatenate([far_left, pltpu.roll(far_left, 4, 0)], axis=1),
        jnp.concatenate([pltpu.roll(far_right, 4, 0), far_right], axis=1),
    )
    patches = jnp.concatenate(all_shifts(edge, 2 * half), axis=0).astype(BF16)
    act, _ = silu_parts(pre_ref[...] + dot(far_one_ref[...], patches))
    pooled = pool_sums(act_ref[...] + act, pattern)
    plane = lax.shift_right_logical(lax.broadcasted_iota(jnp.int32, pooled.shape, 0), 5)
    real = ((plane > 0) | (me > 0)) & ((plane < 1) | (me < slabs - 1))
    pooled = jnp.where(real, pooled, 0.0).astype(BF16)
    moved = all_shifts(pooled, half)

    near, following = near_ref[64:128].astype(F32), next_ref[64:128].astype(F32)
    cots = jnp.where(odd, near, following), jnp.where(odd, following, near)
    for p in range(2):
        columns = jnp.concatenate([m[32 * p : 32 * p + 32] for m in moved], axis=0)
        pre = pre_two_ref[p] + dot(far_two_ref[p], columns)
        act, s = silu_parts(pre)
        delta = (cots[p] * (s + act * (1.0 - s))).astype(BF16)
        taps = dot(k2_ref[576 * (1 - p) : 576 * (1 - p) + 288], delta)
        pgrad_out[0, :, p, :] = (part_ref[p] + spread_taps(taps, half)).astype(BF16)
        feat_out[0, :, p, :] = feat_ref[p]


def on_device(volumes, kernel_one, kernel_two, cotangent):
    _, cin, planes, width, _ = volumes.shape
    half = width // 2
    slabs = lax.axis_size("space")
    copies = lax.axis_size("dp")
    count = copies * planes * slabs * width * width

    to_kernel, to_flat = band_maps()
    weights = (
        jnp.transpose(kernel_one, (2, 3, 4, 1, 0)).reshape(27, 4, 32),
        jnp.transpose(kernel_two, (2, 3, 4, 1, 0)).reshape(864, 64),
        jnp.asarray(to_kernel, BF16),
        jnp.asarray(to_flat, BF16),
    )

    def in_hbm(*arrays):
        return [pltpu.with_memory_space_constraint(x, pltpu.HBM) for x in arrays]

    inputs = in_hbm(volumes, cotangent, *weights)
    hbm = pl.BlockSpec(memory_space=pltpu.HBM)
    limit = pltpu.CompilerParams(vmem_limit_bytes=48 * 1024 * 1024)
    whole = jax.ShapeDtypeStruct((128, width * width // 4), BF16)
    part = jax.ShapeDtypeStruct((2 * cin, width * width // 2), BF16)
    to_next, to_near, to_far_next, to_far_near, *weights = pl.pallas_call(
        prepare_body,
        out_shape=(
            whole, whole, part, part, *(jax.ShapeDtypeStruct(w.shape, BF16) for w in weights)
        ),
        in_specs=[hbm] * len(inputs),
        scratch_shapes=[
            pltpu.VMEM(volumes.shape, BF16),
            pltpu.VMEM(cotangent.shape, BF16),
            pltpu.VMEM((planes * cin * width, width), F32),
            pltpu.SemaphoreType.DMA((len(inputs),)),
        ],
        compiler_params=limit,
    )(*inputs)

    def swap(block, pairs):
        pairs = [p for p in pairs if max(p) < slabs]
        return lax.ppermute(block, "space", pairs + [(t, f) for f, t in pairs])

    evens = range(0, slabs, 2)
    fours = [i + j for i in range(0, slabs, 4) for j in range(2)]
    following = swap(to_next, [(i + 1, i + 2) for i in evens])
    near = swap(to_near, [(i, i + 1) for i in evens])
    far_next = swap(to_far_next, [(i + 2, i + 4) for i in fours])
    far_near = swap(to_far_near, [(i, i + 2) for i in fours])

    cells = half * half
    shapes = {
        "features": ((2, 64, cells), BF16),
        "send": ((128, HALF), BF16),
        "part": ((2, 32, cells), F32),
        "pre": ((64, LANES), F32),
        "act": ((64, LANES), F32),
        "pre_two": ((2, 64, cells), F32),
        "far_one": ((64, 72), BF16),
        "far_two": ((2, 64, 288), BF16),
    }
    feat, send, *inner = pl.pallas_call(
        functools.partial(inner_body, count),
        out_shape=tuple(jax.ShapeDtypeStruct(*x) for x in shapes.values()),
        scratch_shapes=[
            pltpu.VMEM(shape, F32) for shape in ((864, 128), (64, 128), (4, 64, 128), (4, 128, 128))
        ],
        compiler_params=limit,
        cost_estimate=pl.CostEstimate(flops=2 * 10**10, bytes_accessed=2 * 10**6, transcendentals=10**6),
    )(to_next, to_near, following, near, *weights)
    share = 64 // slabs
    send, far_next, far_near = lax.optimization_barrier(
        (send.reshape(slabs, 2 * share, HALF), far_next, far_near)
    )
    parts = lax.all_to_all(send, "space", 0, 0, tiled=True)
    parts, far_next, far_near = lax.optimization_barrier((parts, far_next, far_near))
    features, pooled_grad = pl.pallas_call(
        outer_body,
        out_shape=(
            jax.ShapeDtypeStruct((1, 64, 2, cells), BF16),
            jax.ShapeDtypeStruct((1, 32, 2, cells), BF16),
        ),
        compiler_params=limit,
        cost_estimate=pl.CostEstimate(flops=2 * 10**9, bytes_accessed=10**6, transcendentals=10**5),
    )(far_next, far_near, following, near, weights[1], feat, *inner)
    total = pl.pallas_call(
        sum_body,
        out_shape=jax.ShapeDtypeStruct(parts.shape[1:], F32),
        compiler_params=limit,
    )(parts)

    def other_core(block, step):
        return lax.ppermute(block, "dp", [(i, i ^ step) for i in range(copies)])

    step = 1
    while 2 * step < copies:
        total = total + other_core(total, step)
        step *= 2
    other = other_core(total, step)
    grad_one, grad_two = pl.pallas_call(
        finish_body,
        out_shape=(jax.ShapeDtypeStruct((share * 54,), F32), jax.ShapeDtypeStruct((share * 864,), F32)),
        compiler_params=limit,
    )(total, other)
    return (features, pooled_grad, grad_one, grad_two)


def solution(mesh):
    in_specs = (P("dp", None, "space", None, None), P(), P(), P("dp", None, "space", None))
    out_specs = (P("dp", None, "space", None), P("dp", None, "space", None), P("space"), P("space"))
    return jax.shard_map(
        on_device, mesh=mesh, in_specs=in_specs, out_specs=out_specs, check_vma=False
    )
```

```python
import functools
import math

import jax
import jax.numpy as jnp
import numpy as np
from jax import lax
from jax.experimental import pallas as pl
from jax.experimental.pallas import tpu as pltpu
from jax.sharding import PartitionSpec as P

F32 = jnp.float32
BF16 = jnp.bfloat16
SHIFTS = [(dy, dx) for dy in (-1, 0, 1) for dx in (-1, 0, 1)]
NN = (((1,), (0,)), ((), ()))
NT = (((1,), (1,)), ((), ()))
LANES = 1024
HALF = 512
ONE_AT = 896


def dot(a, b, dims=NN):
    return lax.dot_general(a, b, dims, preferred_element_type=F32)


def inside(cells, width):
    lane = lax.broadcasted_iota(jnp.int32, (1, cells), 1)
    col, row = lane & (width - 1), lax.shift_right_logical(lane, width.bit_length() - 1)

    def factor(pos, step):
        if step == 0:
            return None
        return jnp.where(pos < width - 1 if step > 0 else pos > 0, 1.0, 0.0)

    return [(factor(col, d), factor(row, d)) for d in (-1, 0, 1)]


def moved_by(field, move, factor):
    return field if move == 0 else pltpu.roll(field, (-move) % field.shape[1], 1) * factor


def all_shifts(field, width):
    factors = [
        [f if f is None else f.astype(field.dtype) for f in pair]
        for pair in inside(field.shape[1], width)
    ]
    across = [moved_by(field, dx, factors[dx + 1][0]) for dx in (-1, 0, 1)]
    return [moved_by(across[dx + 1], dy * width, factors[dy + 1][1]) for dy, dx in SHIFTS]


def pool_pattern():
    cell = lax.broadcasted_iota(jnp.int32, (512, 128), 0)
    block = lax.broadcasted_iota(jnp.int32, (512, 128), 1)
    at = 16 * lax.shift_right_logical(cell, 6) + lax.shift_right_logical(cell & 31, 1)
    return jnp.where(at == block, 0.125, 0.0).astype(BF16)


def silu_parts(v):
    s = 0.5 + 0.5 * jnp.tanh(0.5 * v)
    return v * s, s


def band_maps():
    to_kernel = np.zeros((4, 256, 108), np.float32)
    to_flat = np.zeros((4, 256, 128), np.float32)
    for p in range(4):
        for s in range(9):
            for dz in range(3):
                q = p + dz - 1
                for ci in range(4):
                    if 0 <= q <= 3:
                        row = 16 * s + 4 * q + ci
                    else:
                        row = 144 + 8 * s + (0 if q < 0 else 4) + ci
                    tap = 9 * dz + s
                    to_kernel[p, row, 4 * tap + ci] = 1
                    to_flat[p, row, 64 * (ci // 2) + 27 * (ci % 2) + tap] = 1
    return to_kernel, to_flat.reshape(1024, 128)


def prepare_body(
    vol_hbm, cot_hbm, *refs,
):
    weights, (next_ref, near_ref, far_next_ref, far_near_ref) = refs[:4], refs[4:8]
    kept, (vol_ref, cot_ref, cells_ref, sems) = refs[8:12], refs[12:]
    me = lax.axis_index("space")
    odd, upper = me % 2 == 1, (me // 2) % 2 == 1
    vol_copy = pltpu.make_async_copy(vol_hbm, vol_ref, sems.at[0])
    cot_copy = pltpu.make_async_copy(cot_hbm, cot_ref, sems.at[1])
    vol_copy.start()
    cot_copy.start()
    copies = [
        pltpu.make_async_copy(src, dst, sems.at[2 + i])
        for i, (src, dst) in enumerate(zip(weights, kept))
    ]
    for copy in copies:
        copy.start()
    vol_copy.wait()
    cin, planes, width = vol_ref.shape[1:4]
    for plane in range(planes):
        for ch in range(cin):
            at = (plane * cin + ch) * width
            cells_ref[at : at + width] = vol_ref[0, ch, plane].astype(F32)
    count = planes * cin
    blocks = []
    for b in range(4):
        lines = [cells_ref[pl.ds(8 * b + y, count, stride=width), :] for y in range(8)]
        rows = jnp.concatenate(lines, axis=1)
        near_ref[count * b : count * b + count] = rows.astype(BF16)
        next_ref[count * b : count * b + count] = rows.astype(BF16)
        blocks.append(rows)
    halves = [jnp.concatenate(blocks[2 * m : 2 * m + 2], axis=1) for m in range(2)]
    top = lax.broadcasted_iota(jnp.int32, (8, HALF), 0) < 4
    first = jnp.where(top, halves[0][0:8], pltpu.roll(halves[1][0:8], 4, 0))
    last = jnp.where(top, pltpu.roll(halves[0][8:16], 4, 0), halves[1][8:16])
    far_near_ref[...] = jnp.where(upper, first, last).astype(BF16)
    far_next_ref[...] = jnp.where(upper, last, first).astype(BF16)
    cot_copy.wait()
    cot = cot_ref[0].astype(F32)
    cots = (cot[:, 0, :], cot[:, 1, :])
    near_ref[64:128] = jnp.where(odd, cots[0], cots[1]).astype(BF16)
    next_ref[64:128] = jnp.where(odd, cots[1], cots[0]).astype(BF16)
    for copy in copies:
        copy.wait()


def sum_body(parts_ref, total_ref):
    total = parts_ref[0].astype(F32)
    for i in range(1, parts_ref.shape[0]):
        total = total + parts_ref[i].astype(F32)
    total_ref[...] = total


def finish_body(mine_ref, other_ref, one_ref, two_ref):
    total = mine_ref[...] + other_ref[...]
    share = total.shape[0] // 2
    total = jnp.concatenate([total[0:share], total[share:]], axis=1)
    two_ref[...] = jnp.concatenate([total[r, 0:864] for r in range(share)])
    one = total[:, ONE_AT : ONE_AT + 54] + total[:, ONE_AT + 64 : ONE_AT + 118]
    one_ref[...] = jnp.concatenate([one[r] for r in range(share)])


def unfold(block, rows):
    return jnp.concatenate([block[rows * b : rows * b + rows] for b in range(4)], axis=1)


def pool_sums(sums, pattern):
    rows = sums.shape[0]
    high = sums.astype(BF16)
    low = (sums - high.astype(F32)).astype(BF16)
    halves = [part[:, 512 * m : 512 * m + 512] for part in (high, low) for m in range(2)]
    out = dot(jnp.concatenate(halves, axis=0), pattern)
    out = out[0 : 2 * rows] + out[2 * rows : 4 * rows]
    return jnp.concatenate([out[0:rows], out[rows : 2 * rows]], axis=1)


def spread_cells(field, pattern):
    rows = field.shape[0]
    high = field.astype(BF16)
    low = (field - high.astype(F32)).astype(BF16)
    halves = [
        jnp.concatenate([part[:, 128 * m : 128 * m + 128] for part in (high, low)], axis=1)
        for m in range(2)
    ]
    out = dot(jnp.concatenate(halves, axis=0), jnp.concatenate([pattern, pattern], axis=1), NT)
    return jnp.concatenate([out[0:rows], out[rows : 2 * rows]], axis=1)


def spread_taps(taps, half):
    factors = inside(half * half, half)
    total = None
    for dx in (-1, 0, 1):
        column = None
        for dy in (-1, 0, 1):
            s = 3 * (1 - dy) + (1 - dx)
            part = moved_by(taps[32 * s : 32 * s + 32], dy * half, factors[dy + 1][1])
            column = part if column is None else column + part
        column = moved_by(column, dx, factors[dx + 1][0])
        total = column if total is None else total + column
    return total


def inner_body(
    count,
    own_next_ref, own_near_ref, next_ref, near_ref, k1_ref, k2_ref, to_kernel_ref, to_flat_ref,
    feat_ref, send_hbm, part_ref, pre_ref, act_ref, pre_two_ref, far_one_ref, far_two_ref,
    term_ref, pair_ref, rows_ref, out_ref, rounded_ref, sems,
):
    slabs = lax.axis_size("space")
    me = lax.axis_index("space")
    half = 16

    odd = me % 2 == 1
    own = unfold(own_near_ref[0:64].astype(F32), 16)
    near, following = near_ref[0:64].astype(F32), next_ref[0:64].astype(F32)
    left = unfold(jnp.where(odd, near, following), 16)
    right = unfold(jnp.where(odd, following, near), 16)
    top = lax.broadcasted_iota(jnp.int32, (8, LANES), 0) < 4
    edges = (
        jnp.where(top, 0.0, pltpu.roll(own[0:8], 4, 0)),
        jnp.where(top, pltpu.roll(left[8:16], 4, 0), pltpu.roll(right[0:8], 4, 0)),
        jnp.where(top, pltpu.roll(own[8:16], 4, 0), 0.0),
    )
    moved_edges = all_shifts(jnp.concatenate(edges, axis=0), 2 * half)
    moved = all_shifts(jnp.concatenate([left, own, right], axis=0).astype(BF16), 2 * half)
    patches = []
    for g in range(3):
        rows = [m[8 * g : 8 * g + 8] for m in moved_edges] + [jnp.zeros((40, LANES), F32)]
        rows = jnp.concatenate(rows, axis=0).astype(BF16)
        patches.append(jnp.concatenate([*(m[16 * g : 16 * g + 16] for m in moved), rows], axis=0))

    k1t = k1_ref[...].astype(F32).reshape(108, 32).T.astype(BF16)
    two_by_dz = jnp.concatenate(
        [k2_ref[288 * dz : 288 * dz + 288].astype(F32).T for dz in range(3)], axis=0
    ).astype(BF16)
    banded = jnp.concatenate(
        [dot(k1t, to_kernel_ref[p], NT).astype(BF16) for p in range(4)], axis=0
    )
    far_one_ref[...] = jnp.concatenate(
        [dot(k1t, to_kernel_ref[p, 144:216], NT).astype(BF16) for p in (0, 3)], axis=0
    )
    far_two_ref[0] = two_by_dz[0:64]
    far_two_ref[1] = two_by_dz[128:192]
    pattern = pool_pattern()

    pre = dot(banded, patches[0])
    pre_ref[0:32] = pre[0:32]
    act, s = silu_parts(pre[32:128])
    act_ref[0:32] = act[0:32]
    slopes = [(s + act * (1.0 - s))[32:96]]
    sums = [act[32:64] + act[64:96]]
    act, s = silu_parts(dot(banded, patches[1]))
    slopes.append(s + act * (1.0 - s))
    sums += [act[0:32] + act[32:64], act[64:96] + act[96:128]]
    pre = dot(banded, patches[2])
    pre_ref[32:64] = pre[96:128]
    act, s = silu_parts(pre[0:96])
    act_ref[32:64] = act[64:96]
    slopes.append((s + act * (1.0 - s))[0:64])
    sums += [act[0:32] + act[32:64]]
    pooled = pool_sums(jnp.concatenate(sums, axis=0), pattern)
    plane = lax.shift_right_logical(lax.broadcasted_iota(jnp.int32, pooled.shape, 0), 5)
    real = ((plane > 0) | (me > 0)) & ((plane < 3) | (me < slabs - 1))
    pooled = jnp.where(real, pooled, 0.0).astype(BF16)

    moved = all_shifts(pooled, half)
    planes = [jnp.concatenate([m[32 * q : 32 * q + 32] for m in moved], axis=0) for q in range(4)]
    pre_two = [None] * 4
    for q, columns in enumerate(planes):
        by_dz = dot(two_by_dz, columns)
        for dz in range(3):
            p = q + 1 - dz
            if 0 <= p < 4:
                part = by_dz[64 * dz : 64 * dz + 64]
                pre_two[p] = part if pre_two[p] is None else pre_two[p] + part
    pre_two_ref[0], pre_two_ref[1] = pre_two[0], pre_two[3]

    own_cots = own_near_ref[64:128].astype(F32), own_next_ref[64:128].astype(F32)
    cots = jnp.where(odd, *own_cots), jnp.where(odd, *own_cots[::-1])
    deltas = []
    for p in range(2):
        act, s = silu_parts(pre_two[p + 1])
        feat_ref[p] = act.astype(BF16)
        deltas.append((cots[p] * (s + act * (1.0 - s))).astype(BF16))

    share = 64 // slabs

    def place(columns, at):
        for first in range(0, columns.shape[1], 128):
            tile = (at + first) % HALF // 128
            rows_ref[tile] = columns[:, first : first + 128]
            for r in range(share):
                target = pl.ds((at + first) // HALF * share + r, slabs, stride=2 * share)
                out_ref[tile, target, :] = rows_ref[tile, pl.ds(r, slabs, stride=share), :]

    both = jnp.concatenate(deltas, axis=0)
    products = [dot(columns, both, NT) for columns in planes]
    for dz in range(3):
        term = products[dz] + pltpu.roll(products[dz + 1], 64, 1)
        term_ref[288 * dz : 288 * dz + 288] = term * (1.0 / math.sqrt(count // 8))
    rows = jnp.concatenate([term_ref[pl.ds(ch, 27, stride=32), :] for ch in range(32)], axis=0)
    place(rows[0:HALF].T[0:64], 0)
    rows = jnp.concatenate([rows[HALF:864], jnp.zeros((ONE_AT - 864, 128), F32)], axis=0)
    place(rows.T[0:64], HALF)

    def leave(first, last, sem):
        for tile in range(first, last):
            rounded_ref[:, 128 * tile : 128 * tile + 128] = out_ref[tile].astype(BF16)
        lanes = pl.ds(128 * first, 128 * (last - first))
        copy = pltpu.make_async_copy(rounded_ref.at[:, lanes], send_hbm.at[:, lanes], sem)
        copy.start()
        return copy

    copies = [leave(0, 3, sems.at[0])]

    grads = []
    for p in range(-1, 3):
        sources = [q for q in range(2) if abs(q - p) < 2]
        taps = [k2_ref[288 * (1 + p - q) : 288 * (1 + p - q) + 288] for q in sources]
        given = jnp.concatenate([deltas[q] for q in sources], axis=0)
        grads.append(spread_taps(dot(jnp.concatenate(taps, axis=1), given), half))
    part_ref[0], part_ref[1] = grads[1], grads[2]

    grads = jnp.where(real, jnp.concatenate(grads, axis=0), 0.0)
    spread = spread_cells(grads, pattern)
    spread = [spread[32 * q : 32 * q + 32] for q in range(4)]
    wide = []
    for g, under in enumerate(((0,), (1, 2), (3,))):
        field = jnp.concatenate([spread[q] for q in under for _ in range(2)], axis=0)
        wide.append(dot((field * slopes[g]).astype(BF16), patches[g], NT))
    wide = wide[1] + jnp.concatenate([wide[2], wide[0]], axis=0)
    wide = jnp.concatenate([wide[32 * p : 32 * p + 32] for p in range(4)], axis=1)
    high = wide.astype(BF16)
    low = (wide - high.astype(F32)).astype(BF16)
    term_one = dot(jnp.concatenate([high, low], axis=0), to_flat_ref[...])
    term_one = (term_one[0:32] + term_one[32:64]) * (1.0 / math.sqrt(count))
    for h, half_row in enumerate((term_one, pltpu.roll(term_one, 64, 1))):
        pair_ref[pl.ds(h, 32, stride=2), :] = half_row
    rows = pair_ref[...]
    rounded = rows.astype(BF16).astype(F32)
    lane = lax.broadcasted_iota(jnp.int32, rows.shape, 1)
    pair = jnp.where(lane < 64, rounded, pltpu.roll(rows - rounded, 64, 1))
    place(pair, ONE_AT)
    copies.append(leave(3, 4, sems.at[1]))
    for copy in copies:
        copy.wait()


def outer_body(
    far_next_ref, far_near_ref, next_ref, near_ref, k2_ref,
    feat_ref, part_ref, pre_ref, act_ref, pre_two_ref, far_one_ref, far_two_ref,
    feat_out, pgrad_out,
):
    slabs = lax.axis_size("space")
    me = lax.axis_index("space")
    half = 16
    odd, upper = me % 2 == 1, (me // 2) % 2 == 1
    pattern = pool_pattern()
    far_near, far_next = far_near_ref[...].astype(F32), far_next_ref[...].astype(F32)
    far_left, far_right = jnp.where(upper, far_near, far_next), jnp.where(upper, far_next, far_near)
    top = lax.broadcasted_iota(jnp.int32, (8, LANES), 0) < 4
    edge = jnp.where(
        top,
        jnp.concatenate([far_left, pltpu.roll(far_left, 4, 0)], axis=1),
        jnp.concatenate([pltpu.roll(far_right, 4, 0), far_right], axis=1),
    )
    patches = jnp.concatenate(all_shifts(edge, 2 * half), axis=0).astype(BF16)
    act, _ = silu_parts(pre_ref[...] + dot(far_one_ref[...], patches))
    pooled = pool_sums(act_ref[...] + act, pattern)
    plane = lax.shift_right_logical(lax.broadcasted_iota(jnp.int32, pooled.shape, 0), 5)
    real = ((plane > 0) | (me > 0)) & ((plane < 1) | (me < slabs - 1))
    pooled = jnp.where(real, pooled, 0.0).astype(BF16)
    moved = all_shifts(pooled, half)

    near, following = near_ref[64:128].astype(F32), next_ref[64:128].astype(F32)
    cots = jnp.where(odd, near, following), jnp.where(odd, following, near)
    for p in range(2):
        columns = jnp.concatenate([m[32 * p : 32 * p + 32] for m in moved], axis=0)
        pre = pre_two_ref[p] + dot(far_two_ref[p], columns)
        act, s = silu_parts(pre)
        delta = (cots[p] * (s + act * (1.0 - s))).astype(BF16)
        taps = dot(k2_ref[576 * (1 - p) : 576 * (1 - p) + 288], delta)
        pgrad_out[0, :, p, :] = (part_ref[p] + spread_taps(taps, half)).astype(BF16)
        feat_out[0, :, p, :] = feat_ref[p]


def on_device(volumes, kernel_one, kernel_two, cotangent):
    _, cin, planes, width, _ = volumes.shape
    half = width // 2
    slabs = lax.axis_size("space")
    copies = lax.axis_size("dp")
    count = copies * planes * slabs * width * width

    to_kernel, to_flat = band_maps()
    weights = (
        jnp.transpose(kernel_one, (2, 3, 4, 1, 0)).reshape(27, 4, 32),
        jnp.transpose(kernel_two, (2, 3, 4, 1, 0)).reshape(864, 64),
        jnp.asarray(to_kernel, BF16),
        jnp.asarray(to_flat, BF16),
    )

    def in_hbm(*arrays):
        return [pltpu.with_memory_space_constraint(x, pltpu.HBM) for x in arrays]

    inputs = in_hbm(volumes, cotangent, *weights)
    hbm = pl.BlockSpec(memory_space=pltpu.HBM)
    limit = pltpu.CompilerParams(vmem_limit_bytes=48 * 1024 * 1024)
    whole = jax.ShapeDtypeStruct((128, width * width // 4), BF16)
    part = jax.ShapeDtypeStruct((2 * cin, width * width // 2), BF16)
    to_next, to_near, to_far_next, to_far_near, *weights = pl.pallas_call(
        prepare_body,
        out_shape=(
            whole, whole, part, part, *(jax.ShapeDtypeStruct(w.shape, BF16) for w in weights)
        ),
        in_specs=[hbm] * len(inputs),
        scratch_shapes=[
            pltpu.VMEM(volumes.shape, BF16),
            pltpu.VMEM(cotangent.shape, BF16),
            pltpu.VMEM((planes * cin * width, width), F32),
            pltpu.SemaphoreType.DMA((len(inputs),)),
        ],
        compiler_params=limit,
    )(*inputs)

    def swap(block, pairs):
        pairs = [p for p in pairs if max(p) < slabs]
        return lax.ppermute(block, "space", pairs + [(t, f) for f, t in pairs])

    evens = range(0, slabs, 2)
    fours = [i + j for i in range(0, slabs, 4) for j in range(2)]
    following = swap(to_next, [(i + 1, i + 2) for i in evens])
    near = swap(to_near, [(i, i + 1) for i in evens])
    far_next = swap(to_far_next, [(i + 2, i + 4) for i in fours])

    cells = half * half
    shapes = {
        "features": ((2, 64, cells), BF16),
        "send": ((128, HALF), BF16),
        "part": ((2, 32, cells), F32),
        "pre": ((64, LANES), F32),
        "act": ((64, LANES), F32),
        "pre_two": ((2, 64, cells), F32),
        "far_one": ((64, 72), BF16),
        "far_two": ((2, 64, 288), BF16),
    }
    feat, send, *inner = pl.pallas_call(
        functools.partial(inner_body, count),
        out_shape=tuple(jax.ShapeDtypeStruct(*x) for x in shapes.values()),
        out_specs=tuple(
            pl.BlockSpec(memory_space=pltpu.HBM if name == "send" else pltpu.VMEM) for name in shapes
        ),
        scratch_shapes=[
            *(pltpu.VMEM(x, F32) for x in ((864, 128), (64, 128), (4, 64, 128), (4, 128, 128))),
            pltpu.VMEM((128, HALF), BF16),
            pltpu.SemaphoreType.DMA((2,)),
        ],
        compiler_params=limit,
        cost_estimate=pl.CostEstimate(flops=2 * 10**10, bytes_accessed=2 * 10**6, transcendentals=10**6),
    )(to_next, to_near, following, near, *weights)
    share = 64 // slabs
    send, far_next = lax.optimization_barrier((send.reshape(slabs, 2 * share, HALF), far_next))
    parts = lax.all_to_all(send, "space", 0, 0, tiled=True)
    _, to_far_near = lax.optimization_barrier((send, to_far_near))
    far_near = swap(to_far_near, [(i, i + 2) for i in fours])
    features, pooled_grad = pl.pallas_call(
        outer_body,
        out_shape=(
            jax.ShapeDtypeStruct((1, 64, 2, cells), BF16),
            jax.ShapeDtypeStruct((1, 32, 2, cells), BF16),
        ),
        compiler_params=limit,
        cost_estimate=pl.CostEstimate(flops=2 * 10**9, bytes_accessed=10**6, transcendentals=10**5),
    )(far_next, far_near, following, near, weights[1], feat, *inner)
    parts, features, pooled_grad = lax.optimization_barrier((parts, features, pooled_grad))
    total = pl.pallas_call(
        sum_body,
        out_shape=jax.ShapeDtypeStruct(parts.shape[1:], F32),
        compiler_params=limit,
    )(parts)

    def other_core(block, step):
        return lax.ppermute(block, "dp", [(i, i ^ step) for i in range(copies)])

    step = 1
    while 2 * step < copies:
        total = total + other_core(total, step)
        step *= 2
    other = other_core(total, step)
    grad_one, grad_two = pl.pallas_call(
        finish_body,
        out_shape=(jax.ShapeDtypeStruct((share * 54,), F32), jax.ShapeDtypeStruct((share * 864,), F32)),
        compiler_params=limit,
    )(total, other)
    return (features, pooled_grad, grad_one, grad_two)


def solution(mesh):
    in_specs = (P("dp", None, "space", None, None), P(), P(), P("dp", None, "space", None))
    out_specs = (P("dp", None, "space", None), P("dp", None, "space", None), P("space"), P("space"))
    return jax.shard_map(
        on_device, mesh=mesh, in_specs=in_specs, out_specs=out_specs, check_vma=False
    )
```

```python
import functools
import math

import jax
import jax.numpy as jnp
import numpy as np
from jax import lax
from jax.experimental import pallas as pl
from jax.experimental.pallas import tpu as pltpu
from jax.sharding import PartitionSpec as P

F32 = jnp.float32
BF16 = jnp.bfloat16
SHIFTS = [(dy, dx) for dy in (-1, 0, 1) for dx in (-1, 0, 1)]
NN = (((1,), (0,)), ((), ()))
NT = (((1,), (1,)), ((), ()))
LANES = 1024
HALF = 512
ONE_AT = 896


def dot(a, b, dims=NN):
    return lax.dot_general(a, b, dims, preferred_element_type=F32)


def inside(cells, width):
    lane = lax.broadcasted_iota(jnp.int32, (1, cells), 1)
    col, row = lane & (width - 1), lax.shift_right_logical(lane, width.bit_length() - 1)

    def factor(pos, step):
        if step == 0:
            return None
        return jnp.where(pos < width - 1 if step > 0 else pos > 0, 1.0, 0.0)

    return [(factor(col, d), factor(row, d)) for d in (-1, 0, 1)]


def moved_by(field, move, factor):
    return field if move == 0 else pltpu.roll(field, (-move) % field.shape[1], 1) * factor


def all_shifts(field, width):
    factors = [
        [f if f is None else f.astype(field.dtype) for f in pair]
        for pair in inside(field.shape[1], width)
    ]
    across = [moved_by(field, dx, factors[dx + 1][0]) for dx in (-1, 0, 1)]
    return [moved_by(across[dx + 1], dy * width, factors[dy + 1][1]) for dy, dx in SHIFTS]


def pool_pattern():
    cell = lax.broadcasted_iota(jnp.int32, (512, 128), 0)
    block = lax.broadcasted_iota(jnp.int32, (512, 128), 1)
    at = 16 * lax.shift_right_logical(cell, 6) + lax.shift_right_logical(cell & 31, 1)
    return jnp.where(at == block, 0.125, 0.0).astype(BF16)


def silu_parts(v):
    s = 0.5 + 0.5 * jnp.tanh(0.5 * v)
    return v * s, s


def band_maps():
    to_kernel = np.zeros((4, 256, 108), np.float32)
    to_flat = np.zeros((4, 256, 128), np.float32)
    for p in range(4):
        for s in range(9):
            for dz in range(3):
                q = p + dz - 1
                for ci in range(4):
                    if 0 <= q <= 3:
                        row = 16 * s + 4 * q + ci
                    else:
                        row = 144 + 8 * s + (0 if q < 0 else 4) + ci
                    tap = 9 * dz + s
                    to_kernel[p, row, 4 * tap + ci] = 1
                    to_flat[p, row, 64 * (ci // 2) + 27 * (ci % 2) + tap] = 1
    return to_kernel, to_flat.reshape(1024, 128)


def prepare_body(
    vol_hbm, cot_hbm, *refs,
):
    weights, (next_ref, near_ref, far_next_ref, far_near_ref) = refs[:4], refs[4:8]
    kept, (vol_ref, cot_ref, cells_ref, sems) = refs[8:12], refs[12:]
    me = lax.axis_index("space")
    odd, upper = me % 2 == 1, (me // 2) % 2 == 1
    vol_copy = pltpu.make_async_copy(vol_hbm, vol_ref, sems.at[0])
    cot_copy = pltpu.make_async_copy(cot_hbm, cot_ref, sems.at[1])
    vol_copy.start()
    cot_copy.start()
    copies = [
        pltpu.make_async_copy(src, dst, sems.at[2 + i])
        for i, (src, dst) in enumerate(zip(weights, kept))
    ]
    for copy in copies:
        copy.start()
    vol_copy.wait()
    cin, planes, width = vol_ref.shape[1:4]
    for plane in range(planes):
        for ch in range(cin):
            at = (plane * cin + ch) * width
            cells_ref[at : at + width] = vol_ref[0, ch, plane].astype(F32)
    count = planes * cin
    blocks = []
    for b in range(4):
        lines = [cells_ref[pl.ds(8 * b + y, count, stride=width), :] for y in range(8)]
        rows = jnp.concatenate(lines, axis=1)
        near_ref[count * b : count * b + count] = rows.astype(BF16)
        next_ref[count * b : count * b + count] = rows.astype(BF16)
        blocks.append(rows)
    halves = [jnp.concatenate(blocks[2 * m : 2 * m + 2], axis=1) for m in range(2)]
    top = lax.broadcasted_iota(jnp.int32, (8, HALF), 0) < 4
    first = jnp.where(top, halves[0][0:8], pltpu.roll(halves[1][0:8], 4, 0))
    last = jnp.where(top, pltpu.roll(halves[0][8:16], 4, 0), halves[1][8:16])
    far_near_ref[...] = jnp.where(upper, first, last).astype(BF16)
    far_next_ref[...] = jnp.where(upper, last, first).astype(BF16)
    cot_copy.wait()
    cot = cot_ref[0].astype(F32)
    cots = (cot[:, 0, :], cot[:, 1, :])
    near_ref[64:128] = jnp.where(odd, cots[0], cots[1]).astype(BF16)
    next_ref[64:128] = jnp.where(odd, cots[1], cots[0]).astype(BF16)
    for copy in copies:
        copy.wait()


def sum_body(parts_ref, total_ref):
    total = parts_ref[0].astype(F32)
    for i in range(1, parts_ref.shape[0]):
        total = total + parts_ref[i].astype(F32)
    total_ref[...] = total


def finish_body(mine_ref, other_ref, one_ref, two_ref):
    total = mine_ref[...] + other_ref[...]
    share = total.shape[0] // 2
    total = jnp.concatenate([total[0:share], total[share:]], axis=1)
    two_ref[...] = jnp.concatenate([total[r, 0:864] for r in range(share)])
    one = total[:, ONE_AT : ONE_AT + 54] + total[:, ONE_AT + 64 : ONE_AT + 118]
    one_ref[...] = jnp.concatenate([one[r] for r in range(share)])


def unfold(block, rows):
    return jnp.concatenate([block[rows * b : rows * b + rows] for b in range(4)], axis=1)


def pool_sums(sums, pattern):
    rows = sums.shape[0]
    high = sums.astype(BF16)
    low = (sums - high.astype(F32)).astype(BF16)
    halves = [part[:, 512 * m : 512 * m + 512] for part in (high, low) for m in range(2)]
    out = dot(jnp.concatenate(halves, axis=0), pattern)
    out = out[0 : 2 * rows] + out[2 * rows : 4 * rows]
    return jnp.concatenate([out[0:rows], out[rows : 2 * rows]], axis=1)


def spread_cells(field, pattern):
    rows = field.shape[0]
    high = field.astype(BF16)
    low = (field - high.astype(F32)).astype(BF16)
    halves = [
        jnp.concatenate([part[:, 128 * m : 128 * m + 128] for part in (high, low)], axis=1)
        for m in range(2)
    ]
    out = dot(jnp.concatenate(halves, axis=0), jnp.concatenate([pattern, pattern], axis=1), NT)
    return jnp.concatenate([out[0:rows], out[rows : 2 * rows]], axis=1)


def spread_taps(taps, half):
    factors = inside(half * half, half)
    total = None
    for dx in (-1, 0, 1):
        column = None
        for dy in (-1, 0, 1):
            s = 3 * (1 - dy) + (1 - dx)
            part = moved_by(taps[32 * s : 32 * s + 32], dy * half, factors[dy + 1][1])
            column = part if column is None else column + part
        column = moved_by(column, dx, factors[dx + 1][0])
        total = column if total is None else total + column
    return total


def inner_body(
    count,
    own_next_ref, own_near_ref, next_ref, near_ref, k1_ref, k2_ref, to_kernel_ref, to_flat_ref,
    feat_ref, send_ref, part_ref, pre_ref, act_ref, pre_two_ref, far_one_ref, far_two_ref,
    term_ref, pair_ref, rows_ref, out_ref,
):
    slabs = lax.axis_size("space")
    me = lax.axis_index("space")
    half = 16

    odd = me % 2 == 1
    near, following = near_ref[0:64], next_ref[0:64]
    slabs_of = (
        unfold(jnp.where(odd, near, following), 16),
        unfold(own_near_ref[0:64], 16),
        unfold(jnp.where(odd, following, near), 16),
    )
    left, own, right = (slab.astype(F32) for slab in slabs_of)
    top = lax.broadcasted_iota(jnp.int32, (8, LANES), 0) < 4
    edges = (
        jnp.where(top, 0.0, pltpu.roll(own[0:8], 4, 0)),
        jnp.where(top, pltpu.roll(left[8:16], 4, 0), pltpu.roll(right[0:8], 4, 0)),
        jnp.where(top, pltpu.roll(own[8:16], 4, 0), 0.0),
    )
    moved_edges = all_shifts(jnp.concatenate(edges, axis=0), 2 * half)
    moved = all_shifts(jnp.concatenate(slabs_of, axis=0), 2 * half)
    patches = []
    for g in range(3):
        rows = [m[8 * g : 8 * g + 8] for m in moved_edges] + [jnp.zeros((40, LANES), F32)]
        rows = jnp.concatenate(rows, axis=0).astype(BF16)
        patches.append(jnp.concatenate([*(m[16 * g : 16 * g + 16] for m in moved), rows], axis=0))

    k1t = k1_ref[...].astype(F32).reshape(108, 32).T.astype(BF16)
    two_by_dz = jnp.concatenate(
        [k2_ref[288 * dz : 288 * dz + 288].astype(F32).T for dz in range(3)], axis=0
    ).astype(BF16)
    banded = jnp.concatenate(
        [dot(k1t, to_kernel_ref[p], NT).astype(BF16) for p in range(4)], axis=0
    )
    far_one_ref[...] = jnp.concatenate(
        [dot(k1t, to_kernel_ref[p, 144:216], NT).astype(BF16) for p in (0, 3)], axis=0
    )
    far_two_ref[0] = two_by_dz[0:64]
    far_two_ref[1] = two_by_dz[128:192]
    pattern = pool_pattern()

    pre = dot(banded, patches[0])
    pre_ref[0:32] = pre[0:32]
    act, s = silu_parts(pre[32:128])
    act_ref[0:32] = act[0:32]
    slopes = [(s + act * (1.0 - s))[32:96]]
    sums = [act[32:64] + act[64:96]]
    act, s = silu_parts(dot(banded, patches[1]))
    slopes.append(s + act * (1.0 - s))
    sums += [act[0:32] + act[32:64], act[64:96] + act[96:128]]
    pre = dot(banded, patches[2])
    pre_ref[32:64] = pre[96:128]
    act, s = silu_parts(pre[0:96])
    act_ref[32:64] = act[64:96]
    slopes.append((s + act * (1.0 - s))[0:64])
    sums += [act[0:32] + act[32:64]]
    pooled = pool_sums(jnp.concatenate(sums, axis=0), pattern)
    plane = lax.shift_right_logical(lax.broadcasted_iota(jnp.int32, pooled.shape, 0), 5)
    real = ((plane > 0) | (me > 0)) & ((plane < 3) | (me < slabs - 1))
    pooled = jnp.where(real, pooled, 0.0).astype(BF16)

    moved = all_shifts(pooled, half)
    planes = [jnp.concatenate([m[32 * q : 32 * q + 32] for m in moved], axis=0) for q in range(4)]
    pre_two = [None] * 4
    for q, columns in enumerate(planes):
        by_dz = dot(two_by_dz, columns)
        for dz in range(3):
            p = q + 1 - dz
            if 0 <= p < 4:
                part = by_dz[64 * dz : 64 * dz + 64]
                pre_two[p] = part if pre_two[p] is None else pre_two[p] + part
    pre_two_ref[0], pre_two_ref[1] = pre_two[0], pre_two[3]

    own_cots = own_near_ref[64:128].astype(F32), own_next_ref[64:128].astype(F32)
    cots = jnp.where(odd, *own_cots), jnp.where(odd, *own_cots[::-1])
    deltas = []
    for p in range(2):
        act, s = silu_parts(pre_two[p + 1])
        feat_ref[p] = act.astype(BF16)
        deltas.append((cots[p] * (s + act * (1.0 - s))).astype(BF16))

    share = 64 // slabs

    def place(columns, at):
        for first in range(0, columns.shape[1], 128):
            tile = (at + first) % HALF // 128
            rows_ref[tile] = columns[:, first : first + 128]
            for r in range(share):
                target = pl.ds((at + first) // HALF * share + r, slabs, stride=2 * share)
                out_ref[tile, target, :] = rows_ref[tile, pl.ds(r, slabs, stride=share), :]

    both = jnp.concatenate(deltas, axis=0)
    products = [dot(columns, both, NT) for columns in planes]
    for dz in range(3):
        term = products[dz] + pltpu.roll(products[dz + 1], 64, 1)
        term_ref[288 * dz : 288 * dz + 288] = term * (1.0 / math.sqrt(count // 8))
    rows = jnp.concatenate([term_ref[pl.ds(ch, 27, stride=32), :] for ch in range(32)], axis=0)
    place(rows[0:HALF].T[0:64], 0)
    rows = jnp.concatenate([rows[HALF:864], jnp.zeros((ONE_AT - 864, 128), F32)], axis=0)
    place(rows.T[0:64], HALF)

    grads = []
    for p in range(-1, 3):
        sources = [q for q in range(2) if abs(q - p) < 2]
        taps = [k2_ref[288 * (1 + p - q) : 288 * (1 + p - q) + 288] for q in sources]
        given = jnp.concatenate([deltas[q] for q in sources], axis=0)
        grads.append(spread_taps(dot(jnp.concatenate(taps, axis=1), given), half))
    part_ref[0], part_ref[1] = grads[1], grads[2]

    grads = jnp.where(real, jnp.concatenate(grads, axis=0), 0.0)
    spread = spread_cells(grads, pattern)
    spread = [spread[32 * q : 32 * q + 32] for q in range(4)]
    wide = []
    for g, under in enumerate(((0,), (1, 2), (3,))):
        field = jnp.concatenate([spread[q] for q in under for _ in range(2)], axis=0)
        wide.append(dot((field * slopes[g]).astype(BF16), patches[g], NT))
    wide = wide[1] + jnp.concatenate([wide[2], wide[0]], axis=0)
    wide = jnp.concatenate([wide[32 * p : 32 * p + 32] for p in range(4)], axis=1)
    high = wide.astype(BF16)
    low = (wide - high.astype(F32)).astype(BF16)
    term_one = dot(jnp.concatenate([high, low], axis=0), to_flat_ref[...])
    term_one = (term_one[0:32] + term_one[32:64]) * (1.0 / math.sqrt(count))
    for h, half_row in enumerate((term_one, pltpu.roll(term_one, 64, 1))):
        pair_ref[pl.ds(h, 32, stride=2), :] = half_row
    rows = pair_ref[...]
    rounded = rows.astype(BF16).astype(F32)
    lane = lax.broadcasted_iota(jnp.int32, rows.shape, 1)
    pair = jnp.where(lane < 64, rounded, pltpu.roll(rows - rounded, 64, 1))
    place(pair, ONE_AT)
    for tile in range(4):
        send_ref[:, 128 * tile : 128 * tile + 128] = out_ref[tile].astype(BF16)


def outer_body(
    far_next_ref, far_near_ref, next_ref, near_ref, k2_ref,
    feat_ref, part_ref, pre_ref, act_ref, pre_two_ref, far_one_ref, far_two_ref,
    feat_out, pgrad_out,
):
    slabs = lax.axis_size("space")
    me = lax.axis_index("space")
    half = 16
    odd, upper = me % 2 == 1, (me // 2) % 2 == 1
    pattern = pool_pattern()
    far_near, far_next = far_near_ref[...].astype(F32), far_next_ref[...].astype(F32)
    far_left, far_right = jnp.where(upper, far_near, far_next), jnp.where(upper, far_next, far_near)
    top = lax.broadcasted_iota(jnp.int32, (8, LANES), 0) < 4
    edge = jnp.where(
        top,
        jnp.concatenate([far_left, pltpu.roll(far_left, 4, 0)], axis=1),
        jnp.concatenate([pltpu.roll(far_right, 4, 0), far_right], axis=1),
    )
    patches = jnp.concatenate(all_shifts(edge, 2 * half), axis=0).astype(BF16)
    act, _ = silu_parts(pre_ref[...] + dot(far_one_ref[...], patches))
    pooled = pool_sums(act_ref[...] + act, pattern)
    plane = lax.shift_right_logical(lax.broadcasted_iota(jnp.int32, pooled.shape, 0), 5)
    real = ((plane > 0) | (me > 0)) & ((plane < 1) | (me < slabs - 1))
    pooled = jnp.where(real, pooled, 0.0).astype(BF16)
    moved = all_shifts(pooled, half)

    near, following = near_ref[64:128].astype(F32), next_ref[64:128].astype(F32)
    cots = jnp.where(odd, near, following), jnp.where(odd, following, near)
    for p in range(2):
        columns = jnp.concatenate([m[32 * p : 32 * p + 32] for m in moved], axis=0)
        pre = pre_two_ref[p] + dot(far_two_ref[p], columns)
        act, s = silu_parts(pre)
        delta = (cots[p] * (s + act * (1.0 - s))).astype(BF16)
        taps = dot(k2_ref[576 * (1 - p) : 576 * (1 - p) + 288], delta)
        pgrad_out[0, :, p, :] = (part_ref[p] + spread_taps(taps, half)).astype(BF16)
        feat_out[0, :, p, :] = feat_ref[p]


def on_device(volumes, kernel_one, kernel_two, cotangent):
    _, cin, planes, width, _ = volumes.shape
    half = width // 2
    slabs = lax.axis_size("space")
    copies = lax.axis_size("dp")
    count = copies * planes * slabs * width * width

    to_kernel, to_flat = band_maps()
    weights = (
        jnp.transpose(kernel_one, (2, 3, 4, 1, 0)).reshape(27, 4, 32),
        jnp.transpose(kernel_two, (2, 3, 4, 1, 0)).reshape(864, 64),
        jnp.asarray(to_kernel, BF16),
        jnp.asarray(to_flat, BF16),
    )

    def in_hbm(*arrays):
        return [pltpu.with_memory_space_constraint(x, pltpu.HBM) for x in arrays]

    inputs = in_hbm(volumes, cotangent, *weights)
    hbm = pl.BlockSpec(memory_space=pltpu.HBM)
    limit = pltpu.CompilerParams(vmem_limit_bytes=48 * 1024 * 1024)
    whole = jax.ShapeDtypeStruct((128, width * width // 4), BF16)
    part = jax.ShapeDtypeStruct((2 * cin, width * width // 2), BF16)
    to_next, to_near, to_far_next, to_far_near, *weights = pl.pallas_call(
        prepare_body,
        out_shape=(
            whole, whole, part, part, *(jax.ShapeDtypeStruct(w.shape, BF16) for w in weights)
        ),
        in_specs=[hbm] * len(inputs),
        scratch_shapes=[
            pltpu.VMEM(volumes.shape, BF16),
            pltpu.VMEM(cotangent.shape, BF16),
            pltpu.VMEM((planes * cin * width, width), F32),
            pltpu.SemaphoreType.DMA((len(inputs),)),
        ],
        compiler_params=limit,
    )(*inputs)

    def swap(block, pairs):
        pairs = [p for p in pairs if max(p) < slabs]
        return lax.ppermute(block, "space", pairs + [(t, f) for f, t in pairs])

    evens = range(0, slabs, 2)
    fours = [i + j for i in range(0, slabs, 4) for j in range(2)]
    following = swap(to_next, [(i + 1, i + 2) for i in evens])
    near = swap(to_near, [(i, i + 1) for i in evens])
    far_next = swap(to_far_next, [(i + 2, i + 4) for i in fours])

    cells = half * half
    shapes = {
        "features": ((2, 64, cells), BF16),
        "send": ((128, HALF), BF16),
        "part": ((2, 32, cells), F32),
        "pre": ((64, LANES), F32),
        "act": ((64, LANES), F32),
        "pre_two": ((2, 64, cells), F32),
        "far_one": ((64, 72), BF16),
        "far_two": ((2, 64, 288), BF16),
    }
    feat, send, *inner = pl.pallas_call(
        functools.partial(inner_body, count),
        out_shape=tuple(jax.ShapeDtypeStruct(*x) for x in shapes.values()),
        scratch_shapes=[
            pltpu.VMEM(shape, F32) for shape in ((864, 128), (64, 128), (4, 64, 128), (4, 128, 128))
        ],
        compiler_params=limit,
        cost_estimate=pl.CostEstimate(flops=2 * 10**10, bytes_accessed=2 * 10**6, transcendentals=10**6),
    )(to_next, to_near, following, near, *weights)
    share = 64 // slabs
    send, far_next = lax.optimization_barrier((send.reshape(slabs, 2 * share, HALF), far_next))
    send = pltpu.with_memory_space_constraint(send, pltpu.VMEM)
    parts = lax.all_to_all(send, "space", 0, 0, tiled=True)
    _, to_far_near = lax.optimization_barrier((send, to_far_near))
    far_near = swap(to_far_near, [(i, i + 2) for i in fours])
    features, pooled_grad = pl.pallas_call(
        outer_body,
        out_shape=(
            jax.ShapeDtypeStruct((1, 64, 2, cells), BF16),
            jax.ShapeDtypeStruct((1, 32, 2, cells), BF16),
        ),
        compiler_params=limit,
        cost_estimate=pl.CostEstimate(flops=2 * 10**9, bytes_accessed=10**6, transcendentals=10**5),
    )(far_next, far_near, following, near, weights[1], feat, *inner)
    parts, features, pooled_grad = lax.optimization_barrier((parts, features, pooled_grad))
    total = pl.pallas_call(
        sum_body,
        out_shape=jax.ShapeDtypeStruct(parts.shape[1:], F32),
        compiler_params=limit,
    )(parts)

    def other_core(block, step):
        return lax.ppermute(block, "dp", [(i, i ^ step) for i in range(copies)])

    step = 1
    while 2 * step < copies:
        total = total + other_core(total, step)
        step *= 2
    other = other_core(total, step)
    grad_one, grad_two = pl.pallas_call(
        finish_body,
        out_shape=(jax.ShapeDtypeStruct((share * 54,), F32), jax.ShapeDtypeStruct((share * 864,), F32)),
        compiler_params=limit,
    )(total, other)
    return (features, pooled_grad, grad_one, grad_two)


def solution(mesh):
    in_specs = (P("dp", None, "space", None, None), P(), P(), P("dp", None, "space", None))
    out_specs = (P("dp", None, "space", None), P("dp", None, "space", None), P("space"), P("space"))
    return jax.shard_map(
        on_device, mesh=mesh, in_specs=in_specs, out_specs=out_specs, check_vma=False
    )
```
